32 devices in a mesh: dp: 8 (over y, x, core), head: 4 (over z).
Axes of the slice: x: 2, y: 2, z: 4, core: 2. Of those that a mesh axis runs over, the one named last changes fastest.
Arguments:
- inputs: bfloat16 [16384, 768], P(('dp', 'head')), may hold values from -6 to 6
- seg_lengths: int32 [8, 8], P('dp'), may hold values from 0 to 1024, as said below
- ln1_gain: bfloat16 [768], replicated, may hold values from 0.5 to 1.5
- ln1_bias: bfloat16 [768], replicated, may hold values from -1.75 to 1.75
- qkv_weight: bfloat16 [768, 3, 768], P(None, None, 'head'), may hold values from -0.3125 to 0.3125
- qkv_bias: bfloat16 [3, 768], P(None, 'head'), may hold values from -1.75 to 1.75
- out_weight: bfloat16 [768, 768], P('head'), may hold values from -0.875 to 0.875
- out_bias: bfloat16 [768], replicated, may hold values from -1.75 to 1.75
- mem_mu: bfloat16 [12, 512], P('head'), may hold values from -0.25 to 0.25
- mem_sig: bfloat16 [12, 512], P('head'), may hold values from -0.25 to 0.25
- ln2_gain: bfloat16 [768], replicated, may hold values from 0.5 to 1.5
- ln2_bias: bfloat16 [768], replicated, may hold values from -1.75 to 1.75
- ff_in: bfloat16 [768, 3072], P(None, 'head'), may hold values from -0.21875 to 0.21875
- ff_in_bias: bfloat16 [3072], P('head'), may hold values from -1.75 to 1.75
- ff_out: bfloat16 [3072, 768], P('head'), may hold values from -0.109375 to 0.109375
- ff_out_bias: bfloat16 [768], replicated, may hold values from -1.75 to 1.75
- cotangent: bfloat16 [16384, 768], P(('dp', 'head')), may hold values from -6 to 6
Outputs:
- outputs: bfloat16 [16384, 768], P(('dp', 'head'))
- input_grad: bfloat16 [16384, 768], P(('dp', 'head'))
- ln1_gain_grad: float32 [768], replicated
- ln1_bias_grad: float32 [768], replicated
- qkv_weight_grad: float32 [768, 3, 768], P(None, None, 'head')
- qkv_bias_grad: float32 [3, 768], P(None, 'head')
- out_weight_grad: float32 [768, 768], P('head')
- out_bias_grad: float32 [768], replicated
- mem_mu_grad: float32 [12, 512], P('head')
- mem_sig_grad: float32 [12, 512], P('head')
- ln2_gain_grad: float32 [768], replicated
- ln2_bias_grad: float32 [768], replicated
- ff_in_grad: float32 [768, 3072], P(None, 'head')
- ff_in_bias_grad: float32 [3072], P('head')
- ff_out_grad: float32 [3072, 768], P('head')
- ff_out_bias_grad: float32 [768], replicated
The draws below stay inside these ranges and needn't reach their ends.
Inputs may be any that keep to these rules, and one draw needn't show every extreme that they name: `seg_lengths`: each row lists one group's segments in order, four slots for each aligned run of 1024 tokens: lengths of 1, 2 or 4 times 256 that fill the run, then zeros; every group has a segment of 1024.
All inputs are finite; a program needn't handle non-finite values.
Results may differ from the reference program's by a relative error of at most 0.019.
The reference program's roundings to bfloat16 on the way count: a program that leaves them out, or rounds other values in their place, can miss the bound.
Values may be sent and summed in bfloat16 or wider, within the bound.
A program may use at most 256 MiB of HBM per device.

```python
import math
import jax
import jax.numpy as jnp
import numpy as np
from jax import lax

D = 768
HEADS = 12
HEAD_DIM = 64
FF = 3072
BASIS = 512
SEG_UNIT = 256
GROUP_ROWS = 2048
TOKENS = 16384
N_DP = 8


PATTERNS = np.array([[4, 0, 0, 0], [2, 2, 0, 0], [2, 1, 1, 0], [1, 2, 1, 0], [1, 1, 2, 0], [1, 1, 1, 1]], dtype=np.int32)


def draw_seg_lengths(key, part):
    key = jax.random.fold_in(key, 7)
    blocks = GROUP_ROWS // (4 * SEG_UNIT)
    first_key, second_key = jax.random.split(key)
    pattern = jax.random.randint(first_key, (N_DP, blocks), 0, 6)
    forced = jax.random.randint(second_key, (N_DP, 1), 0, blocks)
    pattern = jnp.where(jnp.arange(blocks)[None, :] == forced, 0, pattern)
    table = jnp.array(PATTERNS)
    return (table[pattern] * SEG_UNIT).reshape(N_DP, blocks * 4).astype(jnp.int32)


def level_of(key, extent, pieces, low, high):
    def one(dim, blocks):
        steps = jax.random.uniform(jax.random.fold_in(jax.random.fold_in(key, 6), dim), (blocks,), jnp.float32, low / len(pieces), high / len(pieces))
        return jnp.repeat(jnp.exp(steps), extent[dim] // blocks).reshape((-1,) + (1,) * (len(extent) - dim - 1))

    level = one(*pieces[0])
    for cut in pieces[1:]:
        level = level * one(*cut)
    return level


def bell_draw(key, extent, scale, most, cuts=(), kind=jnp.bfloat16):
    drawn = scale * jax.random.normal(key, extent, jnp.float32)
    if cuts:
        drawn = drawn * level_of(key, extent, cuts, -0.22, 0.18)
    return jnp.clip(drawn, -most, most).astype(kind)


def setup_inputs(seed: int = 0) -> dict:
    key_list = jax.random.split(jax.random.key(seed), 18)
    return {
        "inputs": bell_draw(key_list[0], (TOKENS, D), 1.0, 6.0, ((0, 32),)),
        "seg_lengths": draw_seg_lengths(jax.random.fold_in(key_list[17], 71), 0),
        "ln1_gain": jnp.clip(1.0 + 0.1 * jax.random.normal(key_list[2], (D,), jnp.float32), 0.5, 1.5).astype(jnp.bfloat16),
        "ln1_bias": bell_draw(key_list[3], (D,), 0.3, 1.75),
        "qkv_weight": bell_draw(key_list[4], (D, 3, D), (D // 2) ** -0.5, 0.3125, ((2, 4),)),
        "qkv_bias": bell_draw(key_list[5], (3, D), 0.3, 1.75, ((1, 4),)),
        "out_weight": bell_draw(key_list[6], (D, D), (D // 16) ** -0.5, 0.875, ((0, 4),)),
        "out_bias": bell_draw(key_list[7], (D,), 0.3, 1.75),
        "mem_mu": bell_draw(key_list[8], (HEADS, BASIS), BASIS ** -0.5, 0.25, ((0, 4),)),
        "mem_sig": bell_draw(key_list[9], (HEADS, BASIS), BASIS ** -0.5, 0.25, ((0, 4),)),
        "ln2_gain": jnp.clip(1.0 + 0.1 * jax.random.normal(key_list[10], (D,), jnp.float32), 0.5, 1.5).astype(jnp.bfloat16),
        "ln2_bias": bell_draw(key_list[11], (D,), 0.3, 1.75),
        "ff_in": bell_draw(key_list[12], (D, FF), D ** -0.5, 0.21875, ((1, 4),)),
        "ff_in_bias": bell_draw(key_list[13], (FF,), 0.3, 1.75, ((0, 4),)),
        "ff_out": bell_draw(key_list[14], (FF, D), FF ** -0.5, 0.109375, ((0, 4),)),
        "ff_out_bias": bell_draw(key_list[15], (D,), 0.3, 1.75),
        "cotangent": bell_draw(key_list[16], (TOKENS, D), 1.0, 6.0, ((0, 32),)),
    }


TAU = 0.75
RIDGE = 0.5
EPSILON = 1e-05
SPREAD = 1.0 / 64.0
HIGHEST = lax.Precision.HIGHEST

@jax.custom_vjp
def low(v):
    return lax.optimization_barrier(v.astype(jnp.bfloat16)).astype(jnp.float32)

@jax.custom_vjp
def low_back(v):
    return v

def low_keep(v):
    return (low(v), None)

def low_pass(kept, grad):
    return (grad,)

def back_keep(v):
    return (v, None)

def back_low(kept, grad):
    return (low(grad),)
low.defvjp(low_keep, low_pass)
low_back.defvjp(back_keep, back_low)

def basis_tables(count, dtype):
    centres = jnp.arange(count).astype(dtype) / (count - 1)
    width = 1.0 / count
    apart = centres[:, None] - centres[None, :]
    gram = jnp.exp(-apart * apart / (4.0 * width * width)) + RIDGE * jnp.eye(count, dtype=dtype)
    factor = jnp.linalg.cholesky(gram)
    solve = jax.scipy.linalg.cho_solve((factor, True), jnp.eye(count, dtype=dtype))
    samples = (jnp.arange(count).astype(dtype) + 0.5) / count
    near_gap = TAU * samples[:, None] - centres[None, :]
    far_gap = samples[:, None] - centres[None, :]
    near = jnp.exp(-near_gap * near_gap / (2.0 * width * width))
    far = jnp.exp(-far_gap * far_gap / (2.0 * width * width))
    contract = jnp.dot(near.T, far, precision=HIGHEST) * (TAU / (count * width * math.sqrt(math.pi)))
    advance = jnp.dot(solve, contract, precision=HIGHEST)
    return (centres, solve, advance)

def segment_layout(lengths, rows, unit):
    units = rows // unit
    slot_units = (lengths // unit).astype(jnp.int32)
    ends = jnp.cumsum(slot_units).astype(jnp.int32)
    starts = ends - slot_units
    unit_index = jnp.arange(units, dtype=jnp.int32)
    member = (unit_index[:, None] >= starts[None, :]) & (unit_index[:, None] < ends[None, :])
    slot_ids = jnp.arange(lengths.shape[0], dtype=jnp.int32)
    unit_slot = lax.optimization_barrier(jnp.sum(jnp.where(member, slot_ids[None, :], 0), axis=1)).astype(jnp.int32)
    unit_start = (lax.optimization_barrier(jnp.sum(jnp.where(member, starts[None, :], 0), axis=1)) * unit).astype(jnp.int32)
    unit_length = lax.optimization_barrier(jnp.sum(jnp.where(member, lengths[None, :], 0), axis=1)).astype(jnp.int32)
    row_index = jnp.arange(rows, dtype=jnp.int32)
    row_slot = jnp.repeat(unit_slot, unit)
    row_pos = row_index - jnp.repeat(unit_start, unit)
    row_len = jnp.repeat(unit_length, unit)
    return (member, row_slot, row_pos, row_len)

def memory_read(queries, keys, values, mu_weight, sig_weight, lengths, layout, tables):
    centres, solve, advance = tables
    member, row_slot, row_pos, row_len = layout
    rows, heads, depth = queries.shape
    count = centres.shape[0]
    units = member.shape[0]
    unit = rows // units
    kind = queries.dtype
    member_f = member.astype(kind)
    width = 1.0 / count
    place = TAU + (1.0 - TAU) * (row_pos.astype(kind) + 0.5) / row_len.astype(kind)
    gap = place[:, None] - centres[None, :]
    psi = jnp.exp(-gap * gap / (2.0 * width * width))
    stacked = jnp.concatenate([keys.reshape(rows, heads * depth), values.reshape(rows, heads * depth)], axis=1)
    unit_terms = jnp.einsum('uin,uic->unc', psi.reshape(units, unit, count), stacked.reshape(units, unit, -1), precision=HIGHEST)
    slot_terms = jnp.einsum('us,unc->snc', member_f, unit_terms, precision=HIGHEST)
    scale = (1.0 - TAU) / (jnp.maximum(lengths, 1).astype(kind) * (width * math.sqrt(math.pi)))
    projected = jnp.einsum('mn,snc->smc', solve, slot_terms, precision=HIGHEST) * scale[:, None, None]

    def advance_step(state, inputs):
        term, length = inputs
        updated = jnp.dot(advance, state, precision=HIGHEST) + term
        return (jnp.where(length > 0, updated, state), state)
    _, before = lax.scan(advance_step, jnp.zeros_like(projected[0]), (projected, lengths))
    unit_memory = jnp.einsum('us,snc->unc', member_f, before, precision=HIGHEST)
    memory_keys = unit_memory[:, :, :heads * depth].reshape(units, count, heads, depth)
    memory_values = unit_memory[:, :, heads * depth:].reshape(units, count, heads, depth)
    query_units = queries.reshape(units, unit, heads, depth)
    basis_scores = jnp.einsum('uihd,ujhd->uihj', query_units, memory_keys, precision=HIGHEST) / math.sqrt(depth)
    location = jax.nn.sigmoid(jnp.einsum('uihj,hj->uih', basis_scores, mu_weight, precision=HIGHEST))
    variance = jax.nn.softplus(jnp.einsum('uihj,hj->uih', basis_scores, sig_weight, precision=HIGHEST)) * SPREAD + width * width
    offset = location[..., None] - centres
    density = jnp.sqrt(width * width / variance)[..., None] * jnp.exp(-offset * offset / (2.0 * variance[..., None]))
    gathered = jnp.einsum('uihj,ujhd->uihd', density, memory_values, precision=HIGHEST)
    return gathered.reshape(rows, heads, depth)

def norm_rows(values, gain, shift):
    centred = values - lax.optimization_barrier(jnp.mean(values, axis=-1, keepdims=True))
    inverse = lax.rsqrt(lax.optimization_barrier(jnp.mean(centred * centred, axis=-1, keepdims=True)) + EPSILON)
    return centred * inverse * gain + shift

def block_attention(queries, keys, values, row_slot, block):
    rows, heads, depth = queries.shape
    count = rows // block
    index = jnp.arange(block, dtype=jnp.int32)

    def one_block(args):
        query_part, key_part, value_part, slot_part = args
        scores = low_back(jnp.einsum('qhd,khd->hqk', query_part, key_part, precision=HIGHEST) / math.sqrt(depth))
        allowed = (slot_part[:, None] == slot_part[None, :]) & (index[:, None] >= index[None, :])
        scores = jnp.where(allowed[None], scores, -1e+30)
        probs = jax.nn.softmax(scores, axis=-1)
        return jnp.einsum('hqk,khd->qhd', low(probs), value_part, precision=HIGHEST)
    shaped = (queries.reshape(count, block, heads, depth), keys.reshape(count, block, heads, depth), values.reshape(count, block, heads, depth), row_slot.reshape(count, block))
    return lax.map(jax.checkpoint(one_block), shaped).reshape(rows, heads, depth)

def group_forward(source, lengths, params, tables):
    ln1_gain, ln1_bias, qkv_weight, qkv_bias, out_weight, out_bias, mem_mu, mem_sig, ln2_gain, ln2_bias, ff_in, ff_in_bias, ff_out, ff_out_bias = params
    rows = source.shape[0]
    layout = segment_layout(lengths, rows, SEG_UNIT)
    first = low(norm_rows(source, ln1_gain, ln1_bias))
    projected = jnp.dot(first.astype(jnp.float32), qkv_weight.reshape(D, 3 * D).astype(jnp.float32), precision=HIGHEST, preferred_element_type=jnp.float32) + qkv_bias.reshape(3 * D)
    qkv = low(low_back(projected)).reshape(rows, 3, HEADS, HEAD_DIM)
    queries, keys, values = (qkv[:, 0], qkv[:, 1], qkv[:, 2])
    discrete = block_attention(queries, keys, values, layout[1], 4 * SEG_UNIT)
    gathered = memory_read(queries, keys, values, mem_mu, mem_sig, lengths, layout, tables)
    mixed = low(low_back(discrete + gathered)).reshape(rows, D)
    attended = low_back(jnp.dot(mixed.astype(jnp.float32), out_weight.astype(jnp.float32), precision=HIGHEST, preferred_element_type=jnp.float32))
    residual = source + attended + out_bias
    second = low(norm_rows(residual, ln2_gain, ln2_bias))
    hidden = low_back(jnp.dot(second.astype(jnp.float32), ff_in.astype(jnp.float32), precision=HIGHEST, preferred_element_type=jnp.float32) + ff_in_bias)
    activation = low(jax.nn.gelu(hidden, approximate=True))
    return residual + jnp.dot(activation.astype(jnp.float32), ff_out.astype(jnp.float32), precision=HIGHEST, preferred_element_type=jnp.float32) + ff_out_bias

def reference(inputs, seg_lengths, ln1_gain, ln1_bias, qkv_weight, qkv_bias, out_weight, out_bias, mem_mu, mem_sig, ln2_gain, ln2_bias, ff_in, ff_in_bias, ff_out, ff_out_bias, cotangent):
    params = tuple((weight.astype(jnp.float32) for weight in (ln1_gain, ln1_bias, qkv_weight, qkv_bias, out_weight, out_bias, mem_mu, mem_sig, ln2_gain, ln2_bias, ff_in, ff_in_bias, ff_out, ff_out_bias)))

    def forward(source, weights):
        tables = basis_tables(BASIS, jnp.float32)
        groups = source.reshape(N_DP, GROUP_ROWS, D)

        def one_group(args):
            group_rows, lengths = args
            return group_forward(group_rows, lengths, weights, tables)
        return lax.map(jax.checkpoint(one_group), (groups, seg_lengths)).reshape(TOKENS, D)
    outputs, pullback = jax.vjp(forward, inputs.astype(jnp.float32), params)
    grad_source, grads = pullback(cotangent.astype(jnp.float32))
    return (outputs.astype(jnp.bfloat16), grad_source.astype(jnp.bfloat16), grads[0], grads[1], grads[2], grads[3], grads[4], grads[5], grads[6], grads[7], grads[8], grads[9], grads[10], grads[11], grads[12], grads[13])
```

```python
import functools
import math

import jax
import jax.numpy as jnp
import ml_dtypes
import numpy as np
from jax import lax
from jax.experimental import pallas as pl
from jax.experimental.pallas import tpu as pltpu
from jax.sharding import PartitionSpec as P

HEAD_DIM = 64
BASIS = 512
UNIT = 256
LANES = 256
TAU = 0.75
RIDGE = 0.5
EPSILON = 1e-05
SPREAD = 1.0 / 64.0
WIDTH = 1.0 / BASIS
LIVE = BASIS // 2
HIGHEST = lax.Precision.HIGHEST
F32 = jnp.float32
BF16 = jnp.bfloat16


def split_table(table):
    high = table.astype(np.float32).astype(ml_dtypes.bfloat16)
    low = (table.astype(np.float32) - high.astype(np.float32)).astype(ml_dtypes.bfloat16)
    return high, low


@functools.lru_cache(maxsize=None)
def basis_tables():
    centres = np.arange(BASIS) / (BASIS - 1)
    apart = centres[:, None] - centres[None, :]
    gram = np.exp(-apart * apart / (4.0 * WIDTH * WIDTH)) + RIDGE * np.eye(BASIS)
    solve = np.linalg.inv(gram)
    samples = (np.arange(BASIS) + 0.5) / BASIS
    near_gap = TAU * samples[:, None] - centres[None, :]
    far_gap = samples[:, None] - centres[None, :]
    near = np.exp(-near_gap * near_gap / (2.0 * WIDTH * WIDTH))
    far = np.exp(-far_gap * far_gap / (2.0 * WIDTH * WIDTH))
    contract = (near.T @ far) * (TAU / (BASIS * WIDTH * math.sqrt(math.pi)))
    joined = np.concatenate([solve @ contract, solve[:, LIVE:]], axis=1)
    high, low = split_table(joined)
    forward = np.concatenate([high, high, low], axis=1)
    backward = np.concatenate([high.T, high.T, low.T], axis=1)
    return forward, backward


def term_scale(units):
    return (1.0 - TAU) / (WIDTH * math.sqrt(math.pi) * UNIT) / units.astype(F32)


def split3(value):
    high = value.astype(BF16)
    low = (value - high.astype(F32)).astype(BF16)
    return jnp.concatenate([high, low, high], axis=0)


def dot(a, b, contract=((1,), (0,)), precision=None):
    return lax.dot_general(a, b, (contract, ((), ())), precision=precision, preferred_element_type=F32)


def head_rows(heads, width):
    row = lax.broadcasted_iota(jnp.int32, (8, width), 0)
    lane = lax.broadcasted_iota(jnp.int32, (8, width), 1) // HEAD_DIM
    return ((row == lane) | (row == lane + heads)) & (lane < heads)


def read_parts(logits, heads):
    location = 1.0 / (1.0 + jnp.exp(-logits))
    variance = (jnp.maximum(logits, 0.0) + jnp.log1p(jnp.exp(-jnp.abs(logits)))) * SPREAD + WIDTH * WIDTH
    return location[:heads], variance[heads : 2 * heads]


def place_of(index, length):
    return TAU + (1.0 - TAU) * (index.astype(F32) + 0.5) / (length.astype(F32) * UNIT)


def forward_kernel(heads, info, qkv, musig, table, mixed, logsum, states, memory, sums, probe_rows, value_cols, turned, cols):
    u = pl.program_id(0)
    width = heads * HEAD_DIM
    start, length = info[0, u], info[1, u]
    base = pl.multiple_of(u * UNIT, UNIT)
    here = pl.ds(base, UNIT)

    @pl.when(u == 0)
    def _():
        memory[...] = jnp.zeros_like(memory)

    @pl.when((start == u) & (u > 0))
    def _():
        scale = term_scale(info[1, jnp.maximum(u - 1, 0)])
        stacked = jnp.concatenate([memory[...], sums[...] * scale], axis=0)
        memory[...] = dot(table[...], split3(stacked))
        rows = dot(musig[...], memory[:, :LANES], precision=HIGHEST) * (1.0 / math.sqrt(HEAD_DIM))
        probe_rows[...] = jnp.where(head_rows(heads, LANES), rows, 0.0)
        value_cols[...] = memory[:, LANES:].T.astype(BF16)

    @pl.when(start == u)
    def _():
        states[0] = memory[...]
        sums[...] = jnp.zeros_like(sums)

    value_rows = qkv[here, 2 * LANES : 3 * LANES]
    cols[u] = value_rows.astype(F32).T.astype(BF16)

    token = lax.broadcasted_iota(jnp.int32, (LIVE, UNIT), 1) + (u - start) * UNIT
    centre = (lax.broadcasted_iota(jnp.int32, (LIVE, UNIT), 0) + LIVE).astype(F32) / (BASIS - 1)
    gap = place_of(token, length) - centre
    psi = jnp.exp(gap * gap * (-0.5 / (WIDTH * WIDTH)))
    psi_high = psi.astype(BF16)
    psi_low = (psi - psi_high.astype(F32)).astype(BF16)
    pairs = qkv[here, LANES : 3 * LANES]
    sums[...] += dot(psi_high, pairs) + dot(psi_low, pairs)

    query = qkv[here, 0:LANES]
    lane_head = lax.broadcasted_iota(jnp.int32, (UNIT, LANES), 1) // HEAD_DIM

    def attend(blocks):
        first = pl.multiple_of(start * UNIT, UNIT)
        keys = qkv[pl.ds(first, blocks * UNIT), LANES : 2 * LANES]
        causal = lax.broadcasted_iota(jnp.int32, (UNIT, UNIT), 0) <= lax.broadcasted_iota(
            jnp.int32, (UNIT, UNIT), 1
        )
        for h in range(heads):
            own = jnp.where(lane_head == h, query.astype(F32) * (1.0 / math.sqrt(HEAD_DIM)), 0.0).astype(BF16)
            scores = [dot(keys[j * UNIT : (j + 1) * UNIT], own, ((1,), (1,))) for j in range(blocks)]
            scores[-1] = jnp.where(causal, scores[-1], -1e30)
            highest = functools.reduce(jnp.maximum, [jnp.max(s, axis=0, keepdims=True) for s in scores])
            weights = [jnp.exp(s - highest) for s in scores]
            total = sum(jnp.sum(w, axis=0, keepdims=True) for w in weights)
            rows = slice(h * HEAD_DIM, (h + 1) * HEAD_DIM)
            result = sum(dot(cols[start + j, rows], weights[j].astype(BF16)) for j in range(blocks))
            turned[rows] = result * (1.0 / total)
            logsum[h : h + 1] = highest + jnp.log(total)

    for blocks in range(1, 5):
        pl.when(u - start + 1 == blocks)(functools.partial(attend, blocks))

    @pl.when(start > 0)
    def _():
        probes = probe_rows[...]
        high = probes.astype(BF16)
        rest = probes - high.astype(F32)
        mid = rest.astype(BF16)
        low = (rest - mid.astype(F32)).astype(BF16)
        logits = sum(dot(part, query, ((1,), (1,))) for part in (high, mid, low))
        location, variance = read_parts(logits, heads)
        fall = -0.5 / variance
        peak = WIDTH * lax.rsqrt(variance)
        centres = lax.broadcasted_iota(jnp.int32, (BASIS, UNIT), 0).astype(F32) / (BASIS - 1)
        for h in range(heads):
            gap = centres - location[h : h + 1]
            density = jnp.exp(gap * gap * fall[h : h + 1]).astype(BF16)
            rows = slice(h * HEAD_DIM, (h + 1) * HEAD_DIM)
            turned[rows] += dot(value_cols[rows], density) * peak[h : h + 1]

    mixed[...] = turned[...].T.astype(BF16)


def backward_kernel(
    heads, info, qkv, grad_mixed, logsum, states, musig, musig_cols, table, out, probe_grad,
    carried, spread, value_high, value_low, grad_values, probe_rows, probe_cols, row_grad, key_grad, value_grad, cols, turned,
):
    step = pl.program_id(0)
    units = pl.num_programs(0)
    u = units - 1 - step
    width = heads * HEAD_DIM
    start, length = info[0, u], info[1, u]
    base = pl.multiple_of(u * UNIT, UNIT)
    here = pl.ds(base, UNIT)

    @pl.when(step == 0)
    def _():
        carried[...] = jnp.zeros_like(carried)
        probe_grad[...] = jnp.zeros_like(probe_grad)
        for i in range(cols.shape[0]):
            cols[i] = qkv[i * UNIT : (i + 1) * UNIT, LANES : 2 * LANES].astype(F32).T.astype(BF16)

    @pl.when(u + 1 == start + length)
    def _():
        seg_rows = pl.ds(pl.multiple_of(start * UNIT, UNIT), UNIT)
        key_grad[...] = jnp.zeros_like(key_grad)
        value_grad[...] = jnp.zeros_like(value_grad)
        grad_values[...] = jnp.zeros_like(grad_values)
        row_grad[...] = jnp.zeros_like(row_grad)
        rows = dot(musig[...], states[0, :, :LANES], precision=HIGHEST) * (1.0 / math.sqrt(HEAD_DIM))
        rows = jnp.where(head_rows(heads, LANES), rows, 0.0)
        probe_rows[...] = rows
        probe_cols[...] = jnp.concatenate([rows, jnp.zeros((120, LANES), F32)], axis=0).T
        value = states[0, :, LANES:]
        high = value.astype(BF16)
        value_high[...] = high
        value_low[...] = (value - high.astype(F32)).astype(BF16)

    query = qkv[here, 0:LANES]
    given = jnp.concatenate([grad_mixed[...], jnp.zeros((UNIT, LANES - width), BF16)], axis=1)
    lane_head = lax.broadcasted_iota(jnp.int32, (UNIT, LANES), 1) // HEAD_DIM

    def attend_back(blocks):
        first = pl.multiple_of(start * UNIT, UNIT)
        keys = qkv[pl.ds(first, blocks * UNIT), LANES : 2 * LANES]
        values = qkv[pl.ds(first, blocks * UNIT), 2 * LANES : 3 * LANES]
        causal = lax.broadcasted_iota(jnp.int32, (UNIT, UNIT), 0) <= lax.broadcasted_iota(
            jnp.int32, (UNIT, UNIT), 1
        )
        for h in range(heads):
            own = jnp.where(lane_head == h, query.astype(F32) * (1.0 / math.sqrt(HEAD_DIM)), 0.0).astype(BF16)
            own_given = jnp.where(lane_head == h, given.astype(F32), 0.0).astype(BF16)
            probs, products = [], []
            inner = jnp.zeros((1, UNIT), F32)
            for j in range(blocks):
                part = slice(j * UNIT, (j + 1) * UNIT)
                score = dot(keys[part], own, ((1,), (1,)))
                if j == blocks - 1:
                    score = jnp.where(causal, score, -1e30)
                prob = jnp.exp(score - logsum[h : h + 1])
                product = prob * dot(values[part], own_given, ((1,), (1,)))
                inner += jnp.sum(product, axis=0, keepdims=True)
                probs.append(prob)
                products.append(product)
            rows = slice(h * HEAD_DIM, (h + 1) * HEAD_DIM)
            result = jnp.zeros((HEAD_DIM, UNIT), F32)
            for j in range(blocks):
                part = slice(j * UNIT, (j + 1) * UNIT)
                grad_score = (products[j] - probs[j] * inner).astype(BF16)
                key_grad[part] += dot(grad_score, own)
                value_grad[part] += dot(probs[j].astype(BF16), own_given)
                result += dot(cols[start + j, rows], grad_score)
            turned[rows] = result * (1.0 / math.sqrt(HEAD_DIM))

    for blocks in range(1, 5):
        pl.when(u - start + 1 == blocks)(functools.partial(attend_back, blocks))

    @pl.when(start > 0)
    def _():
        probes = probe_rows[...]
        high = probes.astype(BF16)
        rest = probes - high.astype(F32)
        mid = rest.astype(BF16)
        low = (rest - mid.astype(F32)).astype(BF16)
        logits = sum(dot(part, query, ((1,), (1,))) for part in (high, mid, low))
        location, variance = read_parts(logits, heads)
        inverse = 1.0 / variance
        fall = -0.5 * inverse
        peak = WIDTH * lax.rsqrt(variance)
        centres = lax.broadcasted_iota(jnp.int32, (BASIS, UNIT), 0).astype(F32) / (BASIS - 1)
        along, across = [], []
        for h in range(heads):
            own_given = jnp.where(lane_head == h, given.astype(F32), 0.0).astype(BF16)
            gap = centres - location[h : h + 1]
            square = gap * gap
            density = jnp.exp(square * fall[h : h + 1]) * peak[h : h + 1]
            grad_density = dot(value_high[...], own_given, ((1,), (1,))) + dot(
                value_low[...], own_given, ((1,), (1,))
            )
            grad_values[...] += dot(density.astype(BF16), own_given)
            weighed = density * grad_density
            zeroth = jnp.sum(weighed, axis=0, keepdims=True)
            first = jnp.sum(weighed * gap, axis=0, keepdims=True)
            second = jnp.sum(weighed * square, axis=0, keepdims=True)
            along.append(first * inverse[h : h + 1])
            across.append(0.5 * inverse[h : h + 1] * (second * inverse[h : h + 1] - zeroth))
        sigmoid = 1.0 / (1.0 + jnp.exp(-logits))
        grad_location = jnp.concatenate(along, axis=0) * location * (1.0 - location)
        grad_variance = jnp.concatenate(across, axis=0) * SPREAD * sigmoid[heads : 2 * heads]
        grad_logits = jnp.concatenate(
            [grad_location, grad_variance, jnp.zeros((8 - 2 * heads, UNIT), F32)], axis=0
        )
        padded = jnp.concatenate([grad_logits, jnp.zeros((120, UNIT), F32)], axis=0)
        turned[...] += dot(probe_cols[...], padded, precision=HIGHEST)[:width]
        row_grad[...] += dot(grad_logits, query.astype(F32), precision=HIGHEST)

    local = pl.ds(pl.multiple_of((u - start) * UNIT, UNIT), UNIT)

    @pl.when(start + length < units)
    def _():
        token = lax.broadcasted_iota(jnp.int32, (UNIT, LIVE), 0) + (u - start) * UNIT
        centre = (lax.broadcasted_iota(jnp.int32, (UNIT, LIVE), 1) + LIVE).astype(F32) / (BASIS - 1)
        gap = place_of(token, length) - centre
        psi = jnp.exp(gap * gap * (-0.5 / (WIDTH * WIDTH))).astype(BF16)
        pair_grad = dot(psi, spread[...])
        key_grad[local] += pair_grad[:, :LANES]
        value_grad[local] += pair_grad[:, LANES:]

    query_grad = turned[...].T.astype(BF16)
    out[:, :LANES] = jnp.concatenate([query_grad, jnp.zeros((UNIT, LANES - width), BF16)], axis=1)
    out[:, LANES : 2 * LANES] = key_grad[local].astype(BF16)
    out[:, 2 * LANES :] = value_grad[local].astype(BF16)

    @pl.when((u == start) & (start > 0))
    def _():
        rows = jnp.where(head_rows(heads, LANES), row_grad[...], 0.0) * (1.0 / math.sqrt(HEAD_DIM))
        probe_grad[...] += dot(rows, states[0, :, :LANES], ((1,), (1,)), HIGHEST)
        padded = jnp.concatenate([rows, jnp.zeros((120, LANES), F32)], axis=0)
        grad_keys = dot(musig_cols[...], padded, precision=HIGHEST)
        total = carried[...] + jnp.concatenate([grad_keys, grad_values[...]], axis=1)
        moved = dot(table[...], split3(total))
        carried[...] = moved[:BASIS]
        scale = term_scale(info[1, jnp.maximum(start - 1, 0)])
        spread[...] = (moved[BASIS:] * scale).astype(BF16)


def segment_info(lengths, units):
    slot_units = lengths // UNIT
    slots = jnp.arange(lengths.shape[0], dtype=jnp.int32)
    ends = jnp.sum(jnp.where(slots[None, :] <= slots[:, None], slot_units[None, :], 0), axis=1)
    starts = ends - slot_units
    unit = jnp.arange(units, dtype=jnp.int32)[:, None]
    member = (unit >= starts[None, :]) & (unit < ends[None, :])
    start = jnp.sum(jnp.where(member, starts[None, :], 0), axis=1)
    length = jnp.sum(jnp.where(member, slot_units[None, :], 0), axis=1)
    place = jnp.sum(((ends[None, :] <= unit) & (slot_units > 0)[None, :]).astype(jnp.int32), axis=1)
    return jnp.stack([start, length, place]).astype(jnp.int32)


def attention_forward(info, qkv, musig, heads):
    group = qkv.shape[0]
    units = group // UNIT
    width = heads * HEAD_DIM
    table = jnp.asarray(basis_tables()[0])
    whole = lambda shape: pl.BlockSpec(shape, lambda i, info: (0,) * len(shape))
    return pl.pallas_call(
        functools.partial(forward_kernel, heads),
        grid_spec=pltpu.PrefetchScalarGridSpec(
            num_scalar_prefetch=1,
            grid=(units,),
            in_specs=[whole(qkv.shape), whole(musig.shape), whole(table.shape)],
            out_specs=[
                pl.BlockSpec((UNIT, width), lambda i, info: (i, 0)),
                pl.BlockSpec((8, UNIT), lambda i, info: (0, i)),
                pl.BlockSpec((1, BASIS, 2 * LANES), lambda i, info: (info[2, i], 0, 0)),
            ],
            scratch_shapes=[
                pltpu.VMEM((BASIS, 2 * LANES), F32),
                pltpu.VMEM((LIVE, 2 * LANES), F32),
                pltpu.VMEM((8, LANES), F32),
                pltpu.VMEM((LANES, BASIS), BF16),
                pltpu.VMEM((width, UNIT), F32),
                pltpu.VMEM((units, LANES, UNIT), BF16),
            ],
        ),
        out_shape=[
            jax.ShapeDtypeStruct((group, width), BF16),
            jax.ShapeDtypeStruct((8, group), F32),
            jax.ShapeDtypeStruct((units, BASIS, 2 * LANES), F32),
        ],
        compiler_params=pltpu.CompilerParams(vmem_limit_bytes=56 << 20),
        name="attention_forward",
    )(info, qkv, musig, table)


def attention_backward(info, qkv, grad_mixed, logsum, states, musig, musig_cols, heads):
    group = qkv.shape[0]
    units = group // UNIT
    width = heads * HEAD_DIM
    table = jnp.asarray(basis_tables()[1])
    last = units - 1
    whole = lambda shape: pl.BlockSpec(shape, lambda i, info: (0,) * len(shape))
    return pl.pallas_call(
        functools.partial(backward_kernel, heads),
        grid_spec=pltpu.PrefetchScalarGridSpec(
            num_scalar_prefetch=1,
            grid=(units,),
            in_specs=[
                whole(qkv.shape),
                pl.BlockSpec((UNIT, width), lambda i, info: (last - i, 0)),
                pl.BlockSpec((8, UNIT), lambda i, info: (0, last - i)),
                pl.BlockSpec((1, BASIS, 2 * LANES), lambda i, info: (info[2, last - i], 0, 0)),
                whole(musig.shape),
                whole(musig_cols.shape),
                whole(table.shape),
            ],
            out_specs=[
                pl.BlockSpec((UNIT, 3 * LANES), lambda i, info: (last - i, 0)),
                whole(musig.shape),
            ],
            scratch_shapes=[
                pltpu.VMEM((BASIS, 2 * LANES), F32),
                pltpu.VMEM((LIVE, 2 * LANES), BF16),
                pltpu.VMEM((BASIS, LANES), BF16),
                pltpu.VMEM((BASIS, LANES), BF16),
                pltpu.VMEM((BASIS, LANES), F32),
                pltpu.VMEM((8, LANES), F32),
                pltpu.VMEM((LANES, 128), F32),
                pltpu.VMEM((8, LANES), F32),
                pltpu.VMEM((4 * UNIT, LANES), F32),
                pltpu.VMEM((4 * UNIT, LANES), F32),
                pltpu.VMEM((units, LANES, UNIT), BF16),
                pltpu.VMEM((width, UNIT), F32),
            ],
        ),
        out_shape=[
            jax.ShapeDtypeStruct((group, 3 * LANES), BF16),
            jax.ShapeDtypeStruct(musig.shape, F32),
        ],
        compiler_params=pltpu.CompilerParams(vmem_limit_bytes=56 << 20),
        name="attention_backward",
    )(info, qkv, grad_mixed, logsum, states, musig, musig_cols, table)


def layer_norm(values, gain, shift):
    centred = values - jnp.mean(values, axis=-1, keepdims=True)
    inverse = lax.rsqrt(jnp.mean(centred * centred, axis=-1, keepdims=True) + EPSILON)
    normal = centred * inverse
    return (normal * gain + shift, normal, inverse)


def norm_back(grad, normal, inverse, gain):
    scaled = grad * gain
    return inverse * (
        scaled
        - jnp.mean(scaled, axis=-1, keepdims=True)
        - normal * jnp.mean(scaled * normal, axis=-1, keepdims=True)
    )


def gelu_tanh(values):
    return jax.nn.gelu(values, approximate=True)


def gather_weight(shard, members):
    rows = shard.shape[0] // members
    mine = lax.dynamic_slice_in_dim(shard, lax.axis_index("dp") * rows, rows, 0)
    return lax.all_gather(mine, ("head", "dp"), axis=0, tiled=True)


def scatter_grad(grad, members):
    heads = lax.axis_size("head")
    rows = grad.shape[0] // (heads * members)
    part = lax.psum_scatter(grad, ("head", "dp"), scatter_dimension=0, tiled=True)
    return lax.all_gather(part, "dp", axis=0, tiled=True).astype(F32)


def local(
    inputs, seg_lengths, ln1_gain, ln1_bias, qkv_weight, qkv_bias, out_weight, out_bias, mem_mu, mem_sig,
    ln2_gain, ln2_bias, ff_in, ff_in_bias, ff_out, ff_out_bias, cotangent,
):
    own_rows, model = inputs.shape
    heads_axis = lax.axis_size("head")
    members = lax.axis_size("dp")
    group = heads_axis * own_rows
    units = group // UNIT
    width = qkv_weight.shape[2]
    heads = width // HEAD_DIM
    hidden_part = ff_in.shape[1]

    info = segment_info(seg_lengths[0], units)
    source = inputs.astype(F32)
    gain_one = ln1_gain.astype(F32)
    gain_two = ln2_gain.astype(F32)
    normed1, normal1, inverse1 = layer_norm(source, gain_one, ln1_bias.astype(F32))
    first_rows = lax.all_gather(normed1.astype(BF16), "head", axis=0, tiled=True)

    out_full = gather_weight(out_weight, members)
    in_full = gather_weight(ff_in, members).reshape(heads_axis, model, hidden_part)
    back_full = gather_weight(ff_out, members)
    in_bias = lax.all_gather(ff_in_bias, "head", axis=0, tiled=True).astype(F32)

    pad = ((0, 0), (0, 0), (0, LANES - width))
    weight_flat = jnp.pad(qkv_weight, pad).reshape(model, 3 * LANES)
    bias_flat = jnp.pad(qkv_bias, pad[1:]).reshape(3 * LANES).astype(F32)
    qkv = (jnp.dot(first_rows, weight_flat, preferred_element_type=F32) + bias_flat).astype(BF16)
    musig = jnp.concatenate([mem_mu, mem_sig, jnp.zeros((8 - 2 * heads, BASIS), BF16)], axis=0).astype(F32)
    musig_cols = jnp.pad(musig.T, ((0, 0), (0, 120)))
    mixed_heads, logsum, states = attention_forward(info, qkv, musig, heads)

    mixed = lax.all_to_all(mixed_heads, "head", split_axis=0, concat_axis=1, tiled=True)
    attended = jnp.dot(mixed, out_full, preferred_element_type=F32)
    residual = source + attended + out_bias.astype(F32)
    normed2, normal2, inverse2 = layer_norm(residual, gain_two, ln2_bias.astype(F32))
    second = normed2.astype(BF16)
    grad_out = cotangent.astype(F32)
    hidden = jnp.einsum("rd,zdf->rzf", second, in_full, preferred_element_type=F32).reshape(
        own_rows, -1
    ) + in_bias
    activation, gelu_back = jax.vjp(gelu_tanh, hidden)
    act_low = activation.astype(BF16)
    outputs = residual + jnp.dot(act_low, back_full, preferred_element_type=F32) + ff_out_bias.astype(F32)
    grad_act = jnp.dot(cotangent, back_full.T, preferred_element_type=F32)
    grad_hidden = gelu_back(grad_act)[0].astype(BF16)
    grad_second = jnp.einsum(
        "rzf,zdf->rd", grad_hidden.reshape(own_rows, heads_axis, hidden_part), in_full, preferred_element_type=F32
    )
    grad_residual = grad_out + norm_back(grad_second, normal2, inverse2, gain_two)
    grad_attended = grad_residual.astype(BF16)
    grad_mixed = jnp.dot(grad_attended, out_full.T, preferred_element_type=F32).astype(BF16)
    grad_heads = lax.all_to_all(grad_mixed, "head", split_axis=1, concat_axis=0, tiled=True)

    ff_out_grad = jnp.dot(act_low.T, cotangent, preferred_element_type=F32).astype(BF16)
    ff_in_grad = jnp.einsum(
        "rd,rzf->zdf", second, grad_hidden.reshape(own_rows, heads_axis, hidden_part), preferred_element_type=F32
    ).astype(BF16)
    out_weight_grad = jnp.dot(mixed.T, grad_attended, preferred_element_type=F32).astype(BF16)
    ff_out_sum = scatter_grad(ff_out_grad, members)
    ff_in_sum = scatter_grad(ff_in_grad.reshape(heads_axis * model, hidden_part), members)
    out_weight_sum = scatter_grad(out_weight_grad, members)

    grad_qkv, probe_grad = attention_backward(
        info, qkv, grad_heads, logsum, states, musig, musig_cols, heads
    )
    grad_first = lax.psum_scatter(
        jnp.dot(grad_qkv, weight_flat.T, preferred_element_type=F32).astype(BF16),
        "head", scatter_dimension=0, tiled=True,
    ).astype(F32)
    qkv_weight_grad = (
        jnp.dot(first_rows.T, grad_qkv, preferred_element_type=F32)
        .reshape(model, 3, LANES)[:, :, :width].astype(BF16)
    )
    qkv_bias_grad = jnp.sum(grad_qkv.astype(F32), axis=0).reshape(3, LANES)[:, :width]
    grad_source = grad_residual + norm_back(grad_first, normal1, inverse1, gain_one)
    qkv_weight_sum = lax.psum(qkv_weight_grad, "dp").astype(F32)
    ff_in_bias_part = jnp.sum(grad_hidden.astype(F32), axis=0)
    own_small = lax.psum((qkv_bias_grad, probe_grad), "dp")
    shared = lax.psum(
        jnp.concatenate([
            jnp.sum(grad_first * normal1, axis=0), jnp.sum(grad_first, axis=0), jnp.sum(grad_residual, axis=0),
            jnp.sum(grad_second * normal2, axis=0), jnp.sum(grad_second, axis=0), jnp.sum(grad_out, axis=0),
            ff_in_bias_part,
        ]),
        ("dp", "head"),
    )
    rows = [shared[i * model : (i + 1) * model] for i in range(6)]
    ff_in_bias_grad = lax.dynamic_slice_in_dim(shared, 6 * model + lax.axis_index("head") * hidden_part, hidden_part, 0)
    return (
        outputs.astype(BF16), grad_source.astype(BF16), rows[0], rows[1], qkv_weight_sum, own_small[0], out_weight_sum,
        rows[2], own_small[1][:heads], own_small[1][heads : 2 * heads], rows[3], rows[4], ff_in_sum, ff_in_bias_grad,
        ff_out_sum, rows[5],
    )


def solution(mesh):
    rows, whole = P(("dp", "head"), None), P()
    return jax.shard_map(
        local,
        mesh=mesh,
        in_specs=(
            rows, P("dp", None), whole, whole, P(None, None, "head"), P(None, "head"), P("head", None), whole,
            P("head", None), P("head", None), whole, whole, P(None, "head"), P("head"), P("head", None), whole, rows,
        ),
        out_specs=(
            rows, rows, whole, whole, P(None, None, "head"), P(None, "head"), P("head", None), whole,
            P("head", None), P("head", None), whole, whole, P(None, "head"), P("head"), P("head", None), whole,
        ),
        check_vma=False,
    )
```

```python
import functools
import math

import jax
import jax.numpy as jnp
import ml_dtypes
import numpy as np
from jax import lax
from jax.experimental import pallas as pl
from jax.experimental.pallas import tpu as pltpu
from jax.sharding import PartitionSpec as P

HEAD_DIM = 64
BASIS = 512
UNIT = 256
LANES = 256
TAU = 0.75
RIDGE = 0.5
EPSILON = 1e-05
SPREAD = 1.0 / 64.0
WIDTH = 1.0 / BASIS
LIVE = BASIS // 2
HIGHEST = lax.Precision.HIGHEST
F32 = jnp.float32
BF16 = jnp.bfloat16


def split_table(table):
    high = table.astype(np.float32).astype(ml_dtypes.bfloat16)
    low = (table.astype(np.float32) - high.astype(np.float32)).astype(ml_dtypes.bfloat16)
    return high, low


@functools.lru_cache(maxsize=None)
def basis_tables():
    centres = np.arange(BASIS) / (BASIS - 1)
    apart = centres[:, None] - centres[None, :]
    gram = np.exp(-apart * apart / (4.0 * WIDTH * WIDTH)) + RIDGE * np.eye(BASIS)
    solve = np.linalg.inv(gram)
    samples = (np.arange(BASIS) + 0.5) / BASIS
    near_gap = TAU * samples[:, None] - centres[None, :]
    far_gap = samples[:, None] - centres[None, :]
    near = np.exp(-near_gap * near_gap / (2.0 * WIDTH * WIDTH))
    far = np.exp(-far_gap * far_gap / (2.0 * WIDTH * WIDTH))
    contract = (near.T @ far) * (TAU / (BASIS * WIDTH * math.sqrt(math.pi)))
    joined = np.concatenate([solve @ contract, solve[:, LIVE:]], axis=1)
    high, low = split_table(joined)
    forward = np.concatenate([high, high, low], axis=1)
    backward = np.concatenate([high.T, high.T, low.T], axis=1)
    return forward, backward


def term_scale(units):
    return (1.0 - TAU) / (WIDTH * math.sqrt(math.pi) * UNIT) / units.astype(F32)


def split3(value):
    high = value.astype(BF16)
    low = (value - high.astype(F32)).astype(BF16)
    return jnp.concatenate([high, low, high], axis=0)


def dot(a, b, contract=((1,), (0,)), precision=None):
    return lax.dot_general(a, b, (contract, ((), ())), precision=precision, preferred_element_type=F32)


def head_rows(heads, width):
    row = lax.broadcasted_iota(jnp.int32, (8, width), 0)
    lane = lax.broadcasted_iota(jnp.int32, (8, width), 1) // HEAD_DIM
    return ((row == lane) | (row == lane + heads)) & (lane < heads)


def read_parts(logits, heads):
    location = 1.0 / (1.0 + jnp.exp(-logits))
    variance = (jnp.maximum(logits, 0.0) + jnp.log1p(jnp.exp(-jnp.abs(logits)))) * SPREAD + WIDTH * WIDTH
    return location[:heads], variance[heads : 2 * heads]


def place_of(index, length):
    return TAU + (1.0 - TAU) * (index.astype(F32) + 0.5) / (length.astype(F32) * UNIT)


def forward_kernel(heads, info, qkv, musig, table, mixed, logsum, states, memory, sums, probe_rows, value_cols, turned, cols):
    u = pl.program_id(0)
    width = heads * HEAD_DIM
    start, length = info[0, u], info[1, u]
    base = pl.multiple_of(u * UNIT, UNIT)
    here = pl.ds(base, UNIT)

    @pl.when(u == 0)
    def _():
        memory[...] = jnp.zeros_like(memory)

    @pl.when((start == u) & (u > 0))
    def _():
        scale = term_scale(info[1, jnp.maximum(u - 1, 0)])
        stacked = jnp.concatenate([memory[...], sums[...] * scale], axis=0)
        memory[...] = dot(table[...], split3(stacked))
        rows = dot(musig[...], memory[:, :LANES], precision=HIGHEST) * (1.0 / math.sqrt(HEAD_DIM))
        probe_rows[...] = jnp.where(head_rows(heads, LANES), rows, 0.0)
        value_cols[...] = memory[:, LANES:].T.astype(BF16)

    @pl.when(start == u)
    def _():
        states[0] = memory[...]
        sums[...] = jnp.zeros_like(sums)

    value_rows = qkv[here, 2 * LANES : 3 * LANES]
    cols[u] = value_rows.astype(F32).T.astype(BF16)

    token = lax.broadcasted_iota(jnp.int32, (LIVE, UNIT), 1) + (u - start) * UNIT
    centre = (lax.broadcasted_iota(jnp.int32, (LIVE, UNIT), 0) + LIVE).astype(F32) / (BASIS - 1)
    gap = place_of(token, length) - centre
    psi = jnp.exp(gap * gap * (-0.5 / (WIDTH * WIDTH)))
    psi_high = psi.astype(BF16)
    psi_low = (psi - psi_high.astype(F32)).astype(BF16)
    pairs = qkv[here, LANES : 3 * LANES]
    sums[...] += dot(psi_high, pairs) + dot(psi_low, pairs)

    query = qkv[here, 0:LANES]
    lane_head = lax.broadcasted_iota(jnp.int32, (UNIT, LANES), 1) // HEAD_DIM

    def attend(blocks):
        first = pl.multiple_of(start * UNIT, UNIT)
        keys = qkv[pl.ds(first, blocks * UNIT), LANES : 2 * LANES]
        causal = lax.broadcasted_iota(jnp.int32, (UNIT, UNIT), 0) <= lax.broadcasted_iota(
            jnp.int32, (UNIT, UNIT), 1
        )
        for h in range(heads):
            own = jnp.where(lane_head == h, query.astype(F32) * (1.0 / math.sqrt(HEAD_DIM)), 0.0).astype(BF16)
            scores = [dot(keys[j * UNIT : (j + 1) * UNIT], own, ((1,), (1,))) for j in range(blocks)]
            scores[-1] = jnp.where(causal, scores[-1], -1e30)
            highest = functools.reduce(jnp.maximum, [jnp.max(s, axis=0, keepdims=True) for s in scores])
            weights = [jnp.exp(s - highest) for s in scores]
            total = sum(jnp.sum(w, axis=0, keepdims=True) for w in weights)
            rows = slice(h * HEAD_DIM, (h + 1) * HEAD_DIM)
            result = sum(dot(cols[start + j, rows], weights[j].astype(BF16)) for j in range(blocks))
            turned[rows] = result * (1.0 / total)
            logsum[h : h + 1] = highest + jnp.log(total)

    for blocks in range(1, 5):
        pl.when(u - start + 1 == blocks)(functools.partial(attend, blocks))

    @pl.when(start > 0)
    def _():
        probes = probe_rows[...]
        high = probes.astype(BF16)
        rest = probes - high.astype(F32)
        mid = rest.astype(BF16)
        low = (rest - mid.astype(F32)).astype(BF16)
        logits = sum(dot(part, query, ((1,), (1,))) for part in (high, mid, low))
        location, variance = read_parts(logits, heads)
        fall = -0.5 / variance
        peak = WIDTH * lax.rsqrt(variance)
        centres = lax.broadcasted_iota(jnp.int32, (BASIS, UNIT), 0).astype(F32) / (BASIS - 1)
        for h in range(heads):
            gap = centres - location[h : h + 1]
            density = jnp.exp(gap * gap * fall[h : h + 1]).astype(BF16)
            rows = slice(h * HEAD_DIM, (h + 1) * HEAD_DIM)
            turned[rows] += dot(value_cols[rows], density) * peak[h : h + 1]

    mixed[...] = turned[...].T.astype(BF16)


def backward_kernel(
    heads, info, qkv, grad_mixed, logsum, states, musig, musig_cols, table, out, probe_grad,
    carried, spread, value_high, value_low, grad_values, probe_rows, probe_cols, row_grad, key_grad, value_grad, cols, turned,
):
    step = pl.program_id(0)
    units = pl.num_programs(0)
    u = units - 1 - step
    width = heads * HEAD_DIM
    start, length = info[0, u], info[1, u]
    base = pl.multiple_of(u * UNIT, UNIT)
    here = pl.ds(base, UNIT)

    @pl.when(step == 0)
    def _():
        carried[...] = jnp.zeros_like(carried)
        probe_grad[...] = jnp.zeros_like(probe_grad)
        for i in range(cols.shape[0]):
            cols[i] = qkv[i * UNIT : (i + 1) * UNIT, LANES : 2 * LANES].astype(F32).T.astype(BF16)

    @pl.when(u + 1 == start + length)
    def _():
        seg_rows = pl.ds(pl.multiple_of(start * UNIT, UNIT), UNIT)
        key_grad[...] = jnp.zeros_like(key_grad)
        value_grad[...] = jnp.zeros_like(value_grad)
        grad_values[...] = jnp.zeros_like(grad_values)
        row_grad[...] = jnp.zeros_like(row_grad)
        rows = dot(musig[...], states[0, :, :LANES], precision=HIGHEST) * (1.0 / math.sqrt(HEAD_DIM))
        rows = jnp.where(head_rows(heads, LANES), rows, 0.0)
        probe_rows[...] = rows
        probe_cols[...] = jnp.concatenate([rows, jnp.zeros((120, LANES), F32)], axis=0).T
        value = states[0, :, LANES:]
        high = value.astype(BF16)
        value_high[...] = high
        value_low[...] = (value - high.astype(F32)).astype(BF16)

    query = qkv[here, 0:LANES]
    given = jnp.concatenate([grad_mixed[...], jnp.zeros((UNIT, LANES - width), BF16)], axis=1)
    lane_head = lax.broadcasted_iota(jnp.int32, (UNIT, LANES), 1) // HEAD_DIM

    def attend_back(blocks):
        first = pl.multiple_of(start * UNIT, UNIT)
        keys = qkv[pl.ds(first, blocks * UNIT), LANES : 2 * LANES]
        values = qkv[pl.ds(first, blocks * UNIT), 2 * LANES : 3 * LANES]
        causal = lax.broadcasted_iota(jnp.int32, (UNIT, UNIT), 0) <= lax.broadcasted_iota(
            jnp.int32, (UNIT, UNIT), 1
        )
        for h in range(heads):
            own = jnp.where(lane_head == h, query.astype(F32) * (1.0 / math.sqrt(HEAD_DIM)), 0.0).astype(BF16)
            own_given = jnp.where(lane_head == h, given.astype(F32), 0.0).astype(BF16)
            probs, products = [], []
            inner = jnp.zeros((1, UNIT), F32)
            for j in range(blocks):
                part = slice(j * UNIT, (j + 1) * UNIT)
                score = dot(keys[part], own, ((1,), (1,)))
                if j == blocks - 1:
                    score = jnp.where(causal, score, -1e30)
                prob = jnp.exp(score - logsum[h : h + 1])
                product = prob * dot(values[part], own_given, ((1,), (1,)))
                inner += jnp.sum(product, axis=0, keepdims=True)
                probs.append(prob)
                products.append(product)
            rows = slice(h * HEAD_DIM, (h + 1) * HEAD_DIM)
            result = jnp.zeros((HEAD_DIM, UNIT), F32)
            for j in range(blocks):
                part = slice(j * UNIT, (j + 1) * UNIT)
                grad_score = (products[j] - probs[j] * inner).astype(BF16)
                key_grad[part] += dot(grad_score, own)
                value_grad[part] += dot(probs[j].astype(BF16), own_given)
                result += dot(cols[start + j, rows], grad_score)
            turned[rows] = result * (1.0 / math.sqrt(HEAD_DIM))

    for blocks in range(1, 5):
        pl.when(u - start + 1 == blocks)(functools.partial(attend_back, blocks))

    @pl.when(start > 0)
    def _():
        probes = probe_rows[...]
        high = probes.astype(BF16)
        rest = probes - high.astype(F32)
        mid = rest.astype(BF16)
        low = (rest - mid.astype(F32)).astype(BF16)
        logits = sum(dot(part, query, ((1,), (1,))) for part in (high, mid, low))
        location, variance = read_parts(logits, heads)
        inverse = 1.0 / variance
        fall = -0.5 * inverse
        peak = WIDTH * lax.rsqrt(variance)
        centres = lax.broadcasted_iota(jnp.int32, (BASIS, UNIT), 0).astype(F32) / (BASIS - 1)
        along, across = [], []
        for h in range(heads):
            own_given = jnp.where(lane_head == h, given.astype(F32), 0.0).astype(BF16)
            gap = centres - location[h : h + 1]
            square = gap * gap
            density = jnp.exp(square * fall[h : h + 1]) * peak[h : h + 1]
            grad_density = dot(value_high[...], own_given, ((1,), (1,))) + dot(
                value_low[...], own_given, ((1,), (1,))
            )
            grad_values[...] += dot(density.astype(BF16), own_given)
            weighed = density * grad_density
            zeroth = jnp.sum(weighed, axis=0, keepdims=True)
            first = jnp.sum(weighed * gap, axis=0, keepdims=True)
            second = jnp.sum(weighed * square, axis=0, keepdims=True)
            along.append(first * inverse[h : h + 1])
            across.append(0.5 * inverse[h : h + 1] * (second * inverse[h : h + 1] - zeroth))
        sigmoid = 1.0 / (1.0 + jnp.exp(-logits))
        grad_location = jnp.concatenate(along, axis=0) * location * (1.0 - location)
        grad_variance = jnp.concatenate(across, axis=0) * SPREAD * sigmoid[heads : 2 * heads]
        grad_logits = jnp.concatenate(
            [grad_location, grad_variance, jnp.zeros((8 - 2 * heads, UNIT), F32)], axis=0
        )
        padded = jnp.concatenate([grad_logits, jnp.zeros((120, UNIT), F32)], axis=0)
        turned[...] += dot(probe_cols[...], padded, precision=HIGHEST)[:width]
        row_grad[...] += dot(grad_logits, query.astype(F32), precision=HIGHEST)

    local = pl.ds(pl.multiple_of((u - start) * UNIT, UNIT), UNIT)

    @pl.when(start + length < units)
    def _():
        token = lax.broadcasted_iota(jnp.int32, (UNIT, LIVE), 0) + (u - start) * UNIT
        centre = (lax.broadcasted_iota(jnp.int32, (UNIT, LIVE), 1) + LIVE).astype(F32) / (BASIS - 1)
        gap = place_of(token, length) - centre
        psi = jnp.exp(gap * gap * (-0.5 / (WIDTH * WIDTH))).astype(BF16)
        pair_grad = dot(psi, spread[...])
        key_grad[local] += pair_grad[:, :LANES]
        value_grad[local] += pair_grad[:, LANES:]

    query_grad = turned[...].T.astype(BF16)
    out[:, :LANES] = jnp.concatenate([query_grad, jnp.zeros((UNIT, LANES - width), BF16)], axis=1)
    out[:, LANES : 2 * LANES] = key_grad[local].astype(BF16)
    out[:, 2 * LANES :] = value_grad[local].astype(BF16)

    @pl.when((u == start) & (start > 0))
    def _():
        rows = jnp.where(head_rows(heads, LANES), row_grad[...], 0.0) * (1.0 / math.sqrt(HEAD_DIM))
        probe_grad[...] += dot(rows, states[0, :, :LANES], ((1,), (1,)), HIGHEST)
        padded = jnp.concatenate([rows, jnp.zeros((120, LANES), F32)], axis=0)
        grad_keys = dot(musig_cols[...], padded, precision=HIGHEST)
        total = carried[...] + jnp.concatenate([grad_keys, grad_values[...]], axis=1)
        moved = dot(table[...], split3(total))
        carried[...] = moved[:BASIS]
        scale = term_scale(info[1, jnp.maximum(start - 1, 0)])
        spread[...] = (moved[BASIS:] * scale).astype(BF16)


def segment_info(lengths, units):
    slot_units = lengths // UNIT
    slots = jnp.arange(lengths.shape[0], dtype=jnp.int32)
    ends = jnp.sum(jnp.where(slots[None, :] <= slots[:, None], slot_units[None, :], 0), axis=1)
    starts = ends - slot_units
    unit = jnp.arange(units, dtype=jnp.int32)[:, None]
    member = (unit >= starts[None, :]) & (unit < ends[None, :])
    start = jnp.sum(jnp.where(member, starts[None, :], 0), axis=1)
    length = jnp.sum(jnp.where(member, slot_units[None, :], 0), axis=1)
    place = jnp.sum(((ends[None, :] <= unit) & (slot_units > 0)[None, :]).astype(jnp.int32), axis=1)
    return jnp.stack([start, length, place]).astype(jnp.int32)


def attention_forward(info, qkv, musig, heads):
    group = qkv.shape[0]
    units = group // UNIT
    width = heads * HEAD_DIM
    table = jnp.asarray(basis_tables()[0])
    whole = lambda shape: pl.BlockSpec(shape, lambda i, info: (0,) * len(shape))
    return pl.pallas_call(
        functools.partial(forward_kernel, heads),
        grid_spec=pltpu.PrefetchScalarGridSpec(
            num_scalar_prefetch=1,
            grid=(units,),
            in_specs=[whole(qkv.shape), whole(musig.shape), whole(table.shape)],
            out_specs=[
                pl.BlockSpec((UNIT, width), lambda i, info: (i, 0)),
                pl.BlockSpec((8, UNIT), lambda i, info: (0, i)),
                pl.BlockSpec((1, BASIS, 2 * LANES), lambda i, info: (info[2, i], 0, 0)),
            ],
            scratch_shapes=[
                pltpu.VMEM((BASIS, 2 * LANES), F32),
                pltpu.VMEM((LIVE, 2 * LANES), F32),
                pltpu.VMEM((8, LANES), F32),
                pltpu.VMEM((LANES, BASIS), BF16),
                pltpu.VMEM((width, UNIT), F32),
                pltpu.VMEM((units, LANES, UNIT), BF16),
            ],
        ),
        out_shape=[
            jax.ShapeDtypeStruct((group, width), BF16),
            jax.ShapeDtypeStruct((8, group), F32),
            jax.ShapeDtypeStruct((units, BASIS, 2 * LANES), F32),
        ],
        compiler_params=pltpu.CompilerParams(vmem_limit_bytes=56 << 20),
        name="attention_forward",
    )(info, qkv, musig, table)


def attention_backward(info, qkv, grad_mixed, logsum, states, musig, musig_cols, heads):
    group = qkv.shape[0]
    units = group // UNIT
    width = heads * HEAD_DIM
    table = jnp.asarray(basis_tables()[1])
    last = units - 1
    whole = lambda shape: pl.BlockSpec(shape, lambda i, info: (0,) * len(shape))
    return pl.pallas_call(
        functools.partial(backward_kernel, heads),
        grid_spec=pltpu.PrefetchScalarGridSpec(
            num_scalar_prefetch=1,
            grid=(units,),
            in_specs=[
                whole(qkv.shape),
                pl.BlockSpec((UNIT, width), lambda i, info: (last - i, 0)),
                pl.BlockSpec((8, UNIT), lambda i, info: (0, last - i)),
                pl.BlockSpec((1, BASIS, 2 * LANES), lambda i, info: (info[2, last - i], 0, 0)),
                whole(musig.shape),
                whole(musig_cols.shape),
                whole(table.shape),
            ],
            out_specs=[
                pl.BlockSpec((UNIT, 3 * LANES), lambda i, info: (last - i, 0)),
                whole(musig.shape),
            ],
            scratch_shapes=[
                pltpu.VMEM((BASIS, 2 * LANES), F32),
                pltpu.VMEM((LIVE, 2 * LANES), BF16),
                pltpu.VMEM((BASIS, LANES), BF16),
                pltpu.VMEM((BASIS, LANES), BF16),
                pltpu.VMEM((BASIS, LANES), F32),
                pltpu.VMEM((8, LANES), F32),
                pltpu.VMEM((LANES, 128), F32),
                pltpu.VMEM((8, LANES), F32),
                pltpu.VMEM((4 * UNIT, LANES), F32),
                pltpu.VMEM((4 * UNIT, LANES), F32),
                pltpu.VMEM((units, LANES, UNIT), BF16),
                pltpu.VMEM((width, UNIT), F32),
            ],
        ),
        out_shape=[
            jax.ShapeDtypeStruct((group, 3 * LANES), BF16),
            jax.ShapeDtypeStruct(musig.shape, F32),
        ],
        compiler_params=pltpu.CompilerParams(vmem_limit_bytes=56 << 20),
        name="attention_backward",
    )(info, qkv, grad_mixed, logsum, states, musig, musig_cols, table)


def middle_kernel(
    place, source, cotangent, mixed, out_weight, vectors, in_bias, own_in, own_out, far_in, far_out,
    outputs, grad_residual, grad_mixed, grad_in, grad_out, grad_out_weight, sums, grad_in_bias,
    residual, inverse, second, second_cols, total, grad_second, in_now, out_now,
):
    r = pl.program_id(0)
    own = place[0]
    slices, rows = own_in.shape[0], own_in.shape[1]
    model = source.shape[1]
    hidden_part = own_in.shape[2]
    out_bias, gain, shift, last_bias = (vectors[k : k + 1] for k in range(4))

    @pl.when(r == 0)
    def _():
        value = source[...].astype(F32) + dot(mixed[...], out_weight[...]) + out_bias
        residual[...] = value
        centred = value - jnp.mean(value, axis=-1, keepdims=True)
        factor = lax.rsqrt(jnp.mean(centred * centred, axis=-1, keepdims=True) + EPSILON)
        inverse[...] = factor
        normal = centred * factor
        grad_residual[...] = normal
        rounded = (normal * gain + shift).astype(BF16)
        second[...] = rounded
        second_cols[...] = rounded.astype(F32).T.astype(BF16)
        total[...] = jnp.zeros_like(total)
        grad_second[...] = jnp.zeros_like(grad_second)
        grad_in_bias[...] = jnp.zeros_like(grad_in_bias)
        for j in range(slices):
            in_now[j * rows : (j + 1) * rows] = own_in[j]
            out_now[j * rows : (j + 1) * rows] = own_out[j]

    @pl.when(r > 0)
    def _():
        for j in range(slices):
            in_now[j * rows : (j + 1) * rows] = far_in[0, j ^ own]
            out_now[j * rows : (j + 1) * rows] = far_out[0, j ^ own]

    half = hidden_part // 2
    for t in range(2):
        span = slice(t * half, (t + 1) * half)
        hidden = dot(second[...], in_now[:, span]) + in_bias[pl.ds(r, 1), span]
        cube = hidden * hidden
        root = math.sqrt(2.0 / math.pi)
        bent = jnp.tanh(hidden * (root + (root * 0.044715) * cube))
        lifted = 0.5 + 0.5 * bent
        activation = (hidden * lifted).astype(BF16)
        slope = lifted + hidden * ((0.5 - 0.5 * bent * bent) * (root + (3.0 * root * 0.044715) * cube))
        total[...] += dot(activation, out_now[span])
        given = dot(cotangent[...], out_now[span], ((1,), (1,)))
        grad_hidden = (given * slope).astype(BF16)
        grad_second[...] += dot(grad_hidden, in_now[:, span], ((1,), (1,)))
        grad_in_bias[pl.ds(r, 1), span] = jnp.sum(grad_hidden.astype(F32), axis=0, keepdims=True)
        part = dot(activation, cotangent[...], ((0,), (0,))).astype(BF16)
        per = half // rows
        for k in range(per):
            grad_out[0, (t * per + k) ^ own] = part[k * rows : (k + 1) * rows]
        part = dot(second_cols[...], grad_hidden).astype(BF16)
        for j in range(slices):
            grad_in[0, j ^ own, :, span] = part[j * rows : (j + 1) * rows]

    @pl.when(r == pl.num_programs(0) - 1)
    def _():
        given = cotangent[...].astype(F32)
        outputs[...] = (residual[...] + total[...] + last_bias).astype(BF16)
        normal = grad_residual[...]
        grad = grad_second[...]
        scaled = grad * gain
        value = given + inverse[...] * (
            scaled
            - jnp.mean(scaled, axis=-1, keepdims=True)
            - normal * jnp.mean(scaled * normal, axis=-1, keepdims=True)
        )
        sums[0:1] = jnp.sum(value, axis=0, keepdims=True)
        sums[1:2] = jnp.sum(grad * normal, axis=0, keepdims=True)
        sums[2:3] = jnp.sum(grad, axis=0, keepdims=True)
        sums[3:4] = jnp.sum(given, axis=0, keepdims=True)
        sums[4:8] = jnp.zeros((4, model), F32)
        grad_residual[...] = value
        rounded = value.astype(BF16)
        grad_mixed[...] = dot(rounded, out_weight[...], ((1,), (1,))).astype(BF16)
        grad_out_weight[...] = dot(mixed[...], rounded, ((0,), (0,))).astype(BF16)


def middle(place, source, cotangent, mixed, out_weight, vectors, in_bias, own_in, own_out, far_in, far_out):
    own_rows, model = source.shape
    shards = far_in.shape[0] + 1
    slices, rows, hidden_part = own_in.shape
    whole = lambda shape: pl.BlockSpec(shape, lambda r, place: (0,) * len(shape))
    far = pl.BlockSpec((1,) + own_in.shape, lambda r, place: (jnp.maximum(r - 1, 0), 0, 0, 0))
    part = pl.BlockSpec((1,) + own_in.shape, lambda r, place: (r, 0, 0, 0))
    square = (model, model)
    macs = own_rows * model * (6 * shards * hidden_part + 3 * model)
    return pl.pallas_call(
        middle_kernel,
        grid_spec=pltpu.PrefetchScalarGridSpec(
            num_scalar_prefetch=1,
            grid=(shards,),
            in_specs=[whole(source.shape)] * 3 + [
                whole(square), whole(vectors.shape), whole(in_bias.shape), whole(own_in.shape), whole(own_out.shape),
                far, far,
            ],
            out_specs=[whole(source.shape)] * 3 + [part, part, whole(square), whole((8, model)), whole(in_bias.shape)],
            scratch_shapes=[
                pltpu.VMEM((own_rows, model), F32),
                pltpu.VMEM((own_rows, 1), F32),
                pltpu.VMEM((own_rows, model), BF16),
                pltpu.VMEM((model, own_rows), BF16),
                pltpu.VMEM((own_rows, model), F32),
                pltpu.VMEM((own_rows, model), F32),
                pltpu.VMEM((model, hidden_part), BF16),
                pltpu.VMEM((hidden_part, model), BF16),
            ],
        ),
        out_shape=[
            jax.ShapeDtypeStruct(source.shape, BF16),
            jax.ShapeDtypeStruct(source.shape, F32),
            jax.ShapeDtypeStruct(source.shape, BF16),
            jax.ShapeDtypeStruct((shards, slices, rows, hidden_part), BF16),
            jax.ShapeDtypeStruct((shards, slices, rows, hidden_part), BF16),
            jax.ShapeDtypeStruct(square, BF16),
            jax.ShapeDtypeStruct((8, model), F32),
            jax.ShapeDtypeStruct(in_bias.shape, F32),
        ],
        compiler_params=pltpu.CompilerParams(vmem_limit_bytes=60 << 20),
        cost_estimate=pl.CostEstimate(flops=2 * macs, bytes_accessed=30 << 20, transcendentals=own_rows * shards * hidden_part),
        name="middle",
    )(place, source, cotangent, mixed, out_weight, vectors, in_bias, own_in, own_out, far_in, far_out)


def finish_kernel(place, given_in, given_out, grad_in, grad_out):
    own = place[0]
    slices, rows = given_in.shape[0], given_in.shape[1]
    for j in range(slices):
        grad_in[j * rows : (j + 1) * rows] = given_in[j ^ own].astype(F32)
        grad_out[j * rows : (j + 1) * rows] = given_out[j ^ own].astype(F32)


def finish(place, given_in, given_out):
    slices, rows, columns = given_in.shape
    return pl.pallas_call(
        finish_kernel,
        grid_spec=pltpu.PrefetchScalarGridSpec(
            num_scalar_prefetch=1,
            grid=(1,),
            in_specs=[pl.BlockSpec(given_in.shape, lambda k, place: (0, 0, 0))] * 2,
            out_specs=[pl.BlockSpec((slices * rows, columns), lambda k, place: (0, 0))] * 2,
        ),
        out_shape=[jax.ShapeDtypeStruct((slices * rows, columns), F32)] * 2,
        compiler_params=pltpu.CompilerParams(vmem_limit_bytes=40 << 20),
        name="finish",
    )(place, given_in, given_out)


def layer_norm(values, gain, shift):
    centred = values - jnp.mean(values, axis=-1, keepdims=True)
    inverse = lax.rsqrt(jnp.mean(centred * centred, axis=-1, keepdims=True) + EPSILON)
    normal = centred * inverse
    return (normal * gain + shift, normal, inverse)


def norm_back(grad, normal, inverse, gain):
    scaled = grad * gain
    return inverse * (
        scaled
        - jnp.mean(scaled, axis=-1, keepdims=True)
        - normal * jnp.mean(scaled * normal, axis=-1, keepdims=True)
    )


def exchange(value, axis, bit):
    size = lax.axis_size(axis)
    return lax.ppermute(value, axis, [(j, j ^ bit) for j in range(size)])


def plane_gather(part, bits):
    held = {0: part}
    for bit in bits:
        order = sorted(held)
        sent = jnp.stack([held[m] for m in order])
        received = exchange(sent, "dp", bit)
        held.update({m ^ bit: received[k] for k, m in enumerate(order)})
    return jnp.stack([held[m] for m in sorted(held)])


def plane_sum(stacked, bits, outer):
    order = list(range(stacked.shape[0]))
    for bit in bits:
        keep = [k for k, m in enumerate(order) if not m & bit]
        send = [order.index(order[k] | bit) for k in keep]
        received = exchange(take(stacked, send), "dp", bit)
        stacked = (take(stacked, keep).astype(F32) + received.astype(F32)).astype(BF16)
        order = [order[k] for k in keep]
    own = stacked[0]
    for bit in outer:
        own = (own.astype(F32) + exchange(own, "dp", bit).astype(F32)).astype(BF16)
    return own


def take(stacked, indices):
    return jnp.concatenate([stacked[k : k + 1] for k in indices])


def to_order(stacked, own):
    size = stacked.shape[0]
    bit = 1
    while bit < size:
        shaped = stacked.reshape((size // (2 * bit), 2, bit) + stacked.shape[1:])
        stacked = jnp.where((own & bit) > 0, shaped[:, ::-1], shaped).reshape(stacked.shape)
        bit *= 2
    return stacked


def local(
    inputs, seg_lengths, ln1_gain, ln1_bias, qkv_weight, qkv_bias, out_weight, out_bias, mem_mu, mem_sig,
    ln2_gain, ln2_bias, ff_in, ff_in_bias, ff_out, ff_out_bias, cotangent,
):
    own_rows, model = inputs.shape
    heads_axis = lax.axis_size("head")
    members = lax.axis_size("dp")
    group = heads_axis * own_rows
    units = group // UNIT
    width = qkv_weight.shape[2]
    heads = width // HEAD_DIM
    hidden_part = ff_in.shape[1]

    info = segment_info(seg_lengths[0], units)
    source = inputs.astype(F32)
    gain_one = ln1_gain.astype(F32)
    gain_two = ln2_gain.astype(F32)
    normed1, normal1, inverse1 = layer_norm(source, gain_one, ln1_bias.astype(F32))
    first_rows = lax.all_gather(normed1.astype(BF16), "head", axis=0, tiled=True)

    slices = min(8, members)
    inner = [bit for bit in (2, 4, 1) if bit < slices]
    outer = [1 << k for k in range(3, 16) if 1 << k < members]
    turned = inner[1::-1] + inner[2:]
    own = lax.axis_index("dp") % slices
    place = own.reshape(1).astype(jnp.int32)
    rows = model // slices
    narrow = width // slices
    mine = lambda array, count: lax.dynamic_slice_in_dim(array, own * count, count, 0)
    small = jnp.concatenate(
        [mine(out_weight, narrow), jnp.broadcast_to(ff_in_bias[None], (8, hidden_part))[:, :model]], axis=0
    )
    small = jnp.stack([small] + [exchange(small, "head", r) for r in range(1, heads_axis)])
    in_bias = small[:, narrow].astype(F32)
    out_full = to_order(plane_gather(small[:, :narrow], [1] + inner[:-1]), own)
    out_full = jnp.swapaxes(out_full, 0, 1)
    z = lax.axis_index("head")
    out_full = to_order(out_full, z).reshape(model, model)
    ff_mine = (mine(ff_in, rows), mine(ff_out, rows))
    far_in = jnp.stack([exchange(ff_mine[0], "head", r) for r in range(1, heads_axis)])
    far_out = jnp.stack([exchange(ff_mine[1], "head", r) for r in range(1, heads_axis)])
    far_in = jnp.swapaxes(plane_gather(far_in, inner), 0, 1)
    far_out = jnp.swapaxes(plane_gather(far_out, turned), 0, 1)

    pad = ((0, 0), (0, 0), (0, LANES - width))
    weight_flat = jnp.pad(qkv_weight, pad).reshape(model, 3 * LANES)
    bias_flat = jnp.pad(qkv_bias, pad[1:]).reshape(3 * LANES).astype(F32)
    qkv = (jnp.dot(first_rows, weight_flat, preferred_element_type=F32) + bias_flat).astype(BF16)
    musig = jnp.concatenate([mem_mu, mem_sig, jnp.zeros((8 - 2 * heads, BASIS), BF16)], axis=0).astype(F32)
    musig_cols = jnp.pad(musig.T, ((0, 0), (0, 120)))
    mixed_heads, logsum, states = attention_forward(info, qkv, musig, heads)

    mixed = lax.all_to_all(mixed_heads, "head", split_axis=0, concat_axis=1, tiled=True)
    vectors = jnp.concatenate(
        [out_bias[None], ln2_gain[None], ln2_bias[None], ff_out_bias[None], jnp.zeros((4, model), BF16)], axis=0
    ).astype(F32)
    outputs, grad_residual, grad_mixed, ff_in_part, ff_out_part, out_weight_part, sums, in_bias_part = middle(
        place, inputs, cotangent, mixed, out_full, vectors, in_bias,
        ff_in.reshape(slices, rows, hidden_part), ff_out.reshape(slices, rows, model), far_in, far_out,
    )
    grad_heads = lax.all_to_all(grad_mixed, "head", split_axis=1, concat_axis=0, tiled=True)

    reduce_bits = [bit for bit in [1] + inner[:-1] if bit < slices]
    reduce_turned = [reduce_bits[0]] + reduce_bits[:0:-1]

    def owner_sum(part, bits):
        summed = plane_sum(jnp.swapaxes(part, 0, 1), bits, outer)
        terms = [summed[0]] + [exchange(summed[r], "head", r) for r in range(1, heads_axis)]
        return sum(term.astype(F32) for term in terms).astype(BF16)

    ff_out_slice = owner_sum(ff_out_part, reduce_bits)
    ff_in_slice = owner_sum(ff_in_part, reduce_turned)
    out_part = to_order(out_weight_part.reshape(heads_axis, slices, narrow, model), z)
    out_part = jnp.swapaxes(to_order(jnp.swapaxes(out_part, 0, 1), own), 0, 1)
    out_slice = owner_sum(out_part, reduce_bits)
    ff_in_sum, ff_out_sum = finish(
        place, plane_gather(ff_in_slice, inner), plane_gather(ff_out_slice, turned)
    )
    out_weight_sum = to_order(plane_gather(out_slice, inner), own).reshape(width, model).astype(F32)

    grad_qkv, probe_grad = attention_backward(
        info, qkv, grad_heads, logsum, states, musig, musig_cols, heads
    )
    grad_first = lax.psum_scatter(
        jnp.dot(grad_qkv, weight_flat.T, preferred_element_type=F32).astype(BF16),
        "head", scatter_dimension=0, tiled=True,
    ).astype(F32)
    qkv_weight_grad = (
        jnp.dot(first_rows.T, grad_qkv, preferred_element_type=F32)
        .reshape(model, 3, LANES)[:, :, :width].astype(BF16)
    )
    qkv_bias_grad = jnp.sum(grad_qkv.astype(F32), axis=0).reshape(3, LANES)[:, :width]
    grad_source = grad_residual + norm_back(grad_first, normal1, inverse1, gain_one)
    qkv_weight_sum = lax.psum(qkv_weight_grad, "dp").astype(F32)
    own_small = lax.psum((qkv_bias_grad, probe_grad), "dp")
    shared = lax.psum(
        jnp.concatenate([
            jnp.sum(grad_first * normal1, axis=0)[None], jnp.sum(grad_first, axis=0)[None], sums[:4],
            to_order(in_bias_part, z),
        ]),
        ("dp", "head"),
    )
    ff_in_bias_grad = lax.dynamic_index_in_dim(shared, 6 + z, 0, False)
    return (
        outputs, grad_source.astype(BF16), shared[0], shared[1], qkv_weight_sum, own_small[0], out_weight_sum,
        shared[2], own_small[1][:heads], own_small[1][heads : 2 * heads], shared[3], shared[4], ff_in_sum,
        ff_in_bias_grad, ff_out_sum, shared[5],
    )


def solution(mesh):
    rows, whole = P(("dp", "head"), None), P()
    return jax.shard_map(
        local,
        mesh=mesh,
        in_specs=(
            rows, P("dp", None), whole, whole, P(None, None, "head"), P(None, "head"), P("head", None), whole,
            P("head", None), P("head", None), whole, whole, P(None, "head"), P("head"), P("head", None), whole, rows,
        ),
        out_specs=(
            rows, rows, whole, whole, P(None, None, "head"), P(None, "head"), P("head", None), whole,
            P("head", None), P("head", None), whole, whole, P(None, "head"), P("head"), P("head", None), whole,
        ),
        check_vma=False,
    )
```

```python
import functools
import math

import jax
import jax.numpy as jnp
import ml_dtypes
import numpy as np
from jax import lax
from jax.experimental import pallas as pl
from jax.experimental.pallas import tpu as pltpu
from jax.sharding import PartitionSpec as P

HEAD_DIM = 64
BASIS = 512
UNIT = 256
LANES = 256
TAU = 0.75
RIDGE = 0.5
EPSILON = 1e-05
SPREAD = 1.0 / 64.0
WIDTH = 1.0 / BASIS
LIVE = BASIS // 2
HIGHEST = lax.Precision.HIGHEST
F32 = jnp.float32
BF16 = jnp.bfloat16


def split_table(table):
    high = table.astype(np.float32).astype(ml_dtypes.bfloat16)
    low = (table.astype(np.float32) - high.astype(np.float32)).astype(ml_dtypes.bfloat16)
    return high, low


@functools.lru_cache(maxsize=None)
def basis_tables():
    centres = np.arange(BASIS) / (BASIS - 1)
    apart = centres[:, None] - centres[None, :]
    gram = np.exp(-apart * apart / (4.0 * WIDTH * WIDTH)) + RIDGE * np.eye(BASIS)
    solve = np.linalg.inv(gram)
    samples = (np.arange(BASIS) + 0.5) / BASIS
    near_gap = TAU * samples[:, None] - centres[None, :]
    far_gap = samples[:, None] - centres[None, :]
    near = np.exp(-near_gap * near_gap / (2.0 * WIDTH * WIDTH))
    far = np.exp(-far_gap * far_gap / (2.0 * WIDTH * WIDTH))
    contract = (near.T @ far) * (TAU / (BASIS * WIDTH * math.sqrt(math.pi)))
    joined = np.concatenate([solve @ contract, solve[:, LIVE:]], axis=1)
    high, low = split_table(joined)
    forward = np.concatenate([high, high, low], axis=1)
    backward = np.concatenate([high.T, high.T, low.T], axis=1)
    return forward, backward


def term_scale(units):
    return (1.0 - TAU) / (WIDTH * math.sqrt(math.pi) * UNIT) / units.astype(F32)


def split3(value):
    high = value.astype(BF16)
    low = (value - high.astype(F32)).astype(BF16)
    return jnp.concatenate([high, low, high], axis=0)


def dot(a, b, contract=((1,), (0,)), precision=None):
    return lax.dot_general(a, b, (contract, ((), ())), precision=precision, preferred_element_type=F32)


def head_rows(heads, width):
    row = lax.broadcasted_iota(jnp.int32, (8, width), 0)
    lane = lax.broadcasted_iota(jnp.int32, (8, width), 1) // HEAD_DIM
    return ((row == lane) | (row == lane + heads)) & (lane < heads)


def read_parts(logits, heads):
    location = 1.0 / (1.0 + jnp.exp(-logits))
    variance = (jnp.maximum(logits, 0.0) + jnp.log1p(jnp.exp(-jnp.abs(logits)))) * SPREAD + WIDTH * WIDTH
    return location[:heads], variance[heads : 2 * heads]


def place_of(index, length):
    return TAU + (1.0 - TAU) * (index.astype(F32) + 0.5) / (length.astype(F32) * UNIT)


def split_rows(value):
    high = value.astype(BF16)
    rest = value - high.astype(F32)
    mid = rest.astype(BF16)
    return high, mid, (rest - mid.astype(F32)).astype(BF16)


def three_pass(left, right_high, right_low, contract=((1,), (0,))):
    high = left.astype(BF16)
    low = (left - high.astype(F32)).astype(BF16)
    return dot(high, right_high, contract) + dot(low, right_high, contract) + dot(high, right_low, contract)


def advance_values(table, value):
    joined = BASIS + LIVE if table.shape[0] == BASIS else BASIS
    high, low = table[:BASIS, :BASIS], table[:BASIS, 2 * joined : 2 * joined + BASIS]
    value_high = value.astype(BF16)
    value_low = (value - value_high.astype(F32)).astype(BF16)
    return dot(high, value_high) + dot(high, value_low) + dot(low, value_high)


def state_kernel(heads, info, qkv, musig, table, states, value_end, key_end, rows, proj, memory, sums):
    b = pl.program_id(0)
    width = heads * HEAD_DIM
    start, length = info[0, b], info[1, b]

    @pl.when(b == 0)
    def _():
        memory[...] = jnp.zeros_like(memory)
        row = musig[...]
        rows[0:8] = row
        wide = 2 * (BASIS + LIVE)
        for k in range(1, 4):
            row = three_pass(row, table[:, :BASIS], table[:, wide : wide + BASIS])
            rows[8 * k : 8 * k + 8] = row

    @pl.when(start == b)
    def _():
        states[0] = memory[...]
        sums[...] = jnp.zeros_like(sums)

    token = lax.broadcasted_iota(jnp.int32, (LIVE, UNIT), 1) + (b - start) * UNIT
    centre = (lax.broadcasted_iota(jnp.int32, (LIVE, UNIT), 0) + LIVE).astype(F32) / (BASIS - 1)
    gap = place_of(token, length) - centre
    psi = jnp.exp(gap * gap * (-0.5 / (WIDTH * WIDTH)))
    psi_high = psi.astype(BF16)
    psi_low = (psi - psi_high.astype(F32)).astype(BF16)
    pairs = qkv[0, :, LANES : 3 * LANES]
    sums[...] += dot(psi_high, pairs) + dot(psi_low, pairs)

    @pl.when(b + 1 == start + length)
    def _():
        stacked = jnp.concatenate([memory[...], sums[...] * term_scale(length)], axis=0)
        memory[...] = dot(table[...], split3(stacked))

    @pl.when(b == pl.num_programs(0) - 1)
    def _():
        key = memory[:, :LANES]
        key_end[...] = key
        value_end[...] = memory[:, LANES : LANES + width].astype(BF16)
        seen = dot(rows[...], key, precision=HIGHEST)
        mask = head_rows(heads, LANES)
        for k in range(4):
            proj[8 * k : 8 * k + 8] = jnp.where(mask, seen[8 * k : 8 * k + 8], 0.0)


def attend_kernel(heads, info, qkv, result, logsum, cols):
    b = pl.program_id(0)
    start = info[0, b]
    flip = info[3, 0] * (pl.num_programs(0) // 2)
    cols[b] = qkv[b ^ flip, :, 2 * LANES : 3 * LANES].astype(F32).T.astype(BF16)
    query = qkv[b ^ flip, :, 0:LANES]
    lane_head = lax.broadcasted_iota(jnp.int32, (UNIT, LANES), 1) // HEAD_DIM

    def attend(blocks):
        causal = lax.broadcasted_iota(jnp.int32, (UNIT, UNIT), 0) <= lax.broadcasted_iota(
            jnp.int32, (UNIT, UNIT), 1
        )
        for h in range(heads):
            own = jnp.where(lane_head == h, query.astype(F32) * (1.0 / math.sqrt(HEAD_DIM)), 0.0).astype(BF16)
            scores = [
                dot(qkv[(start + j) ^ flip, :, LANES : 2 * LANES], own, ((1,), (1,))) for j in range(blocks)
            ]
            scores[-1] = jnp.where(causal, scores[-1], -1e30)
            highest = functools.reduce(jnp.maximum, [jnp.max(s, axis=0, keepdims=True) for s in scores])
            weights = [jnp.exp(s - highest) for s in scores]
            total = sum(jnp.sum(w, axis=0, keepdims=True) for w in weights)
            rows = slice(h * HEAD_DIM, (h + 1) * HEAD_DIM)
            part = sum(dot(cols[start + j, rows], weights[j].astype(BF16)) for j in range(blocks))
            result[0, rows] = part * (1.0 / total)
            logsum[0, h : h + 1] = highest + jnp.log(total)

    for blocks in range(1, 5):
        pl.when(b - start + 1 == blocks)(functools.partial(attend, blocks))


def read_kernel(
    heads, info, qkv, discrete, states, musig, table, value_in, proj, mixed, values, probes, carried, value_cols,
):
    b = pl.program_id(0)
    width = heads * HEAD_DIM
    start, order, run = info[0, b], info[2, b], info[3, 1]

    @pl.when(b == 0)
    def _():
        carried[...] = jnp.zeros_like(carried)
        carried[:, :width] = value_in[...].astype(F32)

    @pl.when((start == b) & (b > 0) & (run > 0))
    def _():
        carried[...] = advance_values(table, carried[...])

    seen = (start > 0) | (run > 0)

    @pl.when(start == b)
    def _():
        rows = dot(musig[...], states[0, :, :LANES], precision=HIGHEST)
        rows = jnp.where(head_rows(heads, LANES), rows, 0.0)
        incoming = proj[pl.ds(pl.multiple_of(order * 8, 8), 8)]
        probes[0] = (rows + incoming) * (1.0 / math.sqrt(HEAD_DIM))
        value = states[0, :, LANES:] + carried[...]
        values[0] = value
        value_cols[...] = value.T.astype(BF16)

    @pl.when(jnp.logical_not(seen))
    def _():
        mixed[0] = discrete[0].T.astype(BF16)

    @pl.when(seen)
    def _():
        query = qkv[0]
        logits = sum(dot(part, query, ((1,), (1,))) for part in split_rows(probes[0]))
        location, variance = read_parts(logits, heads)
        fall = -0.5 / variance
        peak = WIDTH * lax.rsqrt(variance)
        centres = lax.broadcasted_iota(jnp.int32, (BASIS, UNIT), 0).astype(F32) / (BASIS - 1)
        parts = []
        for h in range(heads):
            gap = centres - location[h : h + 1]
            density = jnp.exp(gap * gap * fall[h : h + 1]).astype(BF16)
            rows = slice(h * HEAD_DIM, (h + 1) * HEAD_DIM)
            parts.append(discrete[0, rows] + dot(value_cols[rows], density) * peak[h : h + 1])
        mixed[0] = jnp.concatenate(parts, axis=0).T.astype(BF16)


def read_back_kernel(
    heads, info, qkv, grad_mixed, values, probes, states, table, query_grad, value_back, row_grads, value_grads,
    probe_grad, carried, value_high, value_low, grad_values, probe_cols, row_grad,
):
    step = pl.program_id(0)
    b = pl.num_programs(0) - 1 - step
    width = heads * HEAD_DIM
    start, length, order, run = info[0, b], info[1, b], info[2, b], info[3, 1]
    seen = (start > 0) | (run > 0)

    @pl.when(step == 0)
    def _():
        carried[...] = jnp.zeros_like(carried)
        probe_grad[...] = jnp.zeros_like(probe_grad)
        row_grads[...] = jnp.zeros_like(row_grads)

    @pl.when(b + 1 == start + length)
    def _():
        grad_values[...] = jnp.zeros_like(grad_values)
        row_grad[...] = jnp.zeros_like(row_grad)
        probe_cols[...] = jnp.concatenate([probes[0], jnp.zeros((120, LANES), F32)], axis=0).T
        value = values[0]
        high = value.astype(BF16)
        value_high[...] = high
        value_low[...] = (value - high.astype(F32)).astype(BF16)

    @pl.when(jnp.logical_not(seen))
    def _():
        query_grad[...] = jnp.zeros_like(query_grad)

    @pl.when(seen)
    def _():
        query = qkv[0]
        given = jnp.concatenate([grad_mixed[0], jnp.zeros((UNIT, LANES - width), BF16)], axis=1)
        lane_head = lax.broadcasted_iota(jnp.int32, (UNIT, LANES), 1) // HEAD_DIM
        logits = sum(dot(part, query, ((1,), (1,))) for part in split_rows(probes[0]))
        location, variance = read_parts(logits, heads)
        inverse = 1.0 / variance
        fall = -0.5 * inverse
        peak = WIDTH * lax.rsqrt(variance)
        centres = lax.broadcasted_iota(jnp.int32, (BASIS, UNIT), 0).astype(F32) / (BASIS - 1)
        along, across = [], []
        for h in range(heads):
            own_given = jnp.where(lane_head == h, given.astype(F32), 0.0).astype(BF16)
            gap = centres - location[h : h + 1]
            square = gap * gap
            density = jnp.exp(square * fall[h : h + 1]) * peak[h : h + 1]
            grad_density = dot(value_high[...], own_given, ((1,), (1,))) + dot(
                value_low[...], own_given, ((1,), (1,))
            )
            grad_values[...] += dot(density.astype(BF16), own_given)
            weighed = density * grad_density
            zeroth = jnp.sum(weighed, axis=0, keepdims=True)
            first = jnp.sum(weighed * gap, axis=0, keepdims=True)
            second = jnp.sum(weighed * square, axis=0, keepdims=True)
            along.append(first * inverse[h : h + 1])
            across.append(0.5 * inverse[h : h + 1] * (second * inverse[h : h + 1] - zeroth))
        sigmoid = 1.0 / (1.0 + jnp.exp(-logits))
        grad_location = jnp.concatenate(along, axis=0) * location * (1.0 - location)
        grad_variance = jnp.concatenate(across, axis=0) * SPREAD * sigmoid[heads : 2 * heads]
        grad_logits = jnp.concatenate(
            [grad_location, grad_variance, jnp.zeros((8 - 2 * heads, UNIT), F32)], axis=0
        )
        padded = jnp.concatenate([grad_logits, jnp.zeros((120, UNIT), F32)], axis=0)
        query_grad[0] = dot(probe_cols[...], padded, precision=HIGHEST)[:width]
        row_grad[...] += dot(grad_logits, query.astype(F32), precision=HIGHEST)

    @pl.when((b == start) & seen)
    def _():
        rows = jnp.where(head_rows(heads, LANES), row_grad[...], 0.0) * (1.0 / math.sqrt(HEAD_DIM))
        row_grads[pl.ds(pl.multiple_of(order * 8, 8), 8)] = rows
        probe_grad[...] += dot(rows, states[0], ((1,), (1,)), HIGHEST)

    @pl.when(b == start)
    def _():
        value_grads[0] = grad_values[...]
        total = carried[...] + grad_values[...]
        value_back[...] = total[:, :width].astype(BF16)

        @pl.when(start > 0)
        def _():
            carried[...] = advance_values(table, total)


def attend_back_kernel(
    heads, info, qkv, grad_mixed, logsum, read_query, row_grads, value_grads, musig, rows_in, row_back, value_back,
    key_end, probe_part, table, out, probe_grad, carried, spread, key_grad, value_grad, cols, turned,
):
    step = pl.program_id(0)
    units = pl.num_programs(0)
    b = units - 1 - step
    width = heads * HEAD_DIM
    start, length, order, run = info[0, b], info[1, b], info[2, b], info[3, 1]
    flip = info[3, 0] * (units // 2)

    @pl.when(step == 0)
    def _():
        for i in range(cols.shape[0]):
            cols[i] = qkv[i, :, LANES : 2 * LANES].astype(F32).T.astype(BF16)
        probe_grad[...] = probe_part[...]

    def carry(total, units_before):
        moved = dot(table[...], split3(total))
        carried[...] = moved[:BASIS]
        spread[...] = (moved[BASIS:] * term_scale(units_before)).astype(BF16)

    @pl.when((step == 0) & (run > 0))
    def _():
        carried[...] = jnp.zeros_like(carried)
        spread[...] = jnp.zeros_like(spread)

    @pl.when((step == 0) & (run == 0))
    def _():
        grad_keys = dot(rows_in[...], row_back[...], ((0,), (0,)), HIGHEST)
        pad = jnp.zeros((BASIS, LANES - width), F32)
        carry(jnp.concatenate([grad_keys, value_back[...].astype(F32), pad], axis=1), length)
        seen = dot(row_back[...], key_end[...], ((1,), (1,)), HIGHEST)
        gained = seen[24:32]
        for k in (2, 1, 0):
            gained = three_pass(gained, table[:BASIS, :BASIS], table[:BASIS, 2 * BASIS : 3 * BASIS])
            gained = gained + seen[8 * k : 8 * k + 8]
        probe_grad[...] += gained

    @pl.when(b + 1 == start + length)
    def _():
        key_grad[...] = jnp.zeros_like(key_grad)
        value_grad[...] = jnp.zeros_like(value_grad)

    query = qkv[b ^ flip, :, 0:LANES]
    given = jnp.concatenate([grad_mixed[0], jnp.zeros((UNIT, LANES - width), BF16)], axis=1)
    lane_head = lax.broadcasted_iota(jnp.int32, (UNIT, LANES), 1) // HEAD_DIM

    def attend_back(blocks):
        causal = lax.broadcasted_iota(jnp.int32, (UNIT, UNIT), 0) <= lax.broadcasted_iota(
            jnp.int32, (UNIT, UNIT), 1
        )
        for h in range(heads):
            own = jnp.where(lane_head == h, query.astype(F32) * (1.0 / math.sqrt(HEAD_DIM)), 0.0).astype(BF16)
            own_given = jnp.where(lane_head == h, given.astype(F32), 0.0).astype(BF16)
            probs, products = [], []
            inner = jnp.zeros((1, UNIT), F32)
            for j in range(blocks):
                score = dot(qkv[(start + j) ^ flip, :, LANES : 2 * LANES], own, ((1,), (1,)))
                if j == blocks - 1:
                    score = jnp.where(causal, score, -1e30)
                prob = jnp.exp(score - logsum[0, h : h + 1])
                product = prob * dot(qkv[(start + j) ^ flip, :, 2 * LANES : 3 * LANES], own_given, ((1,), (1,)))
                inner += jnp.sum(product, axis=0, keepdims=True)
                probs.append(prob)
                products.append(product)
            rows = slice(h * HEAD_DIM, (h + 1) * HEAD_DIM)
            result = jnp.zeros((HEAD_DIM, UNIT), F32)
            for j in range(blocks):
                part = slice(j * UNIT, (j + 1) * UNIT)
                grad_score = (products[j] - probs[j] * inner).astype(BF16)
                key_grad[part] += dot(grad_score, own)
                value_grad[part] += dot(probs[j].astype(BF16), own_given)
                result += dot(cols[(start + j) ^ flip, rows], grad_score)
            turned[rows] = result * (1.0 / math.sqrt(HEAD_DIM)) + read_query[0, rows]

    for blocks in range(1, 5):
        pl.when(b - start + 1 == blocks)(functools.partial(attend_back, blocks))

    local = pl.ds(pl.multiple_of((b - start) * UNIT, UNIT), UNIT)

    @pl.when((start + length < units) | (run == 0))
    def _():
        token = lax.broadcasted_iota(jnp.int32, (UNIT, LIVE), 0) + (b - start) * UNIT
        centre = (lax.broadcasted_iota(jnp.int32, (UNIT, LIVE), 1) + LIVE).astype(F32) / (BASIS - 1)
        gap = place_of(token, length) - centre
        psi = jnp.exp(gap * gap * (-0.5 / (WIDTH * WIDTH))).astype(BF16)
        pair_grad = dot(psi, spread[...])
        key_grad[local] += pair_grad[:, :LANES]
        value_grad[local] += pair_grad[:, LANES:]

    query_grad = turned[...].T.astype(BF16)
    out[0, :, :LANES] = jnp.concatenate([query_grad, jnp.zeros((UNIT, LANES - width), BF16)], axis=1)
    out[0, :, LANES : 2 * LANES] = key_grad[local].astype(BF16)
    out[0, :, 2 * LANES :] = value_grad[local].astype(BF16)

    @pl.when((b == start) & (start > 0))
    def _():
        rows = row_grads[pl.ds(pl.multiple_of(order * 8, 8), 8)]
        grad_keys = dot(musig[...], rows, ((0,), (0,)), HIGHEST)
        total = carried[...] + jnp.concatenate([grad_keys, value_grads[0]], axis=1)
        carry(total, info[1, jnp.maximum(start - 1, 0)])


def segment_info(lengths, units, flip, run):
    slot_units = lengths // UNIT
    slots = jnp.arange(lengths.shape[0], dtype=jnp.int32)
    ends = jnp.sum(jnp.where(slots[None, :] <= slots[:, None], slot_units[None, :], 0), axis=1)
    starts = ends - slot_units
    unit = jnp.arange(units, dtype=jnp.int32)[:, None]
    member = (unit >= starts[None, :]) & (unit < ends[None, :])
    start = jnp.sum(jnp.where(member, starts[None, :], 0), axis=1)
    length = jnp.sum(jnp.where(member, slot_units[None, :], 0), axis=1)
    place = jnp.sum(((ends[None, :] <= unit) & (slot_units > 0)[None, :]).astype(jnp.int32), axis=1)
    own = jnp.where(jnp.arange(units) == 0, flip, run)
    return jnp.stack([start, length, place, own]).astype(jnp.int32)


def whole(shape):
    return pl.BlockSpec(shape, lambda i, info: (0,) * len(shape))


def call(kernel, heads, units, in_specs, out_specs, out_shape, scratch, flops, exps, name):
    return pl.pallas_call(
        functools.partial(kernel, heads),
        grid_spec=pltpu.PrefetchScalarGridSpec(
            num_scalar_prefetch=1, grid=(units,), in_specs=in_specs, out_specs=out_specs, scratch_shapes=scratch
        ),
        out_shape=[jax.ShapeDtypeStruct(shape, kind) for shape, kind in out_shape],
        compiler_params=pltpu.CompilerParams(vmem_limit_bytes=56 << 20),
        cost_estimate=pl.CostEstimate(flops=flops, bytes_accessed=8 << 20, transcendentals=exps),
        name=name,
    )


def unit_block(shape, turn, back=False):
    last = shape[0] - 1

    def index(i, info):
        b = last - i if back else i
        b = b ^ (info[3, 0] * ((last + 1) // 2)) if turn else b
        return (b,) + (0,) * (len(shape) - 1)

    return pl.BlockSpec((1,) + shape[1:], index)


def place_block(shape, back=False):
    last = shape[0] - 1
    return pl.BlockSpec(
        (1,) + shape[1:], lambda i, info: (info[2, last - i if back else i],) + (0,) * (len(shape) - 1)
    )


def memory_state(info, qkv, musig, heads):
    units, width = qkv.shape[0], heads * HEAD_DIM
    table = jnp.asarray(basis_tables()[0])
    states = (units, BASIS, 2 * LANES)
    return call(
        state_kernel, heads, units,
        [unit_block(qkv.shape, True), whole(musig.shape), whole(table.shape)],
        [place_block(states), whole((BASIS, width)), whole((BASIS, LANES)), whole((32, BASIS)), whole((32, LANES))],
        [(states, F32), ((BASIS, width), BF16), ((BASIS, LANES), F32), ((32, BASIS), F32), ((32, LANES), F32)],
        [pltpu.VMEM((BASIS, 2 * LANES), F32), pltpu.VMEM((LIVE, 2 * LANES), F32)],
        5 << 30, units * UNIT * LIVE, "memory_state",
    )(info, qkv, musig, table)


def attention(info, qkv, heads):
    units, width = qkv.shape[0], heads * HEAD_DIM
    return call(
        attend_kernel, heads, units,
        [whole(qkv.shape)],
        [unit_block((units, width, UNIT), False), unit_block((units, 8, UNIT), False)],
        [((units, width, UNIT), F32), ((units, 8, UNIT), F32)],
        [pltpu.VMEM((units, LANES, UNIT), BF16)],
        8 << 30, 2 << 20, "attention",
    )(info, qkv)


def memory_read(info, qkv, discrete, states, musig, value_in, proj, heads):
    units, width = qkv.shape[0], heads * HEAD_DIM
    table = jnp.asarray(basis_tables()[0])
    return call(
        read_kernel, heads, units,
        [
            unit_block((units, UNIT, LANES), True), unit_block(discrete.shape, False), place_block(states.shape),
            whole(musig.shape), whole(table.shape), whole(value_in.shape), whole(proj.shape),
        ],
        [unit_block((units, UNIT, width), True), place_block((units, BASIS, LANES)), place_block((units, 8, LANES))],
        [((units, UNIT, width), BF16), ((units, BASIS, LANES), F32), ((units, 8, LANES), F32)],
        [pltpu.VMEM((BASIS, LANES), F32), pltpu.VMEM((LANES, BASIS), BF16)],
        3 << 30, 2 << 20, "memory_read",
    )(info, qkv, discrete, states, musig, table, value_in, proj)


def memory_read_back(info, qkv, grad_mixed, values, probes, states, heads):
    units, width = qkv.shape[0], heads * HEAD_DIM
    table = jnp.asarray(basis_tables()[1])
    return call(
        read_back_kernel, heads, units,
        [
            unit_block((units, UNIT, LANES), True, True), unit_block(grad_mixed.shape, True, True),
            place_block(values.shape, True), place_block(probes.shape, True),
            place_block((units, BASIS, LANES), True), whole(table.shape),
        ],
        [
            unit_block((units, width, UNIT), False, True), whole((BASIS, width)), whole((32, LANES)),
            place_block((units, BASIS, LANES), True), whole((8, BASIS)),
        ],
        [
            ((units, width, UNIT), F32), ((BASIS, width), BF16), ((32, LANES), F32), ((units, BASIS, LANES), F32),
            ((8, BASIS), F32),
        ],
        [
            pltpu.VMEM((BASIS, LANES), F32), pltpu.VMEM((BASIS, LANES), BF16), pltpu.VMEM((BASIS, LANES), BF16),
            pltpu.VMEM((BASIS, LANES), F32), pltpu.VMEM((LANES, 128), F32), pltpu.VMEM((8, LANES), F32),
        ],
        6 << 30, 2 << 20, "memory_read_back",
    )(info, qkv, grad_mixed, values, probes, states, table)


def attention_back(
    info, qkv, grad_mixed, logsum, read_query, row_grads, value_grads, musig, rows, row_back, value_back, key_end,
    probe_part, heads,
):
    units, width = qkv.shape[0], heads * HEAD_DIM
    table = jnp.asarray(basis_tables()[1])
    return call(
        attend_back_kernel, heads, units,
        [
            whole(qkv.shape), unit_block(grad_mixed.shape, True, True), unit_block(logsum.shape, False, True),
            unit_block(read_query.shape, False, True), whole(row_grads.shape), place_block(value_grads.shape, True),
            whole(musig.shape), whole(rows.shape), whole(row_back.shape), whole(value_back.shape), whole(key_end.shape),
            whole(probe_part.shape), whole(table.shape),
        ],
        [unit_block(qkv.shape, True, True), whole((8, BASIS))],
        [(qkv.shape, BF16), ((8, BASIS), F32)],
        [
            pltpu.VMEM((BASIS, 2 * LANES), F32), pltpu.VMEM((LIVE, 2 * LANES), BF16),
            pltpu.VMEM((4 * UNIT, LANES), F32), pltpu.VMEM((4 * UNIT, LANES), F32),
            pltpu.VMEM((units, LANES, UNIT), BF16), pltpu.VMEM((width, UNIT), F32),
        ],
        20 << 30, 2 << 20, "attention_back",
    )(
        info, qkv, grad_mixed, logsum, read_query, row_grads, value_grads, musig, rows, row_back, value_back, key_end,
        probe_part, table,
    )


def middle_kernel(
    place, source, cotangent, mixed_0, mixed_1, mixed_2, mixed_3, out_weight, vectors, in_bias, own_in, own_out, far_in,
    far_out, outputs, grad_residual, grad_mixed_0, grad_mixed_1, grad_mixed_2, grad_mixed_3, grad_in, grad_out,
    grad_out_weight, sums, grad_in_bias,
    residual, inverse, second, second_cols, total, grad_second, in_now, out_now,
):
    r = pl.program_id(0)
    own = place[0]
    slices, rows = own_in.shape[0], own_in.shape[1]
    model = source.shape[1]
    hidden_part = own_in.shape[2]
    out_bias, gain, shift, last_bias = (vectors[k : k + 1] for k in range(4))

    @pl.when(r == 0)
    def _():
        value = source[...].astype(F32) + out_bias
        for k, mixed in enumerate((mixed_0, mixed_1, mixed_2, mixed_3)):
            value += dot(mixed[...], out_weight[k])
        residual[...] = value
        centred = value - jnp.mean(value, axis=-1, keepdims=True)
        factor = lax.rsqrt(jnp.mean(centred * centred, axis=-1, keepdims=True) + EPSILON)
        inverse[...] = factor
        normal = centred * factor
        grad_residual[...] = normal
        rounded = (normal * gain + shift).astype(BF16)
        second[...] = rounded
        second_cols[...] = rounded.astype(F32).T.astype(BF16)
        total[...] = jnp.zeros_like(total)
        grad_second[...] = jnp.zeros_like(grad_second)
        grad_in_bias[...] = jnp.zeros_like(grad_in_bias)
        for j in range(slices):
            in_now[j * rows : (j + 1) * rows] = own_in[j]
            out_now[j * rows : (j + 1) * rows] = own_out[j]

    @pl.when(r > 0)
    def _():
        for j in range(slices):
            in_now[j * rows : (j + 1) * rows] = far_in[0, j ^ own]
            out_now[j * rows : (j + 1) * rows] = far_out[0, j ^ own]

    half = hidden_part // 2
    for t in range(2):
        span = slice(t * half, (t + 1) * half)
        hidden = dot(second[...], in_now[:, span]) + in_bias[pl.ds(r, 1), span]
        cube = hidden * hidden
        root = math.sqrt(2.0 / math.pi)
        bent = jnp.tanh(hidden * (root + (root * 0.044715) * cube))
        lifted = 0.5 + 0.5 * bent
        activation = (hidden * lifted).astype(BF16)
        slope = lifted + hidden * ((0.5 - 0.5 * bent * bent) * (root + (3.0 * root * 0.044715) * cube))
        total[...] += dot(activation, out_now[span])
        given = dot(cotangent[...], out_now[span], ((1,), (1,)))
        grad_hidden = (given * slope).astype(BF16)
        grad_second[...] += dot(grad_hidden, in_now[:, span], ((1,), (1,)))
        grad_in_bias[pl.ds(r, 1), span] = jnp.sum(grad_hidden.astype(F32), axis=0, keepdims=True)
        part = dot(activation, cotangent[...], ((0,), (0,))).astype(BF16)
        per = half // rows
        for k in range(per):
            grad_out[0, (t * per + k) ^ own] = part[k * rows : (k + 1) * rows]
        part = dot(second_cols[...], grad_hidden).astype(BF16)
        for j in range(slices):
            grad_in[0, j ^ own, :, span] = part[j * rows : (j + 1) * rows]

    @pl.when(r == pl.num_programs(0) - 1)
    def _():
        given = cotangent[...].astype(F32)
        outputs[...] = (residual[...] + total[...] + last_bias).astype(BF16)
        normal = grad_residual[...]
        grad = grad_second[...]
        scaled = grad * gain
        value = given + inverse[...] * (
            scaled
            - jnp.mean(scaled, axis=-1, keepdims=True)
            - normal * jnp.mean(scaled * normal, axis=-1, keepdims=True)
        )
        sums[0:1] = jnp.sum(value, axis=0, keepdims=True)
        sums[1:2] = jnp.sum(grad * normal, axis=0, keepdims=True)
        sums[2:3] = jnp.sum(grad, axis=0, keepdims=True)
        sums[3:4] = jnp.sum(given, axis=0, keepdims=True)
        sums[4:8] = jnp.zeros((4, model), F32)
        grad_residual[...] = value
        rounded = value.astype(BF16)
        grads = (grad_mixed_0, grad_mixed_1, grad_mixed_2, grad_mixed_3)
        for k, mixed in enumerate((mixed_0, mixed_1, mixed_2, mixed_3)):
            grads[k][...] = dot(rounded, out_weight[k], ((1,), (1,))).astype(BF16)
            grad_out_weight[k] = dot(mixed[...], rounded, ((0,), (0,))).astype(BF16)


def middle(place, source, cotangent, mixed, out_weight, vectors, in_bias, own_in, own_out, far_in, far_out):
    own_rows, model = source.shape
    shards = far_in.shape[0] + 1
    slices, rows, hidden_part = own_in.shape
    narrow = mixed[0].shape
    far = pl.BlockSpec((1,) + own_in.shape, lambda r, place: (jnp.maximum(r - 1, 0), 0, 0, 0))
    part = pl.BlockSpec((1,) + own_in.shape, lambda r, place: (r, 0, 0, 0))
    macs = own_rows * model * (6 * shards * hidden_part + 3 * model)
    return pl.pallas_call(
        middle_kernel,
        grid_spec=pltpu.PrefetchScalarGridSpec(
            num_scalar_prefetch=1,
            grid=(shards,),
            in_specs=[whole(source.shape)] * 2 + [whole(narrow)] * 4 + [
                whole(out_weight.shape), whole(vectors.shape), whole(in_bias.shape), whole(own_in.shape),
                whole(own_out.shape), far, far,
            ],
            out_specs=[whole(source.shape)] * 2 + [whole(narrow)] * 4 + [
                part, part, whole(out_weight.shape), whole((8, model)), whole(in_bias.shape)
            ],
            scratch_shapes=[
                pltpu.VMEM((own_rows, model), F32),
                pltpu.VMEM((own_rows, 1), F32),
                pltpu.VMEM((own_rows, model), BF16),
                pltpu.VMEM((model, own_rows), BF16),
                pltpu.VMEM((own_rows, model), F32),
                pltpu.VMEM((own_rows, model), F32),
                pltpu.VMEM((model, hidden_part), BF16),
                pltpu.VMEM((hidden_part, model), BF16),
            ],
        ),
        out_shape=[
            jax.ShapeDtypeStruct(source.shape, BF16),
            jax.ShapeDtypeStruct(source.shape, F32),
        ] + [jax.ShapeDtypeStruct(narrow, BF16)] * 4 + [
            jax.ShapeDtypeStruct((shards, slices, rows, hidden_part), BF16),
            jax.ShapeDtypeStruct((shards, slices, rows, hidden_part), BF16),
            jax.ShapeDtypeStruct(out_weight.shape, BF16),
            jax.ShapeDtypeStruct((8, model), F32),
            jax.ShapeDtypeStruct(in_bias.shape, F32),
        ],
        compiler_params=pltpu.CompilerParams(vmem_limit_bytes=60 << 20),
        cost_estimate=pl.CostEstimate(
            flops=2 * macs, bytes_accessed=30 << 20, transcendentals=own_rows * shards * hidden_part
        ),
        name="middle",
    )(place, source, cotangent, *mixed, out_weight, vectors, in_bias, own_in, own_out, far_in, far_out)


def finish_kernel(place, given_in, given_out, grad_in, grad_out):
    own = place[0]
    slices, rows = given_in.shape[0], given_in.shape[1]
    for j in range(slices):
        grad_in[j * rows : (j + 1) * rows] = given_in[j ^ own].astype(F32)
        grad_out[j * rows : (j + 1) * rows] = given_out[j ^ own].astype(F32)


def finish(place, given_in, given_out):
    slices, rows, columns = given_in.shape
    return pl.pallas_call(
        finish_kernel,
        grid_spec=pltpu.PrefetchScalarGridSpec(
            num_scalar_prefetch=1,
            grid=(1,),
            in_specs=[pl.BlockSpec(given_in.shape, lambda k, place: (0, 0, 0))] * 2,
            out_specs=[pl.BlockSpec((slices * rows, columns), lambda k, place: (0, 0))] * 2,
        ),
        out_shape=[jax.ShapeDtypeStruct((slices * rows, columns), F32)] * 2,
        compiler_params=pltpu.CompilerParams(vmem_limit_bytes=40 << 20),
        name="finish",
    )(place, given_in, given_out)


def layer_norm(values, gain, shift):
    centred = values - jnp.mean(values, axis=-1, keepdims=True)
    inverse = lax.rsqrt(jnp.mean(centred * centred, axis=-1, keepdims=True) + EPSILON)
    normal = centred * inverse
    return (normal * gain + shift, normal, inverse)


def norm_back(grad, normal, inverse, gain):
    scaled = grad * gain
    return inverse * (
        scaled
        - jnp.mean(scaled, axis=-1, keepdims=True)
        - normal * jnp.mean(scaled * normal, axis=-1, keepdims=True)
    )


def exchange(value, axis, bit):
    size = lax.axis_size(axis)
    return lax.ppermute(value, axis, [(j, j ^ bit) for j in range(size)])


def plane_gather(part, bits):
    held = {0: part}
    for bit in bits:
        order = sorted(held)
        sent = jnp.stack([held[m] for m in order])
        received = exchange(sent, "dp", bit)
        held.update({m ^ bit: received[k] for k, m in enumerate(order)})
    return jnp.stack([held[m] for m in sorted(held)])


def plane_sum(stacked, bits, outer):
    order = list(range(stacked.shape[0]))
    for bit in bits:
        keep = [k for k, m in enumerate(order) if not m & bit]
        send = [order.index(order[k] | bit) for k in keep]
        received = exchange(take(stacked, send), "dp", bit)
        stacked = (take(stacked, keep).astype(F32) + received.astype(F32)).astype(BF16)
        order = [order[k] for k in keep]
    own = stacked[0]
    for bit in outer:
        own = (own.astype(F32) + exchange(own, "dp", bit).astype(F32)).astype(BF16)
    return own


def take(stacked, indices):
    return jnp.concatenate([stacked[k : k + 1] for k in indices])


def to_order(stacked, own):
    size = stacked.shape[0]
    bit = 1
    while bit < size:
        shaped = stacked.reshape((size // (2 * bit), 2, bit) + stacked.shape[1:])
        stacked = jnp.where((own & bit) > 0, shaped[:, ::-1], shaped).reshape(stacked.shape)
        bit *= 2
    return stacked


def local(
    inputs, seg_lengths, ln1_gain, ln1_bias, qkv_weight, qkv_bias, out_weight, out_bias, mem_mu, mem_sig,
    ln2_gain, ln2_bias, ff_in, ff_in_bias, ff_out, ff_out_bias, cotangent,
):
    own_rows, model = inputs.shape
    shards = lax.axis_size("head")
    members = lax.axis_size("dp")
    width = qkv_weight.shape[2]
    heads = width // HEAD_DIM
    hidden_part = ff_in.shape[1]
    units = 2 * own_rows // UNIT
    slots = seg_lengths.shape[1] // 2
    z = lax.axis_index("head")
    run = z // 2
    next_run = lambda value: lax.ppermute(value, "head", [(0, 2), (1, 3)])
    last_run = lambda value: lax.ppermute(value, "head", [(2, 0), (3, 1)])

    slices = min(8, members)
    forth = [bit for bit in (2, 4, 1) if bit < slices]
    turned = forth[1::-1] + forth[2:]
    plain = [bit for bit in (1, 2, 4) if bit < slices]
    back_turned = plain[:1] + plain[:0:-1]
    outer = [1 << k for k in range(3, 16) if 1 << k < members]
    own = lax.axis_index("dp") % slices
    place = own.reshape(1).astype(jnp.int32)
    rows = model // slices
    narrow = width // slices
    mine = lambda array, count: lax.dynamic_slice_in_dim(array, own * count, count, 0)

    source = inputs.astype(F32)
    gain_one = ln1_gain.astype(F32)
    normed1, normal1, inverse1 = layer_norm(source, gain_one, ln1_bias.astype(F32))
    first_own = normed1.astype(BF16)
    first_rows = jnp.concatenate([first_own, exchange(first_own, "head", 1)], axis=0)

    info = segment_info(lax.dynamic_slice_in_dim(seg_lengths[0], run * slots, slots, 0), units, z % 2, run)

    far_slice = exchange(mine(qkv_weight.reshape(model, 3 * width), rows), "head", 2)
    far_weight = to_order(plane_gather(far_slice, plain), own).reshape(model, 3, width)
    far_small = exchange(
        jnp.concatenate([qkv_bias.reshape(1, 3 * width), mem_mu.reshape(1, -1), mem_sig.reshape(1, -1)], axis=1),
        "head", 2,
    )
    far_bias, far_probe = far_small[:, : 3 * width].reshape(3, width), far_small[0, 3 * width :].reshape(-1, BASIS)

    def project(weight, bias, probe):
        pad = ((0, 0), (0, 0), (0, LANES - width))
        flat = jnp.pad(weight, pad).reshape(model, 3 * LANES)
        shift = jnp.pad(bias, pad[1:]).reshape(3 * LANES).astype(F32)
        value = (jnp.dot(first_rows, flat, preferred_element_type=F32) + shift).astype(BF16)
        musig = jnp.concatenate([probe, jnp.zeros((8 - 2 * heads, BASIS), BF16)], axis=0).astype(F32)
        return flat, value.reshape(units, UNIT, 3 * LANES), musig

    sides = [
        project(qkv_weight, qkv_bias, jnp.concatenate([mem_mu, mem_sig], axis=0)),
        project(far_weight, far_bias, far_probe),
    ]
    states = [memory_state(info, qkv, musig, heads) for _, qkv, musig in sides]
    arrived = [(next_run(state[1]), next_run(state[4])) for state in states[::-1]]
    discrete = [attention(info, qkv, heads) for _, qkv, _ in sides]
    reads = [
        memory_read(info, qkv, discrete[k][0], states[k][0], musig, *arrived[k], heads)
        for k, (_, qkv, musig) in enumerate(sides)
    ]
    mixed = [None] * 4
    for k in range(2):
        shared_rows = reads[k][0].reshape(2, own_rows, width)
        mixed[2 * k] = shared_rows[0]
        mixed[2 * k + 1] = exchange(shared_rows[1], "head", 1)

    small = jnp.concatenate(
        [mine(out_weight, narrow), jnp.broadcast_to(ff_in_bias[None], (8, hidden_part))[:, :model]], axis=0
    )
    ff_mine = (mine(ff_in, rows), mine(ff_out, rows))
    small, ff_mine, first_rows = lax.optimization_barrier((small, ff_mine, first_rows))
    small = jnp.stack([small] + [exchange(small, "head", r) for r in range(1, shards)])
    in_bias = small[:, narrow].astype(F32)
    out_full = to_order(plane_gather(small[:, :narrow], plain), own)
    out_full = jnp.swapaxes(out_full, 0, 1).reshape(shards, width, model)
    far_in = jnp.stack([exchange(ff_mine[0], "head", r) for r in range(1, shards)])
    far_out = jnp.stack([exchange(ff_mine[1], "head", r) for r in range(1, shards)])
    far_in = jnp.swapaxes(plane_gather(far_in, forth), 0, 1)
    far_out = jnp.swapaxes(plane_gather(far_out, turned), 0, 1)

    vectors = jnp.concatenate(
        [out_bias[None], ln2_gain[None], ln2_bias[None], ff_out_bias[None], jnp.zeros((4, model), BF16)], axis=0
    ).astype(F32)
    outputs, grad_residual, *rest = middle(
        place, inputs, cotangent, mixed, out_full, vectors, in_bias,
        ff_in.reshape(slices, rows, hidden_part), ff_out.reshape(slices, rows, model), far_in, far_out,
    )
    grad_mixed, (ff_in_part, ff_out_part, out_weight_part, sums, in_bias_part) = rest[:4], rest[4:]
    given = [
        jnp.stack([grad_mixed[2 * k], exchange(grad_mixed[2 * k + 1], "head", 1)]).reshape(units, UNIT, width)
        for k in range(2)
    ]

    read_backs = [
        memory_read_back(info, qkv, given[k], reads[k][1], reads[k][2], states[k][0], heads)
        for k, (_, qkv, _) in enumerate(sides)
    ]
    returned = [(last_run(back[1]), last_run(back[2])) for back in read_backs[::-1]]
    grads = []
    for k, (_, qkv, musig) in enumerate(sides):
        query_part, _, row_grads, value_grads, probe_part = read_backs[k]
        grads.append(attention_back(
            info, qkv, given[k], discrete[k][1], query_part, row_grads, value_grads, musig, states[k][3],
            returned[k][1], returned[k][0], states[k][2], probe_part, heads,
        ))
    flats = [grad[0].reshape(2 * own_rows, 3 * LANES) for grad in grads]
    grad_rows = sum(
        jnp.dot(flat, sides[k][0].T, preferred_element_type=F32) for k, flat in enumerate(flats)
    ).astype(BF16)
    grad_first = grad_rows[:own_rows].astype(F32) + exchange(grad_rows[own_rows:], "head", 1).astype(F32)
    grad_source = grad_residual + norm_back(grad_first, normal1, inverse1, gain_one)

    def owner_sum(part, bits):
        summed = plane_sum(jnp.swapaxes(part, 0, 1), bits, outer)
        terms = [summed[0]] + [exchange(summed[r], "head", r) for r in range(1, shards)]
        return sum(term.astype(F32) for term in terms).astype(BF16)

    ff_out_slice = owner_sum(ff_out_part, plain)
    ff_in_slice = owner_sum(ff_in_part, back_turned)
    out_part = out_weight_part.reshape(shards, slices, narrow, model)
    out_slice = owner_sum(jnp.swapaxes(to_order(jnp.swapaxes(out_part, 0, 1), own), 0, 1), plain)
    ff_in_sum, ff_out_sum = finish(place, plane_gather(ff_in_slice, forth), plane_gather(ff_out_slice, turned))
    out_weight_sum = to_order(plane_gather(out_slice, forth), own).reshape(width, model).astype(F32)

    def qkv_part(flat):
        part = jnp.dot(first_rows.T, flat, preferred_element_type=F32).reshape(model, 3, LANES)[:, :, :width]
        part = to_order(part.astype(BF16).reshape(slices, rows, 3 * width), own)
        return plane_sum(part, plain, outer)

    qkv_slice = qkv_part(flats[0]).astype(F32) + exchange(qkv_part(flats[1]), "head", 2).astype(F32)
    qkv_weight_sum = to_order(plane_gather(qkv_slice.astype(BF16), forth), own).reshape(model, 3, width).astype(F32)

    def owned(k):
        bias = jnp.sum(flats[k].astype(F32), axis=0).reshape(3, LANES)[:, :width].reshape(-1)
        probe = grads[k][1][: 2 * heads].reshape(-1)
        return jnp.concatenate([bias, probe])

    kept = jnp.concatenate([in_bias_part[0], owned(0)])
    kept = kept + exchange(jnp.concatenate([in_bias_part[2], owned(1)]), "head", 2)
    other = in_bias_part[1] + exchange(in_bias_part[3], "head", 2)
    kept = kept.at[:hidden_part].add(exchange(other, "head", 1))
    kept = lax.psum(kept, "dp")
    shared = jnp.concatenate([
        jnp.sum(grad_first * normal1, axis=0)[None], jnp.sum(grad_first, axis=0)[None], sums[:4]
    ])
    for axis, count in (("dp", members), ("head", shards)):
        bit = 1
        while bit < count:
            shared = shared + exchange(shared, axis, bit)
            bit *= 2
    bias_end = hidden_part + 3 * width
    probe_sum = kept[bias_end:].reshape(2 * heads, BASIS)
    return (
        outputs, grad_source.astype(BF16), shared[0], shared[1], qkv_weight_sum,
        kept[hidden_part:bias_end].reshape(3, width), out_weight_sum, shared[2], probe_sum[:heads], probe_sum[heads:],
        shared[3], shared[4], ff_in_sum, kept[:hidden_part], ff_out_sum, shared[5],
    )


def solution(mesh):
    rows, whole = P(("dp", "head"), None), P()
    return jax.shard_map(
        local,
        mesh=mesh,
        in_specs=(
            rows, P("dp", None), whole, whole, P(None, None, "head"), P(None, "head"), P("head", None), whole,
            P("head", None), P("head", None), whole, whole, P(None, "head"), P("head"), P("head", None), whole, rows,
        ),
        out_specs=(
            rows, rows, whole, whole, P(None, None, "head"), P(None, "head"), P("head", None), whole,
            P("head", None), P("head", None), whole, whole, P(None, "head"), P("head"), P("head", None), whole,
        ),
        check_vma=False,
    )
```

```python
import functools
import math

import jax
import jax.numpy as jnp
import ml_dtypes
import numpy as np
from jax import lax
from jax.experimental import pallas as pl
from jax.experimental.pallas import tpu as pltpu
from jax.sharding import PartitionSpec as P

HEAD_DIM = 64
BASIS = 512
UNIT = 256
LANES = 256
TAU = 0.75
RIDGE = 0.5
EPSILON = 1e-05
MESH = pl.DeviceIdType.MESH
SPREAD = 1.0 / 64.0
WIDTH = 1.0 / BASIS
LIVE = BASIS // 2
HIGHEST = lax.Precision.HIGHEST
F32 = jnp.float32
BF16 = jnp.bfloat16


def split_table(table):
    high = table.astype(np.float32).astype(ml_dtypes.bfloat16)
    low = (table.astype(np.float32) - high.astype(np.float32)).astype(ml_dtypes.bfloat16)
    return high, low


@functools.lru_cache(maxsize=None)
def basis_tables():
    centres = np.arange(BASIS) / (BASIS - 1)
    apart = centres[:, None] - centres[None, :]
    gram = np.exp(-apart * apart / (4.0 * WIDTH * WIDTH)) + RIDGE * np.eye(BASIS)
    solve = np.linalg.inv(gram)
    samples = (np.arange(BASIS) + 0.5) / BASIS
    near_gap = TAU * samples[:, None] - centres[None, :]
    far_gap = samples[:, None] - centres[None, :]
    near = np.exp(-near_gap * near_gap / (2.0 * WIDTH * WIDTH))
    far = np.exp(-far_gap * far_gap / (2.0 * WIDTH * WIDTH))
    contract = (near.T @ far) * (TAU / (BASIS * WIDTH * math.sqrt(math.pi)))
    joined = np.concatenate([solve @ contract, solve[:, LIVE:]], axis=1)
    high, low = split_table(joined)
    forward = np.concatenate([high, high, low], axis=1)
    backward = np.concatenate([high.T, high.T, low.T], axis=1)
    return forward, backward


def term_scale(units):
    return (1.0 - TAU) / (WIDTH * math.sqrt(math.pi) * UNIT) / units.astype(F32)


def split3(value):
    high = value.astype(BF16)
    low = (value - high.astype(F32)).astype(BF16)
    return jnp.concatenate([high, low, high], axis=0)


def dot(a, b, contract=((1,), (0,)), precision=None):
    return lax.dot_general(a, b, (contract, ((), ())), precision=precision, preferred_element_type=F32)


def head_rows(heads, width):
    row = lax.broadcasted_iota(jnp.int32, (8, width), 0)
    lane = lax.broadcasted_iota(jnp.int32, (8, width), 1) // HEAD_DIM
    return ((row == lane) | (row == lane + heads)) & (lane < heads)


def read_parts(logits, heads):
    location = 1.0 / (1.0 + jnp.exp(-logits))
    variance = (jnp.maximum(logits, 0.0) + jnp.log1p(jnp.exp(-jnp.abs(logits)))) * SPREAD + WIDTH * WIDTH
    return location[:heads], variance[heads : 2 * heads]


def place_of(index, length):
    return TAU + (1.0 - TAU) * (index.astype(F32) + 0.5) / (length.astype(F32) * UNIT)


def split_rows(value):
    high = value.astype(BF16)
    rest = value - high.astype(F32)
    mid = rest.astype(BF16)
    return high, mid, (rest - mid.astype(F32)).astype(BF16)


def three_pass(left, right_high, right_low, contract=((1,), (0,))):
    high = left.astype(BF16)
    low = (left - high.astype(F32)).astype(BF16)
    return dot(high, right_high, contract) + dot(low, right_high, contract) + dot(high, right_low, contract)


def advance_values(table, value):
    joined = BASIS + LIVE if table.shape[0] == BASIS else BASIS
    high, low = table[:BASIS, :BASIS], table[:BASIS, 2 * joined : 2 * joined + BASIS]
    value_high = value.astype(BF16)
    value_low = (value - value_high.astype(F32)).astype(BF16)
    return dot(high, value_high) + dot(high, value_low) + dot(low, value_high)


def state_kernel(heads, info, qkv, musig, table, states, value_end, key_end, rows, proj, memory, sums):
    b = pl.program_id(0)
    width = heads * HEAD_DIM
    start, length = info[0, b], info[1, b]

    @pl.when(b == 0)
    def _():
        memory[...] = jnp.zeros_like(memory)
        row = musig[...]
        rows[0:8] = row
        wide = 2 * (BASIS + LIVE)
        for k in range(1, 4):
            row = three_pass(row, table[:, :BASIS], table[:, wide : wide + BASIS])
            rows[8 * k : 8 * k + 8] = row

    @pl.when(start == b)
    def _():
        states[0] = memory[...]
        sums[...] = jnp.zeros_like(sums)

    token = lax.broadcasted_iota(jnp.int32, (LIVE, UNIT), 1) + (b - start) * UNIT
    centre = (lax.broadcasted_iota(jnp.int32, (LIVE, UNIT), 0) + LIVE).astype(F32) / (BASIS - 1)
    gap = place_of(token, length) - centre
    psi = jnp.exp(gap * gap * (-0.5 / (WIDTH * WIDTH)))
    psi_high = psi.astype(BF16)
    psi_low = (psi - psi_high.astype(F32)).astype(BF16)
    pairs = qkv[0, :, LANES : 3 * LANES]
    sums[...] += dot(psi_high, pairs) + dot(psi_low, pairs)

    @pl.when(b + 1 == start + length)
    def _():
        stacked = jnp.concatenate([memory[...], sums[...] * term_scale(length)], axis=0)
        memory[...] = dot(table[...], split3(stacked))

    @pl.when(b == pl.num_programs(0) - 1)
    def _():
        key = memory[:, :LANES]
        key_end[...] = key
        value_end[...] = memory[:, LANES : LANES + width].astype(BF16)
        seen = dot(rows[...], key, precision=HIGHEST)
        mask = head_rows(heads, LANES)
        for k in range(4):
            proj[8 * k : 8 * k + 8] = jnp.where(mask, seen[8 * k : 8 * k + 8], 0.0)


def attend_kernel(heads, info, qkv, result, logsum, cols):
    b = pl.program_id(0)
    start = info[0, b]
    flip = info[3, 0] * (pl.num_programs(0) // 2)
    cols[b] = qkv[b ^ flip, :, 2 * LANES : 3 * LANES].astype(F32).T.astype(BF16)
    query = qkv[b ^ flip, :, 0:LANES]
    lane_head = lax.broadcasted_iota(jnp.int32, (UNIT, LANES), 1) // HEAD_DIM

    def attend(blocks):
        causal = lax.broadcasted_iota(jnp.int32, (UNIT, UNIT), 0) <= lax.broadcasted_iota(
            jnp.int32, (UNIT, UNIT), 1
        )
        for h in range(heads):
            own = jnp.where(lane_head == h, query.astype(F32) * (1.0 / math.sqrt(HEAD_DIM)), 0.0).astype(BF16)
            scores = [
                dot(qkv[(start + j) ^ flip, :, LANES : 2 * LANES], own, ((1,), (1,))) for j in range(blocks)
            ]
            scores[-1] = jnp.where(causal, scores[-1], -1e30)
            highest = functools.reduce(jnp.maximum, [jnp.max(s, axis=0, keepdims=True) for s in scores])
            weights = [jnp.exp(s - highest) for s in scores]
            total = sum(jnp.sum(w, axis=0, keepdims=True) for w in weights)
            rows = slice(h * HEAD_DIM, (h + 1) * HEAD_DIM)
            part = sum(dot(cols[start + j, rows], weights[j].astype(BF16)) for j in range(blocks))
            result[0, rows] = part * (1.0 / total)
            logsum[0, h : h + 1] = highest + jnp.log(total)

    for blocks in range(1, 5):
        pl.when(b - start + 1 == blocks)(functools.partial(attend, blocks))


def read_kernel(
    heads, info, qkv, discrete, states, musig, table, value_in, proj, mixed, values, probes, carried, value_cols,
):
    b = pl.program_id(0)
    width = heads * HEAD_DIM
    start, order, run = info[0, b], info[2, b], info[3, 1]

    @pl.when(b == 0)
    def _():
        carried[...] = jnp.zeros_like(carried)
        carried[:, :width] = value_in[...].astype(F32)

    @pl.when((start == b) & (b > 0) & (run > 0))
    def _():
        carried[...] = advance_values(table, carried[...])

    seen = (start > 0) | (run > 0)

    @pl.when(start == b)
    def _():
        rows = dot(musig[...], states[0, :, :LANES], precision=HIGHEST)
        rows = jnp.where(head_rows(heads, LANES), rows, 0.0)
        incoming = proj[pl.ds(pl.multiple_of(order * 8, 8), 8)]
        probes[0] = (rows + incoming) * (1.0 / math.sqrt(HEAD_DIM))
        value = states[0, :, LANES:] + carried[...]
        values[0] = value
        value_cols[...] = value.T.astype(BF16)

    @pl.when(jnp.logical_not(seen))
    def _():
        mixed[0] = discrete[0].T.astype(BF16)

    @pl.when(seen)
    def _():
        query = qkv[0]
        logits = sum(dot(part, query, ((1,), (1,))) for part in split_rows(probes[0]))
        location, variance = read_parts(logits, heads)
        fall = -0.5 / variance
        peak = WIDTH * lax.rsqrt(variance)
        centres = lax.broadcasted_iota(jnp.int32, (BASIS, UNIT), 0).astype(F32) / (BASIS - 1)
        parts = []
        for h in range(heads):
            gap = centres - location[h : h + 1]
            density = jnp.exp(gap * gap * fall[h : h + 1]).astype(BF16)
            rows = slice(h * HEAD_DIM, (h + 1) * HEAD_DIM)
            parts.append(discrete[0, rows] + dot(value_cols[rows], density) * peak[h : h + 1])
        mixed[0] = jnp.concatenate(parts, axis=0).T.astype(BF16)


def read_back_kernel(
    heads, info, qkv, grad_mixed, values, probes, states, table, query_grad, value_back, row_grads, value_grads,
    probe_grad, carried, value_high, value_low, grad_values, probe_cols, row_grad,
):
    step = pl.program_id(0)
    b = pl.num_programs(0) - 1 - step
    width = heads * HEAD_DIM
    start, length, order, run = info[0, b], info[1, b], info[2, b], info[3, 1]
    seen = (start > 0) | (run > 0)

    @pl.when(step == 0)
    def _():
        carried[...] = jnp.zeros_like(carried)
        probe_grad[...] = jnp.zeros_like(probe_grad)
        row_grads[...] = jnp.zeros_like(row_grads)

    @pl.when(b + 1 == start + length)
    def _():
        grad_values[...] = jnp.zeros_like(grad_values)
        row_grad[...] = jnp.zeros_like(row_grad)
        probe_cols[...] = jnp.concatenate([probes[0], jnp.zeros((120, LANES), F32)], axis=0).T
        value = values[0]
        high = value.astype(BF16)
        value_high[...] = high
        value_low[...] = (value - high.astype(F32)).astype(BF16)

    @pl.when(jnp.logical_not(seen))
    def _():
        query_grad[...] = jnp.zeros_like(query_grad)

    @pl.when(seen)
    def _():
        query = qkv[0]
        given = jnp.concatenate([grad_mixed[0], jnp.zeros((UNIT, LANES - width), BF16)], axis=1)
        lane_head = lax.broadcasted_iota(jnp.int32, (UNIT, LANES), 1) // HEAD_DIM
        logits = sum(dot(part, query, ((1,), (1,))) for part in split_rows(probes[0]))
        location, variance = read_parts(logits, heads)
        inverse = 1.0 / variance
        fall = -0.5 * inverse
        peak = WIDTH * lax.rsqrt(variance)
        centres = lax.broadcasted_iota(jnp.int32, (BASIS, UNIT), 0).astype(F32) / (BASIS - 1)
        along, across = [], []
        for h in range(heads):
            own_given = jnp.where(lane_head == h, given.astype(F32), 0.0).astype(BF16)
            gap = centres - location[h : h + 1]
            square = gap * gap
            density = jnp.exp(square * fall[h : h + 1]) * peak[h : h + 1]
            grad_density = dot(value_high[...], own_given, ((1,), (1,))) + dot(
                value_low[...], own_given, ((1,), (1,))
            )
            grad_values[...] += dot(density.astype(BF16), own_given)
            weighed = density * grad_density
            zeroth = jnp.sum(weighed, axis=0, keepdims=True)
            first = jnp.sum(weighed * gap, axis=0, keepdims=True)
            second = jnp.sum(weighed * square, axis=0, keepdims=True)
            along.append(first * inverse[h : h + 1])
            across.append(0.5 * inverse[h : h + 1] * (second * inverse[h : h + 1] - zeroth))
        sigmoid = 1.0 / (1.0 + jnp.exp(-logits))
        grad_location = jnp.concatenate(along, axis=0) * location * (1.0 - location)
        grad_variance = jnp.concatenate(across, axis=0) * SPREAD * sigmoid[heads : 2 * heads]
        grad_logits = jnp.concatenate(
            [grad_location, grad_variance, jnp.zeros((8 - 2 * heads, UNIT), F32)], axis=0
        )
        padded = jnp.concatenate([grad_logits, jnp.zeros((120, UNIT), F32)], axis=0)
        query_grad[0] = dot(probe_cols[...], padded, precision=HIGHEST)[:width]
        row_grad[...] += dot(grad_logits, query.astype(F32), precision=HIGHEST)

    @pl.when((b == start) & seen)
    def _():
        rows = jnp.where(head_rows(heads, LANES), row_grad[...], 0.0) * (1.0 / math.sqrt(HEAD_DIM))
        row_grads[pl.ds(pl.multiple_of(order * 8, 8), 8)] = rows
        probe_grad[...] += dot(rows, states[0], ((1,), (1,)), HIGHEST)

    @pl.when(b == start)
    def _():
        value_grads[0] = grad_values[...]
        total = carried[...] + grad_values[...]
        value_back[...] = total[:, :width].astype(BF16)

        @pl.when(start > 0)
        def _():
            carried[...] = advance_values(table, total)


def attend_back_kernel(
    heads, info, qkv, grad_mixed, logsum, read_query, row_grads, value_grads, musig, rows_in, row_back, value_back,
    key_end, probe_part, table, out, probe_grad, carried, spread, key_grad, value_grad, cols, turned,
):
    step = pl.program_id(0)
    units = pl.num_programs(0)
    b = units - 1 - step
    width = heads * HEAD_DIM
    start, length, order, run = info[0, b], info[1, b], info[2, b], info[3, 1]
    flip = info[3, 0] * (units // 2)

    @pl.when(step == 0)
    def _():
        for i in range(cols.shape[0]):
            cols[i] = qkv[i, :, LANES : 2 * LANES].astype(F32).T.astype(BF16)
        probe_grad[...] = probe_part[...]

    def carry(total, units_before):
        moved = dot(table[...], split3(total))
        carried[...] = moved[:BASIS]
        spread[...] = (moved[BASIS:] * term_scale(units_before)).astype(BF16)

    @pl.when((step == 0) & (run > 0))
    def _():
        carried[...] = jnp.zeros_like(carried)
        spread[...] = jnp.zeros_like(spread)

    @pl.when((step == 0) & (run == 0))
    def _():
        grad_keys = dot(rows_in[...], row_back[...], ((0,), (0,)), HIGHEST)
        pad = jnp.zeros((BASIS, LANES - width), F32)
        carry(jnp.concatenate([grad_keys, value_back[...].astype(F32), pad], axis=1), length)
        seen = dot(row_back[...], key_end[...], ((1,), (1,)), HIGHEST)
        gained = seen[24:32]
        for k in (2, 1, 0):
            gained = three_pass(gained, table[:BASIS, :BASIS], table[:BASIS, 2 * BASIS : 3 * BASIS])
            gained = gained + seen[8 * k : 8 * k + 8]
        probe_grad[...] += gained

    @pl.when(b + 1 == start + length)
    def _():
        key_grad[...] = jnp.zeros_like(key_grad)
        value_grad[...] = jnp.zeros_like(value_grad)

    query = qkv[b ^ flip, :, 0:LANES]
    given = jnp.concatenate([grad_mixed[0], jnp.zeros((UNIT, LANES - width), BF16)], axis=1)
    lane_head = lax.broadcasted_iota(jnp.int32, (UNIT, LANES), 1) // HEAD_DIM

    def attend_back(blocks):
        causal = lax.broadcasted_iota(jnp.int32, (UNIT, UNIT), 0) <= lax.broadcasted_iota(
            jnp.int32, (UNIT, UNIT), 1
        )
        for h in range(heads):
            own = jnp.where(lane_head == h, query.astype(F32) * (1.0 / math.sqrt(HEAD_DIM)), 0.0).astype(BF16)
            own_given = jnp.where(lane_head == h, given.astype(F32), 0.0).astype(BF16)
            probs, products = [], []
            inner = jnp.zeros((1, UNIT), F32)
            for j in range(blocks):
                score = dot(qkv[(start + j) ^ flip, :, LANES : 2 * LANES], own, ((1,), (1,)))
                if j == blocks - 1:
                    score = jnp.where(causal, score, -1e30)
                prob = jnp.exp(score - logsum[0, h : h + 1])
                product = prob * dot(qkv[(start + j) ^ flip, :, 2 * LANES : 3 * LANES], own_given, ((1,), (1,)))
                inner += jnp.sum(product, axis=0, keepdims=True)
                probs.append(prob)
                products.append(product)
            rows = slice(h * HEAD_DIM, (h + 1) * HEAD_DIM)
            result = jnp.zeros((HEAD_DIM, UNIT), F32)
            for j in range(blocks):
                part = slice(j * UNIT, (j + 1) * UNIT)
                grad_score = (products[j] - probs[j] * inner).astype(BF16)
                key_grad[part] += dot(grad_score, own)
                value_grad[part] += dot(probs[j].astype(BF16), own_given)
                result += dot(cols[(start + j) ^ flip, rows], grad_score)
            turned[rows] = result * (1.0 / math.sqrt(HEAD_DIM)) + read_query[0, rows]

    for blocks in range(1, 5):
        pl.when(b - start + 1 == blocks)(functools.partial(attend_back, blocks))

    local = pl.ds(pl.multiple_of((b - start) * UNIT, UNIT), UNIT)

    @pl.when((start + length < units) | (run == 0))
    def _():
        token = lax.broadcasted_iota(jnp.int32, (UNIT, LIVE), 0) + (b - start) * UNIT
        centre = (lax.broadcasted_iota(jnp.int32, (UNIT, LIVE), 1) + LIVE).astype(F32) / (BASIS - 1)
        gap = place_of(token, length) - centre
        psi = jnp.exp(gap * gap * (-0.5 / (WIDTH * WIDTH))).astype(BF16)
        pair_grad = dot(psi, spread[...])
        key_grad[local] += pair_grad[:, :LANES]
        value_grad[local] += pair_grad[:, LANES:]

    query_grad = turned[...].T.astype(BF16)
    out[0, :, :LANES] = jnp.concatenate([query_grad, jnp.zeros((UNIT, LANES - width), BF16)], axis=1)
    out[0, :, LANES : 2 * LANES] = key_grad[local].astype(BF16)
    out[0, :, 2 * LANES :] = value_grad[local].astype(BF16)

    @pl.when((b == start) & (start > 0))
    def _():
        rows = row_grads[pl.ds(pl.multiple_of(order * 8, 8), 8)]
        grad_keys = dot(musig[...], rows, ((0,), (0,)), HIGHEST)
        total = carried[...] + jnp.concatenate([grad_keys, value_grads[0]], axis=1)
        carry(total, info[1, jnp.maximum(start - 1, 0)])


def segment_info(lengths, units, flip, run):
    slot_units = lengths // UNIT
    slots = jnp.arange(lengths.shape[0], dtype=jnp.int32)
    ends = jnp.sum(jnp.where(slots[None, :] <= slots[:, None], slot_units[None, :], 0), axis=1)
    starts = ends - slot_units
    unit = jnp.arange(units, dtype=jnp.int32)[:, None]
    member = (unit >= starts[None, :]) & (unit < ends[None, :])
    start = jnp.sum(jnp.where(member, starts[None, :], 0), axis=1)
    length = jnp.sum(jnp.where(member, slot_units[None, :], 0), axis=1)
    place = jnp.sum(((ends[None, :] <= unit) & (slot_units > 0)[None, :]).astype(jnp.int32), axis=1)
    own = jnp.where(jnp.arange(units) == 0, flip, run)
    return jnp.stack([start, length, place, own]).astype(jnp.int32)


def whole(shape):
    return pl.BlockSpec(shape, lambda i, info: (0,) * len(shape))


def call(kernel, heads, units, in_specs, out_specs, out_shape, scratch, flops, exps, name):
    return pl.pallas_call(
        functools.partial(kernel, heads),
        grid_spec=pltpu.PrefetchScalarGridSpec(
            num_scalar_prefetch=1, grid=(units,), in_specs=in_specs, out_specs=out_specs, scratch_shapes=scratch
        ),
        out_shape=[jax.ShapeDtypeStruct(shape, kind) for shape, kind in out_shape],
        compiler_params=pltpu.CompilerParams(vmem_limit_bytes=56 << 20),
        cost_estimate=pl.CostEstimate(flops=flops, bytes_accessed=8 << 20, transcendentals=exps),
        name=name,
    )


def unit_block(shape, turn, back=False):
    last = shape[0] - 1

    def index(i, info):
        b = last - i if back else i
        b = b ^ (info[3, 0] * ((last + 1) // 2)) if turn else b
        return (b,) + (0,) * (len(shape) - 1)

    return pl.BlockSpec((1,) + shape[1:], index)


def place_block(shape, back=False):
    last = shape[0] - 1
    return pl.BlockSpec(
        (1,) + shape[1:], lambda i, info: (info[2, last - i if back else i],) + (0,) * (len(shape) - 1)
    )


def memory_state(info, qkv, musig, heads):
    units, width = qkv.shape[0], heads * HEAD_DIM
    table = jnp.asarray(basis_tables()[0])
    states = (units, BASIS, 2 * LANES)
    return call(
        state_kernel, heads, units,
        [unit_block(qkv.shape, True), whole(musig.shape), whole(table.shape)],
        [place_block(states), whole((BASIS, width)), whole((BASIS, LANES)), whole((32, BASIS)), whole((32, LANES))],
        [(states, F32), ((BASIS, width), BF16), ((BASIS, LANES), F32), ((32, BASIS), F32), ((32, LANES), F32)],
        [pltpu.VMEM((BASIS, 2 * LANES), F32), pltpu.VMEM((LIVE, 2 * LANES), F32)],
        5 << 30, units * UNIT * LIVE, "memory_state",
    )(info, qkv, musig, table)


def attention(info, qkv, heads):
    units, width = qkv.shape[0], heads * HEAD_DIM
    return call(
        attend_kernel, heads, units,
        [whole(qkv.shape)],
        [unit_block((units, width, UNIT), False), unit_block((units, 8, UNIT), False)],
        [((units, width, UNIT), F32), ((units, 8, UNIT), F32)],
        [pltpu.VMEM((units, LANES, UNIT), BF16)],
        8 << 30, 2 << 20, "attention",
    )(info, qkv)


def memory_read(info, qkv, discrete, states, musig, value_in, proj, heads):
    units, width = qkv.shape[0], heads * HEAD_DIM
    table = jnp.asarray(basis_tables()[0])
    return call(
        read_kernel, heads, units,
        [
            unit_block((units, UNIT, LANES), True), unit_block(discrete.shape, False), place_block(states.shape),
            whole(musig.shape), whole(table.shape), whole(value_in.shape), whole(proj.shape),
        ],
        [unit_block((units, UNIT, width), True), place_block((units, BASIS, LANES)), place_block((units, 8, LANES))],
        [((units, UNIT, width), BF16), ((units, BASIS, LANES), F32), ((units, 8, LANES), F32)],
        [pltpu.VMEM((BASIS, LANES), F32), pltpu.VMEM((LANES, BASIS), BF16)],
        3 << 30, 2 << 20, "memory_read",
    )(info, qkv, discrete, states, musig, table, value_in, proj)


def memory_read_back(info, qkv, grad_mixed, values, probes, states, heads):
    units, width = qkv.shape[0], heads * HEAD_DIM
    table = jnp.asarray(basis_tables()[1])
    return call(
        read_back_kernel, heads, units,
        [
            unit_block((units, UNIT, LANES), True, True), unit_block(grad_mixed.shape, True, True),
            place_block(values.shape, True), place_block(probes.shape, True),
            place_block((units, BASIS, LANES), True), whole(table.shape),
        ],
        [
            unit_block((units, width, UNIT), False, True), whole((BASIS, width)), whole((32, LANES)),
            place_block((units, BASIS, LANES), True), whole((8, BASIS)),
        ],
        [
            ((units, width, UNIT), F32), ((BASIS, width), BF16), ((32, LANES), F32), ((units, BASIS, LANES), F32),
            ((8, BASIS), F32),
        ],
        [
            pltpu.VMEM((BASIS, LANES), F32), pltpu.VMEM((BASIS, LANES), BF16), pltpu.VMEM((BASIS, LANES), BF16),
            pltpu.VMEM((BASIS, LANES), F32), pltpu.VMEM((LANES, 128), F32), pltpu.VMEM((8, LANES), F32),
        ],
        6 << 30, 2 << 20, "memory_read_back",
    )(info, qkv, grad_mixed, values, probes, states, table)


def attention_back(
    info, qkv, grad_mixed, logsum, read_query, row_grads, value_grads, musig, rows, row_back, value_back, key_end,
    probe_part, heads,
):
    units, width = qkv.shape[0], heads * HEAD_DIM
    table = jnp.asarray(basis_tables()[1])
    return call(
        attend_back_kernel, heads, units,
        [
            whole(qkv.shape), unit_block(grad_mixed.shape, True, True), unit_block(logsum.shape, False, True),
            unit_block(read_query.shape, False, True), whole(row_grads.shape), place_block(value_grads.shape, True),
            whole(musig.shape), whole(rows.shape), whole(row_back.shape), whole(value_back.shape), whole(key_end.shape),
            whole(probe_part.shape), whole(table.shape),
        ],
        [unit_block(qkv.shape, True, True), whole((8, BASIS))],
        [(qkv.shape, BF16), ((8, BASIS), F32)],
        [
            pltpu.VMEM((BASIS, 2 * LANES), F32), pltpu.VMEM((LIVE, 2 * LANES), BF16),
            pltpu.VMEM((4 * UNIT, LANES), F32), pltpu.VMEM((4 * UNIT, LANES), F32),
            pltpu.VMEM((units, LANES, UNIT), BF16), pltpu.VMEM((width, UNIT), F32),
        ],
        20 << 30, 2 << 20, "attention_back",
    )(
        info, qkv, grad_mixed, logsum, read_query, row_grads, value_grads, musig, rows, row_back, value_back, key_end,
        probe_part, table,
    )


def other_of(index, bit):
    return index + bit - 2 * bit * ((index // bit) % 2)


class Hops:
    def __init__(self, send, recv):
        self.send, self.recv, self.used = send, recv, 0

    def start(self, source, target, axis, bit):
        copy = pltpu.make_async_remote_copy(
            src_ref=source,
            dst_ref=target,
            send_sem=self.send.at[self.used],
            recv_sem=self.recv.at[self.used],
            device_id={axis: other_of(lax.axis_index(axis), bit)},
            device_id_type=MESH,
        )
        self.used += 1
        copy.start()
        return copy


def greet(neighbours):
    barrier = pltpu.get_barrier_semaphore()
    for axis, bit in neighbours:
        pl.semaphore_signal(
            barrier, inc=1, device_id={axis: other_of(lax.axis_index(axis), bit)}, device_id_type=MESH
        )
    pl.semaphore_wait(barrier, len(neighbours))


def front_kernel(
    source, scales, weight, small, qkv_a, qkv_b, first_rows, first_cols, flat_a, flat_b, far_small,
    near, far, far_row, send, recv,
):
    own_rows, model = source.shape
    wide = weight.shape[1]
    width = wide // 3
    place = lax.axis_index("dp") % 8
    y, x, c = place // 4, (place // 2) % 2, place % 2
    rows = model // 8
    greet((("head", 1), ("head", 2), ("dp", 1), ("dp", 2), ("dp", 4)))
    hops = Hops(send, recv)
    mine = weight.at[pl.ds(pl.multiple_of(place * rows, 16), rows)]
    slice_copy = hops.start(mine, far.at[y, x, c], "head", 2)
    small_copy = hops.start(small, far_row, "head", 2)

    def norm(part):
        value = source[part].astype(F32)
        centred = value - jnp.mean(value, axis=-1, keepdims=True)
        factor = lax.rsqrt(jnp.mean(centred * centred, axis=-1, keepdims=True) + EPSILON)
        return (centred * factor * scales[0:1] + scales[1:2]).astype(BF16)

    row_copies = []
    for k in range(own_rows // UNIT):
        part = slice(k * UNIT, (k + 1) * UNIT)
        first_rows[part] = norm(part)
        row_copies.append(hops.start(first_rows.at[part], near.at[part], "head", 1))

    slice_copy.wait_recv()
    x_copy = hops.start(far.at[y, x, c], far.at[y, x, c], "dp", 2)

    def widen(flat, read):
        flat[...] = jnp.zeros_like(flat)
        for k in range(3):
            flat[:, k * LANES : k * LANES + width] = read(slice(k * width, (k + 1) * width))

    widen(flat_a, lambda span: weight[:, span])

    def project(unit, rows_in, flat, shift, out):
        out[unit] = (dot(rows_in, flat[...]) + shift).astype(BF16)

    for k in range(own_rows // UNIT):
        project(k, first_rows[k * UNIT : (k + 1) * UNIT], flat_a, small[0:1], qkv_a)
    x_copy.wait_recv()
    y_copy = hops.start(far.at[y, :, c], far.at[y, :, c], "dp", 4)
    first_cols[:, :own_rows] = first_rows[:own_rows].astype(F32).T.astype(BF16)
    y_copy.wait_recv()
    core_copy = hops.start(far.at[:, :, c], far.at[:, :, c], "dp", 1)
    small_copy.wait_recv()
    far_small[...] = far_row[...]
    for k, copy in enumerate(row_copies):
        copy.wait_recv()
        part = slice(k * UNIT, (k + 1) * UNIT)
        first_rows[own_rows + k * UNIT : own_rows + (k + 1) * UNIT] = near[part]
        project(own_rows // UNIT + k, near[part], flat_a, small[0:1], qkv_a)
    first_cols[:, own_rows:] = near[...].astype(F32).T.astype(BF16)
    core_copy.wait_recv()
    widen(flat_b, lambda span: far[:, :, :, :, span].reshape(model, width))
    for k in range(2 * own_rows // UNIT):
        project(k, first_rows[k * UNIT : (k + 1) * UNIT], flat_b, far_row[0:1], qkv_b)
    for copy in [slice_copy, small_copy, x_copy, y_copy, core_copy] + row_copies:
        copy.wait_send()


def front(source, scales, weight, small):
    own_rows, model = source.shape
    wide = weight.shape[1]
    units = 2 * own_rows // UNIT
    hops = 5 + own_rows // UNIT
    vmem = pl.BlockSpec(memory_space=pltpu.VMEM)
    qkv = jax.ShapeDtypeStruct((units, UNIT, 3 * LANES), BF16)
    flat = jax.ShapeDtypeStruct((model, 3 * LANES), BF16)
    return pl.pallas_call(
        front_kernel,
        in_specs=[vmem] * 4,
        out_specs=[vmem] * 7,
        out_shape=[
            qkv, qkv, jax.ShapeDtypeStruct((2 * own_rows, model), BF16),
            jax.ShapeDtypeStruct((model, 2 * own_rows), BF16), flat, flat, jax.ShapeDtypeStruct(small.shape, F32),
        ],
        scratch_shapes=[
            pltpu.VMEM((own_rows, model), BF16),
            pltpu.VMEM((2, 2, 2, model // 8, wide), BF16),
            pltpu.VMEM(small.shape, F32),
            pltpu.SemaphoreType.DMA((hops,)),
            pltpu.SemaphoreType.DMA((hops,)),
        ],
        compiler_params=pltpu.CompilerParams(
            collective_id=1, has_side_effects=True, vmem_limit_bytes=56 << 20
        ),
        name="front",
    )(source, scales, weight, small)


def middle_kernel(
    place, source, cotangent, mixed_0, mixed_1, mixed_2, mixed_3, out_weight, vectors, in_bias, own_in, own_out, far_in,
    far_out, outputs, grad_residual, grad_mixed_0, grad_mixed_1, grad_mixed_2, grad_mixed_3, grad_in, grad_out,
    grad_out_weight, sums, grad_in_bias,
    residual, inverse, second, second_cols, total, grad_second, in_now, out_now,
):
    r = pl.program_id(0)
    own = place[0]
    slices, rows = own_in.shape[0], own_in.shape[1]
    model = source.shape[1]
    hidden_part = own_in.shape[2]
    out_bias, gain, shift, last_bias = (vectors[k : k + 1] for k in range(4))

    @pl.when(r == 0)
    def _():
        value = source[...].astype(F32) + out_bias
        for k, mixed in enumerate((mixed_0, mixed_1, mixed_2, mixed_3)):
            value += dot(mixed[...], out_weight[k])
        residual[...] = value
        centred = value - jnp.mean(value, axis=-1, keepdims=True)
        factor = lax.rsqrt(jnp.mean(centred * centred, axis=-1, keepdims=True) + EPSILON)
        inverse[...] = factor
        normal = centred * factor
        grad_residual[...] = normal
        rounded = (normal * gain + shift).astype(BF16)
        second[...] = rounded
        second_cols[...] = rounded.astype(F32).T.astype(BF16)
        total[...] = jnp.zeros_like(total)
        grad_second[...] = jnp.zeros_like(grad_second)
        grad_in_bias[...] = jnp.zeros_like(grad_in_bias)
        for j in range(slices):
            in_now[j * rows : (j + 1) * rows] = own_in[j]
            out_now[j * rows : (j + 1) * rows] = own_out[j]

    @pl.when(r > 0)
    def _():
        for j in range(slices):
            in_now[j * rows : (j + 1) * rows] = far_in[0, j ^ own]
            out_now[j * rows : (j + 1) * rows] = far_out[0, j ^ own]

    half = hidden_part // 2
    for t in range(2):
        span = slice(t * half, (t + 1) * half)
        hidden = dot(second[...], in_now[:, span]) + in_bias[pl.ds(r, 1), span]
        cube = hidden * hidden
        root = math.sqrt(2.0 / math.pi)
        bent = jnp.tanh(hidden * (root + (root * 0.044715) * cube))
        lifted = 0.5 + 0.5 * bent
        activation = (hidden * lifted).astype(BF16)
        slope = lifted + hidden * ((0.5 - 0.5 * bent * bent) * (root + (3.0 * root * 0.044715) * cube))
        total[...] += dot(activation, out_now[span])
        given = dot(cotangent[...], out_now[span], ((1,), (1,)))
        grad_hidden = (given * slope).astype(BF16)
        grad_second[...] += dot(grad_hidden, in_now[:, span], ((1,), (1,)))
        grad_in_bias[pl.ds(r, 1), span] = jnp.sum(grad_hidden.astype(F32), axis=0, keepdims=True)
        part = dot(activation, cotangent[...], ((0,), (0,))).astype(BF16)
        per = half // rows
        for k in range(per):
            grad_out[0, (t * per + k) ^ own] = part[k * rows : (k + 1) * rows]
        part = dot(second_cols[...], grad_hidden).astype(BF16)
        for j in range(slices):
            grad_in[0, j ^ own, :, span] = part[j * rows : (j + 1) * rows]

    @pl.when(r == pl.num_programs(0) - 1)
    def _():
        given = cotangent[...].astype(F32)
        outputs[...] = (residual[...] + total[...] + last_bias).astype(BF16)
        normal = grad_residual[...]
        grad = grad_second[...]
        scaled = grad * gain
        value = given + inverse[...] * (
            scaled
            - jnp.mean(scaled, axis=-1, keepdims=True)
            - normal * jnp.mean(scaled * normal, axis=-1, keepdims=True)
        )
        sums[0:1] = jnp.sum(value, axis=0, keepdims=True)
        sums[1:2] = jnp.sum(grad * normal, axis=0, keepdims=True)
        sums[2:3] = jnp.sum(grad, axis=0, keepdims=True)
        sums[3:4] = jnp.sum(given, axis=0, keepdims=True)
        sums[4:8] = jnp.zeros((4, model), F32)
        grad_residual[...] = value
        rounded = value.astype(BF16)
        grads = (grad_mixed_0, grad_mixed_1, grad_mixed_2, grad_mixed_3)
        for k, mixed in enumerate((mixed_0, mixed_1, mixed_2, mixed_3)):
            grads[k][...] = dot(rounded, out_weight[k], ((1,), (1,))).astype(BF16)
            grad_out_weight[k] = dot(mixed[...], rounded, ((0,), (0,))).astype(BF16)


def middle(place, source, cotangent, mixed, out_weight, vectors, in_bias, own_in, own_out, far_in, far_out):
    own_rows, model = source.shape
    shards = far_in.shape[0] + 1
    slices, rows, hidden_part = own_in.shape
    narrow = mixed[0].shape
    far = pl.BlockSpec((1,) + own_in.shape, lambda r, place: (jnp.maximum(r - 1, 0), 0, 0, 0))
    part = pl.BlockSpec((1,) + own_in.shape, lambda r, place: (r, 0, 0, 0))
    macs = own_rows * model * (6 * shards * hidden_part + 3 * model)
    return pl.pallas_call(
        middle_kernel,
        grid_spec=pltpu.PrefetchScalarGridSpec(
            num_scalar_prefetch=1,
            grid=(shards,),
            in_specs=[whole(source.shape)] * 2 + [whole(narrow)] * 4 + [
                whole(out_weight.shape), whole(vectors.shape), whole(in_bias.shape), whole(own_in.shape),
                whole(own_out.shape), far, far,
            ],
            out_specs=[whole(source.shape)] * 2 + [whole(narrow)] * 4 + [
                part, part, whole(out_weight.shape), whole((8, model)), whole(in_bias.shape)
            ],
            scratch_shapes=[
                pltpu.VMEM((own_rows, model), F32),
                pltpu.VMEM((own_rows, 1), F32),
                pltpu.VMEM((own_rows, model), BF16),
                pltpu.VMEM((model, own_rows), BF16),
                pltpu.VMEM((own_rows, model), F32),
                pltpu.VMEM((own_rows, model), F32),
                pltpu.VMEM((model, hidden_part), BF16),
                pltpu.VMEM((hidden_part, model), BF16),
            ],
        ),
        out_shape=[
            jax.ShapeDtypeStruct(source.shape, BF16),
            jax.ShapeDtypeStruct(source.shape, F32),
        ] + [jax.ShapeDtypeStruct(narrow, BF16)] * 4 + [
            jax.ShapeDtypeStruct((shards, slices, rows, hidden_part), BF16),
            jax.ShapeDtypeStruct((shards, slices, rows, hidden_part), BF16),
            jax.ShapeDtypeStruct(out_weight.shape, BF16),
            jax.ShapeDtypeStruct((8, model), F32),
            jax.ShapeDtypeStruct(in_bias.shape, F32),
        ],
        compiler_params=pltpu.CompilerParams(vmem_limit_bytes=60 << 20),
        cost_estimate=pl.CostEstimate(
            flops=2 * macs, bytes_accessed=30 << 20, transcendentals=own_rows * shards * hidden_part
        ),
        name="middle",
    )(place, source, cotangent, *mixed, out_weight, vectors, in_bias, own_in, own_out, far_in, far_out)


def finish_kernel(place, given_in, given_out, grad_in, grad_out):
    own = place[0]
    slices, rows = given_in.shape[0], given_in.shape[1]
    for j in range(slices):
        grad_in[j * rows : (j + 1) * rows] = given_in[j ^ own].astype(F32)
        grad_out[j * rows : (j + 1) * rows] = given_out[j ^ own].astype(F32)


def finish(place, given_in, given_out):
    slices, rows, columns = given_in.shape
    return pl.pallas_call(
        finish_kernel,
        grid_spec=pltpu.PrefetchScalarGridSpec(
            num_scalar_prefetch=1,
            grid=(1,),
            in_specs=[pl.BlockSpec(given_in.shape, lambda k, place: (0, 0, 0))] * 2,
            out_specs=[pl.BlockSpec((slices * rows, columns), lambda k, place: (0, 0))] * 2,
        ),
        out_shape=[jax.ShapeDtypeStruct((slices * rows, columns), F32)] * 2,
        compiler_params=pltpu.CompilerParams(vmem_limit_bytes=40 << 20),
        name="finish",
    )(place, given_in, given_out)


def layer_norm(values, gain, shift):
    centred = values - jnp.mean(values, axis=-1, keepdims=True)
    inverse = lax.rsqrt(jnp.mean(centred * centred, axis=-1, keepdims=True) + EPSILON)
    normal = centred * inverse
    return (normal * gain + shift, normal, inverse)


def norm_back(grad, normal, inverse, gain):
    scaled = grad * gain
    return inverse * (
        scaled
        - jnp.mean(scaled, axis=-1, keepdims=True)
        - normal * jnp.mean(scaled * normal, axis=-1, keepdims=True)
    )


def exchange(value, axis, bit):
    size = lax.axis_size(axis)
    return lax.ppermute(value, axis, [(j, j ^ bit) for j in range(size)])


def plane_gather(part, bits):
    held = {0: part}
    for bit in bits:
        order = sorted(held)
        sent = jnp.stack([held[m] for m in order])
        received = exchange(sent, "dp", bit)
        held.update({m ^ bit: received[k] for k, m in enumerate(order)})
    return jnp.stack([held[m] for m in sorted(held)])


def plane_sum(stacked, bits, outer):
    order = list(range(stacked.shape[0]))
    for bit in bits:
        keep = [k for k, m in enumerate(order) if not m & bit]
        send = [order.index(order[k] | bit) for k in keep]
        received = exchange(take(stacked, send), "dp", bit)
        stacked = (take(stacked, keep).astype(F32) + received.astype(F32)).astype(BF16)
        order = [order[k] for k in keep]
    own = stacked[0]
    for bit in outer:
        own = (own.astype(F32) + exchange(own, "dp", bit).astype(F32)).astype(BF16)
    return own


def take(stacked, indices):
    return jnp.concatenate([stacked[k : k + 1] for k in indices])


def to_order(stacked, own):
    size = stacked.shape[0]
    bit = 1
    while bit < size:
        shaped = stacked.reshape((size // (2 * bit), 2, bit) + stacked.shape[1:])
        stacked = jnp.where((own & bit) > 0, shaped[:, ::-1], shaped).reshape(stacked.shape)
        bit *= 2
    return stacked


def local(
    inputs, seg_lengths, ln1_gain, ln1_bias, qkv_weight, qkv_bias, out_weight, out_bias, mem_mu, mem_sig,
    ln2_gain, ln2_bias, ff_in, ff_in_bias, ff_out, ff_out_bias, cotangent,
):
    own_rows, model = inputs.shape
    shards = lax.axis_size("head")
    members = lax.axis_size("dp")
    width = qkv_weight.shape[2]
    heads = width // HEAD_DIM
    hidden_part = ff_in.shape[1]
    units = 2 * own_rows // UNIT
    slots = seg_lengths.shape[1] // 2
    z = lax.axis_index("head")
    run = z // 2
    next_run = lambda value: lax.ppermute(value, "head", [(0, 2), (1, 3)])
    last_run = lambda value: lax.ppermute(value, "head", [(2, 0), (3, 1)])

    slices = min(8, members)
    forth = [bit for bit in (2, 4, 1) if bit < slices]
    turned = forth[1::-1] + forth[2:]
    plain = [bit for bit in (1, 2, 4) if bit < slices]
    back_turned = plain[:1] + plain[:0:-1]
    outer = [1 << k for k in range(3, 16) if 1 << k < members]
    own = lax.axis_index("dp") % slices
    place = own.reshape(1).astype(jnp.int32)
    rows = model // slices
    narrow = width // slices
    mine = lambda array, count: lax.dynamic_slice_in_dim(array, own * count, count, 0)

    source = inputs.astype(F32)
    gain_one = ln1_gain.astype(F32)
    _, normal1, inverse1 = layer_norm(source, gain_one, ln1_bias.astype(F32))
    info = segment_info(lax.dynamic_slice_in_dim(seg_lengths[0], run * slots, slots, 0), units, z % 2, run)
    scales = jnp.concatenate([ln1_gain[None], ln1_bias[None], jnp.zeros((6, model), BF16)], axis=0).astype(F32)
    bias_row = jnp.pad(qkv_bias, ((0, 0), (0, LANES - width))).reshape(1, 3 * LANES)
    probe_rows = jnp.pad(jnp.concatenate([mem_mu, mem_sig], axis=0), ((0, 15 - 2 * heads), (0, 3 * LANES - BASIS)))
    small = jnp.concatenate([bias_row, probe_rows], axis=0).astype(F32)
    qkv_a, qkv_b, first_rows, first_cols, flat_a, flat_b, far_small = front(
        inputs, scales, qkv_weight.reshape(model, 3 * width), small
    )
    sides = [(flat_a, qkv_a, small[1:9, :BASIS]), (flat_b, qkv_b, far_small[1:9, :BASIS])]
    states = [memory_state(info, qkv, musig, heads) for _, qkv, musig in sides]
    arrived = [(next_run(state[1]), next_run(state[4])) for state in states[::-1]]
    discrete = [attention(info, qkv, heads) for _, qkv, _ in sides]
    reads = [
        memory_read(info, qkv, discrete[k][0], states[k][0], musig, *arrived[k], heads)
        for k, (_, qkv, musig) in enumerate(sides)
    ]
    mixed = [None] * 4
    for k in range(2):
        shared_rows = reads[k][0].reshape(2, own_rows, width)
        mixed[2 * k] = shared_rows[0]
        mixed[2 * k + 1] = exchange(shared_rows[1], "head", 1)

    small = jnp.concatenate(
        [mine(out_weight, narrow), jnp.broadcast_to(ff_in_bias[None], (8, hidden_part))[:, :model]], axis=0
    )
    ff_mine = (mine(ff_in, rows), mine(ff_out, rows))
    small, ff_mine, first_rows = lax.optimization_barrier((small, ff_mine, first_rows))
    small = jnp.stack([small] + [exchange(small, "head", r) for r in range(1, shards)])
    in_bias = small[:, narrow].astype(F32)
    out_full = to_order(plane_gather(small[:, :narrow], plain), own)
    out_full = jnp.swapaxes(out_full, 0, 1).reshape(shards, width, model)
    far_in = jnp.stack([exchange(ff_mine[0], "head", r) for r in range(1, shards)])
    far_out = jnp.stack([exchange(ff_mine[1], "head", r) for r in range(1, shards)])
    far_in = jnp.swapaxes(plane_gather(far_in, forth), 0, 1)
    far_out = jnp.swapaxes(plane_gather(far_out, turned), 0, 1)

    vectors = jnp.concatenate(
        [out_bias[None], ln2_gain[None], ln2_bias[None], ff_out_bias[None], jnp.zeros((4, model), BF16)], axis=0
    ).astype(F32)
    outputs, grad_residual, *rest = middle(
        place, inputs, cotangent, mixed, out_full, vectors, in_bias,
        ff_in.reshape(slices, rows, hidden_part), ff_out.reshape(slices, rows, model), far_in, far_out,
    )
    grad_mixed, (ff_in_part, ff_out_part, out_weight_part, sums, in_bias_part) = rest[:4], rest[4:]
    given = [
        jnp.stack([grad_mixed[2 * k], exchange(grad_mixed[2 * k + 1], "head", 1)]).reshape(units, UNIT, width)
        for k in range(2)
    ]

    read_backs = [
        memory_read_back(info, qkv, given[k], reads[k][1], reads[k][2], states[k][0], heads)
        for k, (_, qkv, _) in enumerate(sides)
    ]
    returned = [(last_run(back[1]), last_run(back[2])) for back in read_backs[::-1]]
    grads = []
    for k, (_, qkv, musig) in enumerate(sides):
        query_part, _, row_grads, value_grads, probe_part = read_backs[k]
        grads.append(attention_back(
            info, qkv, given[k], discrete[k][1], query_part, row_grads, value_grads, musig, states[k][3],
            returned[k][1], returned[k][0], states[k][2], probe_part, heads,
        ))
    flats = [grad[0].reshape(2 * own_rows, 3 * LANES) for grad in grads]
    grad_rows = sum(
        jnp.dot(flat, sides[k][0].T, preferred_element_type=F32) for k, flat in enumerate(flats)
    ).astype(BF16)
    grad_first = grad_rows[:own_rows].astype(F32) + exchange(grad_rows[own_rows:], "head", 1).astype(F32)
    grad_source = grad_residual + norm_back(grad_first, normal1, inverse1, gain_one)

    def owner_sum(part, bits):
        summed = plane_sum(jnp.swapaxes(part, 0, 1), bits, outer)
        terms = [summed[0]] + [exchange(summed[r], "head", r) for r in range(1, shards)]
        return sum(term.astype(F32) for term in terms).astype(BF16)

    ff_out_slice = owner_sum(ff_out_part, plain)
    ff_in_slice = owner_sum(ff_in_part, back_turned)
    out_part = out_weight_part.reshape(shards, slices, narrow, model)
    out_slice = owner_sum(jnp.swapaxes(to_order(jnp.swapaxes(out_part, 0, 1), own), 0, 1), plain)
    ff_in_sum, ff_out_sum = finish(place, plane_gather(ff_in_slice, forth), plane_gather(ff_out_slice, turned))
    out_weight_sum = to_order(plane_gather(out_slice, forth), own).reshape(width, model).astype(F32)

    def qkv_part(flat):
        part = jnp.dot(first_cols, flat, preferred_element_type=F32).reshape(model, 3, LANES)[:, :, :width]
        part = to_order(part.astype(BF16).reshape(slices, rows, 3 * width), own)
        return plane_sum(part, plain, outer)

    qkv_slice = qkv_part(flats[0]).astype(F32) + exchange(qkv_part(flats[1]), "head", 2).astype(F32)
    qkv_weight_sum = to_order(plane_gather(qkv_slice.astype(BF16), forth), own).reshape(model, 3, width).astype(F32)

    def owned(k):
        bias = jnp.sum(flats[k].astype(F32), axis=0).reshape(3, LANES)[:, :width].reshape(-1)
        probe = grads[k][1][: 2 * heads].reshape(-1)
        return jnp.concatenate([bias, probe])

    kept = jnp.concatenate([in_bias_part[0], owned(0)])
    kept = kept + exchange(jnp.concatenate([in_bias_part[2], owned(1)]), "head", 2)
    other = in_bias_part[1] + exchange(in_bias_part[3], "head", 2)
    kept = kept.at[:hidden_part].add(exchange(other, "head", 1))
    kept = lax.psum(kept, "dp")
    shared = jnp.concatenate([
        jnp.sum(grad_first * normal1, axis=0)[None], jnp.sum(grad_first, axis=0)[None], sums[:4]
    ])
    for axis, count in (("dp", members), ("head", shards)):
        bit = 1
        while bit < count:
            shared = shared + exchange(shared, axis, bit)
            bit *= 2
    bias_end = hidden_part + 3 * width
    probe_sum = kept[bias_end:].reshape(2 * heads, BASIS)
    return (
        outputs, grad_source.astype(BF16), shared[0], shared[1], qkv_weight_sum,
        kept[hidden_part:bias_end].reshape(3, width), out_weight_sum, shared[2], probe_sum[:heads], probe_sum[heads:],
        shared[3], shared[4], ff_in_sum, kept[:hidden_part], ff_out_sum, shared[5],
    )


def solution(mesh):
    rows, whole = P(("dp", "head"), None), P()
    return jax.shard_map(
        local,
        mesh=mesh,
        in_specs=(
            rows, P("dp", None), whole, whole, P(None, None, "head"), P(None, "head"), P("head", None), whole,
            P("head", None), P("head", None), whole, whole, P(None, "head"), P("head"), P("head", None), whole, rows,
        ),
        out_specs=(
            rows, rows, whole, whole, P(None, None, "head"), P(None, "head"), P("head", None), whole,
            P("head", None), P("head", None), whole, whole, P(None, "head"), P("head"), P("head", None), whole,
        ),
        check_vma=False,
    )
```

```python
import functools
import math

import jax
import jax.numpy as jnp
import ml_dtypes
import numpy as np
from jax import lax
from jax.experimental import pallas as pl
from jax.experimental.pallas import tpu as pltpu
from jax.sharding import PartitionSpec as P

HEAD_DIM = 64
BASIS = 512
UNIT = 256
LANES = 256
TAU = 0.75
RIDGE = 0.5
EPSILON = 1e-05
MESH = pl.DeviceIdType.MESH
SPREAD = 1.0 / 64.0
WIDTH = 1.0 / BASIS
LIVE = BASIS // 2
HIGHEST = lax.Precision.HIGHEST
F32 = jnp.float32
BF16 = jnp.bfloat16


def split_table(table):
    high = table.astype(np.float32).astype(ml_dtypes.bfloat16)
    low = (table.astype(np.float32) - high.astype(np.float32)).astype(ml_dtypes.bfloat16)
    return high, low


@functools.lru_cache(maxsize=None)
def basis_tables():
    centres = np.arange(BASIS) / (BASIS - 1)
    apart = centres[:, None] - centres[None, :]
    gram = np.exp(-apart * apart / (4.0 * WIDTH * WIDTH)) + RIDGE * np.eye(BASIS)
    solve = np.linalg.inv(gram)
    samples = (np.arange(BASIS) + 0.5) / BASIS
    near_gap = TAU * samples[:, None] - centres[None, :]
    far_gap = samples[:, None] - centres[None, :]
    near = np.exp(-near_gap * near_gap / (2.0 * WIDTH * WIDTH))
    far = np.exp(-far_gap * far_gap / (2.0 * WIDTH * WIDTH))
    contract = (near.T @ far) * (TAU / (BASIS * WIDTH * math.sqrt(math.pi)))
    joined = np.concatenate([solve @ contract, solve[:, LIVE:]], axis=1)
    high, low = split_table(joined)
    forward = np.concatenate([high, high, low], axis=1)
    backward = np.concatenate([high.T, high.T, low.T], axis=1)
    return forward, backward


def term_scale(units):
    return (1.0 - TAU) / (WIDTH * math.sqrt(math.pi) * UNIT) / units.astype(F32)


def split3(value):
    high = value.astype(BF16)
    low = (value - high.astype(F32)).astype(BF16)
    return jnp.concatenate([high, low, high], axis=0)


def dot(a, b, contract=((1,), (0,)), precision=None):
    return lax.dot_general(a, b, (contract, ((), ())), precision=precision, preferred_element_type=F32)


def head_rows(heads, width):
    row = lax.broadcasted_iota(jnp.int32, (8, width), 0)
    lane = lax.broadcasted_iota(jnp.int32, (8, width), 1) // HEAD_DIM
    return ((row == lane) | (row == lane + heads)) & (lane < heads)


def read_parts(logits, heads):
    location = 1.0 / (1.0 + jnp.exp(-logits))
    variance = (jnp.maximum(logits, 0.0) + jnp.log1p(jnp.exp(-jnp.abs(logits)))) * SPREAD + WIDTH * WIDTH
    return location[:heads], variance[heads : 2 * heads]


def place_of(index, length):
    return TAU + (1.0 - TAU) * (index.astype(F32) + 0.5) / (length.astype(F32) * UNIT)


def split_rows(value):
    high = value.astype(BF16)
    rest = value - high.astype(F32)
    mid = rest.astype(BF16)
    return high, mid, (rest - mid.astype(F32)).astype(BF16)


def three_pass(left, right_high, right_low, contract=((1,), (0,))):
    high = left.astype(BF16)
    low = (left - high.astype(F32)).astype(BF16)
    return dot(high, right_high, contract) + dot(low, right_high, contract) + dot(high, right_low, contract)


def advance_values(table, value):
    joined = BASIS + LIVE if table.shape[0] == BASIS else BASIS
    high, low = table[:BASIS, :BASIS], table[:BASIS, 2 * joined : 2 * joined + BASIS]
    value_high = value.astype(BF16)
    value_low = (value - value_high.astype(F32)).astype(BF16)
    return dot(high, value_high) + dot(high, value_low) + dot(low, value_high)


def read_back_kernel(
    heads, info, qkv, grad_mixed, values, probes, states, table, query_grad, value_back, row_grads, value_grads,
    probe_grad, carried, grad_values, probe_cols, row_grad,
):
    step = pl.program_id(0)
    b = pl.num_programs(0) - 1 - step
    width = heads * HEAD_DIM
    start, length, order, run = info[0, b], info[1, b], info[2, b], info[3, 1]
    seen = (start > 0) | (run > 0)

    @pl.when(step == 0)
    def _():
        carried[...] = jnp.zeros_like(carried)
        probe_grad[...] = jnp.zeros_like(probe_grad)
        row_grads[...] = jnp.zeros_like(row_grads)

    @pl.when(b + 1 == start + length)
    def _():
        grad_values[...] = jnp.zeros_like(grad_values)
        row_grad[...] = jnp.zeros_like(row_grad)
        probe_cols[...] = jnp.concatenate([probes[0], jnp.zeros((120, LANES), F32)], axis=0).T

    @pl.when(jnp.logical_not(seen))
    def _():
        query_grad[...] = jnp.zeros_like(query_grad)

    @pl.when(seen)
    def _():
        query = qkv[0]
        given = jnp.concatenate([grad_mixed[0], jnp.zeros((UNIT, LANES - width), BF16)], axis=1)
        lane_head = lax.broadcasted_iota(jnp.int32, (UNIT, LANES), 1) // HEAD_DIM
        logits = sum(dot(part, query, ((1,), (1,))) for part in split_rows(probes[0]))
        location, variance = read_parts(logits, heads)
        inverse = 1.0 / variance
        fall = -0.5 * inverse
        peak = WIDTH * lax.rsqrt(variance)
        centres = lax.broadcasted_iota(jnp.int32, (BASIS, UNIT), 0).astype(F32) / (BASIS - 1)
        along, across = [], []
        for h in range(heads):
            own_given = jnp.where(lane_head == h, given.astype(F32), 0.0).astype(BF16)
            gap = centres - location[h : h + 1]
            square = gap * gap
            density = jnp.exp(square * fall[h : h + 1]) * peak[h : h + 1]
            grad_density = dot(values[0], own_given, ((1,), (1,)))
            grad_values[...] += dot(density.astype(BF16), own_given)
            weighed = density * grad_density
            zeroth = jnp.sum(weighed, axis=0, keepdims=True)
            first = jnp.sum(weighed * gap, axis=0, keepdims=True)
            second = jnp.sum(weighed * square, axis=0, keepdims=True)
            along.append(first * inverse[h : h + 1])
            across.append(0.5 * inverse[h : h + 1] * (second * inverse[h : h + 1] - zeroth))
        sigmoid = 1.0 / (1.0 + jnp.exp(-logits))
        grad_location = jnp.concatenate(along, axis=0) * location * (1.0 - location)
        grad_variance = jnp.concatenate(across, axis=0) * SPREAD * sigmoid[heads : 2 * heads]
        grad_logits = jnp.concatenate(
            [grad_location, grad_variance, jnp.zeros((8 - 2 * heads, UNIT), F32)], axis=0
        )
        padded = jnp.concatenate([grad_logits, jnp.zeros((120, UNIT), F32)], axis=0)
        query_grad[0] = dot(probe_cols[...], padded, precision=HIGHEST)[:width]
        row_grad[...] += dot(grad_logits, query.astype(F32), precision=HIGHEST)

    @pl.when((b == start) & seen)
    def _():
        rows = jnp.where(head_rows(heads, LANES), row_grad[...], 0.0) * (1.0 / math.sqrt(HEAD_DIM))
        row_grads[pl.ds(pl.multiple_of(order * 8, 8), 8)] = rows
        probe_grad[...] += dot(rows, states[0].astype(F32), ((1,), (1,)), HIGHEST)

    @pl.when(b == start)
    def _():
        value_grads[0] = grad_values[...]
        total = carried[...] + grad_values[...]
        value_back[...] = total[:, :width].astype(BF16)

        @pl.when(start > 0)
        def _():
            carried[...] = advance_values(table, total)


def attend_back_kernel(
    heads, info, qkv, grad_mixed, logsum, read_query, row_grads, value_grads, musig, rows_in, row_back, value_back,
    key_end, probe_part, table, out, probe_grad, carried, spread, key_grad, value_grad, cols, turned,
):
    step = pl.program_id(0)
    units = pl.num_programs(0)
    b = units - 1 - step
    width = heads * HEAD_DIM
    start, length, order, run = info[0, b], info[1, b], info[2, b], info[3, 1]
    flip = info[3, 0] * (units // 2)

    @pl.when(step == 0)
    def _():
        for i in range(cols.shape[0]):
            cols[i] = qkv[i, :, LANES : 2 * LANES].astype(F32).T.astype(BF16)
        probe_grad[...] = probe_part[...]

    def carry(total, units_before):
        moved = dot(table[...], split3(total))
        carried[...] = moved[:BASIS]
        spread[...] = (moved[BASIS:] * term_scale(units_before)).astype(BF16)

    @pl.when((step == 0) & (run > 0))
    def _():
        carried[...] = jnp.zeros_like(carried)
        spread[...] = jnp.zeros_like(spread)

    @pl.when((step == 0) & (run == 0))
    def _():
        grad_keys = dot(rows_in[...], row_back[...], ((0,), (0,)), HIGHEST)
        pad = jnp.zeros((BASIS, LANES - width), F32)
        carry(jnp.concatenate([grad_keys, value_back[...].astype(F32), pad], axis=1), length)
        seen = dot(row_back[...], key_end[...], ((1,), (1,)), HIGHEST)
        gained = seen[24:32]
        for k in (2, 1, 0):
            gained = three_pass(gained, table[:BASIS, :BASIS], table[:BASIS, 2 * BASIS : 3 * BASIS])
            gained = gained + seen[8 * k : 8 * k + 8]
        probe_grad[...] += gained

    @pl.when(b + 1 == start + length)
    def _():
        key_grad[...] = jnp.zeros_like(key_grad)
        value_grad[...] = jnp.zeros_like(value_grad)

    query = qkv[b ^ flip, :, 0:LANES]
    given = jnp.concatenate([grad_mixed[0], jnp.zeros((UNIT, LANES - width), BF16)], axis=1)
    lane_head = lax.broadcasted_iota(jnp.int32, (UNIT, LANES), 1) // HEAD_DIM

    def attend_back(blocks):
        causal = lax.broadcasted_iota(jnp.int32, (UNIT, UNIT), 0) <= lax.broadcasted_iota(
            jnp.int32, (UNIT, UNIT), 1
        )
        for h in range(heads):
            own = jnp.where(lane_head == h, query.astype(F32) * (1.0 / math.sqrt(HEAD_DIM)), 0.0).astype(BF16)
            own_given = jnp.where(lane_head == h, given.astype(F32), 0.0).astype(BF16)
            probs, products = [], []
            inner = jnp.zeros((1, UNIT), F32)
            for j in range(blocks):
                score = dot(qkv[(start + j) ^ flip, :, LANES : 2 * LANES], own, ((1,), (1,)))
                if j == blocks - 1:
                    score = jnp.where(causal, score, -1e30)
                prob = jnp.exp(score - logsum[0, h : h + 1])
                product = prob * dot(qkv[(start + j) ^ flip, :, 2 * LANES : 3 * LANES], own_given, ((1,), (1,)))
                inner += jnp.sum(product, axis=0, keepdims=True)
                probs.append(prob)
                products.append(product)
            rows = slice(h * HEAD_DIM, (h + 1) * HEAD_DIM)
            result = jnp.zeros((HEAD_DIM, UNIT), F32)
            for j in range(blocks):
                part = slice(j * UNIT, (j + 1) * UNIT)
                grad_score = (products[j] - probs[j] * inner).astype(BF16)
                key_grad[part] += dot(grad_score, own)
                value_grad[part] += dot(probs[j].astype(BF16), own_given)
                result += dot(cols[(start + j) ^ flip, rows], grad_score)
            turned[rows] = result * (1.0 / math.sqrt(HEAD_DIM)) + read_query[0, rows]

    for blocks in range(1, 5):
        pl.when(b - start + 1 == blocks)(functools.partial(attend_back, blocks))

    local = pl.ds(pl.multiple_of((b - start) * UNIT, UNIT), UNIT)

    @pl.when((start + length < units) | (run == 0))
    def _():
        token = lax.broadcasted_iota(jnp.int32, (UNIT, LIVE), 0) + (b - start) * UNIT
        centre = (lax.broadcasted_iota(jnp.int32, (UNIT, LIVE), 1) + LIVE).astype(F32) / (BASIS - 1)
        gap = place_of(token, length) - centre
        psi = jnp.exp(gap * gap * (-0.5 / (WIDTH * WIDTH))).astype(BF16)
        pair_grad = dot(psi, spread[...])
        key_grad[local] += pair_grad[:, :LANES]
        value_grad[local] += pair_grad[:, LANES:]

    query_grad = turned[...].T.astype(BF16)
    out[0, :, :LANES] = jnp.concatenate([query_grad, jnp.zeros((UNIT, LANES - width), BF16)], axis=1)
    out[0, :, LANES : 2 * LANES] = key_grad[local].astype(BF16)
    out[0, :, 2 * LANES :] = value_grad[local].astype(BF16)

    @pl.when((b == start) & (start > 0))
    def _():
        rows = row_grads[pl.ds(pl.multiple_of(order * 8, 8), 8)]
        grad_keys = dot(musig[...], rows, ((0,), (0,)), HIGHEST)
        total = carried[...] + jnp.concatenate([grad_keys, value_grads[0]], axis=1)
        carry(total, info[1, jnp.maximum(start - 1, 0)])


def segment_info(lengths, units, flip, run):
    slot_units = lengths // UNIT
    slots = jnp.arange(lengths.shape[0], dtype=jnp.int32)
    ends = jnp.sum(jnp.where(slots[None, :] <= slots[:, None], slot_units[None, :], 0), axis=1)
    starts = ends - slot_units
    unit = jnp.arange(units, dtype=jnp.int32)[:, None]
    member = (unit >= starts[None, :]) & (unit < ends[None, :])
    start = jnp.sum(jnp.where(member, starts[None, :], 0), axis=1)
    length = jnp.sum(jnp.where(member, slot_units[None, :], 0), axis=1)
    place = jnp.sum(((ends[None, :] <= unit) & (slot_units > 0)[None, :]).astype(jnp.int32), axis=1)
    own = jnp.where(jnp.arange(units) == 0, flip, run)
    return jnp.stack([start, length, place, own]).astype(jnp.int32)


def whole(shape):
    return pl.BlockSpec(shape, lambda i, info: (0,) * len(shape))


def call(kernel, heads, units, in_specs, out_specs, out_shape, scratch, flops, exps, name):
    return pl.pallas_call(
        functools.partial(kernel, heads),
        grid_spec=pltpu.PrefetchScalarGridSpec(
            num_scalar_prefetch=1, grid=(units,), in_specs=in_specs, out_specs=out_specs, scratch_shapes=scratch
        ),
        out_shape=[jax.ShapeDtypeStruct(shape, kind) for shape, kind in out_shape],
        compiler_params=pltpu.CompilerParams(vmem_limit_bytes=56 << 20),
        cost_estimate=pl.CostEstimate(flops=flops, bytes_accessed=8 << 20, transcendentals=exps),
        name=name,
    )


def unit_block(shape, turn, back=False):
    last = shape[0] - 1

    def index(i, info):
        b = last - i if back else i
        b = b ^ (info[3, 0] * ((last + 1) // 2)) if turn else b
        return (b,) + (0,) * (len(shape) - 1)

    return pl.BlockSpec((1,) + shape[1:], index)


def place_block(shape, back=False):
    last = shape[0] - 1
    return pl.BlockSpec(
        (1,) + shape[1:], lambda i, info: (info[2, last - i if back else i],) + (0,) * (len(shape) - 1)
    )


def memory_read_back(info, qkv, grad_mixed, values, probes, states, heads):
    units, width = qkv.shape[0], heads * HEAD_DIM
    table = jnp.asarray(basis_tables()[1])
    return call(
        read_back_kernel, heads, units,
        [
            unit_block((units, UNIT, LANES), True, True), unit_block(grad_mixed.shape, True, True),
            unit_block(values.shape, False, True), unit_block(probes.shape, False, True),
            unit_block((units, BASIS, LANES), False, True), whole(table.shape),
        ],
        [
            unit_block((units, width, UNIT), False, True), whole((BASIS, width)), whole((32, LANES)),
            place_block((units, BASIS, LANES), True), whole((8, BASIS)),
        ],
        [
            ((units, width, UNIT), F32), ((BASIS, width), BF16), ((32, LANES), F32), ((units, BASIS, LANES), F32),
            ((8, BASIS), F32),
        ],
        [
            pltpu.VMEM((BASIS, LANES), F32), pltpu.VMEM((BASIS, LANES), F32), pltpu.VMEM((LANES, 128), F32),
            pltpu.VMEM((8, LANES), F32),
        ],
        6 << 30, 2 << 20, "memory_read_back",
    )(info, qkv, grad_mixed, values, probes, states, table)


def attention_back(
    info, qkv, grad_mixed, logsum, read_query, row_grads, value_grads, musig, rows, row_back, value_back, key_end,
    probe_part, heads,
):
    units, width = qkv.shape[0], heads * HEAD_DIM
    table = jnp.asarray(basis_tables()[1])
    return call(
        attend_back_kernel, heads, units,
        [
            whole(qkv.shape), unit_block(grad_mixed.shape, True, True), unit_block(logsum.shape, False, True),
            unit_block(read_query.shape, False, True), whole(row_grads.shape), place_block(value_grads.shape, True),
            whole(musig.shape), whole(rows.shape), whole(row_back.shape), whole(value_back.shape), whole(key_end.shape),
            whole(probe_part.shape), whole(table.shape),
        ],
        [unit_block(qkv.shape, True, True), whole((8, BASIS))],
        [(qkv.shape, BF16), ((8, BASIS), F32)],
        [
            pltpu.VMEM((BASIS, 2 * LANES), F32), pltpu.VMEM((LIVE, 2 * LANES), BF16),
            pltpu.VMEM((4 * UNIT, LANES), F32), pltpu.VMEM((4 * UNIT, LANES), F32),
            pltpu.VMEM((units, LANES, UNIT), BF16), pltpu.VMEM((width, UNIT), F32),
        ],
        20 << 30, 2 << 20, "attention_back",
    )(
        info, qkv, grad_mixed, logsum, read_query, row_grads, value_grads, musig, rows, row_back, value_back, key_end,
        probe_part, table,
    )


def other_of(index, distance):
    bit = 1
    while bit <= distance:
        if distance & bit:
            index = index + bit - 2 * bit * ((index // bit) % 2)
        bit *= 2
    return index


class Hops:
    def __init__(self, send, recv):
        self.send, self.recv, self.used = send, recv, 0

    def start(self, source, target, axis, bit):
        copy = pltpu.make_async_remote_copy(
            src_ref=source,
            dst_ref=target,
            send_sem=self.send.at[self.used],
            recv_sem=self.recv.at[self.used],
            device_id={axis: other_of(lax.axis_index(axis), bit)},
            device_id_type=MESH,
        )
        self.used += 1
        copy.start()
        return copy


def greet(neighbours):
    barrier = pltpu.get_barrier_semaphore()
    for axis, bit in neighbours:
        pl.semaphore_signal(
            barrier, inc=1, device_id={axis: other_of(lax.axis_index(axis), bit)}, device_id_type=MESH
        )
    pl.semaphore_wait(barrier, len(neighbours))


def set_out(pairs, sems, first):
    copies = [pltpu.make_async_copy(a, b, sems.at[first + k]) for k, (a, b) in enumerate(pairs)]
    for copy in copies:
        copy.start()
    return copies


def forward_kernel(
    heads, info, source, scales, weight, small, bias_row, table, ff_in, ff_out, out_weight,
    qkv_out, first_cols_out, flat_a_out, flat_b_out, logsum, values, probes, key_states, key_end, rows,
    mixed_0, mixed_1, mixed_2, mixed_3, in_bias, far_in, far_out, far_weight,
    qkv, first_rows, first_cols, flats, near, far, far_row, memory, sums, value_states, carried, value_ends, value_ins,
    projs, proj_ins, cols, discrete, mixed, mixed_in, send, recv, local_sems,
):
    own_rows, model = source.shape
    width = heads * HEAD_DIM
    units = qkv.shape[1]
    half = units // 2
    root = 1.0 / math.sqrt(HEAD_DIM)
    z = lax.axis_index("head")
    flip, run = (z % 2) * half, z // 2
    place = lax.axis_index("dp") % 8
    y, x, c = place // 4, (place // 2) % 2, place % 2
    slice_rows = model // 8
    at = lambda b: (b + flip) % units
    starts = [info[0, b] for b in range(units)]
    lengths = [info[1, b] for b in range(units)]
    orders = [info[2, b] for b in range(units)]
    greet((("head", 1), ("head", 2), ("head", 3), ("dp", 1), ("dp", 2), ("dp", 4)))
    hops = Hops(send, recv)
    started = []

    def go(*args):
        started.append(hops.start(*args))
        return started[-1]

    mine = weight.at[pl.ds(pl.multiple_of(place * slice_rows, 16), slice_rows)]
    slice_copy = go(mine, far.at[y, x, c], "head", 2)
    small_copy = go(small, far_row, "head", 2)
    row_copies = []
    for k in range(half):
        part = slice(k * UNIT, (k + 1) * UNIT)
        value = source[part].astype(F32)
        centred = value - jnp.mean(value, axis=-1, keepdims=True)
        factor = lax.rsqrt(jnp.mean(centred * centred, axis=-1, keepdims=True) + EPSILON)
        first_rows[part] = (centred * factor * scales[0:1] + scales[1:2]).astype(BF16)
        row_copies.append(go(first_rows.at[part], near.at[part], "head", 1))
    slice_copy.wait_recv()
    x_copy = go(far.at[y, x, c], far.at[y, x, c], "dp", 2)

    def widen(k, read):
        flats[k] = jnp.zeros((model, 3 * LANES), BF16)
        for i in range(3):
            flats[k, :, i * LANES : i * LANES + width] = read(slice(i * width, (i + 1) * width))

    def project(k, unit, shift):
        span = slice(unit * UNIT, (unit + 1) * UNIT)
        qkv[k, unit] = (dot(first_rows[span], flats[k]) + shift).astype(BF16)

    widen(0, lambda span: weight[:, span])
    for unit in range(half):
        project(0, unit, small[0:1])
    x_copy.wait_recv()
    y_copy = go(far.at[y, :, c], far.at[y, :, c], "dp", 4)
    first_cols[:, :own_rows] = first_rows[:own_rows].astype(F32).T.astype(BF16)
    y_copy.wait_recv()
    core_copy = go(far.at[:, :, c], far.at[:, :, c], "dp", 1)
    small_copy.wait_recv()
    for k, copy in enumerate(row_copies):
        copy.wait_recv()
        part = slice(k * UNIT, (k + 1) * UNIT)
        first_rows[own_rows + k * UNIT : own_rows + (k + 1) * UNIT] = near[part]
        project(0, half + k, small[0:1])

    in_mine = ff_in.at[pl.ds(pl.multiple_of(place * slice_rows, 16), slice_rows)]
    out_mine = ff_out.at[pl.ds(pl.multiple_of(place * slice_rows, 16), slice_rows)]
    gathers = ((far_in, 2, 4), (far_weight, 2, 4), (far_out, 4, 2))
    stage = {}
    for r in (1, 2, 3):
        stage[r] = [
            go(in_mine, far_in.at[r - 1, y, x, c], "head", r),
            go(out_weight.at[place], far_weight.at[r - 1, y, x, c], "head", r),
            go(out_mine, far_out.at[r - 1, y, x, c], "head", r),
        ]
    in_bias[0] = bias_row[...]
    bias_copies = [go(bias_row, in_bias.at[r], "head", r) for r in (1, 2, 3)]

    def advance(r, step):
        for copy in stage[r]:
            copy.wait_recv()
        stage[r] = []
        for array, first, second in gathers:
            block = array.at[r - 1]
            if step == 1:
                part, bit = block.at[y, x, c], first
            elif step == 2:
                part, bit = (block.at[y, :, c] if first == 2 else block.at[:, x, c]), second
            else:
                part, bit = block.at[:, :, c], 1
            stage[r].append(go(part, part, "dp", bit))

    first_cols[:, own_rows:] = near[...].astype(F32).T.astype(BF16)
    core_copy.wait_recv()
    widen(1, lambda span: far[:, :, :, :, span].reshape(model, width))
    for unit in range(units):
        project(1, unit, far_row[0:1])
    saved = set_out(
        [(qkv, qkv_out), (first_cols, first_cols_out), (flats.at[0], flat_a_out), (flats.at[1], flat_b_out)],
        local_sems, 0,
    )

    def probe_of(k):
        return jnp.where(k == 0, small[1:9, :BASIS], far_row[1:9, :BASIS])

    mask = head_rows(heads, LANES)

    def first_state(k, carry):
        memory[k] = jnp.zeros(memory.shape[1:], F32)
        row = probe_of(k)
        rows[k, 0:8] = row
        wide = 2 * (BASIS + LIVE)
        for i in range(1, 4):
            row = three_pass(row, table[:, :BASIS], table[:, wide : wide + BASIS])
            rows[k, 8 * i : 8 * i + 8] = row
        return carry

    lax.fori_loop(0, 2, first_state, 0)

    def state(b, k, carry):
        start, length = starts[b], lengths[b]
        now = memory[k]
        value_states[k, b] = now[:, LANES:]
        key_states[k, b] = now[:, :LANES].astype(BF16)
        if b > 0:
            probes[k, b] = jnp.where(mask, dot(rows[k, 0:8], now[:, :LANES], precision=HIGHEST), 0.0)
        else:
            probes[k, b] = jnp.zeros((8, LANES), F32)
        token = lax.broadcasted_iota(jnp.int32, (LIVE, UNIT), 1) + (b - start) * UNIT
        centre = (lax.broadcasted_iota(jnp.int32, (LIVE, UNIT), 0) + LIVE).astype(F32) / (BASIS - 1)
        gap = place_of(token, length) - centre
        psi = jnp.exp(gap * gap * (-0.5 / (WIDTH * WIDTH)))
        psi_high = psi.astype(BF16)
        psi_low = (psi - psi_high.astype(F32)).astype(BF16)
        pairs = qkv[k, at(b), :, LANES : 3 * LANES]
        fresh = dot(psi_high, pairs) + dot(psi_low, pairs)
        gathered = fresh if b == 0 else jnp.where(start == b, 0.0, sums[k]) + fresh
        sums[k] = gathered
        stacked = jnp.concatenate([now, gathered * term_scale(length)], axis=0)
        later = dot(table[...], split3(stacked))
        memory[k] = jnp.where(start + length == b + 1, later, now)
        return carry

    def end_state(k, carry):
        key = memory[k, :, :LANES]
        key_end[k] = key
        value_ends[k] = memory[k, :, LANES : LANES + width].astype(BF16)
        seen = dot(rows[k], key, precision=HIGHEST)
        for i in range(4):
            projs[k, 8 * i : 8 * i + 8] = jnp.where(mask, seen[8 * i : 8 * i + 8], 0.0)
        return carry

    def attend(b, k, carry):
        cols[k, b] = qkv[k, at(b), :, 2 * LANES : 3 * LANES].astype(F32).T.astype(BF16)
        query = qkv[k, at(b), :, 0:LANES].astype(F32) * root
        lane_head = lax.broadcasted_iota(jnp.int32, (UNIT, LANES), 1) // HEAD_DIM
        causal = lax.broadcasted_iota(jnp.int32, (UNIT, UNIT), 0) <= lax.broadcasted_iota(
            jnp.int32, (UNIT, UNIT), 1
        )
        away = [jnp.where(starts[b] <= j, 0.0, 1e30) for j in range(b)] + [0.0]
        for h in range(heads):
            own = jnp.where(lane_head == h, query, 0.0).astype(BF16)
            scores = [dot(qkv[k, at(j), :, LANES : 2 * LANES], own, ((1,), (1,))) for j in range(b + 1)]
            scores[b] = jnp.where(causal, scores[b], -1e30)
            highest = functools.reduce(
                jnp.maximum, [jnp.max(s, axis=0, keepdims=True) - away[j] for j, s in enumerate(scores)]
            )
            weights = [jnp.exp(s - (highest + away[j])) for j, s in enumerate(scores)]
            total = sum(jnp.sum(w, axis=0, keepdims=True) for w in weights)
            span = slice(h * HEAD_DIM, (h + 1) * HEAD_DIM)
            part = sum(dot(cols[k, j, span], weights[j].astype(BF16)) for j in range(b + 1))
            discrete[k, b, span] = part * (1.0 / total)
            logsum[k, b, h : h + 1] = highest + jnp.log(total)
        return carry

    def seen_value(k, carry):
        incoming = jnp.where(run > 0, value_ins[k].astype(F32), 0.0)
        carried[:, :width] = incoming
        carried[:, width:] = jnp.zeros((BASIS, LANES - width), F32)
        for b in range(units):
            if b > 0:
                carried[...] = jnp.where(starts[b] == b, advance_values(table, carried[...]), carried[...])
            values[k, b] = (value_states[k, b] + carried[...]).astype(BF16)
            gained = jnp.zeros((8, LANES), F32)
            for i in range(4):
                gained += jnp.where((orders[b] == i) & (run > 0), proj_ins[k, 8 * i : 8 * i + 8], 0.0)
            probes[k, b] = (probes[k, b] + gained) * root
        return carry

    def read(rel, k, carry):
        b = at(rel)
        query = qkv[k, rel, :, 0:LANES]
        logits = sum(dot(part, query, ((1,), (1,))) for part in split_rows(probes[k, b]))
        location, variance = read_parts(logits, heads)
        fall = -0.5 / variance
        peak = WIDTH * lax.rsqrt(variance)
        centres = lax.broadcasted_iota(jnp.int32, (BASIS, UNIT), 0).astype(F32) / (BASIS - 1)
        value_cols = values[k, b].astype(F32).T.astype(BF16)
        parts = []
        for h in range(heads):
            gap = centres - location[h : h + 1]
            density = jnp.exp(gap * gap * fall[h : h + 1]).astype(BF16)
            span = slice(h * HEAD_DIM, (h + 1) * HEAD_DIM)
            parts.append(discrete[k, b, span] + dot(value_cols[span], density) * peak[h : h + 1])
        mixed[k, rel] = jnp.concatenate(parts, axis=0).T.astype(BF16)
        return carry

    for b in range(units):
        lax.fori_loop(0, 2, functools.partial(state, b), 0)
        if b == 1:
            advance(1, 1)
    lax.fori_loop(0, 2, end_state, 0)
    state_copies = [go(value_ends.at[k], value_ins.at[1 - k], "head", 2) for k in range(2)]
    state_copies += [go(projs.at[k], proj_ins.at[1 - k], "head", 2) for k in range(2)]
    advance(1, 2)
    for b in range(units):
        lax.fori_loop(0, 2, functools.partial(attend, b), 0)
        if b == 2:
            advance(2, 1)
            advance(3, 1)
    advance(1, 3)
    for copy in state_copies:
        copy.wait_recv()
    lax.fori_loop(0, 2, seen_value, 0)
    advance(2, 2)
    mixed_copies = []
    for rel in (2, 3, 0, 1):
        lax.fori_loop(0, 2, functools.partial(read, rel), 0)
        if rel == 3:
            advance(3, 2)
            mixed_copies = [
                go(mixed.at[k, half:], mixed_in.at[k], "head", 1) for k in range(2)
            ]
    mixed_0[...] = mixed[0, :half].reshape(own_rows, width)
    mixed_2[...] = mixed[1, :half].reshape(own_rows, width)
    advance(2, 3)
    for copy in mixed_copies:
        copy.wait_recv()
    mixed_1[...] = mixed_in[0].reshape(own_rows, width)
    mixed_3[...] = mixed_in[1].reshape(own_rows, width)
    advance(3, 3)
    for copy in bias_copies + stage[1] + stage[2] + stage[3]:
        copy.wait_recv()
    for copy in started:
        copy.wait_send()
    for copy in saved:
        copy.wait()


def forward(info, source, scales, weight, small, bias_row, ff_in, ff_out, out_slices, heads):
    own_rows, model = source.shape
    units = 2 * own_rows // UNIT
    width = heads * HEAD_DIM
    hidden_part = ff_in.shape[1]
    rows = model // 8
    table = jnp.asarray(basis_tables()[0])
    vmem, anywhere = pl.BlockSpec(memory_space=pltpu.VMEM), pl.BlockSpec(memory_space=pl.ANY)
    shape = jax.ShapeDtypeStruct
    hops = 2 + units // 2 + 3 + 3 * 3 * 4 + 3 + 4 + 2
    return pl.pallas_call(
        functools.partial(forward_kernel, heads),
        in_specs=[pl.BlockSpec(memory_space=pltpu.SMEM)] + [vmem] * 6 + [anywhere] * 3,
        out_specs=[anywhere] * 4 + [vmem] * 11 + [anywhere] * 3,
        out_shape=[
            shape((2, units, UNIT, 3 * LANES), BF16),
            shape((model, 2 * own_rows), BF16),
            shape((model, 3 * LANES), BF16),
            shape((model, 3 * LANES), BF16),
            shape((2, units, 8, UNIT), F32),
            shape((2, units, BASIS, LANES), BF16),
            shape((2, units, 8, LANES), F32),
            shape((2, units, BASIS, LANES), BF16),
            shape((2, BASIS, LANES), F32),
            shape((2, 32, BASIS), F32),
        ] + [shape((own_rows, width), BF16)] * 4 + [
            shape((4,) + bias_row.shape, F32),
            shape((3, 2, 2, 2, rows, hidden_part), BF16),
            shape((3, 2, 2, 2, rows, model), BF16),
            shape((3, 2, 2, 2) + out_slices.shape[1:], BF16),
        ],
        scratch_shapes=[
            pltpu.VMEM((2, units, UNIT, 3 * LANES), BF16),
            pltpu.VMEM((2 * own_rows, model), BF16),
            pltpu.VMEM((model, 2 * own_rows), BF16),
            pltpu.VMEM((2, model, 3 * LANES), BF16),
            pltpu.VMEM((own_rows, model), BF16),
            pltpu.VMEM((2, 2, 2, rows, weight.shape[1]), BF16),
            pltpu.VMEM(small.shape, F32),
            pltpu.VMEM((2, BASIS, 2 * LANES), F32),
            pltpu.VMEM((2, LIVE, 2 * LANES), F32),
            pltpu.VMEM((2, units, BASIS, LANES), F32),
            pltpu.VMEM((BASIS, LANES), F32),
            pltpu.VMEM((2, BASIS, width), BF16),
            pltpu.VMEM((2, BASIS, width), BF16),
            pltpu.VMEM((2, 32, LANES), F32),
            pltpu.VMEM((2, 32, LANES), F32),
            pltpu.VMEM((2, units, LANES, UNIT), BF16),
            pltpu.VMEM((2, units, width, UNIT), F32),
            pltpu.VMEM((2, units, UNIT, width), BF16),
            pltpu.VMEM((2, units // 2, UNIT, width), BF16),
            pltpu.SemaphoreType.DMA((hops,)),
            pltpu.SemaphoreType.DMA((hops,)),
            pltpu.SemaphoreType.DMA((4,)),
        ],
        compiler_params=pltpu.CompilerParams(
            collective_id=1, has_side_effects=True, vmem_limit_bytes=60 << 20
        ),
        name="forward",
    )(info, source, scales, weight, small, bias_row, table, ff_in, ff_out, out_slices)


def middle_kernel(
    place, source, cotangent, mixed_0, mixed_1, mixed_2, mixed_3, own_weight, far_weight, vectors, in_bias, own_in, own_out,
    far_in, far_out, outputs, grad_residual, grad_mixed_0, grad_mixed_1, grad_mixed_2, grad_mixed_3, grad_in, grad_out,
    grad_out_weight, sums, grad_in_bias,
    residual, inverse, second, second_cols, total, grad_second, in_now, out_now, out_weight,
):
    r = pl.program_id(0)
    own = place[0]
    slices, rows = own_in.shape[0], own_in.shape[1]
    model = source.shape[1]
    hidden_part = own_in.shape[2]
    out_bias, gain, shift, last_bias = (vectors[k : k + 1] for k in range(4))

    @pl.when(r == 0)
    def _():
        value = source[...].astype(F32) + out_bias
        out_weight[0] = own_weight[...]
        narrow = own_weight.shape[0] // slices
        for k in range(far_weight.shape[0]):
            parts = [far_weight[k, j].astype(F32)[:narrow] for j in range(slices)]
            out_weight[k + 1] = jnp.concatenate(parts, axis=0).astype(BF16)
        for k, mixed in enumerate((mixed_0, mixed_1, mixed_2, mixed_3)):
            value += dot(mixed[...], out_weight[k])
        residual[...] = value
        centred = value - jnp.mean(value, axis=-1, keepdims=True)
        factor = lax.rsqrt(jnp.mean(centred * centred, axis=-1, keepdims=True) + EPSILON)
        inverse[...] = factor
        normal = centred * factor
        grad_residual[...] = normal
        rounded = (normal * gain + shift).astype(BF16)
        second[...] = rounded
        second_cols[...] = rounded.astype(F32).T.astype(BF16)
        total[...] = jnp.zeros_like(total)
        grad_second[...] = jnp.zeros_like(grad_second)
        grad_in_bias[...] = jnp.zeros_like(grad_in_bias)
        for j in range(slices):
            in_now[j * rows : (j + 1) * rows] = own_in[j]
            out_now[j * rows : (j + 1) * rows] = own_out[j]

    @pl.when(r > 0)
    def _():
        for j in range(slices):
            in_now[j * rows : (j + 1) * rows] = far_in[0, j]
            out_now[j * rows : (j + 1) * rows] = far_out[0, j]

    half = hidden_part // 2
    for t in range(2):
        span = slice(t * half, (t + 1) * half)
        hidden = dot(second[...], in_now[:, span]) + in_bias[r, 0:1, span]
        cube = hidden * hidden
        root = math.sqrt(2.0 / math.pi)
        bent = jnp.tanh(hidden * (root + (root * 0.044715) * cube))
        lifted = 0.5 + 0.5 * bent
        activation = (hidden * lifted).astype(BF16)
        slope = lifted + hidden * ((0.5 - 0.5 * bent * bent) * (root + (3.0 * root * 0.044715) * cube))
        total[...] += dot(activation, out_now[span])
        given = dot(cotangent[...], out_now[span], ((1,), (1,)))
        grad_hidden = (given * slope).astype(BF16)
        grad_second[...] += dot(grad_hidden, in_now[:, span], ((1,), (1,)))
        grad_in_bias[pl.ds(r, 1), span] = jnp.sum(grad_hidden.astype(F32), axis=0, keepdims=True)
        part = dot(activation, cotangent[...], ((0,), (0,))).astype(BF16)
        per = half // rows
        for k in range(per):
            grad_out[0, (t * per + k) ^ own] = part[k * rows : (k + 1) * rows]
        part = dot(second_cols[...], grad_hidden).astype(BF16)
        for j in range(slices):
            grad_in[0, j ^ own, :, span] = part[j * rows : (j + 1) * rows]

    @pl.when(r == pl.num_programs(0) - 1)
    def _():
        given = cotangent[...].astype(F32)
        outputs[...] = (residual[...] + total[...] + last_bias).astype(BF16)
        normal = grad_residual[...]
        grad = grad_second[...]
        scaled = grad * gain
        value = given + inverse[...] * (
            scaled
            - jnp.mean(scaled, axis=-1, keepdims=True)
            - normal * jnp.mean(scaled * normal, axis=-1, keepdims=True)
        )
        sums[0:1] = jnp.sum(value, axis=0, keepdims=True)
        sums[1:2] = jnp.sum(grad * normal, axis=0, keepdims=True)
        sums[2:3] = jnp.sum(grad, axis=0, keepdims=True)
        sums[3:4] = jnp.sum(given, axis=0, keepdims=True)
        sums[4:8] = jnp.zeros((4, model), F32)
        grad_residual[...] = value
        rounded = value.astype(BF16)
        grads = (grad_mixed_0, grad_mixed_1, grad_mixed_2, grad_mixed_3)
        for k, mixed in enumerate((mixed_0, mixed_1, mixed_2, mixed_3)):
            grads[k][...] = dot(rounded, out_weight[k], ((1,), (1,))).astype(BF16)
            grad_out_weight[k] = dot(mixed[...], rounded, ((0,), (0,))).astype(BF16)


def middle(place, source, cotangent, mixed, out_weight, far_weight, vectors, in_bias, own_in, own_out, far_in, far_out):
    own_rows, model = source.shape
    shards = far_in.shape[0] + 1
    slices, rows, hidden_part = own_in.shape
    narrow = mixed[0].shape
    far = pl.BlockSpec((1,) + own_in.shape, lambda r, place: (jnp.maximum(r - 1, 0), 0, 0, 0))
    part = pl.BlockSpec((1,) + own_in.shape, lambda r, place: (r, 0, 0, 0))
    macs = own_rows * model * (6 * shards * hidden_part + 3 * model)
    return pl.pallas_call(
        middle_kernel,
        grid_spec=pltpu.PrefetchScalarGridSpec(
            num_scalar_prefetch=1,
            grid=(shards,),
            in_specs=[whole(source.shape)] * 2 + [whole(narrow)] * 4 + [
                whole(out_weight.shape), whole(far_weight.shape), whole(vectors.shape), whole(in_bias.shape), whole(own_in.shape),
                whole(own_out.shape), far, far,
            ],
            out_specs=[whole(source.shape)] * 2 + [whole(narrow)] * 4 + [
                part, part, whole((shards,) + narrow[1:] + (model,)), whole((8, model)), whole((shards, hidden_part))
            ],
            scratch_shapes=[
                pltpu.VMEM((own_rows, model), F32),
                pltpu.VMEM((own_rows, 1), F32),
                pltpu.VMEM((own_rows, model), BF16),
                pltpu.VMEM((model, own_rows), BF16),
                pltpu.VMEM((own_rows, model), F32),
                pltpu.VMEM((own_rows, model), F32),
                pltpu.VMEM((model, hidden_part), BF16),
                pltpu.VMEM((hidden_part, model), BF16),
                pltpu.VMEM((shards,) + narrow[1:] + (model,), BF16),
            ],
        ),
        out_shape=[
            jax.ShapeDtypeStruct(source.shape, BF16),
            jax.ShapeDtypeStruct(source.shape, F32),
        ] + [jax.ShapeDtypeStruct(narrow, BF16)] * 4 + [
            jax.ShapeDtypeStruct((shards, slices, rows, hidden_part), BF16),
            jax.ShapeDtypeStruct((shards, slices, rows, hidden_part), BF16),
            jax.ShapeDtypeStruct((shards,) + narrow[1:] + (model,), BF16),
            jax.ShapeDtypeStruct((8, model), F32),
            jax.ShapeDtypeStruct((shards, hidden_part), F32),
        ],
        compiler_params=pltpu.CompilerParams(vmem_limit_bytes=60 << 20),
        cost_estimate=pl.CostEstimate(
            flops=2 * macs, bytes_accessed=30 << 20, transcendentals=own_rows * shards * hidden_part
        ),
        name="middle",
    )(place, source, cotangent, *mixed, out_weight, far_weight, vectors, in_bias, own_in, own_out, far_in, far_out)


def finish_kernel(place, given_in, given_out, grad_in, grad_out):
    own = place[0]
    slices, rows = given_in.shape[0], given_in.shape[1]
    for j in range(slices):
        grad_in[j * rows : (j + 1) * rows] = given_in[j ^ own].astype(F32)
        grad_out[j * rows : (j + 1) * rows] = given_out[j ^ own].astype(F32)


def finish(place, given_in, given_out):
    slices, rows, columns = given_in.shape
    return pl.pallas_call(
        finish_kernel,
        grid_spec=pltpu.PrefetchScalarGridSpec(
            num_scalar_prefetch=1,
            grid=(1,),
            in_specs=[pl.BlockSpec(given_in.shape, lambda k, place: (0, 0, 0))] * 2,
            out_specs=[pl.BlockSpec((slices * rows, columns), lambda k, place: (0, 0))] * 2,
        ),
        out_shape=[jax.ShapeDtypeStruct((slices * rows, columns), F32)] * 2,
        compiler_params=pltpu.CompilerParams(vmem_limit_bytes=40 << 20),
        name="finish",
    )(place, given_in, given_out)


def layer_norm(values, gain, shift):
    centred = values - jnp.mean(values, axis=-1, keepdims=True)
    inverse = lax.rsqrt(jnp.mean(centred * centred, axis=-1, keepdims=True) + EPSILON)
    normal = centred * inverse
    return (normal * gain + shift, normal, inverse)


def norm_back(grad, normal, inverse, gain):
    scaled = grad * gain
    return inverse * (
        scaled
        - jnp.mean(scaled, axis=-1, keepdims=True)
        - normal * jnp.mean(scaled * normal, axis=-1, keepdims=True)
    )


def exchange(value, axis, bit):
    size = lax.axis_size(axis)
    return lax.ppermute(value, axis, [(j, j ^ bit) for j in range(size)])


def plane_gather(part, bits):
    held = {0: part}
    for bit in bits:
        order = sorted(held)
        sent = jnp.stack([held[m] for m in order])
        received = exchange(sent, "dp", bit)
        held.update({m ^ bit: received[k] for k, m in enumerate(order)})
    return jnp.stack([held[m] for m in sorted(held)])


def plane_sum(stacked, bits, outer):
    order = list(range(stacked.shape[0]))
    for bit in bits:
        keep = [k for k, m in enumerate(order) if not m & bit]
        send = [order.index(order[k] | bit) for k in keep]
        received = exchange(take(stacked, send), "dp", bit)
        stacked = (take(stacked, keep).astype(F32) + received.astype(F32)).astype(BF16)
        order = [order[k] for k in keep]
    own = stacked[0]
    for bit in outer:
        own = (own.astype(F32) + exchange(own, "dp", bit).astype(F32)).astype(BF16)
    return own


def take(stacked, indices):
    return jnp.concatenate([stacked[k : k + 1] for k in indices])


def to_order(stacked, own):
    size = stacked.shape[0]
    bit = 1
    while bit < size:
        shaped = stacked.reshape((size // (2 * bit), 2, bit) + stacked.shape[1:])
        stacked = jnp.where((own & bit) > 0, shaped[:, ::-1], shaped).reshape(stacked.shape)
        bit *= 2
    return stacked


def local(
    inputs, seg_lengths, ln1_gain, ln1_bias, qkv_weight, qkv_bias, out_weight, out_bias, mem_mu, mem_sig,
    ln2_gain, ln2_bias, ff_in, ff_in_bias, ff_out, ff_out_bias, cotangent,
):
    own_rows, model = inputs.shape
    shards = lax.axis_size("head")
    members = lax.axis_size("dp")
    width = qkv_weight.shape[2]
    heads = width // HEAD_DIM
    hidden_part = ff_in.shape[1]
    units = 2 * own_rows // UNIT
    slots = seg_lengths.shape[1] // 2
    z = lax.axis_index("head")
    run = z // 2
    next_run = lambda value: lax.ppermute(value, "head", [(0, 2), (1, 3)])
    last_run = lambda value: lax.ppermute(value, "head", [(2, 0), (3, 1)])

    slices = min(8, members)
    forth = [bit for bit in (2, 4, 1) if bit < slices]
    turned = forth[1::-1] + forth[2:]
    plain = [bit for bit in (1, 2, 4) if bit < slices]
    back_turned = plain[:1] + plain[:0:-1]
    outer = [1 << k for k in range(3, 16) if 1 << k < members]
    own = lax.axis_index("dp") % slices
    place = own.reshape(1).astype(jnp.int32)
    rows = model // slices
    narrow = width // slices
    mine = lambda array, count: lax.dynamic_slice_in_dim(array, own * count, count, 0)

    source = inputs.astype(F32)
    gain_one = ln1_gain.astype(F32)
    _, normal1, inverse1 = layer_norm(source, gain_one, ln1_bias.astype(F32))
    info = segment_info(lax.dynamic_slice_in_dim(seg_lengths[0], run * slots, slots, 0), units, z % 2, run)
    scales = jnp.concatenate([ln1_gain[None], ln1_bias[None], jnp.zeros((6, model), BF16)], axis=0).astype(F32)
    bias_row = jnp.pad(qkv_bias, ((0, 0), (0, LANES - width))).reshape(1, 3 * LANES)
    probe_rows = jnp.pad(jnp.concatenate([mem_mu, mem_sig], axis=0), ((0, 15 - 2 * heads), (0, 3 * LANES - BASIS)))
    small = jnp.concatenate([bias_row, probe_rows], axis=0).astype(F32)
    bias_in = jnp.broadcast_to(ff_in_bias[None].astype(F32), (8, hidden_part))
    out_slices = jnp.pad(out_weight.reshape(slices, narrow, model), ((0, 0), (0, -narrow % 16), (0, 0)))
    (
        qkv, first_cols, flat_a, flat_b, logsum, values, probes, key_states, key_end, state_rows,
        *mixed, in_bias, far_in, far_out, far_weight,
    ) = forward(info, inputs, scales, qkv_weight.reshape(model, 3 * width), small, bias_in, ff_in, ff_out, out_slices, heads)
    flat = lambda array: array.reshape((shards - 1, slices) + array.shape[4:])
    vectors = jnp.concatenate(
        [out_bias[None], ln2_gain[None], ln2_bias[None], ff_out_bias[None], jnp.zeros((4, model), BF16)], axis=0
    ).astype(F32)
    outputs, grad_residual, *rest = middle(
        place, inputs, cotangent, mixed, out_weight, flat(far_weight), vectors, in_bias,
        ff_in.reshape(slices, rows, hidden_part), ff_out.reshape(slices, rows, model), flat(far_in), flat(far_out),
    )
    grad_mixed, (ff_in_part, ff_out_part, out_weight_part, sums, in_bias_part) = rest[:4], rest[4:]
    given = [
        jnp.stack([grad_mixed[2 * k], exchange(grad_mixed[2 * k + 1], "head", 1)]).reshape(units, UNIT, width)
        for k in range(2)
    ]

    musigs = [small[1:9, :BASIS], lax.optimization_barrier(state_rows[1, :8])]
    read_backs = [
        memory_read_back(info, qkv[k], given[k], values[k], probes[k], key_states[k], heads) for k in range(2)
    ]
    returned = [(last_run(back[1]), last_run(back[2])) for back in read_backs[::-1]]
    grads = []
    for k in range(2):
        query_part, _, row_grads, value_grads, probe_part = read_backs[k]
        grads.append(attention_back(
            info, qkv[k], given[k], logsum[k], query_part, row_grads, value_grads, musigs[k], state_rows[k],
            returned[k][1], returned[k][0], key_end[k], probe_part, heads,
        ))
    flats = [grad[0].reshape(2 * own_rows, 3 * LANES) for grad in grads]
    grad_rows = sum(
        jnp.dot(grad, weight.T, preferred_element_type=F32) for grad, weight in zip(flats, (flat_a, flat_b))
    ).astype(BF16)
    grad_first = grad_rows[:own_rows].astype(F32) + exchange(grad_rows[own_rows:], "head", 1).astype(F32)
    grad_source = grad_residual + norm_back(grad_first, normal1, inverse1, gain_one)

    def owner_sum(part, bits):
        summed = plane_sum(jnp.swapaxes(part, 0, 1), bits, outer)
        terms = [summed[0]] + [exchange(summed[r], "head", r) for r in range(1, shards)]
        return sum(term.astype(F32) for term in terms).astype(BF16)

    ff_out_slice = owner_sum(ff_out_part, plain)
    ff_in_slice = owner_sum(ff_in_part, back_turned)
    out_part = out_weight_part.reshape(shards, slices, narrow, model)
    out_slice = owner_sum(jnp.swapaxes(to_order(jnp.swapaxes(out_part, 0, 1), own), 0, 1), plain)
    ff_in_sum, ff_out_sum = finish(place, plane_gather(ff_in_slice, forth), plane_gather(ff_out_slice, turned))
    out_weight_sum = to_order(plane_gather(out_slice, forth), own).reshape(width, model).astype(F32)

    def qkv_part(flat):
        part = jnp.dot(first_cols, flat, preferred_element_type=F32).reshape(model, 3, LANES)[:, :, :width]
        part = to_order(part.astype(BF16).reshape(slices, rows, 3 * width), own)
        return plane_sum(part, plain, outer)

    qkv_slice = qkv_part(flats[0]).astype(F32) + exchange(qkv_part(flats[1]), "head", 2).astype(F32)
    qkv_weight_sum = to_order(plane_gather(qkv_slice.astype(BF16), forth), own).reshape(model, 3, width).astype(F32)

    def owned(k):
        bias = jnp.sum(flats[k].astype(F32), axis=0).reshape(3, LANES)[:, :width].reshape(-1)
        probe = grads[k][1][: 2 * heads].reshape(-1)
        return jnp.concatenate([bias, probe])

    kept = jnp.concatenate([in_bias_part[0], owned(0)])
    kept = kept + exchange(jnp.concatenate([in_bias_part[2], owned(1)]), "head", 2)
    other = in_bias_part[1] + exchange(in_bias_part[3], "head", 2)
    kept = kept.at[:hidden_part].add(exchange(other, "head", 1))
    kept = lax.psum(kept, "dp")
    shared = jnp.concatenate([
        jnp.sum(grad_first * normal1, axis=0)[None], jnp.sum(grad_first, axis=0)[None], sums[:4]
    ])
    for axis, count in (("dp", members), ("head", shards)):
        bit = 1
        while bit < count:
            shared = shared + exchange(shared, axis, bit)
            bit *= 2
    bias_end = hidden_part + 3 * width
    probe_sum = kept[bias_end:].reshape(2 * heads, BASIS)
    return (
        outputs, grad_source.astype(BF16), shared[0], shared[1], qkv_weight_sum,
        kept[hidden_part:bias_end].reshape(3, width), out_weight_sum, shared[2], probe_sum[:heads], probe_sum[heads:],
        shared[3], shared[4], ff_in_sum, kept[:hidden_part], ff_out_sum, shared[5],
    )


def solution(mesh):
    rows, whole = P(("dp", "head"), None), P()
    return jax.shard_map(
        local,
        mesh=mesh,
        in_specs=(
            rows, P("dp", None), whole, whole, P(None, None, "head"), P(None, "head"), P("head", None), whole,
            P("head", None), P("head", None), whole, whole, P(None, "head"), P("head"), P("head", None), whole, rows,
        ),
        out_specs=(
            rows, rows, whole, whole, P(None, None, "head"), P(None, "head"), P("head", None), whole,
            P("head", None), P("head", None), whole, whole, P(None, "head"), P("head"), P("head", None), whole,
        ),
        check_vma=False,
    )
```

```python
import functools
import math

import jax
import jax.numpy as jnp
import ml_dtypes
import numpy as np
from jax import lax
from jax.experimental import pallas as pl
from jax.experimental.pallas import tpu as pltpu
from jax.sharding import PartitionSpec as P

HEAD_DIM = 64
BASIS = 512
UNIT = 256
LANES = 256
TAU = 0.75
RIDGE = 0.5
EPSILON = 1e-05
MESH = pl.DeviceIdType.MESH
SPREAD = 1.0 / 64.0
WIDTH = 1.0 / BASIS
LIVE = BASIS // 2
HIGHEST = lax.Precision.HIGHEST
F32 = jnp.float32
BF16 = jnp.bfloat16


def split_table(table):
    high = table.astype(np.float32).astype(ml_dtypes.bfloat16)
    low = (table.astype(np.float32) - high.astype(np.float32)).astype(ml_dtypes.bfloat16)
    return high, low


@functools.lru_cache(maxsize=None)
def basis_tables():
    centres = np.arange(BASIS) / (BASIS - 1)
    apart = centres[:, None] - centres[None, :]
    gram = np.exp(-apart * apart / (4.0 * WIDTH * WIDTH)) + RIDGE * np.eye(BASIS)
    solve = np.linalg.inv(gram)
    samples = (np.arange(BASIS) + 0.5) / BASIS
    near_gap = TAU * samples[:, None] - centres[None, :]
    far_gap = samples[:, None] - centres[None, :]
    near = np.exp(-near_gap * near_gap / (2.0 * WIDTH * WIDTH))
    far = np.exp(-far_gap * far_gap / (2.0 * WIDTH * WIDTH))
    contract = (near.T @ far) * (TAU / (BASIS * WIDTH * math.sqrt(math.pi)))
    joined = np.concatenate([solve @ contract, solve[:, LIVE:]], axis=1)
    high, low = split_table(joined)
    forward = np.concatenate([high, high, low], axis=1)
    backward = np.concatenate([high.T, high.T, low.T], axis=1)
    return forward, backward


def term_scale(units):
    return (1.0 - TAU) / (WIDTH * math.sqrt(math.pi) * UNIT) / units.astype(F32)


def split3(value):
    high = value.astype(BF16)
    low = (value - high.astype(F32)).astype(BF16)
    return jnp.concatenate([high, low, high], axis=0)


def dot(a, b, contract=((1,), (0,)), precision=None):
    return lax.dot_general(a, b, (contract, ((), ())), precision=precision, preferred_element_type=F32)


def head_rows(heads, width):
    row = lax.broadcasted_iota(jnp.int32, (8, width), 0)
    lane = lax.broadcasted_iota(jnp.int32, (8, width), 1) // HEAD_DIM
    return ((row == lane) | (row == lane + heads)) & (lane < heads)


def read_parts(logits, heads):
    location = 1.0 / (1.0 + jnp.exp(-logits))
    variance = (jnp.maximum(logits, 0.0) + jnp.log1p(jnp.exp(-jnp.abs(logits)))) * SPREAD + WIDTH * WIDTH
    return location[:heads], variance[heads : 2 * heads]


def place_of(index, length):
    return TAU + (1.0 - TAU) * (index.astype(F32) + 0.5) / (length.astype(F32) * UNIT)


def split_rows(value):
    high = value.astype(BF16)
    rest = value - high.astype(F32)
    mid = rest.astype(BF16)
    return high, mid, (rest - mid.astype(F32)).astype(BF16)


def three_pass(left, right_high, right_low, contract=((1,), (0,))):
    high = left.astype(BF16)
    low = (left - high.astype(F32)).astype(BF16)
    return dot(high, right_high, contract) + dot(low, right_high, contract) + dot(high, right_low, contract)


def advance_values(table, value):
    joined = BASIS + LIVE if table.shape[0] == BASIS else BASIS
    high, low = table[:BASIS, :BASIS], table[:BASIS, 2 * joined : 2 * joined + BASIS]
    value_high = value.astype(BF16)
    value_low = (value - value_high.astype(F32)).astype(BF16)
    return dot(high, value_high) + dot(high, value_low) + dot(low, value_high)


def segment_info(lengths, units, flip, run):
    slot_units = lengths // UNIT
    slots = jnp.arange(lengths.shape[0], dtype=jnp.int32)
    ends = jnp.sum(jnp.where(slots[None, :] <= slots[:, None], slot_units[None, :], 0), axis=1)
    starts = ends - slot_units
    unit = jnp.arange(units, dtype=jnp.int32)[:, None]
    member = (unit >= starts[None, :]) & (unit < ends[None, :])
    start = jnp.sum(jnp.where(member, starts[None, :], 0), axis=1)
    length = jnp.sum(jnp.where(member, slot_units[None, :], 0), axis=1)
    place = jnp.sum(((ends[None, :] <= unit) & (slot_units > 0)[None, :]).astype(jnp.int32), axis=1)
    own = jnp.where(jnp.arange(units) == 0, flip, run)
    return jnp.stack([start, length, place, own]).astype(jnp.int32)


def other_of(index, distance):
    bit = 1
    while bit <= distance:
        if distance & bit:
            index = index + bit - 2 * bit * ((index // bit) % 2)
        bit *= 2
    return index


class Hops:
    def __init__(self, send, recv):
        self.send, self.recv, self.used = send, recv, 0

    def start(self, source, target, axis, bit):
        copy = pltpu.make_async_remote_copy(
            src_ref=source,
            dst_ref=target,
            send_sem=self.send.at[self.used],
            recv_sem=self.recv.at[self.used],
            device_id={axis: other_of(lax.axis_index(axis), bit)},
            device_id_type=MESH,
        )
        self.used += 1
        copy.start()
        return copy


def greet(neighbours):
    barrier = pltpu.get_barrier_semaphore()
    for axis, bit in neighbours:
        pl.semaphore_signal(
            barrier, inc=1, device_id={axis: other_of(lax.axis_index(axis), bit)}, device_id_type=MESH
        )
    pl.semaphore_wait(barrier, len(neighbours))


def set_out(pairs, sems, first):
    copies = [pltpu.make_async_copy(a, b, sems.at[first + k]) for k, (a, b) in enumerate(pairs)]
    for copy in copies:
        copy.start()
    return copies


def forward_kernel(
    heads, info, source, scales, weight, small, bias_row, table, ff_in, ff_out, out_weight,
    qkv_out, first_cols_out, flat_a_out, flat_b_out, logsum, values, probes, key_states, key_end, rows,
    mixed_0, mixed_1, mixed_2, mixed_3, in_bias, far_in, far_out, far_weight,
    qkv, first_rows, first_cols, flats, near, far, far_row, memory, sums, value_states, carried, value_ends, value_ins,
    projs, proj_ins, cols, discrete, mixed, mixed_in, send, recv, local_sems,
):
    own_rows, model = source.shape
    width = heads * HEAD_DIM
    units = qkv.shape[1]
    half = units // 2
    root = 1.0 / math.sqrt(HEAD_DIM)
    z = lax.axis_index("head")
    flip, run = (z % 2) * half, z // 2
    place = lax.axis_index("dp") % 8
    y, x, c = place // 4, (place // 2) % 2, place % 2
    slice_rows = model // 8
    at = lambda b: (b + flip) % units
    starts = [info[0, b] for b in range(units)]
    lengths = [info[1, b] for b in range(units)]
    orders = [info[2, b] for b in range(units)]
    greet((("head", 1), ("head", 2), ("head", 3), ("dp", 1), ("dp", 2), ("dp", 4)))
    hops = Hops(send, recv)
    started = []

    def go(*args):
        started.append(hops.start(*args))
        return started[-1]

    mine = weight.at[pl.ds(pl.multiple_of(place * slice_rows, 16), slice_rows)]
    slice_copy = go(mine, far.at[y, x, c], "head", 2)
    small_copy = go(small, far_row, "head", 2)
    row_copies = []
    for k in range(half):
        part = slice(k * UNIT, (k + 1) * UNIT)
        value = source[part].astype(F32)
        centred = value - jnp.mean(value, axis=-1, keepdims=True)
        factor = lax.rsqrt(jnp.mean(centred * centred, axis=-1, keepdims=True) + EPSILON)
        first_rows[part] = (centred * factor * scales[0:1] + scales[1:2]).astype(BF16)
        row_copies.append(go(first_rows.at[part], near.at[part], "head", 1))
    slice_copy.wait_recv()
    x_copy = go(far.at[y, x, c], far.at[y, x, c], "dp", 2)

    def widen(k, read):
        flats[k] = jnp.zeros((model, 3 * LANES), BF16)
        for i in range(3):
            flats[k, :, i * LANES : i * LANES + width] = read(slice(i * width, (i + 1) * width))

    def project(k, unit, shift):
        span = slice(unit * UNIT, (unit + 1) * UNIT)
        qkv[k, unit] = (dot(first_rows[span], flats[k]) + shift).astype(BF16)

    widen(0, lambda span: weight[:, span])
    for unit in range(half):
        project(0, unit, small[0:1])
    x_copy.wait_recv()
    y_copy = go(far.at[y, :, c], far.at[y, :, c], "dp", 4)
    first_cols[:, :own_rows] = first_rows[:own_rows].astype(F32).T.astype(BF16)
    y_copy.wait_recv()
    core_copy = go(far.at[:, :, c], far.at[:, :, c], "dp", 1)
    small_copy.wait_recv()
    for k, copy in enumerate(row_copies):
        copy.wait_recv()
        part = slice(k * UNIT, (k + 1) * UNIT)
        first_rows[own_rows + k * UNIT : own_rows + (k + 1) * UNIT] = near[part]
        project(0, half + k, small[0:1])

    in_mine = ff_in.at[pl.ds(pl.multiple_of(place * slice_rows, 16), slice_rows)]
    out_mine = ff_out.at[pl.ds(pl.multiple_of(place * slice_rows, 16), slice_rows)]
    gathers = ((far_in, 2, 4), (far_weight, 2, 4), (far_out, 4, 2))
    stage = {}
    for r in (1, 2, 3):
        stage[r] = [
            go(in_mine, far_in.at[r - 1, y, x, c], "head", r),
            go(out_weight.at[place], far_weight.at[r - 1, y, x, c], "head", r),
            go(out_mine, far_out.at[r - 1, y, x, c], "head", r),
        ]
    in_bias[0] = bias_row[...]
    bias_copies = [go(bias_row, in_bias.at[r], "head", r) for r in (1, 2, 3)]

    def advance(r, step):
        for copy in stage[r]:
            copy.wait_recv()
        stage[r] = []
        for array, first, second in gathers:
            block = array.at[r - 1]
            if step == 1:
                part, bit = block.at[y, x, c], first
            elif step == 2:
                part, bit = (block.at[y, :, c] if first == 2 else block.at[:, x, c]), second
            else:
                part, bit = block.at[:, :, c], 1
            stage[r].append(go(part, part, "dp", bit))

    first_cols[:, own_rows:] = near[...].astype(F32).T.astype(BF16)
    core_copy.wait_recv()
    widen(1, lambda span: far[:, :, :, :, span].reshape(model, width))
    for unit in range(units):
        project(1, unit, far_row[0:1])
    saved = set_out(
        [(qkv, qkv_out), (first_cols, first_cols_out), (flats.at[0], flat_a_out), (flats.at[1], flat_b_out)],
        local_sems, 0,
    )

    def probe_of(k):
        return jnp.where(k == 0, small[1:9, :BASIS], far_row[1:9, :BASIS])

    mask = head_rows(heads, LANES)

    def first_state(k, carry):
        memory[k] = jnp.zeros(memory.shape[1:], F32)
        row = probe_of(k)
        rows[k, 0:8] = row
        wide = 2 * (BASIS + LIVE)
        for i in range(1, 4):
            row = three_pass(row, table[:, :BASIS], table[:, wide : wide + BASIS])
            rows[k, 8 * i : 8 * i + 8] = row
        return carry

    lax.fori_loop(0, 2, first_state, 0)

    def state(b, k, carry):
        start, length = starts[b], lengths[b]
        now = memory[k]
        value_states[k, b] = now[:, LANES:]
        key_states[k, b] = now[:, :LANES].astype(BF16)
        if b > 0:
            probes[k, b] = jnp.where(mask, dot(rows[k, 0:8], now[:, :LANES], precision=HIGHEST), 0.0)
        else:
            probes[k, b] = jnp.zeros((8, LANES), F32)
        token = lax.broadcasted_iota(jnp.int32, (LIVE, UNIT), 1) + (b - start) * UNIT
        centre = (lax.broadcasted_iota(jnp.int32, (LIVE, UNIT), 0) + LIVE).astype(F32) / (BASIS - 1)
        gap = place_of(token, length) - centre
        psi = jnp.exp(gap * gap * (-0.5 / (WIDTH * WIDTH)))
        psi_high = psi.astype(BF16)
        psi_low = (psi - psi_high.astype(F32)).astype(BF16)
        pairs = qkv[k, at(b), :, LANES : 3 * LANES]
        fresh = dot(psi_high, pairs) + dot(psi_low, pairs)
        gathered = fresh if b == 0 else jnp.where(start == b, 0.0, sums[k]) + fresh
        sums[k] = gathered
        stacked = jnp.concatenate([now, gathered * term_scale(length)], axis=0)
        later = dot(table[...], split3(stacked))
        memory[k] = jnp.where(start + length == b + 1, later, now)
        return carry

    def end_state(k, carry):
        key = memory[k, :, :LANES]
        key_end[k] = key
        value_ends[k] = memory[k, :, LANES : LANES + width].astype(BF16)
        seen = dot(rows[k], key, precision=HIGHEST)
        for i in range(4):
            projs[k, 8 * i : 8 * i + 8] = jnp.where(mask, seen[8 * i : 8 * i + 8], 0.0)
        return carry

    def attend(b, k, carry):
        cols[k, b] = qkv[k, at(b), :, 2 * LANES : 3 * LANES].astype(F32).T.astype(BF16)
        query = qkv[k, at(b), :, 0:LANES].astype(F32) * root
        lane_head = lax.broadcasted_iota(jnp.int32, (UNIT, LANES), 1) // HEAD_DIM
        causal = lax.broadcasted_iota(jnp.int32, (UNIT, UNIT), 0) <= lax.broadcasted_iota(
            jnp.int32, (UNIT, UNIT), 1
        )
        away = [jnp.where(starts[b] <= j, 0.0, 1e30) for j in range(b)] + [0.0]
        for h in range(heads):
            own = jnp.where(lane_head == h, query, 0.0).astype(BF16)
            scores = [dot(qkv[k, at(j), :, LANES : 2 * LANES], own, ((1,), (1,))) for j in range(b + 1)]
            scores[b] = jnp.where(causal, scores[b], -1e30)
            highest = functools.reduce(
                jnp.maximum, [jnp.max(s, axis=0, keepdims=True) - away[j] for j, s in enumerate(scores)]
            )
            weights = [jnp.exp(s - (highest + away[j])) for j, s in enumerate(scores)]
            total = sum(jnp.sum(w, axis=0, keepdims=True) for w in weights)
            span = slice(h * HEAD_DIM, (h + 1) * HEAD_DIM)
            part = sum(dot(cols[k, j, span], weights[j].astype(BF16)) for j in range(b + 1))
            discrete[k, b, span] = part * (1.0 / total)
            logsum[k, b, h : h + 1] = highest + jnp.log(total)
        return carry

    def seen_value(k, carry):
        incoming = jnp.where(run > 0, value_ins[k].astype(F32), 0.0)
        carried[:, :width] = incoming
        carried[:, width:] = jnp.zeros((BASIS, LANES - width), F32)
        for b in range(units):
            if b > 0:
                carried[...] = jnp.where(starts[b] == b, advance_values(table, carried[...]), carried[...])
            values[k, b] = (value_states[k, b] + carried[...]).astype(BF16)
            gained = jnp.zeros((8, LANES), F32)
            for i in range(4):
                gained += jnp.where((orders[b] == i) & (run > 0), proj_ins[k, 8 * i : 8 * i + 8], 0.0)
            probes[k, b] = (probes[k, b] + gained) * root
        return carry

    def read(rel, k, carry):
        b = at(rel)
        query = qkv[k, rel, :, 0:LANES]
        logits = sum(dot(part, query, ((1,), (1,))) for part in split_rows(probes[k, b]))
        location, variance = read_parts(logits, heads)
        fall = -0.5 / variance
        peak = WIDTH * lax.rsqrt(variance)
        centres = lax.broadcasted_iota(jnp.int32, (BASIS, UNIT), 0).astype(F32) / (BASIS - 1)
        value_cols = values[k, b].astype(F32).T.astype(BF16)
        parts = []
        for h in range(heads):
            gap = centres - location[h : h + 1]
            density = jnp.exp(gap * gap * fall[h : h + 1]).astype(BF16)
            span = slice(h * HEAD_DIM, (h + 1) * HEAD_DIM)
            parts.append(discrete[k, b, span] + dot(value_cols[span], density) * peak[h : h + 1])
        mixed[k, rel] = jnp.concatenate(parts, axis=0).T.astype(BF16)
        return carry

    for b in range(units):
        lax.fori_loop(0, 2, functools.partial(state, b), 0)
        if b == 1:
            advance(1, 1)
    lax.fori_loop(0, 2, end_state, 0)
    state_copies = [go(value_ends.at[k], value_ins.at[1 - k], "head", 2) for k in range(2)]
    state_copies += [go(projs.at[k], proj_ins.at[1 - k], "head", 2) for k in range(2)]
    advance(1, 2)
    for b in range(units):
        lax.fori_loop(0, 2, functools.partial(attend, b), 0)
        if b == 2:
            advance(2, 1)
            advance(3, 1)
    advance(1, 3)
    for copy in state_copies:
        copy.wait_recv()
    lax.fori_loop(0, 2, seen_value, 0)
    advance(2, 2)
    mixed_copies = []
    for rel in (2, 3, 0, 1):
        lax.fori_loop(0, 2, functools.partial(read, rel), 0)
        if rel == 3:
            advance(3, 2)
            mixed_copies = [
                go(mixed.at[k, half:], mixed_in.at[k], "head", 1) for k in range(2)
            ]
    mixed_0[...] = mixed[0, :half].reshape(own_rows, width)
    mixed_2[...] = mixed[1, :half].reshape(own_rows, width)
    advance(2, 3)
    for copy in mixed_copies:
        copy.wait_recv()
    mixed_1[...] = mixed_in[0].reshape(own_rows, width)
    mixed_3[...] = mixed_in[1].reshape(own_rows, width)
    advance(3, 3)
    for copy in bias_copies + stage[1] + stage[2] + stage[3]:
        copy.wait_recv()
    for copy in started:
        copy.wait_send()
    for copy in saved:
        copy.wait()


def forward(info, source, scales, weight, small, bias_row, ff_in, ff_out, out_slices, heads):
    own_rows, model = source.shape
    units = 2 * own_rows // UNIT
    width = heads * HEAD_DIM
    hidden_part = ff_in.shape[1]
    rows = model // 8
    table = jnp.asarray(basis_tables()[0])
    vmem, anywhere = pl.BlockSpec(memory_space=pltpu.VMEM), pl.BlockSpec(memory_space=pl.ANY)
    shape = jax.ShapeDtypeStruct
    hops = 2 + units // 2 + 3 + 3 * 3 * 4 + 3 + 4 + 2
    return pl.pallas_call(
        functools.partial(forward_kernel, heads),
        in_specs=[pl.BlockSpec(memory_space=pltpu.SMEM)] + [vmem] * 6 + [anywhere] * 3,
        out_specs=[anywhere] * 4 + [vmem] * 11 + [anywhere] * 3,
        out_shape=[
            shape((2, units, UNIT, 3 * LANES), BF16),
            shape((model, 2 * own_rows), BF16),
            shape((model, 3 * LANES), BF16),
            shape((model, 3 * LANES), BF16),
            shape((2, units, 8, UNIT), F32),
            shape((2, units, BASIS, LANES), BF16),
            shape((2, units, 8, LANES), F32),
            shape((2, units, BASIS, LANES), BF16),
            shape((2, BASIS, LANES), F32),
            shape((2, 32, BASIS), F32),
        ] + [shape((own_rows, width), BF16)] * 4 + [
            shape((4,) + bias_row.shape, F32),
            shape((3, 2, 2, 2, rows, hidden_part), BF16),
            shape((3, 2, 2, 2, rows, model), BF16),
            shape((3, 2, 2, 2) + out_slices.shape[1:], BF16),
        ],
        scratch_shapes=[
            pltpu.VMEM((2, units, UNIT, 3 * LANES), BF16),
            pltpu.VMEM((2 * own_rows, model), BF16),
            pltpu.VMEM((model, 2 * own_rows), BF16),
            pltpu.VMEM((2, model, 3 * LANES), BF16),
            pltpu.VMEM((own_rows, model), BF16),
            pltpu.VMEM((2, 2, 2, rows, weight.shape[1]), BF16),
            pltpu.VMEM(small.shape, F32),
            pltpu.VMEM((2, BASIS, 2 * LANES), F32),
            pltpu.VMEM((2, LIVE, 2 * LANES), F32),
            pltpu.VMEM((2, units, BASIS, LANES), F32),
            pltpu.VMEM((BASIS, LANES), F32),
            pltpu.VMEM((2, BASIS, width), BF16),
            pltpu.VMEM((2, BASIS, width), BF16),
            pltpu.VMEM((2, 32, LANES), F32),
            pltpu.VMEM((2, 32, LANES), F32),
            pltpu.VMEM((2, units, LANES, UNIT), BF16),
            pltpu.VMEM((2, units, width, UNIT), F32),
            pltpu.VMEM((2, units, UNIT, width), BF16),
            pltpu.VMEM((2, units // 2, UNIT, width), BF16),
            pltpu.SemaphoreType.DMA((hops,)),
            pltpu.SemaphoreType.DMA((hops,)),
            pltpu.SemaphoreType.DMA((4,)),
        ],
        compiler_params=pltpu.CompilerParams(
            collective_id=1, has_side_effects=True, vmem_limit_bytes=60 << 20
        ),
        name="forward",
    )(info, source, scales, weight, small, bias_row, table, ff_in, ff_out, out_slices)


def whole(shape):
    return pl.BlockSpec(shape, lambda i, info: (0,) * len(shape))


def middle_kernel(
    place, source, cotangent, mixed_0, mixed_1, mixed_2, mixed_3, own_weight, far_weight, vectors, in_bias, own_in, own_out,
    far_in, far_out, outputs, grad_residual, grad_mixed_0, grad_mixed_1, grad_mixed_2, grad_mixed_3, grad_in, grad_out,
    grad_out_weight, sums, grad_in_bias,
    residual, inverse, second, second_cols, total, grad_second, in_now, out_now, out_weight,
):
    r = pl.program_id(0)
    own = place[0]
    slices, rows = own_in.shape[0], own_in.shape[1]
    model = source.shape[1]
    hidden_part = own_in.shape[2]
    out_bias, gain, shift, last_bias = (vectors[k : k + 1] for k in range(4))

    @pl.when(r == 0)
    def _():
        value = source[...].astype(F32) + out_bias
        out_weight[0] = own_weight[...]
        narrow = own_weight.shape[0] // slices
        for k in range(far_weight.shape[0]):
            parts = [far_weight[k, j].astype(F32)[:narrow] for j in range(slices)]
            out_weight[k + 1] = jnp.concatenate(parts, axis=0).astype(BF16)
        for k, mixed in enumerate((mixed_0, mixed_1, mixed_2, mixed_3)):
            value += dot(mixed[...], out_weight[k])
        residual[...] = value
        centred = value - jnp.mean(value, axis=-1, keepdims=True)
        factor = lax.rsqrt(jnp.mean(centred * centred, axis=-1, keepdims=True) + EPSILON)
        inverse[...] = factor
        normal = centred * factor
        grad_residual[...] = normal
        rounded = (normal * gain + shift).astype(BF16)
        second[...] = rounded
        second_cols[...] = rounded.astype(F32).T.astype(BF16)
        total[...] = jnp.zeros_like(total)
        grad_second[...] = jnp.zeros_like(grad_second)
        grad_in_bias[...] = jnp.zeros_like(grad_in_bias)
        for j in range(slices):
            in_now[j * rows : (j + 1) * rows] = own_in[j]
            out_now[j * rows : (j + 1) * rows] = own_out[j]

    @pl.when(r > 0)
    def _():
        for j in range(slices):
            in_now[j * rows : (j + 1) * rows] = far_in[0, j]
            out_now[j * rows : (j + 1) * rows] = far_out[0, j]

    half = hidden_part // 2
    for t in range(2):
        span = slice(t * half, (t + 1) * half)
        hidden = dot(second[...], in_now[:, span]) + in_bias[r, 0:1, span]
        cube = hidden * hidden
        root = math.sqrt(2.0 / math.pi)
        bent = jnp.tanh(hidden * (root + (root * 0.044715) * cube))
        lifted = 0.5 + 0.5 * bent
        activation = (hidden * lifted).astype(BF16)
        slope = lifted + hidden * ((0.5 - 0.5 * bent * bent) * (root + (3.0 * root * 0.044715) * cube))
        total[...] += dot(activation, out_now[span])
        given = dot(cotangent[...], out_now[span], ((1,), (1,)))
        grad_hidden = (given * slope).astype(BF16)
        grad_second[...] += dot(grad_hidden, in_now[:, span], ((1,), (1,)))
        grad_in_bias[pl.ds(r, 1), span] = jnp.sum(grad_hidden.astype(F32), axis=0, keepdims=True)
        part = dot(activation, cotangent[...], ((0,), (0,))).astype(BF16)
        per = half // rows
        for k in range(per):
            grad_out[0, t * per + k] = part[k * rows : (k + 1) * rows]
        part = dot(second_cols[...], grad_hidden).astype(BF16)
        for j in range(slices):
            grad_in[0, j, :, span] = part[j * rows : (j + 1) * rows]

    @pl.when(r == pl.num_programs(0) - 1)
    def _():
        given = cotangent[...].astype(F32)
        outputs[...] = (residual[...] + total[...] + last_bias).astype(BF16)
        normal = grad_residual[...]
        grad = grad_second[...]
        scaled = grad * gain
        value = given + inverse[...] * (
            scaled
            - jnp.mean(scaled, axis=-1, keepdims=True)
            - normal * jnp.mean(scaled * normal, axis=-1, keepdims=True)
        )
        sums[0:1] = jnp.sum(value, axis=0, keepdims=True)
        sums[1:2] = jnp.sum(grad * normal, axis=0, keepdims=True)
        sums[2:3] = jnp.sum(grad, axis=0, keepdims=True)
        sums[3:4] = jnp.sum(given, axis=0, keepdims=True)
        sums[4:8] = jnp.zeros((4, model), F32)
        grad_residual[...] = value
        rounded = value.astype(BF16)
        grads = (grad_mixed_0, grad_mixed_1, grad_mixed_2, grad_mixed_3)
        for k, mixed in enumerate((mixed_0, mixed_1, mixed_2, mixed_3)):
            grads[k][...] = dot(rounded, out_weight[k], ((1,), (1,))).astype(BF16)
            product = dot(mixed[...], rounded, ((0,), (0,)))
            narrow = product.shape[0] // slices
            spare = jnp.zeros((grad_out_weight.shape[2] - narrow, model), F32)
            for j in range(slices):
                part = jnp.concatenate([product[j * narrow : (j + 1) * narrow], spare], axis=0)
                grad_out_weight[k, j] = part.astype(BF16)


def middle(place, source, cotangent, mixed, out_weight, far_weight, vectors, in_bias, own_in, own_out, far_in, far_out):
    own_rows, model = source.shape
    shards = far_in.shape[0] + 1
    slices, rows, hidden_part = own_in.shape
    narrow = mixed[0].shape
    far = pl.BlockSpec((1,) + own_in.shape, lambda r, place: (jnp.maximum(r - 1, 0), 0, 0, 0))
    part = pl.BlockSpec((1,) + own_in.shape, lambda r, place: (r, 0, 0, 0))
    macs = own_rows * model * (6 * shards * hidden_part + 3 * model)
    return pl.pallas_call(
        middle_kernel,
        grid_spec=pltpu.PrefetchScalarGridSpec(
            num_scalar_prefetch=1,
            grid=(shards,),
            in_specs=[whole(source.shape)] * 2 + [whole(narrow)] * 4 + [
                whole(out_weight.shape), whole(far_weight.shape), whole(vectors.shape), whole(in_bias.shape), whole(own_in.shape),
                whole(own_out.shape), far, far,
            ],
            out_specs=[whole(source.shape)] * 2 + [whole(narrow)] * 4 + [
                part, part, whole((shards,) + far_weight.shape[1:]), whole((8, model)), whole((shards, hidden_part))
            ],
            scratch_shapes=[
                pltpu.VMEM((own_rows, model), F32),
                pltpu.VMEM((own_rows, 1), F32),
                pltpu.VMEM((own_rows, model), BF16),
                pltpu.VMEM((model, own_rows), BF16),
                pltpu.VMEM((own_rows, model), F32),
                pltpu.VMEM((own_rows, model), F32),
                pltpu.VMEM((model, hidden_part), BF16),
                pltpu.VMEM((hidden_part, model), BF16),
                pltpu.VMEM((shards,) + narrow[1:] + (model,), BF16),
            ],
        ),
        out_shape=[
            jax.ShapeDtypeStruct(source.shape, BF16),
            jax.ShapeDtypeStruct(source.shape, F32),
        ] + [jax.ShapeDtypeStruct(narrow, BF16)] * 4 + [
            jax.ShapeDtypeStruct((shards, slices, rows, hidden_part), BF16),
            jax.ShapeDtypeStruct((shards, slices, rows, hidden_part), BF16),
            jax.ShapeDtypeStruct((shards,) + far_weight.shape[1:], BF16),
            jax.ShapeDtypeStruct((8, model), F32),
            jax.ShapeDtypeStruct((shards, hidden_part), F32),
        ],
        compiler_params=pltpu.CompilerParams(vmem_limit_bytes=60 << 20),
        cost_estimate=pl.CostEstimate(
            flops=2 * macs, bytes_accessed=30 << 20, transcendentals=own_rows * shards * hidden_part
        ),
        name="middle",
    )(place, source, cotangent, *mixed, out_weight, far_weight, vectors, in_bias, own_in, own_out, far_in, far_out)


def added(a, b):
    return (a.astype(F32) + b.astype(F32)).astype(BF16)


def backward_kernel(
    heads, info, qkv, gm_0, gm_1, gm_2, gm_3, logsum, values, probes, key_states, key_end, rows, table,
    grad_in, grad_out, grad_weight, out, probe_grad, slice_in, slice_out, slice_weight,
    given, query_grad, memory_grad, row_grad, value_total, value_carried, value_back, value_in, row_back, row_in,
    row_total, carried, spread, key_grad, value_grad, cols,
    keep_in, keep_out, keep_weight, core_in, core_out, core_weight, one_in, one_out, one_weight,
    two_in, two_out, two_weight, z_in, z_out, z_weight, send, recv, local_sems,
):
    units = qkv.shape[1]
    half = units // 2
    width = heads * HEAD_DIM
    root = 1.0 / math.sqrt(HEAD_DIM)
    z = lax.axis_index("head")
    flip, run = (z % 2) * half, z // 2
    place = lax.axis_index("dp") % 8
    y, x, c = place // 4, (place // 2) % 2, place % 2
    at = lambda b: (b + flip) % units
    starts = [info[0, b] for b in range(units)]
    lengths = [info[1, b] for b in range(units)]
    orders = [info[2, b] for b in range(units)]
    greet((("head", 1), ("head", 2), ("head", 3), ("dp", 1), ("dp", 2), ("dp", 4)))
    hops = Hops(send, recv)
    started = []

    def go(*args):
        started.append(hops.start(*args))
        return started[-1]

    given_copies = [go(gm_1, given.at[0, half:], "head", 1), go(gm_3, given.at[1, half:], "head", 1)]
    sums = (
        (grad_in, keep_in, core_in, one_in, two_in, z_in, True),
        (grad_weight, keep_weight, core_weight, one_weight, two_weight, z_weight, True),
        (grad_out, keep_out, core_out, one_out, two_out, z_out, False),
    )
    stage, local_copies = {}, {}
    for i, r in enumerate((2, 1, 3, 0)):
        stage[r], local_copies[r] = [], []
        for n, (term, keep, core, _, _, _, _) in enumerate(sums):
            stage[r].append(go(term.at[r, :, :, 1 - c], core.at[r], "dp", 1))
            copy = pltpu.make_async_copy(term.at[r, :, :, c], keep.at[r], local_sems.at[3 * i + n])
            copy.start()
            local_copies[r].append(copy)

    def first_hop(r):
        for n, (_, keep, core, one, _, _, along_x) in enumerate(sums):
            local_copies[r][n].wait()
            stage[r][n].wait_recv()
            keep[r] = added(keep[r], core[r])
            part = keep.at[r, :, 1 - x] if along_x else keep.at[r, 1 - y]
            stage[r][n] = go(part, one.at[r], "dp", 2 if along_x else 4)

    def second_hop(r):
        for n, (_, keep, _, one, two, _, along_x) in enumerate(sums):
            stage[r][n].wait_recv()
            kept = keep[r, :, x] if along_x else keep[r, y]
            one[r] = added(kept, one[r])
            part = one.at[r, 1 - y] if along_x else one.at[r, 1 - x]
            stage[r][n] = go(part, two.at[r], "dp", 4 if along_x else 2)

    def third_hop(r):
        for n, (_, _, _, one, two, far, along_x) in enumerate(sums):
            stage[r][n].wait_recv()
            kept = one[r, y] if along_x else one[r, x]
            two[r] = added(kept, two[r])
            if r:
                stage[r][n] = go(two.at[r], far.at[r - 1], "head", r)

    for k, own in enumerate((gm_0, gm_2)):
        given[k, :half] = own[...]
    mask = head_rows(heads, LANES)
    lane_head = lax.broadcasted_iota(jnp.int32, (UNIT, LANES), 1) // HEAD_DIM

    def given_of(k, b):
        return jnp.concatenate([given[k, at(b)], jnp.zeros((UNIT, LANES - width), BF16)], axis=1).astype(F32)

    def read_back(b, k, carry):
        query = qkv[k, at(b), :, 0:LANES]
        full = given_of(k, b)
        probe = probes[k, b]
        logits = sum(dot(part, query, ((1,), (1,))) for part in split_rows(probe))
        location, variance = read_parts(logits, heads)
        inverse = 1.0 / variance
        fall = -0.5 * inverse
        peak = WIDTH * lax.rsqrt(variance)
        centres = lax.broadcasted_iota(jnp.int32, (BASIS, UNIT), 0).astype(F32) / (BASIS - 1)
        along, across = [], []
        ends = starts[b] + lengths[b] == b + 1
        total = jnp.zeros((BASIS, LANES), F32)
        for h in range(heads):
            own_given = jnp.where(lane_head == h, full, 0.0).astype(BF16)
            gap = centres - location[h : h + 1]
            square = gap * gap
            density = jnp.exp(square * fall[h : h + 1]) * peak[h : h + 1]
            grad_density = dot(values[k, b], own_given, ((1,), (1,)))
            total += dot(density.astype(BF16), own_given)
            weighed = density * grad_density
            moment = weighed * gap
            zeroth = jnp.sum(weighed, axis=0, keepdims=True)
            first = jnp.sum(moment, axis=0, keepdims=True)
            second = jnp.sum(moment * gap, axis=0, keepdims=True)
            along.append(first * inverse[h : h + 1])
            across.append(0.5 * inverse[h : h + 1] * (second * inverse[h : h + 1] - zeroth))
        sigmoid = 1.0 / (1.0 + jnp.exp(-logits))
        grad_location = jnp.concatenate(along, axis=0) * location * (1.0 - location)
        grad_variance = jnp.concatenate(across, axis=0) * SPREAD * sigmoid[heads : 2 * heads]
        grad_logits = jnp.concatenate(
            [grad_location, grad_variance, jnp.zeros((8 - 2 * heads, UNIT), F32)], axis=0
        )
        padded = jnp.concatenate([grad_logits, jnp.zeros((120, UNIT), F32)], axis=0)
        probe_cols = jnp.concatenate([probe, jnp.zeros((120, LANES), F32)], axis=0).T
        query_grad[k, b] = dot(probe_cols, padded, precision=HIGHEST)[:width]
        fresh = jnp.where(mask, dot(grad_logits, query.astype(F32), precision=HIGHEST), 0.0) * root
        if b == units - 1:
            value_total[k] = total
            row_total[k] = fresh
            probe_grad[k] = dot(fresh, key_states[k, b].astype(F32), ((1,), (1,)), HIGHEST)
            for i in range(4):
                row_back[k, 8 * i : 8 * i + 8] = jnp.where(orders[b] == i, fresh, 0.0)
        else:
            value_total[k] = jnp.where(ends, 0.0, value_total[k]) + total
            row_total[k] = jnp.where(ends, 0.0, row_total[k]) + fresh
            probe_grad[k] += dot(fresh, key_states[k, b].astype(F32), ((1,), (1,)), HIGHEST)
            for i in range(4):
                row_back[k, 8 * i : 8 * i + 8] += jnp.where(orders[b] == i, fresh, 0.0)
        memory_grad[k, b] = value_total[k]
        row_grad[k, b] = row_total[k]
        before = jnp.zeros((BASIS, LANES), F32) if b == units - 1 else value_carried[k]
        whole_grad = before + value_total[k]
        if b > 0:
            value_carried[k] = jnp.where(starts[b] == b, advance_values(table, whole_grad), before)
        else:
            value_back[k] = whole_grad[:, :width].astype(BF16)
        return carry

    def attend_back(b, k, carry):
        query = qkv[k, at(b), :, 0:LANES].astype(F32) * root
        full = given_of(k, b)
        causal = lax.broadcasted_iota(jnp.int32, (UNIT, UNIT), 0) <= lax.broadcasted_iota(
            jnp.int32, (UNIT, UNIT), 1
        )
        away = [jnp.where(starts[b] <= j, 0.0, 1e30) for j in range(b)] + [0.0]
        owns = [jnp.where(lane_head == h, query, 0.0).astype(BF16) for h in range(heads)]
        own_givens = [jnp.where(lane_head == h, full, 0.0).astype(BF16) for h in range(heads)]
        grads, probs = [], []
        for h in range(heads):
            prob_h, product_h = [], []
            inner = jnp.zeros((1, UNIT), F32)
            for j in range(b + 1):
                score = dot(qkv[k, at(j), :, LANES : 2 * LANES], owns[h], ((1,), (1,)))
                if j == b:
                    score = jnp.where(causal, score, -1e30)
                prob = jnp.exp(score - (logsum[k, b, h : h + 1] + away[j]))
                product = prob * dot(qkv[k, at(j), :, 2 * LANES : 3 * LANES], own_givens[h], ((1,), (1,)))
                inner += jnp.sum(product, axis=0, keepdims=True)
                prob_h.append(prob)
                product_h.append(product)
            span = slice(h * HEAD_DIM, (h + 1) * HEAD_DIM)
            grad_h = [(product_h[j] - prob_h[j] * inner).astype(BF16) for j in range(b + 1)]
            result = sum(dot(cols[k, j, span], grad_h[j]) for j in range(b + 1))
            query_grad[k, b, span] = query_grad[k, b, span] + result * root
            grads.append(grad_h)
            probs.append([prob.astype(BF16) for prob in prob_h])
        own_all = jnp.concatenate(owns, axis=0)
        given_all = jnp.concatenate(own_givens, axis=0)
        for j in range(b + 1):
            keys = dot(jnp.concatenate([grads[h][j] for h in range(heads)], axis=1), own_all)
            vals = dot(jnp.concatenate([probs[h][j] for h in range(heads)], axis=1), given_all)
            if b == units - 1:
                key_grad[k, j], value_grad[k, j] = keys, vals
            else:
                key_grad[k, j] += keys
                value_grad[k, j] += vals
        return carry

    def carry_back(k, total, units_before):
        moved = dot(table[...], split3(total))
        return moved[:BASIS], (moved[BASIS:] * term_scale(units_before)).astype(BF16)

    def end_back(k, carry):
        row = jnp.where(run == 0, row_in[k], 0.0)
        value = jnp.where(run == 0, value_in[k].astype(F32), 0.0)
        grad_keys = dot(rows[k], row, ((0,), (0,)), HIGHEST)
        total = jnp.concatenate([grad_keys, value, jnp.zeros((BASIS, LANES - width), F32)], axis=1)
        carried[k], spread[k] = carry_back(k, total, lengths[units - 1])
        seen = dot(row, key_end[k], ((1,), (1,)), HIGHEST)
        gained = seen[24:32]
        for i in (2, 1, 0):
            gained = three_pass(gained, table[:BASIS, :BASIS], table[:BASIS, 2 * BASIS : 3 * BASIS])
            gained = gained + seen[8 * i : 8 * i + 8]
        probe_grad[k] += gained
        return carry

    def finish(b, k, carry):
        start, length = starts[b], lengths[b]
        token = lax.broadcasted_iota(jnp.int32, (UNIT, LIVE), 0) + (b - start) * UNIT
        centre = (lax.broadcasted_iota(jnp.int32, (UNIT, LIVE), 1) + LIVE).astype(F32) / (BASIS - 1)
        gap = place_of(token, length) - centre
        psi = jnp.exp(gap * gap * (-0.5 / (WIDTH * WIDTH))).astype(BF16)
        pair_grad = dot(psi, spread[k])
        query_rows = query_grad[k, b].T.astype(BF16)
        out[k, at(b), :, :LANES] = jnp.concatenate([query_rows, jnp.zeros((UNIT, LANES - width), BF16)], axis=1)
        out[k, at(b), :, LANES : 2 * LANES] = (key_grad[k, b] + pair_grad[:, :LANES]).astype(BF16)
        out[k, at(b), :, 2 * LANES :] = (value_grad[k, b] + pair_grad[:, LANES:]).astype(BF16)
        if b > 0:
            grad_keys = dot(rows[k, 0:8], row_grad[k, b], ((0,), (0,)), HIGHEST)
            total = carried[k] + jnp.concatenate([grad_keys, memory_grad[k, b]], axis=1)
            moved, spread_now = carry_back(k, total, lengths[b - 1])
            carried[k] = jnp.where(start == b, moved, carried[k])
            spread[k] = jnp.where(start == b, spread_now.astype(F32), spread[k].astype(F32)).astype(BF16)
        return carry

    def both(step, *args):
        lax.fori_loop(0, 2, functools.partial(step, *args), 0)

    def turn(k, carry):
        for b in range(units):
            cols[k, b] = qkv[k, at(b), :, LANES : 2 * LANES].astype(F32).T.astype(BF16)
        return carry

    lax.fori_loop(0, 2, turn, 0)
    first_hop(2)
    first_hop(1)
    for copy in given_copies:
        copy.wait_recv()
    both(read_back, 3)
    first_hop(3)
    first_hop(0)
    both(read_back, 2)
    second_hop(2)
    both(read_back, 1)
    second_hop(1)
    both(read_back, 0)
    back_copies = [go(value_back.at[k], value_in.at[1 - k], "head", 2) for k in range(2)]
    back_copies += [go(row_back.at[k], row_in.at[1 - k], "head", 2) for k in range(2)]
    second_hop(3)
    both(attend_back, 3)
    second_hop(0)
    third_hop(2)
    third_hop(1)
    for copy in back_copies:
        copy.wait_recv()
    lax.fori_loop(0, 2, end_back, 0)
    both(finish, 3)
    both(attend_back, 2)
    third_hop(3)
    third_hop(0)
    both(finish, 2)
    for b in (1, 0):
        both(attend_back, b)
        both(finish, b)
    for n, (_, _, _, _, two, far, _) in enumerate(sums):
        total = two[0].astype(F32)
        for r in (1, 2, 3):
            stage[r][n].wait_recv()
            total += far[r - 1].astype(F32)
        (slice_in, slice_weight, slice_out)[n][...] = total.astype(BF16)
    for copy in started:
        copy.wait_send()


def backward(info, qkv, grad_mixed, logsum, values, probes, key_states, key_end, rows, grad_in, grad_out, grad_weight, heads):
    units = qkv.shape[1]
    width = heads * HEAD_DIM
    table = jnp.asarray(basis_tables()[1])
    vmem, anywhere = pl.BlockSpec(memory_space=pltpu.VMEM), pl.BlockSpec(memory_space=pl.ANY)
    shape = jax.ShapeDtypeStruct
    slices = [grad_in.shape[4:], grad_out.shape[4:], grad_weight.shape[4:]]
    hops = 2 + 3 * 4 * 3 + 3 * 3 + 4
    return pl.pallas_call(
        functools.partial(backward_kernel, heads),
        in_specs=[pl.BlockSpec(memory_space=pltpu.SMEM)] + [vmem] * 12 + [anywhere] * 3,
        out_specs=[vmem] * 5,
        out_shape=[shape(qkv.shape, BF16), shape((2, 8, BASIS), F32)] + [shape(part, BF16) for part in slices],
        scratch_shapes=[
            pltpu.VMEM((2, units, UNIT, width), BF16),
            pltpu.VMEM((2, units, width, UNIT), F32),
            pltpu.VMEM((2, units, BASIS, LANES), F32),
            pltpu.VMEM((2, units, 8, LANES), F32),
            pltpu.VMEM((2, BASIS, LANES), F32),
            pltpu.VMEM((2, BASIS, LANES), F32),
            pltpu.VMEM((2, BASIS, width), BF16),
            pltpu.VMEM((2, BASIS, width), BF16),
            pltpu.VMEM((2, 32, LANES), F32),
            pltpu.VMEM((2, 32, LANES), F32),
            pltpu.VMEM((2, 8, LANES), F32),
            pltpu.VMEM((2, BASIS, 2 * LANES), F32),
            pltpu.VMEM((2, LIVE, 2 * LANES), BF16),
            pltpu.VMEM((2, units, UNIT, LANES), F32),
            pltpu.VMEM((2, units, UNIT, LANES), F32),
            pltpu.VMEM((2, units, LANES, UNIT), BF16),
        ]
        + [pltpu.VMEM((4, 2, 2) + part, BF16) for part in slices]
        + [pltpu.VMEM((4, 2, 2) + part, BF16) for part in slices]
        + [pltpu.VMEM((4, 2) + part, BF16) for part in slices]
        + [pltpu.VMEM((4,) + part, BF16) for part in slices]
        + [pltpu.VMEM((3,) + part, BF16) for part in slices]
        + [
            pltpu.SemaphoreType.DMA((hops,)),
            pltpu.SemaphoreType.DMA((hops,)),
            pltpu.SemaphoreType.DMA((12,)),
        ],
        compiler_params=pltpu.CompilerParams(
            collective_id=2, has_side_effects=True, vmem_limit_bytes=62 << 20
        ),
        name="backward",
    )(
        info, qkv, *grad_mixed, logsum, values, probes, key_states, key_end, rows, table, grad_in, grad_out, grad_weight
    )


def tail_kernel(
    heads, outer, grads, first_cols, flat_a, flat_b, grad_residual, source, scales, slice_in, slice_out, slice_weight,
    sums, in_bias_part, probe_grad, input_grad, whole_in, whole_out, whole_weight, whole_qkv, shared_out, owned_out,
    row_grad, near, kept, part_a, part_b, core_a, core_b, one_a, one_b, two_a, two_b, far_b, total, outer_in,
    gather_in, gather_out, gather_weight, gather_qkv,
    shared, shared_in, block, block_in, bias_block, bias_in, joined, joined_in, send, recv,
):
    own_rows, model = source.shape
    units = grads.shape[1]
    half = units // 2
    width = heads * HEAD_DIM
    z = lax.axis_index("head")
    place = lax.axis_index("dp") % 8
    y, x, c = place // 4, (place // 2) % 2, place % 2
    rows = model // 8
    greet(
        (("head", 1), ("head", 2), ("head", 3), ("dp", 1), ("dp", 2), ("dp", 4)) + tuple(("dp", bit) for bit in outer)
    )
    hops = Hops(send, recv)
    started = []

    def go(*args):
        started.append(hops.start(*args))
        return started[-1]

    def row_of(rel):
        return dot(grads[0, rel], flat_a[...], ((1,), (1,))) + dot(grads[1, rel], flat_b[...], ((1,), (1,)))

    row_copies = []
    for k in range(half):
        row_grad[k] = row_of(half + k).astype(BF16)
        row_copies.append(go(row_grad.at[k], near.at[k], "head", 1))

    gathers = ((slice_in, gather_in, True), (slice_weight, gather_weight, True), (slice_out, gather_out, False))
    for own, gather, _ in gathers:
        gather[y, x, c] = own[...]

    def spread_first(gather, along_x):
        part = gather.at[y, x, c]
        return go(part, part, "dp", 2 if along_x else 4)

    def spread_second(gather, along_x):
        part = gather.at[y, :, c] if along_x else gather.at[:, x, c]
        return go(part, part, "dp", 4 if along_x else 2)

    def spread_third(gather):
        part = gather.at[:, :, c]
        return go(part, part, "dp", 1)

    core_copies = []
    for k, part, core in ((1, part_b, core_b), (0, part_a, core_a)):
        product = dot(first_cols[...], grads[k].reshape(2 * own_rows, 3 * LANES)).astype(BF16)
        for j in range(8):
            part[j // 4, (j // 2) % 2, j % 2] = product[j * rows : (j + 1) * rows]
        core_copies.append(go(part.at[:, :, 1 - c], core, "dp", 1))
    spreads = [spread_first(gather, along_x) for _, gather, along_x in gathers]
    for k in range(half):
        kept[k] = row_of(k)

    core_copies[0].wait_recv()
    core_b[...] = added(part_b[:, :, c], core_b[...])
    one_copy_b = go(core_b.at[1 - y], one_b, "dp", 4)
    core_copies[1].wait_recv()
    core_a[...] = added(part_a[:, :, c], core_a[...])
    one_copy_a = go(core_a.at[:, 1 - x], one_a, "dp", 2)

    bias_a = jnp.sum(grads[0].reshape(2 * own_rows, 3 * LANES).astype(F32), axis=0, keepdims=True)
    bias_b = jnp.sum(grads[1].reshape(2 * own_rows, 3 * LANES).astype(F32), axis=0, keepdims=True)
    edge = jnp.zeros((8, model - BASIS), F32)
    fill = jnp.zeros((6, model), F32)
    for k, bias in ((0, bias_a), (1, bias_b)):
        block[k, 0:8] = jnp.concatenate([probe_grad[k], edge], axis=1)
        block[k, 8:16] = jnp.concatenate([bias, in_bias_part[2 * k : 2 * k + 1], fill], axis=0)
        bias_block[k] = jnp.concatenate([in_bias_part[2 * k + 1 : 2 * k + 2], jnp.zeros((7, model), F32)], axis=0)
    block_copy = go(block.at[1], block_in, "head", 2)
    bias_copies = [go(bias_block.at[0], bias_in.at[0], "head", 1), go(bias_block.at[1], bias_in.at[1], "head", 3)]

    value = source[...].astype(F32)
    centred = value - jnp.mean(value, axis=-1, keepdims=True)
    factor = lax.rsqrt(jnp.mean(centred * centred, axis=-1, keepdims=True) + EPSILON)
    normal = centred * factor

    one_copy_b.wait_recv()
    one_b[...] = added(core_b[y], one_b[...])
    two_copy_b = go(one_b.at[1 - x], two_b, "dp", 2)
    one_copy_a.wait_recv()
    one_a[...] = added(core_a[:, x], one_a[...])
    two_copy_a = go(one_a.at[1 - y], two_a, "dp", 4)
    for copy in row_copies:
        copy.wait_recv()
    two_copy_b.wait_recv()
    two_b[...] = added(one_b[x], two_b[...])
    far_copy = go(two_b, far_b, "head", 2)

    grad = kept[...].reshape(own_rows, model) + near[...].reshape(own_rows, model).astype(F32)
    scaled = grad * scales[0:1]
    change = factor * (
        scaled
        - jnp.mean(scaled, axis=-1, keepdims=True)
        - normal * jnp.mean(scaled * normal, axis=-1, keepdims=True)
    )
    input_grad[...] = (grad_residual[...] + change).astype(BF16)
    shared[...] = jnp.concatenate(
        [jnp.sum(grad * normal, axis=0, keepdims=True), jnp.sum(grad, axis=0, keepdims=True), sums[0:6]], axis=0
    )
    shared_copies = [go(shared, shared_in.at[r - 1], "head", r) for r in (1, 2, 3)]
    spreads = [copy.wait_recv() or spread_second(gather, along_x) for copy, (_, gather, along_x) in zip(spreads, gathers)]

    two_copy_a.wait_recv()
    own_sum = added(one_a[y], two_a[...]).astype(F32)
    far_copy.wait_recv()
    total[0] = (own_sum + far_b[...].astype(F32)).astype(BF16)
    for n, bit in enumerate(outer):
        copy = go(total.at[n], outer_in.at[n], "dp", bit)
        copy.wait_recv()
        total[n + 1] = added(total[n], outer_in[n])
    gather_qkv[y, x, c] = total[len(outer)]
    qkv_copy = spread_first(gather_qkv, True)

    block_copy.wait_recv()
    for copy in bias_copies + shared_copies:
        copy.wait_recv()
    owned = block[0] + block_in[...]
    bias_rows = bias_in[0] + bias_in[1]
    owned_rows = jnp.concatenate([owned[8:9], owned[9:10] + bias_rows[0:1], owned[10:16]], axis=0)
    joined[0] = jnp.concatenate(
        [shared[...] + shared_in[0] + shared_in[1] + shared_in[2], owned[0:8], owned_rows], axis=0
    )
    spreads = [copy.wait_recv() or spread_third(gather) for copy, (_, gather, _) in zip(spreads, gathers)]
    for n, bit in enumerate((2, 4, 1) + outer):
        copy = go(joined.at[n], joined_in.at[n], "dp", bit)
        if n == 1:
            qkv_copy.wait_recv()
            qkv_copy = spread_second(gather_qkv, True)
        copy.wait_recv()
        joined[n + 1] = joined[n] + joined_in[n]
    last = joined[3 + len(outer)]
    shared_out[...] = last[0:8]
    owned_out[...] = last[8:24]
    for copy, (_, gather, _), out in zip(spreads, gathers, (whole_in, whole_weight, whole_out)):
        copy.wait_recv()
        out[...] = gather[...]
    qkv_copy.wait_recv()
    spread_third(gather_qkv).wait_recv()
    whole_qkv[...] = gather_qkv[...]
    for copy in started:
        copy.wait_send()


def tail(grads, first_cols, flat_a, flat_b, grad_residual, source, scales, slices, sums, in_bias_part, probe_grad, outer, heads):
    own_rows, model = source.shape
    units = grads.shape[1]
    rows = model // 8
    vmem = pl.BlockSpec(memory_space=pltpu.VMEM)
    shape = jax.ShapeDtypeStruct
    slice_in, slice_out, slice_weight = slices
    plane = lambda part: (2, 2, 2) + part
    part = (rows, 3 * LANES)
    hops = units // 2 + 9 + 2 + 2 + 2 + 1 + 3 + 1 + 2 + 3 + 3 + 2 * len(outer)
    return pl.pallas_call(
        functools.partial(tail_kernel, heads, outer),
        in_specs=[vmem] * 13,
        out_specs=[vmem] * 7,
        out_shape=[
            shape(source.shape, BF16), shape(plane(slice_in.shape), BF16), shape(plane(slice_out.shape), BF16),
            shape(plane(slice_weight.shape), BF16), shape(plane(part), BF16), shape((8, model), F32),
            shape((16, model), F32),
        ],
        scratch_shapes=[
            pltpu.VMEM((units // 2, UNIT, model), BF16),
            pltpu.VMEM((units // 2, UNIT, model), BF16),
            pltpu.VMEM((units // 2, UNIT, model), F32),
            pltpu.VMEM(plane(part), BF16),
            pltpu.VMEM(plane(part), BF16),
            pltpu.VMEM((2, 2) + part, BF16),
            pltpu.VMEM((2, 2) + part, BF16),
            pltpu.VMEM((2,) + part, BF16),
            pltpu.VMEM((2,) + part, BF16),
            pltpu.VMEM(part, BF16),
            pltpu.VMEM(part, BF16),
            pltpu.VMEM(part, BF16),
            pltpu.VMEM((1 + len(outer),) + part, BF16),
            pltpu.VMEM((max(1, len(outer)),) + part, BF16),
            pltpu.VMEM(plane(slice_in.shape), BF16),
            pltpu.VMEM(plane(slice_out.shape), BF16),
            pltpu.VMEM(plane(slice_weight.shape), BF16),
            pltpu.VMEM(plane(part), BF16),
            pltpu.VMEM((8, model), F32),
            pltpu.VMEM((3, 8, model), F32),
            pltpu.VMEM((2, 16, model), F32),
            pltpu.VMEM((16, model), F32),
            pltpu.VMEM((2, 8, model), F32),
            pltpu.VMEM((2, 8, model), F32),
            pltpu.VMEM((4 + len(outer), 24, model), F32),
            pltpu.VMEM((3 + len(outer), 24, model), F32),
            pltpu.SemaphoreType.DMA((hops,)),
            pltpu.SemaphoreType.DMA((hops,)),
        ],
        compiler_params=pltpu.CompilerParams(
            collective_id=3, has_side_effects=True, vmem_limit_bytes=60 << 20
        ),
        name="tail",
    )(
        grads, first_cols, flat_a, flat_b, grad_residual, source, scales, slice_in, slice_out, slice_weight, sums,
        in_bias_part, probe_grad,
    )


def exchange(value, axis, bit):
    size = lax.axis_size(axis)
    return lax.ppermute(value, axis, [(j, j ^ bit) for j in range(size)])


def local(
    inputs, seg_lengths, ln1_gain, ln1_bias, qkv_weight, qkv_bias, out_weight, out_bias, mem_mu, mem_sig,
    ln2_gain, ln2_bias, ff_in, ff_in_bias, ff_out, ff_out_bias, cotangent,
):
    own_rows, model = inputs.shape
    shards = lax.axis_size("head")
    members = lax.axis_size("dp")
    width = qkv_weight.shape[2]
    heads = width // HEAD_DIM
    hidden_part = ff_in.shape[1]
    units = 2 * own_rows // UNIT
    slots = seg_lengths.shape[1] // 2
    z = lax.axis_index("head")
    run = z // 2
    slices = 8
    outer = tuple(1 << k for k in range(3, 16) if 1 << k < members)
    place = (lax.axis_index("dp") % slices).reshape(1).astype(jnp.int32)
    rows = model // slices
    narrow = width // slices

    info = segment_info(lax.dynamic_slice_in_dim(seg_lengths[0], run * slots, slots, 0), units, z % 2, run)
    scales = jnp.concatenate([ln1_gain[None], ln1_bias[None], jnp.zeros((6, model), BF16)], axis=0).astype(F32)
    bias_row = jnp.pad(qkv_bias, ((0, 0), (0, LANES - width))).reshape(1, 3 * LANES)
    probe_rows = jnp.pad(jnp.concatenate([mem_mu, mem_sig], axis=0), ((0, 15 - 2 * heads), (0, 3 * LANES - BASIS)))
    small = jnp.concatenate([bias_row, probe_rows], axis=0).astype(F32)
    bias_in = jnp.broadcast_to(ff_in_bias[None].astype(F32), (8, hidden_part))
    out_slices = jnp.pad(out_weight.reshape(slices, narrow, model), ((0, 0), (0, -narrow % 16), (0, 0)))
    (
        qkv, first_cols, flat_a, flat_b, logsum, values, probes, key_states, key_end, state_rows,
        *mixed, in_bias, far_in, far_out, far_weight,
    ) = forward(info, inputs, scales, qkv_weight.reshape(model, 3 * width), small, bias_in, ff_in, ff_out, out_slices, heads)
    flat = lambda array: array.reshape((shards - 1, slices) + array.shape[4:])
    vectors = jnp.concatenate(
        [out_bias[None], ln2_gain[None], ln2_bias[None], ff_out_bias[None], jnp.zeros((4, model), BF16)], axis=0
    ).astype(F32)
    outputs, grad_residual, *rest = middle(
        place, inputs, cotangent, mixed, out_weight, flat(far_weight), vectors, in_bias,
        ff_in.reshape(slices, rows, hidden_part), ff_out.reshape(slices, rows, model), flat(far_in), flat(far_out),
    )
    grad_mixed, (ff_in_part, ff_out_part, out_weight_part, sums, in_bias_part) = rest[:4], rest[4:]
    paired = [part.reshape(units // 2, UNIT, width) for part in grad_mixed]
    plane = lambda array: array.reshape((shards, 2, 2, 2) + array.shape[2:])
    grads, probe_grad, *parts = backward(
        info, qkv, paired, logsum, values, probes, key_states, key_end, state_rows, plane(ff_in_part),
        plane(ff_out_part), plane(out_weight_part), heads,
    )
    for bit in outer:
        parts = [added(part, exchange(part, "dp", bit)) for part in parts]
    input_grad, whole_in, whole_out, whole_weight, whole_qkv, shared, owned = tail(
        grads, first_cols, flat_a, flat_b, grad_residual, inputs, scales, parts, sums, in_bias_part, probe_grad,
        outer, heads,
    )
    qkv_weight_sum = whole_qkv.reshape(model, 3, LANES)[:, :, :width].astype(F32)
    out_weight_sum = whole_weight.reshape(slices, -1, model)[:, :narrow].reshape(width, model).astype(F32)
    return (
        outputs, input_grad, shared[0], shared[1], qkv_weight_sum, owned[8].reshape(3, LANES)[:, :width],
        out_weight_sum, shared[2], owned[:heads, :BASIS], owned[heads : 2 * heads, :BASIS], shared[3], shared[4],
        whole_in.reshape(model, hidden_part).astype(F32), owned[9, :hidden_part],
        whole_out.reshape(hidden_part, model).astype(F32), shared[5],
    )


def solution(mesh):
    rows, whole = P(("dp", "head"), None), P()
    return jax.shard_map(
        local,
        mesh=mesh,
        in_specs=(
            rows, P("dp", None), whole, whole, P(None, None, "head"), P(None, "head"), P("head", None), whole,
            P("head", None), P("head", None), whole, whole, P(None, "head"), P("head"), P("head", None), whole, rows,
        ),
        out_specs=(
            rows, rows, whole, whole, P(None, None, "head"), P(None, "head"), P("head", None), whole,
            P("head", None), P("head", None), whole, whole, P(None, "head"), P("head"), P("head", None), whole,
        ),
        check_vma=False,
    )
```

```python
import functools
import math

import jax
import jax.numpy as jnp
import ml_dtypes
import numpy as np
from jax import lax
from jax.experimental import pallas as pl
from jax.experimental.pallas import tpu as pltpu
from jax.sharding import PartitionSpec as P

HEAD_DIM = 64
BASIS = 512
UNIT = 256
LANES = 256
TAU = 0.75
RIDGE = 0.5
EPSILON = 1e-05
MESH = pl.DeviceIdType.MESH
SPREAD = 1.0 / 64.0
WIDTH = 1.0 / BASIS
LIVE = BASIS // 2
HIGHEST = lax.Precision.HIGHEST
F32 = jnp.float32
BF16 = jnp.bfloat16


def split_table(table):
    high = table.astype(np.float32).astype(ml_dtypes.bfloat16)
    low = (table.astype(np.float32) - high.astype(np.float32)).astype(ml_dtypes.bfloat16)
    return high, low


@functools.lru_cache(maxsize=None)
def basis_tables():
    centres = np.arange(BASIS) / (BASIS - 1)
    apart = centres[:, None] - centres[None, :]
    gram = np.exp(-apart * apart / (4.0 * WIDTH * WIDTH)) + RIDGE * np.eye(BASIS)
    solve = np.linalg.inv(gram)
    samples = (np.arange(BASIS) + 0.5) / BASIS
    near_gap = TAU * samples[:, None] - centres[None, :]
    far_gap = samples[:, None] - centres[None, :]
    near = np.exp(-near_gap * near_gap / (2.0 * WIDTH * WIDTH))
    far = np.exp(-far_gap * far_gap / (2.0 * WIDTH * WIDTH))
    contract = (near.T @ far) * (TAU / (BASIS * WIDTH * math.sqrt(math.pi)))
    joined = np.concatenate([solve @ contract, solve[:, LIVE:]], axis=1)
    high, low = split_table(joined)
    forward = np.concatenate([high, high, low], axis=1)
    backward = np.concatenate([high.T, high.T, low.T], axis=1)
    return forward, backward


def term_scale(units):
    return (1.0 - TAU) / (WIDTH * math.sqrt(math.pi) * UNIT) / units.astype(F32)


def split3(value):
    high = value.astype(BF16)
    low = (value - high.astype(F32)).astype(BF16)
    return jnp.concatenate([high, low, high], axis=0)


def dot(a, b, contract=((1,), (0,)), precision=None):
    return lax.dot_general(a, b, (contract, ((), ())), precision=precision, preferred_element_type=F32)


def head_rows(heads, width):
    row = lax.broadcasted_iota(jnp.int32, (8, width), 0)
    lane = lax.broadcasted_iota(jnp.int32, (8, width), 1) // HEAD_DIM
    return ((row == lane) | (row == lane + heads)) & (lane < heads)


def read_parts(logits, heads):
    location = 1.0 / (1.0 + jnp.exp(-logits))
    variance = (jnp.maximum(logits, 0.0) + jnp.log1p(jnp.exp(-jnp.abs(logits)))) * SPREAD + WIDTH * WIDTH
    return location[:heads], variance[heads : 2 * heads]


def place_of(index, length):
    return TAU + (1.0 - TAU) * (index.astype(F32) + 0.5) / (length.astype(F32) * UNIT)


def split_rows(value):
    high = value.astype(BF16)
    rest = value - high.astype(F32)
    mid = rest.astype(BF16)
    return high, mid, (rest - mid.astype(F32)).astype(BF16)


def three_pass(left, right_high, right_low, contract=((1,), (0,))):
    high = left.astype(BF16)
    low = (left - high.astype(F32)).astype(BF16)
    return dot(high, right_high, contract) + dot(low, right_high, contract) + dot(high, right_low, contract)


def advance_values(table, value):
    joined = BASIS + LIVE if table.shape[0] == BASIS else BASIS
    high, low = table[:BASIS, :BASIS], table[:BASIS, 2 * joined : 2 * joined + BASIS]
    value_high = value.astype(BF16)
    value_low = (value - value_high.astype(F32)).astype(BF16)
    return dot(high, value_high) + dot(high, value_low) + dot(low, value_high)


def segments_of(lengths, run, units):
    sizes = [lengths[0, run * units + s] // UNIT for s in range(units)]
    ends, total = [], 0
    for size in sizes:
        total = total + size
        ends.append(total)
    starts, spans, orders = [], [], []
    for b in range(units):
        start, span, order = 0, 0, 0
        for size, end in zip(sizes, ends):
            inside = (end > b) & (end - size <= b)
            start = start + jnp.where(inside, end - size, 0)
            span = span + jnp.where(inside, size, 0)
            order = order + jnp.where((end <= b) & (size > 0), 1, 0)
        starts.append(start)
        spans.append(span)
        orders.append(order)
    return starts, spans, orders


def other_of(index, distance):
    bit = 1
    while bit <= distance:
        if distance & bit:
            index = index + bit - 2 * bit * ((index // bit) % 2)
        bit *= 2
    return index


class Hops:
    def __init__(self, send, recv):
        self.send, self.recv, self.used = send, recv, 0

    def start(self, source, target, axis, bit):
        copy = pltpu.make_async_remote_copy(
            src_ref=source,
            dst_ref=target,
            send_sem=self.send.at[self.used],
            recv_sem=self.recv.at[self.used],
            device_id={axis: other_of(lax.axis_index(axis), bit)},
            device_id_type=MESH,
        )
        self.used += 1
        copy.start()
        return copy


def greet(neighbours):
    barrier = pltpu.get_barrier_semaphore()
    for axis, bit in neighbours:
        pl.semaphore_signal(
            barrier, inc=1, device_id={axis: other_of(lax.axis_index(axis), bit)}, device_id_type=MESH
        )
    pl.semaphore_wait(barrier, len(neighbours))


def set_out(pairs, sems, first):
    copies = [pltpu.make_async_copy(a, b, sems.at[first + k]) for k, (a, b) in enumerate(pairs)]
    for copy in copies:
        copy.start()
    return copies


def forward_kernel(
    heads, seg_lengths, source, packed, weight, out_weight, table, ff_in, ff_out,
    qkv_out, first_cols_out, flat_a_out, flat_b_out, logsum, values, probes, key_states, key_end, rows,
    mixed_0, mixed_1, mixed_2, mixed_3, in_bias, far_in, far_out, far_weight,
    qkv, first_rows, first_cols, flats, near, far, far_flat, small, far_row, bias_row, weight_mine, memory, sums, value_states, carried, value_ends, value_ins,
    projs, proj_ins, cols, discrete, mixed, mixed_in, send, recv, local_sems,
):
    own_rows, model = source.shape
    width = heads * HEAD_DIM
    units = qkv.shape[1]
    half = units // 2
    root = 1.0 / math.sqrt(HEAD_DIM)
    z = lax.axis_index("head")
    flip, run = (z % 2) * half, z // 2
    place = lax.axis_index("dp") % 8
    y, x, c = place // 4, (place // 2) % 2, place % 2
    slice_rows = model // 8
    at = lambda b: (b + flip) % units
    starts, lengths, orders = segments_of(seg_lengths, run, units)
    greet((("head", 1), ("head", 2), ("head", 3), ("dp", 1), ("dp", 2), ("dp", 4)))
    hops = Hops(send, recv)
    started = []

    def go(*args):
        started.append(hops.start(*args))
        return started[-1]

    part_rows, part_cols = far.shape[3:]
    mine = weight.at[
        pl.ds(pl.multiple_of((2 * y + x) * part_rows, 16), part_rows),
        pl.ds(pl.multiple_of(c * part_cols, 128), part_cols),
    ]
    small[...] = packed[0:16]
    bias_row[...] = jnp.broadcast_to(packed[22:23], bias_row.shape)
    narrow = width // 8
    chosen = jnp.zeros((narrow, model), F32)
    for j in range(8):
        chosen += jnp.where(place == j, out_weight[j * narrow : (j + 1) * narrow].astype(F32), 0.0)
    spare = jnp.zeros((weight_mine.shape[0] - narrow, model), F32)
    weight_mine[...] = jnp.concatenate([chosen, spare], axis=0).astype(BF16)
    slice_copy = go(mine, far.at[y, x, c], "head", 2)
    small_copy = go(small, far_row, "head", 2)
    row_copies = []
    for k in range(half):
        part = slice(k * UNIT, (k + 1) * UNIT)
        value = source[part].astype(F32)
        centred = value - jnp.mean(value, axis=-1, keepdims=True)
        factor = lax.rsqrt(jnp.mean(centred * centred, axis=-1, keepdims=True) + EPSILON)
        first_rows[part] = (centred * factor * packed[16:17] + packed[17:18]).astype(BF16)
        row_copies.append(go(first_rows.at[part], near.at[part], "head", 1))
    in_mine = ff_in.at[pl.ds(pl.multiple_of(place * slice_rows, 16), slice_rows)]
    out_mine = ff_out.at[pl.ds(pl.multiple_of(place * slice_rows, 16), slice_rows)]
    gathers = ((far_in, 2, 4), (far_weight, 2, 4), (far_out, 4, 2))
    stage = {}
    for r in (1, 2, 3):
        stage[r] = [
            go(in_mine, far_in.at[r - 1, y, x, c], "head", r),
            go(weight_mine, far_weight.at[r - 1, y, x, c], "head", r),
            go(out_mine, far_out.at[r - 1, y, x, c], "head", r),
        ]
    in_bias[0] = bias_row[...]
    bias_copies = [go(bias_row, in_bias.at[r], "head", r) for r in (1, 2, 3)]

    slice_copy.wait_recv()
    x_copy = go(far.at[y, x, c], far.at[y, x, c], "dp", 2)

    def widen(k, read):
        for i in range(3):
            flats[k, i * LANES : i * LANES + width] = read(slice(i * width, (i + 1) * width))
            flats[k, i * LANES + width : (i + 1) * LANES] = jnp.zeros((LANES - width, model), BF16)

    def project(k, unit, shift):
        span = slice(unit * UNIT, (unit + 1) * UNIT)
        qkv[k, unit] = (dot(first_rows[span], flats[k], ((1,), (1,))) + shift).astype(BF16)

    widen(0, lambda span: weight[span])
    for unit in range(half):
        project(0, unit, small[0:1])
    x_copy.wait_recv()
    y_copy = go(far.at[y, :, c], far.at[y, :, c], "dp", 4)
    first_cols[:, :own_rows] = first_rows[:own_rows].astype(F32).T.astype(BF16)
    y_copy.wait_recv()
    core_copy = go(far.at[:, :, c], far.at[:, :, c], "dp", 1)
    small_copy.wait_recv()
    for k, copy in enumerate(row_copies):
        copy.wait_recv()
        part = slice(k * UNIT, (k + 1) * UNIT)
        first_rows[own_rows + k * UNIT : own_rows + (k + 1) * UNIT] = near[part]
        project(0, half + k, small[0:1])

    def advance(r, step):
        for copy in stage[r]:
            copy.wait_recv()
        stage[r] = []
        for array, first, second in gathers:
            block = array.at[r - 1]
            if step == 1:
                part, bit = block.at[y, x, c], first
            elif step == 2:
                part, bit = (block.at[y, :, c] if first == 2 else block.at[:, x, c]), second
            else:
                part, bit = block.at[:, :, c], 1
            stage[r].append(go(part, part, "dp", bit))

    first_cols[:, own_rows:] = near[...].astype(F32).T.astype(BF16)
    core_copy.wait_recv()
    for i in range(8):
        row, col = (i // 2) * part_rows, (i % 2) * part_cols
        far_flat[row : row + part_rows, col : col + part_cols] = far[i // 4, (i // 2) % 2, i % 2]
    widen(1, lambda span: far_flat[span])
    for unit in range(units):
        project(1, unit, far_row[0:1])
    saved = set_out(
        [(qkv, qkv_out), (first_cols, first_cols_out), (flats.at[0], flat_a_out), (flats.at[1], flat_b_out)],
        local_sems, 0,
    )

    def probe_of(k):
        return jnp.where(k == 0, small[1:9, :BASIS], far_row[1:9, :BASIS])

    mask = head_rows(heads, LANES)

    def first_state(k, carry):
        memory[k] = jnp.zeros(memory.shape[1:], F32)
        row = probe_of(k)
        rows[k, 0:8] = row
        wide = 2 * (BASIS + LIVE)
        for i in range(1, 4):
            row = three_pass(row, table[:, :BASIS], table[:, wide : wide + BASIS])
            rows[k, 8 * i : 8 * i + 8] = row
        return carry

    lax.fori_loop(0, 2, first_state, 0)

    def state(b, k, carry):
        start, length = starts[b], lengths[b]
        now = memory[k]
        value_states[k, b] = now[:, LANES:]
        key_states[k, b] = now[:, :LANES].astype(BF16)
        if b > 0:
            probes[k, b] = jnp.where(mask, dot(rows[k, 0:8], now[:, :LANES], precision=HIGHEST), 0.0)
        else:
            probes[k, b] = jnp.zeros((8, LANES), F32)
        token = lax.broadcasted_iota(jnp.int32, (LIVE, UNIT), 1) + (b - start) * UNIT
        centre = (lax.broadcasted_iota(jnp.int32, (LIVE, UNIT), 0) + LIVE).astype(F32) / (BASIS - 1)
        gap = place_of(token, length) - centre
        psi = jnp.exp(gap * gap * (-0.5 / (WIDTH * WIDTH)))
        psi_high = psi.astype(BF16)
        psi_low = (psi - psi_high.astype(F32)).astype(BF16)
        pairs = qkv[k, at(b), :, LANES : 3 * LANES]
        fresh = dot(psi_high, pairs) + dot(psi_low, pairs)
        gathered = fresh if b == 0 else jnp.where(start == b, 0.0, sums[k]) + fresh
        sums[k] = gathered
        stacked = jnp.concatenate([now, gathered * term_scale(length)], axis=0)
        later = dot(table[...], split3(stacked))
        memory[k] = jnp.where(start + length == b + 1, later, now)
        return carry

    def end_state(k, carry):
        key = memory[k, :, :LANES]
        key_end[k] = key
        value_ends[k] = memory[k, :, LANES : LANES + width].astype(BF16)
        seen = dot(rows[k], key, precision=HIGHEST)
        for i in range(4):
            projs[k, 8 * i : 8 * i + 8] = jnp.where(mask, seen[8 * i : 8 * i + 8], 0.0)
        return carry

    def attend(b, k, carry):
        cols[k, b] = qkv[k, at(b), :, 2 * LANES : 3 * LANES].astype(F32).T.astype(BF16)
        query = qkv[k, at(b), :, 0:LANES].astype(F32) * root
        lane_head = lax.broadcasted_iota(jnp.int32, (UNIT, LANES), 1) // HEAD_DIM
        causal = lax.broadcasted_iota(jnp.int32, (UNIT, UNIT), 0) <= lax.broadcasted_iota(
            jnp.int32, (UNIT, UNIT), 1
        )
        away = [jnp.where(starts[b] <= j, 0.0, 1e30) for j in range(b)] + [0.0]
        for h in range(heads):
            own = jnp.where(lane_head == h, query, 0.0).astype(BF16)
            scores = [dot(qkv[k, at(j), :, LANES : 2 * LANES], own, ((1,), (1,))) for j in range(b + 1)]
            scores[b] = jnp.where(causal, scores[b], -1e30)
            highest = functools.reduce(
                jnp.maximum, [jnp.max(s, axis=0, keepdims=True) - away[j] for j, s in enumerate(scores)]
            )
            weights = [jnp.exp(s - (highest + away[j])) for j, s in enumerate(scores)]
            total = sum(jnp.sum(w, axis=0, keepdims=True) for w in weights)
            span = slice(h * HEAD_DIM, (h + 1) * HEAD_DIM)
            part = sum(dot(cols[k, j, span], weights[j].astype(BF16)) for j in range(b + 1))
            discrete[k, b, span] = part * (1.0 / total)
            logsum[k, b, h : h + 1] = highest + jnp.log(total)
        return carry

    def seen_value(k, carry):
        incoming = jnp.where(run > 0, value_ins[k].astype(F32), 0.0)
        carried[:, :width] = incoming
        carried[:, width:] = jnp.zeros((BASIS, LANES - width), F32)
        for b in range(units):
            if b > 0:
                carried[...] = jnp.where(starts[b] == b, advance_values(table, carried[...]), carried[...])
            values[k, b] = (value_states[k, b] + carried[...]).astype(BF16)
            gained = jnp.zeros((8, LANES), F32)
            for i in range(4):
                gained += jnp.where((orders[b] == i) & (run > 0), proj_ins[k, 8 * i : 8 * i + 8], 0.0)
            probes[k, b] = (probes[k, b] + gained) * root
        return carry

    def read(rel, k, carry):
        b = at(rel)
        query = qkv[k, rel, :, 0:LANES]
        logits = sum(dot(part, query, ((1,), (1,))) for part in split_rows(probes[k, b]))
        location, variance = read_parts(logits, heads)
        fall = -0.5 / variance
        peak = WIDTH * lax.rsqrt(variance)
        centres = lax.broadcasted_iota(jnp.int32, (BASIS, UNIT), 0).astype(F32) / (BASIS - 1)
        value_cols = values[k, b].astype(F32).T.astype(BF16)
        parts = []
        for h in range(heads):
            gap = centres - location[h : h + 1]
            density = jnp.exp(gap * gap * fall[h : h + 1]).astype(BF16)
            span = slice(h * HEAD_DIM, (h + 1) * HEAD_DIM)
            parts.append(discrete[k, b, span] + dot(value_cols[span], density) * peak[h : h + 1])
        mixed[k, rel] = jnp.concatenate(parts, axis=0).T.astype(BF16)
        return carry

    advance(1, 1)
    state_copies = []
    for k in range(2):
        for b in range(units):
            state(b, k, 0)
        end_state(k, 0)
        state_copies.append([
            go(value_ends.at[k], value_ins.at[1 - k], "head", 2), go(projs.at[k], proj_ins.at[1 - k], "head", 2)
        ])
        if k == 0:
            advance(2, 1)
            advance(1, 2)
    advance(3, 1)
    for b in range(units):
        lax.fori_loop(0, 2, functools.partial(attend, b), 0)
        if b == 0:
            advance(2, 2)
        if b == 2:
            advance(1, 3)
            advance(3, 2)
    mixed_copies = [None, None]
    for k in (1, 0):
        for copy in state_copies[1 - k]:
            copy.wait_recv()
        seen_value(k, 0)
        for rel in (2, 3, 0, 1):
            read(rel, k, 0)
            if rel == 3:
                mixed_copies[k] = go(mixed.at[k, half:], mixed_in.at[k], "head", 1)
        if k == 1:
            advance(2, 3)
    advance(3, 3)
    mixed_0[...] = mixed[0, :half].reshape(own_rows, width)
    mixed_2[...] = mixed[1, :half].reshape(own_rows, width)
    for copy in mixed_copies:
        copy.wait_recv()
    mixed_1[...] = mixed_in[0].reshape(own_rows, width)
    mixed_3[...] = mixed_in[1].reshape(own_rows, width)
    for copy in bias_copies + stage[1] + stage[2] + stage[3]:
        copy.wait_recv()
    for copy in started:
        copy.wait_send()
    for copy in saved:
        copy.wait()


def forward(seg_lengths, source, packed, weight, out_weight, ff_in, ff_out, heads):
    own_rows, model = source.shape
    units = 2 * own_rows // UNIT
    width = heads * HEAD_DIM
    hidden_part = ff_in.shape[1]
    rows = model // 8
    spaced = -(-width // 8 // 16) * 16
    table = jnp.asarray(basis_tables()[0])
    vmem, anywhere = pl.BlockSpec(memory_space=pltpu.VMEM), pl.BlockSpec(memory_space=pl.ANY)
    shape = jax.ShapeDtypeStruct
    hops = 2 + units // 2 + 3 + 3 * 3 * 4 + 3 + 4 + 2
    return pl.pallas_call(
        functools.partial(forward_kernel, heads),
        in_specs=[pl.BlockSpec(memory_space=pltpu.SMEM)] + [vmem] * 5 + [anywhere] * 2,
        out_specs=[anywhere] * 4 + [vmem] * 11 + [anywhere] * 3,
        out_shape=[
            shape((2, units, UNIT, 3 * LANES), BF16),
            shape((model, 2 * own_rows), BF16),
            shape((3 * LANES, model), BF16),
            shape((3 * LANES, model), BF16),
            shape((2, units, 8, UNIT), F32),
            shape((2, units, BASIS, LANES), BF16),
            shape((2, units, 8, LANES), F32),
            shape((2, units, BASIS, LANES), BF16),
            shape((2, BASIS, LANES), F32),
            shape((2, 32, BASIS), F32),
        ] + [shape((own_rows, width), BF16)] * 4 + [
            shape((4, 8, hidden_part), F32),
            shape((3, 2, 2, 2, rows, hidden_part), BF16),
            shape((3, 2, 2, 2, rows, model), BF16),
            shape((3, 2, 2, 2, spaced, model), BF16),
        ],
        scratch_shapes=[
            pltpu.VMEM((2, units, UNIT, 3 * LANES), BF16),
            pltpu.VMEM((2 * own_rows, model), BF16),
            pltpu.VMEM((model, 2 * own_rows), BF16),
            pltpu.VMEM((2, 3 * LANES, model), BF16),
            pltpu.VMEM((own_rows, model), BF16),
            pltpu.VMEM((2, 2, 2, 3 * width // 4, model // 2), BF16),
            pltpu.VMEM((3 * width, model), BF16),
            pltpu.VMEM((16, 3 * LANES), F32),
            pltpu.VMEM((16, 3 * LANES), F32),
            pltpu.VMEM((8, hidden_part), F32),
            pltpu.VMEM((spaced, model), BF16),
            pltpu.VMEM((2, BASIS, 2 * LANES), F32),
            pltpu.VMEM((2, LIVE, 2 * LANES), F32),
            pltpu.VMEM((2, units, BASIS, LANES), F32),
            pltpu.VMEM((BASIS, LANES), F32),
            pltpu.VMEM((2, BASIS, width), BF16),
            pltpu.VMEM((2, BASIS, width), BF16),
            pltpu.VMEM((2, 32, LANES), F32),
            pltpu.VMEM((2, 32, LANES), F32),
            pltpu.VMEM((2, units, LANES, UNIT), BF16),
            pltpu.VMEM((2, units, width, UNIT), F32),
            pltpu.VMEM((2, units, UNIT, width), BF16),
            pltpu.VMEM((2, units // 2, UNIT, width), BF16),
            pltpu.SemaphoreType.DMA((hops,)),
            pltpu.SemaphoreType.DMA((hops,)),
            pltpu.SemaphoreType.DMA((4,)),
        ],
        compiler_params=pltpu.CompilerParams(
            collective_id=1, has_side_effects=True, vmem_limit_bytes=60 << 20
        ),
        name="forward",
    )(seg_lengths, source, packed, weight, out_weight, table, ff_in, ff_out)


def whole(shape):
    return pl.BlockSpec(shape, lambda i: (0,) * len(shape))


def finish_kernel(given_in, given_out, given_weight, given_qkv, grad_in, grad_out, grad_weight, grad_qkv):
    step = pl.program_id(0)
    grad_in[...] = given_in[...].astype(F32)
    grad_out[...] = given_out[...].astype(F32)
    width = grad_qkv.shape[1]
    turned = given_qkv[...].astype(F32).T
    for i in range(3):

        @pl.when(step == i)
        def _():
            grad_qkv[0] = turned[i * width : (i + 1) * width]

    @pl.when(step == 0)
    def _():
        narrow = grad_weight.shape[0] // given_weight.shape[0]
        for j in range(given_weight.shape[0]):
            grad_weight[j * narrow : (j + 1) * narrow] = given_weight[j].astype(F32)[:narrow]


def finish(given_in, given_out, given_weight, given_qkv, width):
    model, columns = given_in.shape
    hidden_part = given_out.shape[0]
    return pl.pallas_call(
        finish_kernel,
        grid=(3,),
        in_specs=[
            pl.BlockSpec((model // 3, columns), lambda i: (i, 0)),
            pl.BlockSpec((hidden_part // 3, model), lambda i: (i, 0)),
            pl.BlockSpec(given_weight.shape, lambda i: (0, 0, 0)),
            pl.BlockSpec(given_qkv.shape, lambda i: (0, 0)),
        ],
        out_specs=[
            pl.BlockSpec((model // 3, columns), lambda i: (i, 0)),
            pl.BlockSpec((hidden_part // 3, model), lambda i: (i, 0)),
            pl.BlockSpec((width, model), lambda i: (0, 0)),
            pl.BlockSpec((1, width, model), lambda i: (i, 0, 0)),
        ],
        out_shape=[
            jax.ShapeDtypeStruct((model, columns), F32), jax.ShapeDtypeStruct((hidden_part, model), F32),
            jax.ShapeDtypeStruct((width, model), F32), jax.ShapeDtypeStruct((3, width, model), F32),
        ],
        compiler_params=pltpu.CompilerParams(vmem_limit_bytes=48 << 20),
        name="finish",
    )(given_in, given_out, given_weight, given_qkv)


def middle_kernel(
    source, cotangent, mixed_0, mixed_1, mixed_2, mixed_3, own_weight, far_weight, vectors, in_bias, own_in, own_out,
    far_in, far_out, outputs, grad_residual, grad_mixed_0, grad_mixed_1, grad_mixed_2, grad_mixed_3, grad_in, grad_out,
    grad_out_weight, sums, grad_in_bias,
    residual, inverse, second, second_cols, total, grad_second, in_now, out_now, out_weight,
):
    r = pl.program_id(0)
    slices, rows = own_in.shape[0], own_in.shape[1]
    model = source.shape[1]
    hidden_part = own_in.shape[2]
    out_bias, gain, shift, last_bias = (vectors[k : k + 1] for k in range(18, 22))

    @pl.when(r == 0)
    def _():
        value = source[...].astype(F32) + out_bias
        out_weight[0] = own_weight[...]
        narrow = own_weight.shape[0] // slices
        for k in range(far_weight.shape[0]):
            parts = [far_weight[k, j].astype(F32)[:narrow] for j in range(slices)]
            out_weight[k + 1] = jnp.concatenate(parts, axis=0).astype(BF16)
        for k, mixed in enumerate((mixed_0, mixed_1, mixed_2, mixed_3)):
            value += dot(mixed[...], out_weight[k])
        residual[...] = value
        centred = value - jnp.mean(value, axis=-1, keepdims=True)
        factor = lax.rsqrt(jnp.mean(centred * centred, axis=-1, keepdims=True) + EPSILON)
        inverse[...] = factor
        normal = centred * factor
        grad_residual[...] = normal
        rounded = (normal * gain + shift).astype(BF16)
        second[...] = rounded
        second_cols[...] = rounded.astype(F32).T.astype(BF16)
        total[...] = jnp.zeros_like(total)
        grad_second[...] = jnp.zeros_like(grad_second)
        grad_in_bias[...] = jnp.zeros_like(grad_in_bias)
        for j in range(slices):
            in_now[j * rows : (j + 1) * rows] = own_in[j]
            out_now[j * rows : (j + 1) * rows] = own_out[j]

    @pl.when(r > 0)
    def _():
        for j in range(slices):
            in_now[j * rows : (j + 1) * rows] = far_in[0, j]
            out_now[j * rows : (j + 1) * rows] = far_out[0, j]

    half = hidden_part // 2
    for t in range(2):
        span = slice(t * half, (t + 1) * half)
        hidden = dot(second[...], in_now[:, span]) + in_bias[r, 0:1, span]
        cube = hidden * hidden
        root = math.sqrt(2.0 / math.pi)
        bent = jnp.tanh(hidden * (root + (root * 0.044715) * cube))
        lifted = 0.5 + 0.5 * bent
        activation = (hidden * lifted).astype(BF16)
        slope = lifted + hidden * ((0.5 - 0.5 * bent * bent) * (root + (3.0 * root * 0.044715) * cube))
        total[...] += dot(activation, out_now[span])
        given = dot(cotangent[...], out_now[span], ((1,), (1,)))
        grad_hidden = (given * slope).astype(BF16)
        grad_second[...] += dot(grad_hidden, in_now[:, span], ((1,), (1,)))
        grad_in_bias[pl.ds(r, 1), span] = jnp.sum(grad_hidden.astype(F32), axis=0, keepdims=True)
        part = dot(activation, cotangent[...], ((0,), (0,))).astype(BF16)
        per = half // rows
        for k in range(per):
            grad_out[0, t * per + k] = part[k * rows : (k + 1) * rows]
        part = dot(second_cols[...], grad_hidden).astype(BF16)
        for j in range(slices):
            grad_in[0, j, :, span] = part[j * rows : (j + 1) * rows]

    @pl.when(r == pl.num_programs(0) - 1)
    def _():
        given = cotangent[...].astype(F32)
        outputs[...] = (residual[...] + total[...] + last_bias).astype(BF16)
        normal = grad_residual[...]
        grad = grad_second[...]
        scaled = grad * gain
        value = given + inverse[...] * (
            scaled
            - jnp.mean(scaled, axis=-1, keepdims=True)
            - normal * jnp.mean(scaled * normal, axis=-1, keepdims=True)
        )
        sums[0:1] = jnp.sum(value, axis=0, keepdims=True)
        sums[1:2] = jnp.sum(grad * normal, axis=0, keepdims=True)
        sums[2:3] = jnp.sum(grad, axis=0, keepdims=True)
        sums[3:4] = jnp.sum(given, axis=0, keepdims=True)
        sums[4:8] = jnp.zeros((4, model), F32)
        grad_residual[...] = value
        rounded = value.astype(BF16)
        grads = (grad_mixed_0, grad_mixed_1, grad_mixed_2, grad_mixed_3)
        for k, mixed in enumerate((mixed_0, mixed_1, mixed_2, mixed_3)):
            grads[k][...] = dot(rounded, out_weight[k], ((1,), (1,))).astype(BF16)
            product = dot(mixed[...], rounded, ((0,), (0,)))
            narrow = product.shape[0] // slices
            spare = jnp.zeros((grad_out_weight.shape[2] - narrow, model), F32)
            for j in range(slices):
                part = jnp.concatenate([product[j * narrow : (j + 1) * narrow], spare], axis=0)
                grad_out_weight[k, j] = part.astype(BF16)


def middle(source, cotangent, mixed, out_weight, far_weight, vectors, in_bias, own_in, own_out, far_in, far_out):
    own_rows, model = source.shape
    shards = far_in.shape[0] + 1
    slices, rows, hidden_part = own_in.shape
    narrow = mixed[0].shape
    far = pl.BlockSpec((1,) + own_in.shape, lambda r: (jnp.maximum(r - 1, 0), 0, 0, 0))
    part = pl.BlockSpec((1,) + own_in.shape, lambda r: (r, 0, 0, 0))
    macs = own_rows * model * (6 * shards * hidden_part + 3 * model)
    return pl.pallas_call(
        middle_kernel,
        grid_spec=pltpu.PrefetchScalarGridSpec(
            num_scalar_prefetch=0,
            grid=(shards,),
            in_specs=[whole(source.shape)] * 2 + [whole(narrow)] * 4 + [
                whole(out_weight.shape), whole(far_weight.shape), whole(vectors.shape), whole(in_bias.shape), whole(own_in.shape),
                whole(own_out.shape), far, far,
            ],
            out_specs=[whole(source.shape)] * 2 + [whole(narrow)] * 4 + [
                part, part, whole((shards,) + far_weight.shape[1:]), whole((8, model)), whole((shards, hidden_part))
            ],
            scratch_shapes=[
                pltpu.VMEM((own_rows, model), F32),
                pltpu.VMEM((own_rows, 1), F32),
                pltpu.VMEM((own_rows, model), BF16),
                pltpu.VMEM((model, own_rows), BF16),
                pltpu.VMEM((own_rows, model), F32),
                pltpu.VMEM((own_rows, model), F32),
                pltpu.VMEM((model, hidden_part), BF16),
                pltpu.VMEM((hidden_part, model), BF16),
                pltpu.VMEM((shards,) + narrow[1:] + (model,), BF16),
            ],
        ),
        out_shape=[
            jax.ShapeDtypeStruct(source.shape, BF16),
            jax.ShapeDtypeStruct(source.shape, F32),
        ] + [jax.ShapeDtypeStruct(narrow, BF16)] * 4 + [
            jax.ShapeDtypeStruct((shards, slices, rows, hidden_part), BF16),
            jax.ShapeDtypeStruct((shards, slices, rows, hidden_part), BF16),
            jax.ShapeDtypeStruct((shards,) + far_weight.shape[1:], BF16),
            jax.ShapeDtypeStruct((8, model), F32),
            jax.ShapeDtypeStruct((shards, hidden_part), F32),
        ],
        compiler_params=pltpu.CompilerParams(vmem_limit_bytes=60 << 20),
        cost_estimate=pl.CostEstimate(
            flops=2 * macs, bytes_accessed=30 << 20, transcendentals=own_rows * shards * hidden_part
        ),
        name="middle",
    )(source, cotangent, *mixed, out_weight, far_weight, vectors, in_bias, own_in, own_out, far_in, far_out)


def added(a, b):
    return (a.astype(F32) + b.astype(F32)).astype(BF16)


def backward_kernel(
    heads, seg_lengths, qkv, gm_0, gm_1, gm_2, gm_3, logsum, values, probes, key_states, key_end, rows, table,
    grad_in, grad_out, grad_weight, out, probe_grad, slice_in, slice_out, slice_weight,
    given, query_grad, memory_grad, row_grad, value_carried, value_back, value_in, row_back, row_in, carried, spread, key_grad, value_grad, cols,
    keep_in, keep_out, keep_weight, core_in, core_out, core_weight, one_in, one_out, one_weight,
    two_in, two_out, two_weight, z_in, z_out, z_weight, send, recv, local_sems,
):
    units = qkv.shape[1]
    half = units // 2
    width = heads * HEAD_DIM
    root = 1.0 / math.sqrt(HEAD_DIM)
    z = lax.axis_index("head")
    flip, run = (z % 2) * half, z // 2
    place = lax.axis_index("dp") % 8
    y, x, c = place // 4, (place // 2) % 2, place % 2
    at = lambda b: (b + flip) % units
    starts, lengths, orders = segments_of(seg_lengths, run, units)
    greet((("head", 1), ("head", 2), ("head", 3), ("dp", 1), ("dp", 2), ("dp", 4)))
    hops = Hops(send, recv)
    started = []

    def go(*args):
        started.append(hops.start(*args))
        return started[-1]

    given_copies = [go(gm_1, given.at[0, half:], "head", 1), go(gm_3, given.at[1, half:], "head", 1)]
    sums = (
        (grad_in, keep_in, core_in, one_in, two_in, z_in, True),
        (grad_weight, keep_weight, core_weight, one_weight, two_weight, z_weight, True),
        (grad_out, keep_out, core_out, one_out, two_out, z_out, False),
    )
    stage, local_copies = {}, {}
    for i, r in enumerate((2, 1, 3, 0)):
        stage[r], local_copies[r] = [], []
        for n, (term, keep, core, _, _, _, _) in enumerate(sums):
            stage[r].append(go(term.at[r, :, :, 1 - c], core.at[r], "dp", 1))
            copy = pltpu.make_async_copy(term.at[r, :, :, c], keep.at[r], local_sems.at[3 * i + n])
            copy.start()
            local_copies[r].append(copy)

    def first_hop(r):
        for n, (_, keep, core, one, _, _, along_x) in enumerate(sums):
            local_copies[r][n].wait()
            stage[r][n].wait_recv()
            keep[r] = added(keep[r], core[r])
            part = keep.at[r, :, 1 - x] if along_x else keep.at[r, 1 - y]
            stage[r][n] = go(part, one.at[r], "dp", 2 if along_x else 4)

    def second_hop(r):
        for n, (_, keep, _, one, two, _, along_x) in enumerate(sums):
            stage[r][n].wait_recv()
            kept = keep[r, :, x] if along_x else keep[r, y]
            one[r] = added(kept, one[r])
            part = one.at[r, 1 - y] if along_x else one.at[r, 1 - x]
            stage[r][n] = go(part, two.at[r], "dp", 4 if along_x else 2)

    def third_hop(r):
        for n, (_, _, _, one, two, far, along_x) in enumerate(sums):
            stage[r][n].wait_recv()
            kept = one[r, y] if along_x else one[r, x]
            two[r] = added(kept, two[r])
            if r:
                stage[r][n] = go(two.at[r], far.at[r - 1], "head", r)

    for k, own in enumerate((gm_0, gm_2)):
        given[k, :half] = own[...]
    mask = head_rows(heads, LANES)
    lane_head = lax.broadcasted_iota(jnp.int32, (UNIT, LANES), 1) // HEAD_DIM

    def given_of(k, b):
        return jnp.concatenate([given[k, at(b)], jnp.zeros((UNIT, LANES - width), BF16)], axis=1).astype(F32)

    def read_back(rel, k, carry):
        b = at(rel)
        query = qkv[k, rel, :, 0:LANES]
        full = given_of(k, b)
        probe = probes[k, b]
        logits = sum(dot(part, query, ((1,), (1,))) for part in split_rows(probe))
        location, variance = read_parts(logits, heads)
        inverse = 1.0 / variance
        fall = -0.5 * inverse
        peak = WIDTH * lax.rsqrt(variance)
        centres = lax.broadcasted_iota(jnp.int32, (BASIS, UNIT), 0).astype(F32) / (BASIS - 1)
        along, across = [], []
        total = jnp.zeros((BASIS, LANES), F32)
        for h in range(heads):
            own_given = jnp.where(lane_head == h, full, 0.0).astype(BF16)
            gap = centres - location[h : h + 1]
            square = gap * gap
            density = jnp.exp(square * fall[h : h + 1]) * peak[h : h + 1]
            grad_density = dot(values[k, b], own_given, ((1,), (1,)))
            total += dot(density.astype(BF16), own_given)
            weighed = density * grad_density
            moment = weighed * gap
            zeroth = jnp.sum(weighed, axis=0, keepdims=True)
            first = jnp.sum(moment, axis=0, keepdims=True)
            second = jnp.sum(moment * gap, axis=0, keepdims=True)
            along.append(first * inverse[h : h + 1])
            across.append(0.5 * inverse[h : h + 1] * (second * inverse[h : h + 1] - zeroth))
        sigmoid = 1.0 / (1.0 + jnp.exp(-logits))
        grad_location = jnp.concatenate(along, axis=0) * location * (1.0 - location)
        grad_variance = jnp.concatenate(across, axis=0) * SPREAD * sigmoid[heads : 2 * heads]
        grad_logits = jnp.concatenate(
            [grad_location, grad_variance, jnp.zeros((8 - 2 * heads, UNIT), F32)], axis=0
        )
        padded = jnp.concatenate([grad_logits, jnp.zeros((120, UNIT), F32)], axis=0)
        probe_cols = jnp.concatenate([probe, jnp.zeros((120, LANES), F32)], axis=0).T
        query_grad[k, b] = dot(probe_cols, padded, precision=HIGHEST)[:width]
        fresh = jnp.where(mask, dot(grad_logits, query.astype(F32), precision=HIGHEST), 0.0) * root
        memory_grad[k, b] = total
        row_grad[k, b] = fresh
        return carry

    def gather_back(k, carry):
        probe = jnp.zeros((8, BASIS), F32)
        for i in range(4):
            row_back[k, 8 * i : 8 * i + 8] = jnp.zeros((8, LANES), F32)
        for b in range(units - 1, -1, -1):
            fresh, total = row_grad[k, b], memory_grad[k, b]
            probe += dot(fresh, key_states[k, b].astype(F32), ((1,), (1,)), HIGHEST)
            for i in range(4):
                row_back[k, 8 * i : 8 * i + 8] += jnp.where(orders[b] == i, fresh, 0.0)
            if b < units - 1:
                ends = starts[b] + lengths[b] == b + 1
                total = jnp.where(ends, 0.0, memory_grad[k, b + 1]) + total
                memory_grad[k, b] = total
                row_grad[k, b] = jnp.where(ends, 0.0, row_grad[k, b + 1]) + fresh
            before = jnp.zeros((BASIS, LANES), F32) if b == units - 1 else value_carried[k]
            if b > 0:
                value_carried[k] = jnp.where(starts[b] == b, advance_values(table, before + total), before)
            else:
                value_back[k] = (before + total)[:, :width].astype(BF16)
        probe_grad[k] = probe
        return carry

    def attend_back(b, k, carry):
        query = qkv[k, at(b), :, 0:LANES].astype(F32) * root
        full = given_of(k, b)
        causal = lax.broadcasted_iota(jnp.int32, (UNIT, UNIT), 0) <= lax.broadcasted_iota(
            jnp.int32, (UNIT, UNIT), 1
        )
        away = [jnp.where(starts[b] <= j, 0.0, 1e30) for j in range(b)] + [0.0]
        owns = [jnp.where(lane_head == h, query, 0.0).astype(BF16) for h in range(heads)]
        own_givens = [jnp.where(lane_head == h, full, 0.0).astype(BF16) for h in range(heads)]
        grads, probs = [], []
        for h in range(heads):
            prob_h, product_h = [], []
            inner = jnp.zeros((1, UNIT), F32)
            for j in range(b + 1):
                score = dot(qkv[k, at(j), :, LANES : 2 * LANES], owns[h], ((1,), (1,)))
                if j == b:
                    score = jnp.where(causal, score, -1e30)
                prob = jnp.exp(score - (logsum[k, b, h : h + 1] + away[j]))
                product = prob * dot(qkv[k, at(j), :, 2 * LANES : 3 * LANES], own_givens[h], ((1,), (1,)))
                inner += jnp.sum(product, axis=0, keepdims=True)
                prob_h.append(prob)
                product_h.append(product)
            span = slice(h * HEAD_DIM, (h + 1) * HEAD_DIM)
            grad_h = [(product_h[j] - prob_h[j] * inner).astype(BF16) for j in range(b + 1)]
            result = sum(dot(cols[k, j, span], grad_h[j]) for j in range(b + 1))
            query_grad[k, b, span] = query_grad[k, b, span] + result * root
            grads.append(grad_h)
            probs.append([prob.astype(BF16) for prob in prob_h])
        own_all = jnp.concatenate(owns, axis=0)
        given_all = jnp.concatenate(own_givens, axis=0)
        for j in range(b + 1):
            keys = dot(jnp.concatenate([grads[h][j] for h in range(heads)], axis=1), own_all)
            vals = dot(jnp.concatenate([probs[h][j] for h in range(heads)], axis=1), given_all)
            if b == units - 1:
                key_grad[k, j], value_grad[k, j] = keys, vals
            else:
                key_grad[k, j] += keys
                value_grad[k, j] += vals
        return carry

    def carry_back(k, total, units_before):
        moved = dot(table[...], split3(total))
        return moved[:BASIS], (moved[BASIS:] * term_scale(units_before)).astype(BF16)

    def end_back(k, carry):
        row = jnp.where(run == 0, row_in[k], 0.0)
        value = jnp.where(run == 0, value_in[k].astype(F32), 0.0)
        grad_keys = dot(rows[k], row, ((0,), (0,)), HIGHEST)
        total = jnp.concatenate([grad_keys, value, jnp.zeros((BASIS, LANES - width), F32)], axis=1)
        carried[k], spread[k] = carry_back(k, total, lengths[units - 1])
        seen = dot(row, key_end[k], ((1,), (1,)), HIGHEST)
        gained = seen[24:32]
        for i in (2, 1, 0):
            gained = three_pass(gained, table[:BASIS, :BASIS], table[:BASIS, 2 * BASIS : 3 * BASIS])
            gained = gained + seen[8 * i : 8 * i + 8]
        probe_grad[k] += gained
        return carry

    def finish(b, k, carry):
        start, length = starts[b], lengths[b]
        token = lax.broadcasted_iota(jnp.int32, (UNIT, LIVE), 0) + (b - start) * UNIT
        centre = (lax.broadcasted_iota(jnp.int32, (UNIT, LIVE), 1) + LIVE).astype(F32) / (BASIS - 1)
        gap = place_of(token, length) - centre
        psi = jnp.exp(gap * gap * (-0.5 / (WIDTH * WIDTH))).astype(BF16)
        pair_grad = dot(psi, spread[k])
        query_rows = query_grad[k, b].T.astype(BF16)
        out[k, at(b), :, :LANES] = jnp.concatenate([query_rows, jnp.zeros((UNIT, LANES - width), BF16)], axis=1)
        out[k, at(b), :, LANES : 2 * LANES] = (key_grad[k, b] + pair_grad[:, :LANES]).astype(BF16)
        out[k, at(b), :, 2 * LANES :] = (value_grad[k, b] + pair_grad[:, LANES:]).astype(BF16)
        if b > 0:
            grad_keys = dot(rows[k, 0:8], row_grad[k, b], ((0,), (0,)), HIGHEST)
            total = carried[k] + jnp.concatenate([grad_keys, memory_grad[k, b]], axis=1)
            moved, spread_now = carry_back(k, total, lengths[b - 1])
            carried[k] = jnp.where(start == b, moved, carried[k])
            spread[k] = jnp.where(start == b, spread_now.astype(F32), spread[k].astype(F32)).astype(BF16)
        return carry

    def both(step, *args):
        lax.fori_loop(0, 2, functools.partial(step, *args), 0)

    def turn(k, carry):
        for b in range(units):
            cols[k, b] = qkv[k, at(b), :, LANES : 2 * LANES].astype(F32).T.astype(BF16)
        return carry

    lax.fori_loop(0, 2, turn, 0)
    both(read_back, 0)
    first_hop(2)
    both(read_back, 1)
    first_hop(1)
    for copy in given_copies:
        copy.wait_recv()
    both(read_back, 2)
    first_hop(3)
    first_hop(0)
    both(read_back, 3)
    second_hop(2)
    back_copies = []
    for k in range(2):
        gather_back(k, 0)
        back_copies += [
            go(value_back.at[k], value_in.at[1 - k], "head", 2), go(row_back.at[k], row_in.at[1 - k], "head", 2)
        ]
    second_hop(1)
    both(attend_back, 3)
    second_hop(3)
    second_hop(0)
    third_hop(2)
    both(attend_back, 2)
    third_hop(1)
    third_hop(3)
    both(attend_back, 1)
    third_hop(0)
    both(attend_back, 0)
    for copy in back_copies:
        copy.wait_recv()
    lax.fori_loop(0, 2, end_back, 0)
    for b in range(units - 1, -1, -1):
        both(finish, b)
    for n, (_, _, _, _, two, far, _) in enumerate(sums):
        total = two[0].astype(F32)
        for r in (1, 2, 3):
            stage[r][n].wait_recv()
            total += far[r - 1].astype(F32)
        (slice_in, slice_weight, slice_out)[n][...] = total.astype(BF16)
    for copy in started:
        copy.wait_send()


def backward(seg_lengths, qkv, grad_mixed, logsum, values, probes, key_states, key_end, rows, grad_in, grad_out, grad_weight, heads):
    units = qkv.shape[1]
    width = heads * HEAD_DIM
    table = jnp.asarray(basis_tables()[1])
    vmem, anywhere = pl.BlockSpec(memory_space=pltpu.VMEM), pl.BlockSpec(memory_space=pl.ANY)
    shape = jax.ShapeDtypeStruct
    slices = [grad_in.shape[4:], grad_out.shape[4:], grad_weight.shape[4:]]
    hops = 2 + 3 * 4 * 3 + 3 * 3 + 4
    return pl.pallas_call(
        functools.partial(backward_kernel, heads),
        in_specs=[pl.BlockSpec(memory_space=pltpu.SMEM)] + [vmem] * 12 + [anywhere] * 3,
        out_specs=[vmem] * 5,
        out_shape=[shape(qkv.shape, BF16), shape((2, 8, BASIS), F32)] + [shape(part, BF16) for part in slices],
        scratch_shapes=[
            pltpu.VMEM((2, units, UNIT, width), BF16),
            pltpu.VMEM((2, units, width, UNIT), F32),
            pltpu.VMEM((2, units, BASIS, LANES), F32),
            pltpu.VMEM((2, units, 8, LANES), F32),
            pltpu.VMEM((2, BASIS, LANES), F32),
            pltpu.VMEM((2, BASIS, width), BF16),
            pltpu.VMEM((2, BASIS, width), BF16),
            pltpu.VMEM((2, 32, LANES), F32),
            pltpu.VMEM((2, 32, LANES), F32),
            pltpu.VMEM((2, BASIS, 2 * LANES), F32),
            pltpu.VMEM((2, LIVE, 2 * LANES), BF16),
            pltpu.VMEM((2, units, UNIT, LANES), F32),
            pltpu.VMEM((2, units, UNIT, LANES), F32),
            pltpu.VMEM((2, units, LANES, UNIT), BF16),
        ]
        + [pltpu.VMEM((4, 2, 2) + part, BF16) for part in slices]
        + [pltpu.VMEM((4, 2, 2) + part, BF16) for part in slices]
        + [pltpu.VMEM((4, 2) + part, BF16) for part in slices]
        + [pltpu.VMEM((4,) + part, BF16) for part in slices]
        + [pltpu.VMEM((3,) + part, BF16) for part in slices]
        + [
            pltpu.SemaphoreType.DMA((hops,)),
            pltpu.SemaphoreType.DMA((hops,)),
            pltpu.SemaphoreType.DMA((12,)),
        ],
        compiler_params=pltpu.CompilerParams(
            collective_id=2, has_side_effects=True, vmem_limit_bytes=62 << 20
        ),
        name="backward",
    )(
        seg_lengths, qkv, *grad_mixed, logsum, values, probes, key_states, key_end, rows, table, grad_in, grad_out, grad_weight
    )


def tail_kernel(
    heads, outer, grads, first_cols, flat_a, flat_b, grad_residual, source, packed, slice_in, slice_out, slice_weight,
    sums, in_bias_part, probe_grad, input_grad, whole_in, whole_out, whole_weight, whole_qkv, shared_out, owned_out,
    row_grad, near, kept, part_a, part_b, core_a, core_b, one_a, one_b, two_a, two_b, far_b, total, outer_in,
    gather_in, gather_out, gather_weight, gather_qkv,
    shared, shared_in, block, block_in, bias_block, bias_in, joined, joined_in, send, recv,
):
    own_rows, model = source.shape
    units = grads.shape[1]
    half = units // 2
    width = heads * HEAD_DIM
    z = lax.axis_index("head")
    place = lax.axis_index("dp") % 8
    y, x, c = place // 4, (place // 2) % 2, place % 2
    rows = model // 8
    greet(
        (("head", 1), ("head", 2), ("head", 3), ("dp", 1), ("dp", 2), ("dp", 4)) + tuple(("dp", bit) for bit in outer)
    )
    hops = Hops(send, recv)
    started = []

    def go(*args):
        started.append(hops.start(*args))
        return started[-1]

    def row_of(rel):
        return dot(grads[0, rel], flat_a[...]) + dot(grads[1, rel], flat_b[...])

    row_copies = []
    for k in range(half):
        row_grad[k] = row_of(half + k).astype(BF16)
        row_copies.append(go(row_grad.at[k], near.at[k], "head", 1))

    gathers = ((slice_in, gather_in, True), (slice_weight, gather_weight, True), (slice_out, gather_out, False))
    for own, gather, _ in gathers:
        gather[y, x, c] = own[...]

    def spread_first(gather, along_x):
        part = gather.at[y, x, c]
        return go(part, part, "dp", 2 if along_x else 4)

    def spread_second(gather, along_x):
        part = gather.at[y, :, c] if along_x else gather.at[:, x, c]
        return go(part, part, "dp", 4 if along_x else 2)

    def spread_third(gather):
        part = gather.at[:, :, c]
        return go(part, part, "dp", 1)

    core_copies = []
    for k, part, core in ((1, part_b, core_b), (0, part_a, core_a)):
        product = dot(first_cols[...], grads[k].reshape(2 * own_rows, 3 * LANES))
        product = jnp.concatenate([product[:, i * LANES : i * LANES + width] for i in range(3)], axis=1).astype(BF16)
        for j in range(8):
            part[j // 4, (j // 2) % 2, j % 2] = product[j * rows : (j + 1) * rows]
        core_copies.append(go(part.at[:, :, 1 - c], core, "dp", 1))
    spreads = [spread_first(gather, along_x) for _, gather, along_x in gathers]
    for k in range(half):
        kept[k] = row_of(k)

    core_copies[0].wait_recv()
    core_b[...] = added(part_b[:, :, c], core_b[...])
    one_copy_b = go(core_b.at[1 - y], one_b, "dp", 4)
    core_copies[1].wait_recv()
    core_a[...] = added(part_a[:, :, c], core_a[...])
    one_copy_a = go(core_a.at[:, 1 - x], one_a, "dp", 2)

    bias_a = jnp.sum(grads[0].reshape(2 * own_rows, 3 * LANES).astype(F32), axis=0, keepdims=True)
    bias_b = jnp.sum(grads[1].reshape(2 * own_rows, 3 * LANES).astype(F32), axis=0, keepdims=True)
    edge = jnp.zeros((8, model - BASIS), F32)
    fill = jnp.zeros((6, model), F32)
    for k, bias in ((0, bias_a), (1, bias_b)):
        block[k, 0:8] = jnp.concatenate([probe_grad[k], edge], axis=1)
        block[k, 8:16] = jnp.concatenate([bias, in_bias_part[2 * k : 2 * k + 1], fill], axis=0)
        bias_block[k] = jnp.concatenate([in_bias_part[2 * k + 1 : 2 * k + 2], jnp.zeros((7, model), F32)], axis=0)
    block_copy = go(block.at[1], block_in, "head", 2)
    bias_copies = [go(bias_block.at[0], bias_in.at[0], "head", 1), go(bias_block.at[1], bias_in.at[1], "head", 3)]

    value = source[...].astype(F32)
    centred = value - jnp.mean(value, axis=-1, keepdims=True)
    factor = lax.rsqrt(jnp.mean(centred * centred, axis=-1, keepdims=True) + EPSILON)
    normal = centred * factor

    one_copy_b.wait_recv()
    one_b[...] = added(core_b[y], one_b[...])
    two_copy_b = go(one_b.at[1 - x], two_b, "dp", 2)
    one_copy_a.wait_recv()
    one_a[...] = added(core_a[:, x], one_a[...])
    two_copy_a = go(one_a.at[1 - y], two_a, "dp", 4)
    for copy in row_copies:
        copy.wait_recv()
    two_copy_b.wait_recv()
    two_b[...] = added(one_b[x], two_b[...])
    far_copy = go(two_b, far_b, "head", 2)

    grad = kept[...].reshape(own_rows, model) + near[...].reshape(own_rows, model).astype(F32)
    scaled = grad * packed[16:17]
    change = factor * (
        scaled
        - jnp.mean(scaled, axis=-1, keepdims=True)
        - normal * jnp.mean(scaled * normal, axis=-1, keepdims=True)
    )
    input_grad[...] = (grad_residual[...] + change).astype(BF16)
    shared[...] = jnp.concatenate(
        [jnp.sum(grad * normal, axis=0, keepdims=True), jnp.sum(grad, axis=0, keepdims=True), sums[0:6]], axis=0
    )
    shared_copies = [go(shared, shared_in.at[r - 1], "head", r) for r in (1, 2, 3)]
    spreads = [copy.wait_recv() or spread_second(gather, along_x) for copy, (_, gather, along_x) in zip(spreads, gathers)]

    two_copy_a.wait_recv()
    own_sum = added(one_a[y], two_a[...]).astype(F32)
    far_copy.wait_recv()
    total[0] = (own_sum + far_b[...].astype(F32)).astype(BF16)
    for n, bit in enumerate(outer):
        copy = go(total.at[n], outer_in.at[n], "dp", bit)
        copy.wait_recv()
        total[n + 1] = added(total[n], outer_in[n])
    gather_qkv[y, x, c] = total[len(outer)]
    cut = rows // 2
    upper, lower = pl.ds(0, cut), pl.ds(cut, cut)
    qkv_parts = [gather_qkv.at[y, x, c, upper], gather_qkv.at[y, x, c, lower]]
    qkv_copies = [go(qkv_parts[0], qkv_parts[0], "dp", 2), go(qkv_parts[1], qkv_parts[1], "dp", 4)]

    block_copy.wait_recv()
    for copy in bias_copies + shared_copies:
        copy.wait_recv()
    owned = block[0] + block_in[...]
    bias_rows = bias_in[0] + bias_in[1]
    owned_rows = jnp.concatenate([owned[8:9], owned[9:10] + bias_rows[0:1], owned[10:16]], axis=0)
    joined[0] = jnp.concatenate(
        [shared[...] + shared_in[0] + shared_in[1] + shared_in[2], owned[0:8], owned_rows], axis=0
    )
    spreads = [copy.wait_recv() or spread_third(gather) for copy, (_, gather, _) in zip(spreads, gathers)]
    for n, bit in enumerate((2, 4, 1) + outer):
        copy = go(joined.at[n], joined_in.at[n], "dp", bit)
        if n == 1:
            for copy_one in qkv_copies:
                copy_one.wait_recv()
            qkv_parts = [gather_qkv.at[y, :, c, upper], gather_qkv.at[:, x, c, lower]]
            qkv_copies = [go(qkv_parts[0], qkv_parts[0], "dp", 4), go(qkv_parts[1], qkv_parts[1], "dp", 2)]
        copy.wait_recv()
        joined[n + 1] = joined[n] + joined_in[n]
    last = joined[3 + len(outer)]
    shared_out[...] = last[0:8]
    owned_out[...] = last[8:24]
    for copy, (_, gather, _), out in zip(spreads, gathers, (whole_in, whole_weight, whole_out)):
        copy.wait_recv()
        out[...] = gather[...]
    for copy in qkv_copies:
        copy.wait_recv()
    spread_third(gather_qkv).wait_recv()
    whole_qkv[...] = gather_qkv[...]
    for copy in started:
        copy.wait_send()


def tail(grads, first_cols, flat_a, flat_b, grad_residual, source, packed, slices, sums, in_bias_part, probe_grad, outer, heads):
    own_rows, model = source.shape
    units = grads.shape[1]
    rows = model // 8
    vmem = pl.BlockSpec(memory_space=pltpu.VMEM)
    shape = jax.ShapeDtypeStruct
    slice_in, slice_out, slice_weight = slices
    plane = lambda part: (2, 2, 2) + part
    part = (rows, 3 * heads * HEAD_DIM)
    hops = units // 2 + 9 + 2 + 2 + 2 + 1 + 5 + 1 + 2 + 3 + 3 + 2 * len(outer)
    return pl.pallas_call(
        functools.partial(tail_kernel, heads, outer),
        in_specs=[vmem] * 13,
        out_specs=[vmem] * 7,
        out_shape=[
            shape(source.shape, BF16), shape(plane(slice_in.shape), BF16), shape(plane(slice_out.shape), BF16),
            shape(plane(slice_weight.shape), BF16), shape(plane(part), BF16), shape((8, model), F32),
            shape((16, model), F32),
        ],
        scratch_shapes=[
            pltpu.VMEM((units // 2, UNIT, model), BF16),
            pltpu.VMEM((units // 2, UNIT, model), BF16),
            pltpu.VMEM((units // 2, UNIT, model), F32),
            pltpu.VMEM(plane(part), BF16),
            pltpu.VMEM(plane(part), BF16),
            pltpu.VMEM((2, 2) + part, BF16),
            pltpu.VMEM((2, 2) + part, BF16),
            pltpu.VMEM((2,) + part, BF16),
            pltpu.VMEM((2,) + part, BF16),
            pltpu.VMEM(part, BF16),
            pltpu.VMEM(part, BF16),
            pltpu.VMEM(part, BF16),
            pltpu.VMEM((1 + len(outer),) + part, BF16),
            pltpu.VMEM((max(1, len(outer)),) + part, BF16),
            pltpu.VMEM(plane(slice_in.shape), BF16),
            pltpu.VMEM(plane(slice_out.shape), BF16),
            pltpu.VMEM(plane(slice_weight.shape), BF16),
            pltpu.VMEM(plane(part), BF16),
            pltpu.VMEM((8, model), F32),
            pltpu.VMEM((3, 8, model), F32),
            pltpu.VMEM((2, 16, model), F32),
            pltpu.VMEM((16, model), F32),
            pltpu.VMEM((2, 8, model), F32),
            pltpu.VMEM((2, 8, model), F32),
            pltpu.VMEM((4 + len(outer), 24, model), F32),
            pltpu.VMEM((3 + len(outer), 24, model), F32),
            pltpu.SemaphoreType.DMA((hops,)),
            pltpu.SemaphoreType.DMA((hops,)),
        ],
        compiler_params=pltpu.CompilerParams(
            collective_id=3, has_side_effects=True, vmem_limit_bytes=60 << 20
        ),
        name="tail",
    )(
        grads, first_cols, flat_a, flat_b, grad_residual, source, packed, slice_in, slice_out, slice_weight, sums,
        in_bias_part, probe_grad,
    )


def exchange(value, axis, bit):
    size = lax.axis_size(axis)
    return lax.ppermute(value, axis, [(j, j ^ bit) for j in range(size)])


def local(
    inputs, seg_lengths, ln1_gain, ln1_bias, qkv_weight, qkv_bias, out_weight, out_bias, mem_mu, mem_sig,
    ln2_gain, ln2_bias, ff_in, ff_in_bias, ff_out, ff_out_bias, cotangent,
):
    own_rows, model = inputs.shape
    shards = lax.axis_size("head")
    members = lax.axis_size("dp")
    width = qkv_weight.shape[2]
    heads = width // HEAD_DIM
    hidden_part = ff_in.shape[1]
    units = 2 * own_rows // UNIT
    slices = 8
    outer = tuple(1 << k for k in range(3, 16) if 1 << k < members)
    rows = model // slices

    bias_row = jnp.pad(qkv_bias, ((0, 0), (0, LANES - width))).reshape(1, 3 * LANES)
    edge = 3 * LANES - BASIS
    packed = jnp.pad(bias_row, ((0, 23), (0, 0))).astype(F32)
    packed += jnp.pad(mem_mu, ((1, 23 - heads), (0, edge))).astype(F32)
    packed += jnp.pad(mem_sig, ((1 + heads, 23 - 2 * heads), (0, edge))).astype(F32)
    line = jnp.arange(24)[:, None]
    for k, vector in enumerate((ln1_gain, ln1_bias, out_bias, ln2_gain, ln2_bias, ff_out_bias, ff_in_bias)):
        packed += jnp.where(line == 16 + k, vector.astype(F32)[None, :], 0.0)

    turned_weight = jnp.transpose(qkv_weight, (1, 2, 0)).reshape(3 * width, model)
    (
        qkv, first_cols, flat_a, flat_b, logsum, values, probes, key_states, key_end, state_rows,
        *mixed, in_bias, far_in, far_out, far_weight,
    ) = forward(seg_lengths, inputs, packed, turned_weight, out_weight, ff_in, ff_out, heads)
    flat = lambda array: array.reshape((shards - 1, slices) + array.shape[4:])
    outputs, grad_residual, *rest = middle(
        inputs, cotangent, mixed, out_weight, flat(far_weight), packed, in_bias,
        ff_in.reshape(slices, rows, hidden_part), ff_out.reshape(slices, rows, model), flat(far_in), flat(far_out),
    )
    grad_mixed, (ff_in_part, ff_out_part, out_weight_part, sums, in_bias_part) = rest[:4], rest[4:]
    paired = [part.reshape(units // 2, UNIT, width) for part in grad_mixed]
    plane = lambda array: array.reshape((shards, 2, 2, 2) + array.shape[2:])
    grads, probe_grad, *parts = backward(
        seg_lengths, qkv, paired, logsum, values, probes, key_states, key_end, state_rows, plane(ff_in_part),
        plane(ff_out_part), plane(out_weight_part), heads,
    )
    for bit in outer:
        parts = [added(part, exchange(part, "dp", bit)) for part in parts]
    input_grad, whole_in, whole_out, whole_weight, whole_qkv, shared, owned = tail(
        grads, first_cols, flat_a, flat_b, grad_residual, inputs, packed, parts, sums, in_bias_part, probe_grad,
        outer, heads,
    )
    ff_in_sum, ff_out_sum, out_weight_sum, qkv_weight_sum = finish(
        whole_in.reshape(model, hidden_part), whole_out.reshape(hidden_part, model),
        whole_weight.reshape((slices,) + whole_weight.shape[3:]), whole_qkv.reshape(model, 3 * width), width,
    )
    return (
        outputs, input_grad, shared[0], shared[1], jnp.transpose(qkv_weight_sum, (2, 0, 1)),
        owned[8].reshape(3, LANES)[:, :width], out_weight_sum, shared[2], owned[:heads, :BASIS],
        owned[heads : 2 * heads, :BASIS], shared[3], shared[4], ff_in_sum, owned[9, :hidden_part], ff_out_sum, shared[5],
    )


def solution(mesh):
    rows, whole = P(("dp", "head"), None), P()
    return jax.shard_map(
        local,
        mesh=mesh,
        in_specs=(
            rows, P("dp", None), whole, whole, P(None, None, "head"), P(None, "head"), P("head", None), whole,
            P("head", None), P("head", None), whole, whole, P(None, "head"), P("head"), P("head", None), whole, rows,
        ),
        out_specs=(
            rows, rows, whole, whole, P(None, None, "head"), P(None, "head"), P("head", None), whole,
            P("head", None), P("head", None), whole, whole, P(None, "head"), P("head"), P("head", None), whole,
        ),
        check_vma=False,
    )
```

```python
import functools
import math

import jax
import jax.numpy as jnp
import ml_dtypes
import numpy as np
from jax import lax
from jax.experimental import pallas as pl
from jax.experimental.pallas import tpu as pltpu
from jax.sharding import PartitionSpec as P

HEAD_DIM = 64
BASIS = 512
UNIT = 256
LANES = 256
TAU = 0.75
RIDGE = 0.5
EPSILON = 1e-05
MESH = pl.DeviceIdType.MESH
SPREAD = 1.0 / 64.0
WIDTH = 1.0 / BASIS
LIVE = BASIS // 2
HIGHEST = lax.Precision.HIGHEST
F32 = jnp.float32
BF16 = jnp.bfloat16


def split_table(table):
    high = table.astype(np.float32).astype(ml_dtypes.bfloat16)
    low = (table.astype(np.float32) - high.astype(np.float32)).astype(ml_dtypes.bfloat16)
    return high, low


@functools.lru_cache(maxsize=None)
def basis_tables():
    centres = np.arange(BASIS) / (BASIS - 1)
    apart = centres[:, None] - centres[None, :]
    gram = np.exp(-apart * apart / (4.0 * WIDTH * WIDTH)) + RIDGE * np.eye(BASIS)
    solve = np.linalg.inv(gram)
    samples = (np.arange(BASIS) + 0.5) / BASIS
    near_gap = TAU * samples[:, None] - centres[None, :]
    far_gap = samples[:, None] - centres[None, :]
    near = np.exp(-near_gap * near_gap / (2.0 * WIDTH * WIDTH))
    far = np.exp(-far_gap * far_gap / (2.0 * WIDTH * WIDTH))
    contract = (near.T @ far) * (TAU / (BASIS * WIDTH * math.sqrt(math.pi)))
    joined = np.concatenate([solve @ contract, solve[:, LIVE:]], axis=1)
    high, low = split_table(joined)
    forward = np.concatenate([high, high, low], axis=1)
    backward = np.ascontiguousarray(high.T)
    return forward, backward


def term_scale(units):
    return (1.0 - TAU) / (WIDTH * math.sqrt(math.pi) * UNIT) / units.astype(F32)


def split3(value):
    high = value.astype(BF16)
    low = (value - high.astype(F32)).astype(BF16)
    return jnp.concatenate([high, low, high], axis=0)


def dot(a, b, contract=((1,), (0,)), precision=None):
    return lax.dot_general(a, b, (contract, ((), ())), precision=precision, preferred_element_type=F32)


def head_rows(heads, width):
    row = lax.broadcasted_iota(jnp.int32, (8, width), 0)
    lane = lax.broadcasted_iota(jnp.int32, (8, width), 1) // HEAD_DIM
    return ((row == lane) | (row == lane + heads)) & (lane < heads)


def read_parts(logits, heads):
    location = 1.0 / (1.0 + jnp.exp(-logits))
    variance = (jnp.maximum(logits, 0.0) + jnp.log1p(jnp.exp(-jnp.abs(logits)))) * SPREAD + WIDTH * WIDTH
    return location[:heads], variance[heads : 2 * heads]


def place_of(index, length):
    return TAU + (1.0 - TAU) * (index.astype(F32) + 0.5) / (length.astype(F32) * UNIT)


def split_rows(value):
    high = value.astype(BF16)
    rest = value - high.astype(F32)
    mid = rest.astype(BF16)
    return high, mid, (rest - mid.astype(F32)).astype(BF16)


def three_pass(left, right_high, right_low, contract=((1,), (0,))):
    high = left.astype(BF16)
    low = (left - high.astype(F32)).astype(BF16)
    return dot(high, right_high, contract) + dot(low, right_high, contract) + dot(high, right_low, contract)


def advance_values(table, value):
    return dot(table[:BASIS, :BASIS], value.astype(BF16))


def logits_of(probes, query):
    parts = dot(jnp.concatenate(split_rows(probes), axis=0), query, ((1,), (1,)))
    return parts[0:8] + parts[8:16] + parts[16:24]


def segments_of(lengths, run, units):
    sizes = [lengths[0, run * units + s] // UNIT for s in range(units)]
    ends, total = [], 0
    for size in sizes:
        total = total + size
        ends.append(total)
    starts, spans, orders = [], [], []
    for b in range(units):
        start, span, order = 0, 0, 0
        for size, end in zip(sizes, ends):
            inside = (end > b) & (end - size <= b)
            start = start + jnp.where(inside, end - size, 0)
            span = span + jnp.where(inside, size, 0)
            order = order + jnp.where((end <= b) & (size > 0), 1, 0)
        starts.append(start)
        spans.append(span)
        orders.append(order)
    return starts, spans, orders


def other_of(index, distance):
    bit = 1
    while bit <= distance:
        if distance & bit:
            index = index + bit - 2 * bit * ((index // bit) % 2)
        bit *= 2
    return index


class Hops:
    def __init__(self, send, recv):
        self.send, self.recv, self.used = send, recv, 0

    def start(self, source, target, axis, bit):
        copy = pltpu.make_async_remote_copy(
            src_ref=source,
            dst_ref=target,
            send_sem=self.send.at[self.used],
            recv_sem=self.recv.at[self.used],
            device_id={axis: other_of(lax.axis_index(axis), bit)},
            device_id_type=MESH,
        )
        self.used += 1
        copy.start()
        return copy


def greet(neighbours):
    barrier = pltpu.get_barrier_semaphore()
    for axis, bit in neighbours:
        pl.semaphore_signal(
            barrier, inc=1, device_id={axis: other_of(lax.axis_index(axis), bit)}, device_id_type=MESH
        )
    pl.semaphore_wait(barrier, len(neighbours))


def set_out(pairs, sems, first):
    copies = [pltpu.make_async_copy(a, b, sems.at[first + k]) for k, (a, b) in enumerate(pairs)]
    for copy in copies:
        copy.start()
    return copies


def forward_kernel(
    heads, seg_lengths, source, packed, weight, out_weight, table, ff_in, ff_out,
    qkv_out, first_cols_out, flat_a_out, flat_b_out, logsum, values, probes, key_states, key_end, rows,
    mixed_0, mixed_1, mixed_2, mixed_3, in_bias, far_in, far_out, far_weight,
    qkv, first_rows, first_cols, flats, near, far, far_flat, small, far_row, bias_row, weight_mine, memory, sums, value_states, carried, value_ends, value_ins,
    projs, proj_ins, cols, keys, discrete, mixed, mixed_in, send, recv, local_sems,
):
    own_rows, model = source.shape
    width = heads * HEAD_DIM
    units = qkv.shape[1]
    half = units // 2
    root = 1.0 / math.sqrt(HEAD_DIM)
    z = lax.axis_index("head")
    flip, run = (z % 2) * half, z // 2
    place = lax.axis_index("dp") % 8
    y, x, c = place // 4, (place // 2) % 2, place % 2
    slice_rows = model // 8
    at = lambda b: (b + flip) % units
    starts, lengths, orders = segments_of(seg_lengths, run, units)
    greet((("head", 1), ("head", 2), ("head", 3), ("dp", 1), ("dp", 2), ("dp", 4)))
    hops = Hops(send, recv)
    started = []

    def go(*args):
        started.append(hops.start(*args))
        return started[-1]

    part_rows, part_cols = far.shape[3:]
    mine = weight.at[
        pl.ds(pl.multiple_of((2 * y + x) * part_rows, 16), part_rows),
        pl.ds(pl.multiple_of(c * part_cols, 128), part_cols),
    ]
    small[...] = packed[0:16]
    bias_row[...] = jnp.broadcast_to(packed[22:23], bias_row.shape)
    narrow = width // 8
    chosen = jnp.zeros((narrow, model), F32)
    for j in range(8):
        chosen += jnp.where(place == j, out_weight[j * narrow : (j + 1) * narrow].astype(F32), 0.0)
    spare = jnp.zeros((weight_mine.shape[0] - narrow, model), F32)
    weight_mine[...] = jnp.concatenate([chosen, spare], axis=0).astype(BF16)
    slice_copy = go(mine, far.at[y, x, c], "head", 2)
    small_copy = go(small, far_row, "head", 2)
    row_copies = []
    for k in range(half):
        part = slice(k * UNIT, (k + 1) * UNIT)
        value = source[part].astype(F32)
        centred = value - jnp.mean(value, axis=-1, keepdims=True)
        factor = lax.rsqrt(jnp.mean(centred * centred, axis=-1, keepdims=True) + EPSILON)
        first_rows[part] = (centred * factor * packed[16:17] + packed[17:18]).astype(BF16)
        row_copies.append(go(first_rows.at[part], near.at[part], "head", 1))
    in_mine = ff_in.at[pl.ds(pl.multiple_of(place * slice_rows, 16), slice_rows)]
    out_mine = ff_out.at[pl.ds(pl.multiple_of(place * slice_rows, 16), slice_rows)]
    gathers = ((far_in, 2, 4), (far_weight, 2, 4), (far_out, 4, 2))
    stage = {}
    for r in (1, 2, 3):
        stage[r] = [
            go(in_mine, far_in.at[r - 1, y, x, c], "head", r),
            go(weight_mine, far_weight.at[r - 1, y, x, c], "head", r),
            go(out_mine, far_out.at[r - 1, y, x, c], "head", r),
        ]
    in_bias[0] = bias_row[...]
    bias_copies = [go(bias_row, in_bias.at[r], "head", r) for r in (1, 2, 3)]

    slice_copy.wait_recv()
    x_copy = go(far.at[y, x, c], far.at[y, x, c], "dp", 2)

    def widen(k, read):
        for i in range(3):
            flats[k, i * LANES : i * LANES + width] = read(slice(i * width, (i + 1) * width))
            flats[k, i * LANES + width : (i + 1) * LANES] = jnp.zeros((LANES - width, model), BF16)

    def project(k, unit, shift):
        span = slice(unit * UNIT, (unit + 1) * UNIT)
        qkv[k, unit] = (dot(first_rows[span], flats[k], ((1,), (1,))) + shift).astype(BF16)

    widen(0, lambda span: weight[span])
    for unit in range(half):
        project(0, unit, small[0:1])
    x_copy.wait_recv()
    y_copy = go(far.at[y, :, c], far.at[y, :, c], "dp", 4)
    first_cols[:, :own_rows] = first_rows[:own_rows].astype(F32).T.astype(BF16)
    y_copy.wait_recv()
    core_copy = go(far.at[:, :, c], far.at[:, :, c], "dp", 1)
    small_copy.wait_recv()
    for k, copy in enumerate(row_copies):
        copy.wait_recv()
        part = slice(k * UNIT, (k + 1) * UNIT)
        first_rows[own_rows + k * UNIT : own_rows + (k + 1) * UNIT] = near[part]
        project(0, half + k, small[0:1])

    def advance(r, step):
        for copy in stage[r]:
            copy.wait_recv()
        stage[r] = []
        for array, first, second in gathers:
            block = array.at[r - 1]
            if step == 1:
                part, bit = block.at[y, x, c], first
            elif step == 2:
                part, bit = (block.at[y, :, c] if first == 2 else block.at[:, x, c]), second
            else:
                part, bit = block.at[:, :, c], 1
            stage[r].append(go(part, part, "dp", bit))

    first_cols[:, own_rows:] = near[...].astype(F32).T.astype(BF16)
    core_copy.wait_recv()
    for i in range(8):
        row, col = (i // 2) * part_rows, (i % 2) * part_cols
        far_flat[row : row + part_rows, col : col + part_cols] = far[i // 4, (i // 2) % 2, i % 2]
    widen(1, lambda span: far_flat[span])
    for unit in range(units):
        project(1, unit, far_row[0:1])
    saved = set_out(
        [(qkv, qkv_out), (first_cols, first_cols_out), (flats.at[0], flat_a_out), (flats.at[1], flat_b_out)],
        local_sems, 0,
    )

    def probe_of(k):
        return jnp.where(k == 0, small[1:9, :BASIS], far_row[1:9, :BASIS])

    mask = head_rows(heads, LANES)

    def first_state(k, carry):
        memory[k] = jnp.zeros(memory.shape[1:], F32)
        row = probe_of(k)
        rows[k, 0:8] = row
        wide = 2 * (BASIS + LIVE)
        for i in range(1, 4):
            row = three_pass(row, table[:, :BASIS], table[:, wide : wide + BASIS])
            rows[k, 8 * i : 8 * i + 8] = row
        return carry

    lax.fori_loop(0, 2, first_state, 0)

    def state(b, k, carry):
        start, length = starts[b], lengths[b]
        now = memory[k]
        value_states[k, b] = now[:, LANES:]
        key_states[k, b] = now[:, :LANES].astype(BF16)
        if b > 0:
            probes[k, b] = jnp.where(mask, dot(rows[k, 0:8], now[:, :LANES], precision=HIGHEST), 0.0)
        else:
            probes[k, b] = jnp.zeros((8, LANES), F32)
        token = lax.broadcasted_iota(jnp.int32, (LIVE, UNIT), 1) + (b - start) * UNIT
        centre = (lax.broadcasted_iota(jnp.int32, (LIVE, UNIT), 0) + LIVE).astype(F32) / (BASIS - 1)
        gap = place_of(token, length) - centre
        psi = jnp.exp(gap * gap * (-0.5 / (WIDTH * WIDTH)))
        psi_high = psi.astype(BF16)
        psi_low = (psi - psi_high.astype(F32)).astype(BF16)
        pairs = qkv[k, at(b), :, LANES : 3 * LANES]
        exact = dot(psi_high, pairs[:, :LANES]) + dot(psi_low, pairs[:, :LANES])
        fresh = jnp.concatenate([exact, dot(psi_high, pairs[:, LANES:])], axis=1)
        gathered = fresh if b == 0 else jnp.where(start == b, 0.0, sums[k]) + fresh
        sums[k] = gathered
        stacked = jnp.concatenate([now, gathered * term_scale(length)], axis=0)
        later = jnp.concatenate(
            [
                dot(table[...], split3(stacked[:, :LANES])),
                dot(table[:, : BASIS + LIVE], stacked[:, LANES:].astype(BF16)),
            ],
            axis=1,
        )
        memory[k] = jnp.where(start + length == b + 1, later, now)
        return carry

    def end_state(k, carry):
        key = memory[k, :, :LANES]
        key_end[k] = key
        value_ends[k] = memory[k, :, LANES : LANES + width].astype(BF16)
        seen = dot(rows[k], key, precision=HIGHEST)
        for i in range(4):
            projs[k, 8 * i : 8 * i + 8] = jnp.where(mask, seen[8 * i : 8 * i + 8], 0.0)
        return carry

    def attend(b, k, carry):
        cols[k, :, b * UNIT : (b + 1) * UNIT] = qkv[k, at(b), :, 2 * LANES : 3 * LANES].astype(F32).T.astype(BF16)
        keys[k, b * UNIT : (b + 1) * UNIT] = qkv[k, at(b), :, LANES : 2 * LANES]
        query = qkv[k, at(b), :, 0:LANES].astype(F32) * root
        lane_head = lax.broadcasted_iota(jnp.int32, (UNIT, LANES), 1) // HEAD_DIM
        causal = lax.broadcasted_iota(jnp.int32, (UNIT, UNIT), 0) <= lax.broadcasted_iota(
            jnp.int32, (UNIT, UNIT), 1
        )
        away = [jnp.where(starts[b] <= j, 0.0, 1e30) for j in range(b)] + [0.0]
        owns = jnp.concatenate([jnp.where(lane_head == h, query, 0.0).astype(BF16) for h in range(heads)], axis=0)
        seen = (b + 1) * UNIT
        products = dot(keys[k, :seen], owns, ((1,), (1,)))
        for h in range(heads):
            scores = [products[j * UNIT : (j + 1) * UNIT, h * UNIT : (h + 1) * UNIT] for j in range(b + 1)]
            scores[b] = jnp.where(causal, scores[b], -1e30)
            highest = functools.reduce(
                jnp.maximum, [jnp.max(s, axis=0, keepdims=True) - away[j] for j, s in enumerate(scores)]
            )
            weights = [jnp.exp(s - (highest + away[j])) for j, s in enumerate(scores)]
            total = sum(jnp.sum(w, axis=0, keepdims=True) for w in weights)
            span = slice(h * HEAD_DIM, (h + 1) * HEAD_DIM)
            part = dot(cols[k, span, :seen], jnp.concatenate([w.astype(BF16) for w in weights], axis=0))
            discrete[k, b, span] = part * (1.0 / total)
            logsum[k, b, h : h + 1] = highest + jnp.log(total)
        return carry

    def seen_value(k, carry):
        incoming = jnp.where(run > 0, value_ins[k].astype(F32), 0.0)
        carried[:, :width] = incoming
        carried[:, width:] = jnp.zeros((BASIS, LANES - width), F32)
        for b in range(units):
            if b > 0:
                carried[...] = jnp.where(starts[b] == b, advance_values(table, carried[...]), carried[...])
            values[k, b] = (value_states[k, b] + carried[...]).astype(BF16)
            gained = jnp.zeros((8, LANES), F32)
            for i in range(4):
                gained += jnp.where((orders[b] == i) & (run > 0), proj_ins[k, 8 * i : 8 * i + 8], 0.0)
            probes[k, b] = (probes[k, b] + gained) * root
        return carry

    def read(rel, k, carry):
        b = at(rel)
        query = qkv[k, rel, :, 0:LANES]
        logits = logits_of(probes[k, b], query)
        location, variance = read_parts(logits, heads)
        fall = -0.5 / variance
        peak = WIDTH * lax.rsqrt(variance)
        centres = lax.broadcasted_iota(jnp.int32, (BASIS, UNIT), 0).astype(F32) / (BASIS - 1)
        value_cols = values[k, b].astype(F32).T.astype(BF16)
        parts = []
        for h in range(heads):
            gap = centres - location[h : h + 1]
            density = jnp.exp(gap * gap * fall[h : h + 1]).astype(BF16)
            span = slice(h * HEAD_DIM, (h + 1) * HEAD_DIM)
            parts.append(discrete[k, b, span] + dot(value_cols[span], density) * peak[h : h + 1])
        mixed[k, rel] = jnp.concatenate(parts, axis=0).T.astype(BF16)
        return carry

    advance(1, 1)
    state_copies = []
    for k in range(2):
        for b in range(units):
            state(b, k, 0)
        end_state(k, 0)
        state_copies.append([
            go(value_ends.at[k], value_ins.at[1 - k], "head", 2), go(projs.at[k], proj_ins.at[1 - k], "head", 2)
        ])
        if k == 0:
            advance(2, 1)
            advance(1, 2)
    advance(3, 1)
    for b in range(units):
        lax.fori_loop(0, 2, functools.partial(attend, b), 0)
        if b == 0:
            advance(2, 2)
        if b == 2:
            advance(1, 3)
            advance(3, 2)
    mixed_copies = [None, None]
    for k in (1, 0):
        for copy in state_copies[1 - k]:
            copy.wait_recv()
        seen_value(k, 0)
        read(2, k, 0)
        read(3, k, 0)
        mixed_copies[k] = go(mixed.at[k, half:], mixed_in.at[k], "head", 1)
    advance(2, 3)
    lax.fori_loop(0, 2, functools.partial(read, 0), 0)
    lax.fori_loop(0, 2, functools.partial(read, 1), 0)
    advance(3, 3)
    mixed_0[...] = mixed[0, :half].reshape(own_rows, width)
    mixed_2[...] = mixed[1, :half].reshape(own_rows, width)
    for copy in mixed_copies:
        copy.wait_recv()
    mixed_1[...] = mixed_in[0].reshape(own_rows, width)
    mixed_3[...] = mixed_in[1].reshape(own_rows, width)
    for copy in bias_copies + stage[1] + stage[2] + stage[3]:
        copy.wait_recv()
    for copy in started:
        copy.wait_send()
    for copy in saved:
        copy.wait()


def forward(seg_lengths, source, packed, weight, out_weight, ff_in, ff_out, heads):
    own_rows, model = source.shape
    units = 2 * own_rows // UNIT
    width = heads * HEAD_DIM
    hidden_part = ff_in.shape[1]
    rows = model // 8
    spaced = -(-width // 8 // 16) * 16
    table = jnp.asarray(basis_tables()[0])
    vmem, anywhere = pl.BlockSpec(memory_space=pltpu.VMEM), pl.BlockSpec(memory_space=pl.ANY)
    shape = jax.ShapeDtypeStruct
    hops = 2 + units // 2 + 3 + 3 * 3 * 4 + 3 + 4 + 2
    return pl.pallas_call(
        functools.partial(forward_kernel, heads),
        in_specs=[pl.BlockSpec(memory_space=pltpu.SMEM)] + [vmem] * 5 + [anywhere] * 2,
        out_specs=[anywhere] * 4 + [vmem] * 11 + [anywhere] * 3,
        out_shape=[
            shape((2, units, UNIT, 3 * LANES), BF16),
            shape((model, 2 * own_rows), BF16),
            shape((3 * LANES, model), BF16),
            shape((3 * LANES, model), BF16),
            shape((2, units, 8, UNIT), F32),
            shape((2, units, BASIS, LANES), BF16),
            shape((2, units, 8, LANES), F32),
            shape((2, units, BASIS, LANES), BF16),
            shape((2, BASIS, LANES), F32),
            shape((2, 32, BASIS), F32),
        ] + [shape((own_rows, width), BF16)] * 4 + [
            shape((4, 8, hidden_part), F32),
            shape((3, 2, 2, 2, rows, hidden_part), BF16),
            shape((3, 2, 2, 2, rows, model), BF16),
            shape((3, 2, 2, 2, spaced, model), BF16),
        ],
        scratch_shapes=[
            pltpu.VMEM((2, units, UNIT, 3 * LANES), BF16),
            pltpu.VMEM((2 * own_rows, model), BF16),
            pltpu.VMEM((model, 2 * own_rows), BF16),
            pltpu.VMEM((2, 3 * LANES, model), BF16),
            pltpu.VMEM((own_rows, model), BF16),
            pltpu.VMEM((2, 2, 2, 3 * width // 4, model // 2), BF16),
            pltpu.VMEM((3 * width, model), BF16),
            pltpu.VMEM((16, 3 * LANES), F32),
            pltpu.VMEM((16, 3 * LANES), F32),
            pltpu.VMEM((8, hidden_part), F32),
            pltpu.VMEM((spaced, model), BF16),
            pltpu.VMEM((2, BASIS, 2 * LANES), F32),
            pltpu.VMEM((2, LIVE, 2 * LANES), F32),
            pltpu.VMEM((2, units, BASIS, LANES), F32),
            pltpu.VMEM((BASIS, LANES), F32),
            pltpu.VMEM((2, BASIS, width), BF16),
            pltpu.VMEM((2, BASIS, width), BF16),
            pltpu.VMEM((2, 32, LANES), F32),
            pltpu.VMEM((2, 32, LANES), F32),
            pltpu.VMEM((2, LANES, units * UNIT), BF16),
            pltpu.VMEM((2, units * UNIT, LANES), BF16),
            pltpu.VMEM((2, units, width, UNIT), F32),
            pltpu.VMEM((2, units, UNIT, width), BF16),
            pltpu.VMEM((2, units // 2, UNIT, width), BF16),
            pltpu.SemaphoreType.DMA((hops,)),
            pltpu.SemaphoreType.DMA((hops,)),
            pltpu.SemaphoreType.DMA((4,)),
        ],
        compiler_params=pltpu.CompilerParams(
            collective_id=1, has_side_effects=True, vmem_limit_bytes=60 << 20
        ),
        name="forward",
    )(seg_lengths, source, packed, weight, out_weight, table, ff_in, ff_out)


def whole(shape):
    return pl.BlockSpec(shape, lambda i: (0,) * len(shape))


def finish_kernel(given_in, given_out, given_weight, given_qkv, grad_in, grad_out, grad_weight, grad_qkv):
    step = pl.program_id(0)
    grad_in[...] = given_in[...].astype(F32)
    grad_out[...] = given_out[...].astype(F32)
    width = grad_qkv.shape[1]
    turned = given_qkv[...].astype(F32).T
    for i in range(3):

        @pl.when(step == i)
        def _():
            grad_qkv[0] = turned[i * width : (i + 1) * width]

    @pl.when(step == 0)
    def _():
        narrow = grad_weight.shape[0] // given_weight.shape[0]
        for j in range(given_weight.shape[0]):
            grad_weight[j * narrow : (j + 1) * narrow] = given_weight[j].astype(F32)[:narrow]


def finish(given_in, given_out, given_weight, given_qkv, width):
    model, columns = given_in.shape
    hidden_part = given_out.shape[0]
    return pl.pallas_call(
        finish_kernel,
        grid=(3,),
        in_specs=[
            pl.BlockSpec((model // 3, columns), lambda i: (i, 0)),
            pl.BlockSpec((hidden_part // 3, model), lambda i: (i, 0)),
            pl.BlockSpec(given_weight.shape, lambda i: (0, 0, 0)),
            pl.BlockSpec(given_qkv.shape, lambda i: (0, 0)),
        ],
        out_specs=[
            pl.BlockSpec((model // 3, columns), lambda i: (i, 0)),
            pl.BlockSpec((hidden_part // 3, model), lambda i: (i, 0)),
            pl.BlockSpec((width, model), lambda i: (0, 0)),
            pl.BlockSpec((1, width, model), lambda i: (i, 0, 0)),
        ],
        out_shape=[
            jax.ShapeDtypeStruct((model, columns), F32), jax.ShapeDtypeStruct((hidden_part, model), F32),
            jax.ShapeDtypeStruct((width, model), F32), jax.ShapeDtypeStruct((3, width, model), F32),
        ],
        compiler_params=pltpu.CompilerParams(vmem_limit_bytes=62 << 20),
        name="finish",
    )(given_in, given_out, given_weight, given_qkv)


def middle_kernel(
    source, cotangent, mixed_0, mixed_1, mixed_2, mixed_3, own_weight, far_weight, vectors, in_bias, own_in, own_out,
    far_in, far_out, outputs, grad_residual, grad_mixed_0, grad_mixed_1, grad_mixed_2, grad_mixed_3, grad_in, grad_out,
    grad_out_weight, sums, grad_in_bias,
    residual, inverse, second, second_cols, total, grad_second, in_now, out_now, out_weight,
):
    r = pl.program_id(0)
    slices, rows = own_in.shape[0], own_in.shape[1]
    model = source.shape[1]
    hidden_part = own_in.shape[2]
    out_bias, gain, shift, last_bias = (vectors[k : k + 1] for k in range(18, 22))

    @pl.when(r == 0)
    def _():
        value = source[...].astype(F32) + out_bias
        out_weight[0] = own_weight[...]
        narrow = own_weight.shape[0] // slices
        for k in range(far_weight.shape[0]):
            parts = [far_weight[k, j].astype(F32)[:narrow] for j in range(slices)]
            out_weight[k + 1] = jnp.concatenate(parts, axis=0).astype(BF16)
        for k, mixed in enumerate((mixed_0, mixed_1, mixed_2, mixed_3)):
            value += dot(mixed[...], out_weight[k])
        residual[...] = value
        centred = value - jnp.mean(value, axis=-1, keepdims=True)
        factor = lax.rsqrt(jnp.mean(centred * centred, axis=-1, keepdims=True) + EPSILON)
        inverse[...] = factor
        normal = centred * factor
        grad_residual[...] = normal
        rounded = (normal * gain + shift).astype(BF16)
        second[...] = rounded
        second_cols[...] = rounded.astype(F32).T.astype(BF16)
        total[...] = jnp.zeros_like(total)
        grad_second[...] = jnp.zeros_like(grad_second)
        grad_in_bias[...] = jnp.zeros_like(grad_in_bias)
        for j in range(slices):
            in_now[j * rows : (j + 1) * rows] = own_in[j]
            out_now[j * rows : (j + 1) * rows] = own_out[j]

    @pl.when(r > 0)
    def _():
        for j in range(slices):
            in_now[j * rows : (j + 1) * rows] = far_in[0, j]
            out_now[j * rows : (j + 1) * rows] = far_out[0, j]

    half = hidden_part
    for t in range(1):
        span = slice(t * half, (t + 1) * half)
        hidden = dot(second[...], in_now[:, span]) + in_bias[r, 0:1, span]
        cube = hidden * hidden
        root = math.sqrt(2.0 / math.pi)
        bent = jnp.tanh(hidden * (root + (root * 0.044715) * cube))
        lifted = 0.5 + 0.5 * bent
        activation = (hidden * lifted).astype(BF16)
        slope = lifted + hidden * ((0.5 - 0.5 * bent * bent) * (root + (3.0 * root * 0.044715) * cube))
        total[...] += dot(activation, out_now[span])
        given = dot(cotangent[...], out_now[span], ((1,), (1,)))
        grad_hidden = (given * slope).astype(BF16)
        grad_second[...] += dot(grad_hidden, in_now[:, span], ((1,), (1,)))
        grad_in_bias[pl.ds(r, 1), span] = jnp.sum(grad_hidden.astype(F32), axis=0, keepdims=True)
        part = dot(activation, cotangent[...], ((0,), (0,))).astype(BF16)
        per = half // rows
        for k in range(per):
            grad_out[0, t * per + k] = part[k * rows : (k + 1) * rows]
        part = dot(second_cols[...], grad_hidden).astype(BF16)
        for j in range(slices):
            grad_in[0, j, :, span] = part[j * rows : (j + 1) * rows]

    @pl.when(r == pl.num_programs(0) - 1)
    def _():
        given = cotangent[...].astype(F32)
        outputs[...] = (residual[...] + total[...] + last_bias).astype(BF16)
        normal = grad_residual[...]
        grad = grad_second[...]
        scaled = grad * gain
        value = given + inverse[...] * (
            scaled
            - jnp.mean(scaled, axis=-1, keepdims=True)
            - normal * jnp.mean(scaled * normal, axis=-1, keepdims=True)
        )
        sums[0:1] = jnp.sum(value, axis=0, keepdims=True)
        sums[1:2] = jnp.sum(grad * normal, axis=0, keepdims=True)
        sums[2:3] = jnp.sum(grad, axis=0, keepdims=True)
        sums[3:4] = jnp.sum(given, axis=0, keepdims=True)
        sums[4:8] = jnp.zeros((4, model), F32)
        grad_residual[...] = value
        rounded = value.astype(BF16)
        grads = (grad_mixed_0, grad_mixed_1, grad_mixed_2, grad_mixed_3)
        for k, mixed in enumerate((mixed_0, mixed_1, mixed_2, mixed_3)):
            grads[k][...] = dot(rounded, out_weight[k], ((1,), (1,))).astype(BF16)
            product = dot(mixed[...], rounded, ((0,), (0,)))
            narrow = product.shape[0] // slices
            spare = jnp.zeros((grad_out_weight.shape[2] - narrow, model), F32)
            for j in range(slices):
                part = jnp.concatenate([product[j * narrow : (j + 1) * narrow], spare], axis=0)
                grad_out_weight[k, j] = part.astype(BF16)


def middle(source, cotangent, mixed, out_weight, far_weight, vectors, in_bias, own_in, own_out, far_in, far_out):
    own_rows, model = source.shape
    shards = far_in.shape[0] + 1
    slices, rows, hidden_part = own_in.shape
    narrow = mixed[0].shape
    far = pl.BlockSpec((1,) + own_in.shape, lambda r: (jnp.maximum(r - 1, 0), 0, 0, 0))
    part = pl.BlockSpec((1,) + own_in.shape, lambda r: (r, 0, 0, 0))
    macs = own_rows * model * (6 * shards * hidden_part + 3 * model)
    return pl.pallas_call(
        middle_kernel,
        grid_spec=pltpu.PrefetchScalarGridSpec(
            num_scalar_prefetch=0,
            grid=(shards,),
            in_specs=[whole(source.shape)] * 2 + [whole(narrow)] * 4 + [
                whole(out_weight.shape), whole(far_weight.shape), whole(vectors.shape), whole(in_bias.shape), whole(own_in.shape),
                whole(own_out.shape), far, far,
            ],
            out_specs=[whole(source.shape)] * 2 + [whole(narrow)] * 4 + [
                part, part, whole((shards,) + far_weight.shape[1:]), whole((8, model)), whole((shards, hidden_part))
            ],
            scratch_shapes=[
                pltpu.VMEM((own_rows, model), F32),
                pltpu.VMEM((own_rows, 1), F32),
                pltpu.VMEM((own_rows, model), BF16),
                pltpu.VMEM((model, own_rows), BF16),
                pltpu.VMEM((own_rows, model), F32),
                pltpu.VMEM((own_rows, model), F32),
                pltpu.VMEM((model, hidden_part), BF16),
                pltpu.VMEM((hidden_part, model), BF16),
                pltpu.VMEM((shards,) + narrow[1:] + (model,), BF16),
            ],
        ),
        out_shape=[
            jax.ShapeDtypeStruct(source.shape, BF16),
            jax.ShapeDtypeStruct(source.shape, F32),
        ] + [jax.ShapeDtypeStruct(narrow, BF16)] * 4 + [
            jax.ShapeDtypeStruct((shards, slices, rows, hidden_part), BF16),
            jax.ShapeDtypeStruct((shards, slices, rows, hidden_part), BF16),
            jax.ShapeDtypeStruct((shards,) + far_weight.shape[1:], BF16),
            jax.ShapeDtypeStruct((8, model), F32),
            jax.ShapeDtypeStruct((shards, hidden_part), F32),
        ],
        compiler_params=pltpu.CompilerParams(vmem_limit_bytes=60 << 20),
        cost_estimate=pl.CostEstimate(
            flops=2 * macs, bytes_accessed=30 << 20, transcendentals=own_rows * shards * hidden_part
        ),
        name="middle",
    )(source, cotangent, *mixed, out_weight, far_weight, vectors, in_bias, own_in, own_out, far_in, far_out)


def added(a, b):
    return (a.astype(F32) + b.astype(F32)).astype(BF16)


def backward_kernel(
    heads, seg_lengths, qkv, gm_0, gm_1, gm_2, gm_3, logsum, values, probes, key_states, key_end, rows, table,
    grad_in, grad_out, grad_weight, out, probe_grad, slice_in, slice_out, slice_weight,
    given, query_grad, memory_grad, row_grad, value_carried, value_back, value_in, row_back, row_in, carried, spread, key_grad, value_grad, cols, keys, vals,
    keep_in, keep_out, keep_weight, core_in, core_out, core_weight, one_in, one_out, one_weight,
    two_in, two_out, two_weight, z_in, z_out, z_weight, send, recv, local_sems,
):
    units = qkv.shape[1]
    half = units // 2
    width = heads * HEAD_DIM
    root = 1.0 / math.sqrt(HEAD_DIM)
    z = lax.axis_index("head")
    flip, run = (z % 2) * half, z // 2
    place = lax.axis_index("dp") % 8
    y, x, c = place // 4, (place // 2) % 2, place % 2
    at = lambda b: (b + flip) % units
    starts, lengths, orders = segments_of(seg_lengths, run, units)
    greet((("head", 1), ("head", 2), ("head", 3), ("dp", 1), ("dp", 2), ("dp", 4)))
    hops = Hops(send, recv)
    started = []

    def go(*args):
        started.append(hops.start(*args))
        return started[-1]

    given_copies = [go(gm_1, given.at[0, half:], "head", 1), go(gm_3, given.at[1, half:], "head", 1)]
    sums = (
        (grad_in, keep_in, core_in, one_in, two_in, z_in, True),
        (grad_weight, keep_weight, core_weight, one_weight, two_weight, z_weight, True),
        (grad_out, keep_out, core_out, one_out, two_out, z_out, False),
    )
    stage, local_copies = {}, {}
    for i, r in enumerate((2, 1, 3, 0)):
        stage[r], local_copies[r] = [], []
        for n, (term, keep, core, _, _, _, _) in enumerate(sums):
            stage[r].append(go(term.at[r, :, :, 1 - c], core.at[r], "dp", 1))
            copy = pltpu.make_async_copy(term.at[r, :, :, c], keep.at[r], local_sems.at[3 * i + n])
            copy.start()
            local_copies[r].append(copy)

    def first_hop(r):
        for n, (_, keep, core, one, _, _, along_x) in enumerate(sums):
            local_copies[r][n].wait()
            stage[r][n].wait_recv()
            keep[r] = added(keep[r], core[r])
            part = keep.at[r, :, 1 - x] if along_x else keep.at[r, 1 - y]
            stage[r][n] = go(part, one.at[r], "dp", 2 if along_x else 4)

    def second_hop(r):
        for n, (_, keep, _, one, two, _, along_x) in enumerate(sums):
            stage[r][n].wait_recv()
            kept = keep[r, :, x] if along_x else keep[r, y]
            one[r] = added(kept, one[r])
            part = one.at[r, 1 - y] if along_x else one.at[r, 1 - x]
            stage[r][n] = go(part, two.at[r], "dp", 4 if along_x else 2)

    def third_hop(r):
        for n, (_, _, _, one, two, far, along_x) in enumerate(sums):
            stage[r][n].wait_recv()
            kept = one[r, y] if along_x else one[r, x]
            two[r] = added(kept, two[r])
            if r:
                stage[r][n] = go(two.at[r], far.at[r - 1], "head", r)

    for k, own in enumerate((gm_0, gm_2)):
        given[k, :half] = own[...]
    mask = head_rows(heads, LANES)
    lane_head = lax.broadcasted_iota(jnp.int32, (UNIT, LANES), 1) // HEAD_DIM

    def given_of(k, b):
        return jnp.concatenate([given[k, at(b)], jnp.zeros((UNIT, LANES - width), BF16)], axis=1).astype(F32)

    def read_back(rel, k, carry):
        b = at(rel)
        query = qkv[k, rel, :, 0:LANES]
        full = given_of(k, b)
        probe = probes[k, b]
        logits = logits_of(probe, query)
        location, variance = read_parts(logits, heads)
        inverse = 1.0 / variance
        fall = -0.5 * inverse
        peak = WIDTH * lax.rsqrt(variance)
        centres = lax.broadcasted_iota(jnp.int32, (BASIS, UNIT), 0).astype(F32) / (BASIS - 1)
        along, across = [], []
        total = jnp.zeros((BASIS, LANES), F32)
        for h in range(heads):
            own_given = jnp.where(lane_head == h, full, 0.0).astype(BF16)
            gap = centres - location[h : h + 1]
            square = gap * gap
            density = jnp.exp(square * fall[h : h + 1]) * peak[h : h + 1]
            grad_density = dot(values[k, b], own_given, ((1,), (1,)))
            total += dot(density.astype(BF16), own_given)
            weighed = density * grad_density
            moment = weighed * gap
            zeroth = jnp.sum(weighed, axis=0, keepdims=True)
            first = jnp.sum(moment, axis=0, keepdims=True)
            second = jnp.sum(moment * gap, axis=0, keepdims=True)
            along.append(first * inverse[h : h + 1])
            across.append(0.5 * inverse[h : h + 1] * (second * inverse[h : h + 1] - zeroth))
        sigmoid = 1.0 / (1.0 + jnp.exp(-logits))
        grad_location = jnp.concatenate(along, axis=0) * location * (1.0 - location)
        grad_variance = jnp.concatenate(across, axis=0) * SPREAD * sigmoid[heads : 2 * heads]
        grad_logits = jnp.concatenate(
            [grad_location, grad_variance, jnp.zeros((8 - 2 * heads, UNIT), F32)], axis=0
        )
        padded = jnp.concatenate([grad_logits, jnp.zeros((120, UNIT), F32)], axis=0)
        probe_cols = jnp.concatenate([probe, jnp.zeros((120, LANES), F32)], axis=0).T
        query_grad[k, b] = dot(probe_cols.astype(BF16), padded.astype(BF16))[:width]
        fresh = jnp.where(mask, dot(grad_logits.astype(BF16), query), 0.0) * root
        memory_grad[k, b] = total
        row_grad[k, b] = fresh
        return carry

    def gather_back(k, carry):
        probe = jnp.zeros((8, BASIS), F32)
        for i in range(4):
            row_back[k, 8 * i : 8 * i + 8] = jnp.zeros((8, LANES), F32)
        for b in range(units - 1, -1, -1):
            fresh, total = row_grad[k, b], memory_grad[k, b]
            if b > 0:
                probe += dot(fresh.astype(BF16), key_states[k, b], ((1,), (1,)))
            for i in range(4):
                row_back[k, 8 * i : 8 * i + 8] += jnp.where(orders[b] == i, fresh, 0.0)
            if b < units - 1:
                ends = starts[b] + lengths[b] == b + 1
                total = jnp.where(ends, 0.0, memory_grad[k, b + 1]) + total
                memory_grad[k, b] = total
                row_grad[k, b] = jnp.where(ends, 0.0, row_grad[k, b + 1]) + fresh
            before = jnp.zeros((BASIS, LANES), F32) if b == units - 1 else value_carried[k]
            if b > 0:
                value_carried[k] = jnp.where(starts[b] == b, advance_values(table, before + total), before)
            else:
                value_back[k] = (before + total)[:, :width].astype(BF16)
        probe_grad[k] = probe
        return carry

    def attend_back(b, k, carry):
        query = qkv[k, at(b), :, 0:LANES].astype(F32) * root
        full = given_of(k, b)
        causal = lax.broadcasted_iota(jnp.int32, (UNIT, UNIT), 0) <= lax.broadcasted_iota(
            jnp.int32, (UNIT, UNIT), 1
        )
        away = [jnp.where(starts[b] <= j, 0.0, 1e30) for j in range(b)] + [0.0]
        owns = [jnp.where(lane_head == h, query, 0.0).astype(BF16) for h in range(heads)]
        own_givens = [jnp.where(lane_head == h, full, 0.0).astype(BF16) for h in range(heads)]
        own_all = jnp.concatenate(owns, axis=0)
        given_all = jnp.concatenate(own_givens, axis=0)
        seen = (b + 1) * UNIT
        scores = dot(keys[k, :seen], own_all, ((1,), (1,)))
        grad_probs = dot(vals[k, :seen], given_all, ((1,), (1,)))
        grads, probs = [], []
        for h in range(heads):
            prob_h, product_h = [], []
            inner = jnp.zeros((1, UNIT), F32)
            for j in range(b + 1):
                tile = (slice(j * UNIT, (j + 1) * UNIT), slice(h * UNIT, (h + 1) * UNIT))
                score = scores[tile]
                if j == b:
                    score = jnp.where(causal, score, -1e30)
                prob = jnp.exp(score - (logsum[k, b, h : h + 1] + away[j]))
                product = prob * grad_probs[tile]
                inner += jnp.sum(product, axis=0, keepdims=True)
                prob_h.append(prob)
                product_h.append(product)
            span = slice(h * HEAD_DIM, (h + 1) * HEAD_DIM)
            grad_h = [(product_h[j] - prob_h[j] * inner).astype(BF16) for j in range(b + 1)]
            result = dot(cols[k, span, :seen], jnp.concatenate(grad_h, axis=0))
            query_grad[k, b, span] = query_grad[k, b, span] + result * root
            grads.append(grad_h)
            probs.append([prob.astype(BF16) for prob in prob_h])
        fresh_keys = dot(jnp.concatenate([jnp.concatenate(g, axis=0) for g in grads], axis=1), own_all)
        fresh_vals = dot(jnp.concatenate([jnp.concatenate(p, axis=0) for p in probs], axis=1), given_all)
        for j in range(b + 1):
            part = slice(j * UNIT, (j + 1) * UNIT)
            if b == units - 1:
                key_grad[k, j], value_grad[k, j] = fresh_keys[part], fresh_vals[part]
            else:
                key_grad[k, j] += fresh_keys[part]
                value_grad[k, j] += fresh_vals[part]
        return carry

    def carry_back(k, total, units_before):
        moved = dot(table[...], total.astype(BF16))
        return moved[:BASIS], (moved[BASIS:] * term_scale(units_before)).astype(BF16)

    def end_back(k, carry):
        row = jnp.where(run == 0, row_in[k], 0.0)
        value = jnp.where(run == 0, value_in[k].astype(F32), 0.0)
        grad_keys = dot(rows[k].astype(BF16), row.astype(BF16), ((0,), (0,)))
        total = jnp.concatenate([grad_keys, value, jnp.zeros((BASIS, LANES - width), F32)], axis=1)
        carried[k], spread[k] = carry_back(k, total, lengths[units - 1])
        seen = dot(row, key_end[k], ((1,), (1,)), HIGHEST)
        gained = seen[24:32]
        for i in (2, 1, 0):
            high = gained.astype(BF16)
            low = (gained - high.astype(F32)).astype(BF16)
            gained = dot(high, table[:BASIS]) + dot(low, table[:BASIS])
            gained = gained + seen[8 * i : 8 * i + 8]
        probe_grad[k] += gained
        return carry

    def finish(b, k, carry):
        start, length = starts[b], lengths[b]
        token = lax.broadcasted_iota(jnp.int32, (UNIT, LIVE), 0) + (b - start) * UNIT
        centre = (lax.broadcasted_iota(jnp.int32, (UNIT, LIVE), 1) + LIVE).astype(F32) / (BASIS - 1)
        gap = place_of(token, length) - centre
        psi = jnp.exp(gap * gap * (-0.5 / (WIDTH * WIDTH))).astype(BF16)
        pair_grad = dot(psi, spread[k])
        query_rows = query_grad[k, b].T.astype(BF16)
        out[k, at(b), :, :LANES] = jnp.concatenate([query_rows, jnp.zeros((UNIT, LANES - width), BF16)], axis=1)
        out[k, at(b), :, LANES : 2 * LANES] = (key_grad[k, b] + pair_grad[:, :LANES]).astype(BF16)
        out[k, at(b), :, 2 * LANES :] = (value_grad[k, b] + pair_grad[:, LANES:]).astype(BF16)
        if b > 0:
            grad_keys = dot(rows[k, 0:8].astype(BF16), row_grad[k, b].astype(BF16), ((0,), (0,)))
            total = carried[k] + jnp.concatenate([grad_keys, memory_grad[k, b]], axis=1)
            moved, spread_now = carry_back(k, total, lengths[b - 1])
            carried[k] = jnp.where(start == b, moved, carried[k])
            spread[k] = jnp.where(start == b, spread_now.astype(F32), spread[k].astype(F32)).astype(BF16)
        return carry

    def both(step, *args):
        lax.fori_loop(0, 2, functools.partial(step, *args), 0)

    def turn(k, carry):
        for b in range(units):
            part = slice(b * UNIT, (b + 1) * UNIT)
            keys[k, part] = qkv[k, at(b), :, LANES : 2 * LANES]
            vals[k, part] = qkv[k, at(b), :, 2 * LANES : 3 * LANES]
            cols[k, :, part] = qkv[k, at(b), :, LANES : 2 * LANES].astype(F32).T.astype(BF16)
        return carry

    lax.fori_loop(0, 2, turn, 0)
    both(read_back, 0)
    first_hop(2)
    both(read_back, 1)
    first_hop(1)
    for copy in given_copies:
        copy.wait_recv()
    both(read_back, 2)
    first_hop(3)
    first_hop(0)
    both(read_back, 3)
    second_hop(2)
    back_copies = []
    for k in range(2):
        gather_back(k, 0)
        back_copies += [
            go(value_back.at[k], value_in.at[1 - k], "head", 2), go(row_back.at[k], row_in.at[1 - k], "head", 2)
        ]
    second_hop(1)
    both(attend_back, 3)
    second_hop(3)
    second_hop(0)
    third_hop(2)
    both(attend_back, 2)
    third_hop(1)
    third_hop(3)
    both(attend_back, 1)
    third_hop(0)
    both(attend_back, 0)
    for copy in back_copies:
        copy.wait_recv()
    lax.fori_loop(0, 2, end_back, 0)
    for b in range(units - 1, -1, -1):
        both(finish, b)
    for n, (_, _, _, _, two, far, _) in enumerate(sums):
        total = two[0].astype(F32)
        for r in (1, 2, 3):
            stage[r][n].wait_recv()
            total += far[r - 1].astype(F32)
        (slice_in, slice_weight, slice_out)[n][...] = total.astype(BF16)
    for copy in started:
        copy.wait_send()


def backward(seg_lengths, qkv, grad_mixed, logsum, values, probes, key_states, key_end, rows, grad_in, grad_out, grad_weight, heads):
    units = qkv.shape[1]
    width = heads * HEAD_DIM
    table = jnp.asarray(basis_tables()[1])
    vmem, anywhere = pl.BlockSpec(memory_space=pltpu.VMEM), pl.BlockSpec(memory_space=pl.ANY)
    shape = jax.ShapeDtypeStruct
    slices = [grad_in.shape[4:], grad_out.shape[4:], grad_weight.shape[4:]]
    hops = 2 + 3 * 4 * 3 + 3 * 3 + 4
    return pl.pallas_call(
        functools.partial(backward_kernel, heads),
        in_specs=[pl.BlockSpec(memory_space=pltpu.SMEM)] + [vmem] * 12 + [anywhere] * 3,
        out_specs=[vmem] * 5,
        out_shape=[shape(qkv.shape, BF16), shape((2, 8, BASIS), F32)] + [shape(part, BF16) for part in slices],
        scratch_shapes=[
            pltpu.VMEM((2, units, UNIT, width), BF16),
            pltpu.VMEM((2, units, width, UNIT), F32),
            pltpu.VMEM((2, units, BASIS, LANES), F32),
            pltpu.VMEM((2, units, 8, LANES), F32),
            pltpu.VMEM((2, BASIS, LANES), F32),
            pltpu.VMEM((2, BASIS, width), BF16),
            pltpu.VMEM((2, BASIS, width), BF16),
            pltpu.VMEM((2, 32, LANES), F32),
            pltpu.VMEM((2, 32, LANES), F32),
            pltpu.VMEM((2, BASIS, 2 * LANES), F32),
            pltpu.VMEM((2, LIVE, 2 * LANES), BF16),
            pltpu.VMEM((2, units, UNIT, LANES), F32),
            pltpu.VMEM((2, units, UNIT, LANES), F32),
            pltpu.VMEM((2, LANES, units * UNIT), BF16),
            pltpu.VMEM((2, units * UNIT, LANES), BF16),
            pltpu.VMEM((2, units * UNIT, LANES), BF16),
        ]
        + [pltpu.VMEM((4, 2, 2) + part, BF16) for part in slices]
        + [pltpu.VMEM((4, 2, 2) + part, BF16) for part in slices]
        + [pltpu.VMEM((4, 2) + part, BF16) for part in slices]
        + [pltpu.VMEM((4,) + part, BF16) for part in slices]
        + [pltpu.VMEM((3,) + part, BF16) for part in slices]
        + [
            pltpu.SemaphoreType.DMA((hops,)),
            pltpu.SemaphoreType.DMA((hops,)),
            pltpu.SemaphoreType.DMA((12,)),
        ],
        compiler_params=pltpu.CompilerParams(
            collective_id=2, has_side_effects=True, vmem_limit_bytes=62 << 20
        ),
        name="backward",
    )(
        seg_lengths, qkv, *grad_mixed, logsum, values, probes, key_states, key_end, rows, table, grad_in, grad_out, grad_weight
    )


def tail_kernel(
    heads, outer, grads, first_cols, flat_a, flat_b, grad_residual, source, packed, slice_in, slice_out, slice_weight,
    sums, in_bias_part, probe_grad, input_grad, whole_in, whole_out, whole_weight, whole_qkv, shared_out, owned_out,
    row_grad, near, kept, part_a, part_b, core_a, core_b, one_a, one_b, two_a, two_b, far_b, total, outer_in,
    gather_in, gather_out, gather_weight, gather_qkv,
    shared, shared_in, block, block_in, bias_block, bias_in, joined, joined_in, send, recv,
):
    own_rows, model = source.shape
    units = grads.shape[1]
    half = units // 2
    width = heads * HEAD_DIM
    z = lax.axis_index("head")
    place = lax.axis_index("dp") % 8
    y, x, c = place // 4, (place // 2) % 2, place % 2
    rows = model // 8
    greet(
        (("head", 1), ("head", 2), ("head", 3), ("dp", 1), ("dp", 2), ("dp", 4)) + tuple(("dp", bit) for bit in outer)
    )
    hops = Hops(send, recv)
    started = []

    def go(*args):
        started.append(hops.start(*args))
        return started[-1]

    def row_of(rel):
        return dot(grads[0, rel], flat_a[...]) + dot(grads[1, rel], flat_b[...])

    row_copies = []
    for k in range(half):
        row_grad[k] = row_of(half + k).astype(BF16)
        row_copies.append(go(row_grad.at[k], near.at[k], "head", 1))

    gathers = ((slice_in, gather_in, True), (slice_weight, gather_weight, True), (slice_out, gather_out, False))
    for own, gather, _ in gathers:
        gather[y, x, c] = own[...]

    def spread_first(gather, along_x):
        part = gather.at[y, x, c]
        return go(part, part, "dp", 2 if along_x else 4)

    def spread_second(gather, along_x):
        part = gather.at[y, :, c] if along_x else gather.at[:, x, c]
        return go(part, part, "dp", 4 if along_x else 2)

    def spread_third(gather):
        part = gather.at[:, :, c]
        return go(part, part, "dp", 1)

    core_copies = []
    for k, part, core in ((1, part_b, core_b), (0, part_a, core_a)):
        product = dot(first_cols[...], grads[k].reshape(2 * own_rows, 3 * LANES))
        product = jnp.concatenate([product[:, i * LANES : i * LANES + width] for i in range(3)], axis=1).astype(BF16)
        for j in range(8):
            part[j // 4, (j // 2) % 2, j % 2] = product[j * rows : (j + 1) * rows]
        core_copies.append(go(part.at[:, :, 1 - c], core, "dp", 1))
    spreads = [spread_first(gather, along_x) for _, gather, along_x in gathers]
    for k in range(half):
        kept[k] = row_of(k)

    core_copies[0].wait_recv()
    core_b[...] = added(part_b[:, :, c], core_b[...])
    one_copy_b = go(core_b.at[1 - y], one_b, "dp", 4)
    core_copies[1].wait_recv()
    core_a[...] = added(part_a[:, :, c], core_a[...])
    one_copy_a = go(core_a.at[:, 1 - x], one_a, "dp", 2)

    bias_a = jnp.sum(grads[0].reshape(2 * own_rows, 3 * LANES).astype(F32), axis=0, keepdims=True)
    bias_b = jnp.sum(grads[1].reshape(2 * own_rows, 3 * LANES).astype(F32), axis=0, keepdims=True)
    edge = jnp.zeros((8, model - BASIS), F32)
    fill = jnp.zeros((6, model), F32)
    for k, bias in ((0, bias_a), (1, bias_b)):
        block[k, 0:8] = jnp.concatenate([probe_grad[k], edge], axis=1)
        block[k, 8:16] = jnp.concatenate([bias, in_bias_part[2 * k : 2 * k + 1], fill], axis=0)
        bias_block[k] = jnp.concatenate([in_bias_part[2 * k + 1 : 2 * k + 2], jnp.zeros((7, model), F32)], axis=0)
    block_copy = go(block.at[1], block_in, "head", 2)
    bias_copies = [go(bias_block.at[0], bias_in.at[0], "head", 1), go(bias_block.at[1], bias_in.at[1], "head", 3)]

    value = source[...].astype(F32)
    centred = value - jnp.mean(value, axis=-1, keepdims=True)
    factor = lax.rsqrt(jnp.mean(centred * centred, axis=-1, keepdims=True) + EPSILON)
    normal = centred * factor

    one_copy_b.wait_recv()
    one_b[...] = added(core_b[y], one_b[...])
    two_copy_b = go(one_b.at[1 - x], two_b, "dp", 2)
    one_copy_a.wait_recv()
    one_a[...] = added(core_a[:, x], one_a[...])
    two_copy_a = go(one_a.at[1 - y], two_a, "dp", 4)
    for copy in row_copies:
        copy.wait_recv()
    two_copy_b.wait_recv()
    two_b[...] = added(one_b[x], two_b[...])
    far_copy = go(two_b, far_b, "head", 2)

    grad = kept[...].reshape(own_rows, model) + near[...].reshape(own_rows, model).astype(F32)
    scaled = grad * packed[16:17]
    change = factor * (
        scaled
        - jnp.mean(scaled, axis=-1, keepdims=True)
        - normal * jnp.mean(scaled * normal, axis=-1, keepdims=True)
    )
    input_grad[...] = (grad_residual[...] + change).astype(BF16)
    shared[...] = jnp.concatenate(
        [jnp.sum(grad * normal, axis=0, keepdims=True), jnp.sum(grad, axis=0, keepdims=True), sums[0:6]], axis=0
    )
    shared_copies = [go(shared, shared_in.at[r - 1], "head", r) for r in (1, 2, 3)]
    spreads = [copy.wait_recv() or spread_second(gather, along_x) for copy, (_, gather, along_x) in zip(spreads, gathers)]

    two_copy_a.wait_recv()
    own_sum = added(one_a[y], two_a[...]).astype(F32)
    far_copy.wait_recv()
    total[0] = (own_sum + far_b[...].astype(F32)).astype(BF16)
    for n, bit in enumerate(outer):
        copy = go(total.at[n], outer_in.at[n], "dp", bit)
        copy.wait_recv()
        total[n + 1] = added(total[n], outer_in[n])
    gather_qkv[y, x, c] = total[len(outer)]
    cut = rows // 2
    upper, lower = pl.ds(0, cut), pl.ds(cut, cut)
    qkv_parts = [gather_qkv.at[y, x, c, upper], gather_qkv.at[y, x, c, lower]]
    qkv_copies = [go(qkv_parts[0], qkv_parts[0], "dp", 2), go(qkv_parts[1], qkv_parts[1], "dp", 4)]

    block_copy.wait_recv()
    for copy in bias_copies + shared_copies:
        copy.wait_recv()
    owned = block[0] + block_in[...]
    bias_rows = bias_in[0] + bias_in[1]
    owned_rows = jnp.concatenate([owned[8:9], owned[9:10] + bias_rows[0:1], owned[10:16]], axis=0)
    joined[0] = jnp.concatenate(
        [shared[...] + shared_in[0] + shared_in[1] + shared_in[2], owned[0:8], owned_rows], axis=0
    )
    spreads = [copy.wait_recv() or spread_third(gather) for copy, (_, gather, _) in zip(spreads, gathers)]
    for n, bit in enumerate((2, 4, 1) + outer):
        copy = go(joined.at[n], joined_in.at[n], "dp", bit)
        if n == 1:
            for copy_one in qkv_copies:
                copy_one.wait_recv()
            qkv_parts = [gather_qkv.at[y, :, c, upper], gather_qkv.at[:, x, c, lower]]
            qkv_copies = [go(qkv_parts[0], qkv_parts[0], "dp", 4), go(qkv_parts[1], qkv_parts[1], "dp", 2)]
        copy.wait_recv()
        joined[n + 1] = joined[n] + joined_in[n]
    last = joined[3 + len(outer)]
    shared_out[...] = last[0:8]
    owned_out[...] = last[8:24]
    for copy, (_, gather, _), out in zip(spreads, gathers, (whole_in, whole_weight, whole_out)):
        copy.wait_recv()
        out[...] = gather[...]
    for copy in qkv_copies:
        copy.wait_recv()
    spread_third(gather_qkv).wait_recv()
    whole_qkv[...] = gather_qkv[...]
    for copy in started:
        copy.wait_send()


def tail(grads, first_cols, flat_a, flat_b, grad_residual, source, packed, slices, sums, in_bias_part, probe_grad, outer, heads):
    own_rows, model = source.shape
    units = grads.shape[1]
    rows = model // 8
    vmem = pl.BlockSpec(memory_space=pltpu.VMEM)
    shape = jax.ShapeDtypeStruct
    slice_in, slice_out, slice_weight = slices
    plane = lambda part: (2, 2, 2) + part
    part = (rows, 3 * heads * HEAD_DIM)
    hops = units // 2 + 9 + 2 + 2 + 2 + 1 + 5 + 1 + 2 + 3 + 3 + 2 * len(outer)
    return pl.pallas_call(
        functools.partial(tail_kernel, heads, outer),
        in_specs=[vmem] * 13,
        out_specs=[vmem] * 7,
        out_shape=[
            shape(source.shape, BF16), shape(plane(slice_in.shape), BF16), shape(plane(slice_out.shape), BF16),
            shape(plane(slice_weight.shape), BF16), shape(plane(part), BF16), shape((8, model), F32),
            shape((16, model), F32),
        ],
        scratch_shapes=[
            pltpu.VMEM((units // 2, UNIT, model), BF16),
            pltpu.VMEM((units // 2, UNIT, model), BF16),
            pltpu.VMEM((units // 2, UNIT, model), F32),
            pltpu.VMEM(plane(part), BF16),
            pltpu.VMEM(plane(part), BF16),
            pltpu.VMEM((2, 2) + part, BF16),
            pltpu.VMEM((2, 2) + part, BF16),
            pltpu.VMEM((2,) + part, BF16),
            pltpu.VMEM((2,) + part, BF16),
            pltpu.VMEM(part, BF16),
            pltpu.VMEM(part, BF16),
            pltpu.VMEM(part, BF16),
            pltpu.VMEM((1 + len(outer),) + part, BF16),
            pltpu.VMEM((max(1, len(outer)),) + part, BF16),
            pltpu.VMEM(plane(slice_in.shape), BF16),
            pltpu.VMEM(plane(slice_out.shape), BF16),
            pltpu.VMEM(plane(slice_weight.shape), BF16),
            pltpu.VMEM(plane(part), BF16),
            pltpu.VMEM((8, model), F32),
            pltpu.VMEM((3, 8, model), F32),
            pltpu.VMEM((2, 16, model), F32),
            pltpu.VMEM((16, model), F32),
            pltpu.VMEM((2, 8, model), F32),
            pltpu.VMEM((2, 8, model), F32),
            pltpu.VMEM((4 + len(outer), 24, model), F32),
            pltpu.VMEM((3 + len(outer), 24, model), F32),
            pltpu.SemaphoreType.DMA((hops,)),
            pltpu.SemaphoreType.DMA((hops,)),
        ],
        compiler_params=pltpu.CompilerParams(
            collective_id=3, has_side_effects=True, vmem_limit_bytes=60 << 20
        ),
        name="tail",
    )(
        grads, first_cols, flat_a, flat_b, grad_residual, source, packed, slice_in, slice_out, slice_weight, sums,
        in_bias_part, probe_grad,
    )


def exchange(value, axis, bit):
    size = lax.axis_size(axis)
    return lax.ppermute(value, axis, [(j, j ^ bit) for j in range(size)])


def local(
    inputs, seg_lengths, ln1_gain, ln1_bias, qkv_weight, qkv_bias, out_weight, out_bias, mem_mu, mem_sig,
    ln2_gain, ln2_bias, ff_in, ff_in_bias, ff_out, ff_out_bias, cotangent,
):
    own_rows, model = inputs.shape
    shards = lax.axis_size("head")
    members = lax.axis_size("dp")
    width = qkv_weight.shape[2]
    heads = width // HEAD_DIM
    hidden_part = ff_in.shape[1]
    units = 2 * own_rows // UNIT
    slices = 8
    outer = tuple(1 << k for k in range(3, 16) if 1 << k < members)
    rows = model // slices

    bias_row = jnp.pad(qkv_bias, ((0, 0), (0, LANES - width))).reshape(1, 3 * LANES)
    edge = 3 * LANES - BASIS
    packed = jnp.pad(bias_row, ((0, 23), (0, 0))).astype(F32)
    packed += jnp.pad(mem_mu, ((1, 23 - heads), (0, edge))).astype(F32)
    packed += jnp.pad(mem_sig, ((1 + heads, 23 - 2 * heads), (0, edge))).astype(F32)
    vectors = jnp.concatenate([ln1_gain, ln1_bias, out_bias, ln2_gain, ln2_bias, ff_out_bias, ff_in_bias])
    packed += jnp.pad(vectors.reshape(7, model), ((16, 1), (0, 0))).astype(F32)

    turned_weight = jnp.transpose(qkv_weight, (1, 2, 0)).reshape(3 * width, model)
    (
        qkv, first_cols, flat_a, flat_b, logsum, values, probes, key_states, key_end, state_rows,
        *mixed, in_bias, far_in, far_out, far_weight,
    ) = forward(seg_lengths, inputs, packed, turned_weight, out_weight, ff_in, ff_out, heads)
    flat = lambda array: array.reshape((shards - 1, slices) + array.shape[4:])
    outputs, grad_residual, *rest = middle(
        inputs, cotangent, mixed, out_weight, flat(far_weight), packed, in_bias,
        ff_in.reshape(slices, rows, hidden_part), ff_out.reshape(slices, rows, model), flat(far_in), flat(far_out),
    )
    grad_mixed, (ff_in_part, ff_out_part, out_weight_part, sums, in_bias_part) = rest[:4], rest[4:]
    paired = [part.reshape(units // 2, UNIT, width) for part in grad_mixed]
    plane = lambda array: array.reshape((shards, 2, 2, 2) + array.shape[2:])
    grads, probe_grad, *parts = backward(
        seg_lengths, qkv, paired, logsum, values, probes, key_states, key_end, state_rows, plane(ff_in_part),
        plane(ff_out_part), plane(out_weight_part), heads,
    )
    for bit in outer:
        parts = [added(part, exchange(part, "dp", bit)) for part in parts]
    input_grad, whole_in, whole_out, whole_weight, whole_qkv, shared, owned = tail(
        grads, first_cols, flat_a, flat_b, grad_residual, inputs, packed, parts, sums, in_bias_part, probe_grad,
        outer, heads,
    )
    ff_in_sum, ff_out_sum, out_weight_sum, qkv_weight_sum = finish(
        whole_in.reshape(model, hidden_part), whole_out.reshape(hidden_part, model),
        whole_weight.reshape((slices,) + whole_weight.shape[3:]), whole_qkv.reshape(model, 3 * width), width,
    )
    return (
        outputs, input_grad, shared[0], shared[1], jnp.transpose(qkv_weight_sum, (2, 0, 1)),
        owned[8].reshape(3, LANES)[:, :width], out_weight_sum, shared[2], owned[:heads, :BASIS],
        owned[heads : 2 * heads, :BASIS], shared[3], shared[4], ff_in_sum, owned[9, :hidden_part], ff_out_sum, shared[5],
    )


def solution(mesh):
    rows, whole = P(("dp", "head"), None), P()
    return jax.shard_map(
        local,
        mesh=mesh,
        in_specs=(
            rows, P("dp", None), whole, whole, P(None, None, "head"), P(None, "head"), P("head", None), whole,
            P("head", None), P("head", None), whole, whole, P(None, "head"), P("head"), P("head", None), whole, rows,
        ),
        out_specs=(
            rows, rows, whole, whole, P(None, None, "head"), P(None, "head"), P("head", None), whole,
            P("head", None), P("head", None), whole, whole, P(None, "head"), P("head"), P("head", None), whole,
        ),
        check_vma=False,
    )
```

```python
import functools
import math

import jax
import jax.numpy as jnp
import ml_dtypes
import numpy as np
from jax import lax
from jax.experimental import pallas as pl
from jax.experimental.pallas import tpu as pltpu
from jax.sharding import PartitionSpec as P

HEAD_DIM = 64
BASIS = 512
UNIT = 256
LANES = 256
TAU = 0.75
RIDGE = 0.5
EPSILON = 1e-05
MESH = pl.DeviceIdType.MESH
SPREAD = 1.0 / 64.0
WIDTH = 1.0 / BASIS
LIVE = BASIS // 2
HIGHEST = lax.Precision.HIGHEST
F32 = jnp.float32
BF16 = jnp.bfloat16


def split_table(table):
    high = table.astype(np.float32).astype(ml_dtypes.bfloat16)
    low = (table.astype(np.float32) - high.astype(np.float32)).astype(ml_dtypes.bfloat16)
    return high, low


@functools.lru_cache(maxsize=None)
def basis_tables():
    centres = np.arange(BASIS) / (BASIS - 1)
    apart = centres[:, None] - centres[None, :]
    gram = np.exp(-apart * apart / (4.0 * WIDTH * WIDTH)) + RIDGE * np.eye(BASIS)
    solve = np.linalg.inv(gram)
    samples = (np.arange(BASIS) + 0.5) / BASIS
    near_gap = TAU * samples[:, None] - centres[None, :]
    far_gap = samples[:, None] - centres[None, :]
    near = np.exp(-near_gap * near_gap / (2.0 * WIDTH * WIDTH))
    far = np.exp(-far_gap * far_gap / (2.0 * WIDTH * WIDTH))
    contract = (near.T @ far) * (TAU / (BASIS * WIDTH * math.sqrt(math.pi)))
    joined = np.concatenate([solve @ contract, solve[:, LIVE:]], axis=1)
    high, low = split_table(joined)
    forward = np.concatenate([high, high, low], axis=1)
    backward = np.ascontiguousarray(high.T)
    return forward, backward


def term_scale(units):
    return (1.0 - TAU) / (WIDTH * math.sqrt(math.pi) * UNIT) / units.astype(F32)


def split3(value):
    high = value.astype(BF16)
    low = (value - high.astype(F32)).astype(BF16)
    return jnp.concatenate([high, low, high], axis=0)


def dot(a, b, contract=((1,), (0,)), precision=None):
    return lax.dot_general(a, b, (contract, ((), ())), precision=precision, preferred_element_type=F32)


def head_rows(heads, width):
    row = lax.broadcasted_iota(jnp.int32, (8, width), 0)
    lane = lax.broadcasted_iota(jnp.int32, (8, width), 1) // HEAD_DIM
    return ((row == lane) | (row == lane + heads)) & (lane < heads)


def read_parts(logits, heads):
    location = 1.0 / (1.0 + jnp.exp(-logits))
    variance = (jnp.maximum(logits, 0.0) + jnp.log1p(jnp.exp(-jnp.abs(logits)))) * SPREAD + WIDTH * WIDTH
    return location[:heads], variance[heads : 2 * heads]


def place_of(index, length):
    return TAU + (1.0 - TAU) * (index.astype(F32) + 0.5) / (length.astype(F32) * UNIT)


def split_rows(value):
    high = value.astype(BF16)
    rest = value - high.astype(F32)
    mid = rest.astype(BF16)
    return high, mid, (rest - mid.astype(F32)).astype(BF16)


def three_pass(left, right_high, right_low, contract=((1,), (0,))):
    high = left.astype(BF16)
    low = (left - high.astype(F32)).astype(BF16)
    return dot(high, right_high, contract) + dot(low, right_high, contract) + dot(high, right_low, contract)


def advance_values(table, value):
    return dot(table[:BASIS, :BASIS], value.astype(BF16))


def logits_of(probes, query):
    parts = dot(jnp.concatenate(split_rows(probes), axis=0), query, ((1,), (1,)))
    return parts[0:8] + parts[8:16] + parts[16:24]


def segments_of(lengths, run, units):
    sizes = [lengths[0, run * units + s] // UNIT for s in range(units)]
    ends, total = [], 0
    for size in sizes:
        total = total + size
        ends.append(total)
    starts, spans, orders = [], [], []
    for b in range(units):
        start, span, order = 0, 0, 0
        for size, end in zip(sizes, ends):
            inside = (end > b) & (end - size <= b)
            start = start + jnp.where(inside, end - size, 0)
            span = span + jnp.where(inside, size, 0)
            order = order + jnp.where((end <= b) & (size > 0), 1, 0)
        starts.append(start)
        spans.append(span)
        orders.append(order)
    return starts, spans, orders


def other_of(index, distance):
    bit = 1
    while bit <= distance:
        if distance & bit:
            index = index + bit - 2 * bit * ((index // bit) % 2)
        bit *= 2
    return index


class Hops:
    def __init__(self, send, recv):
        self.send, self.recv, self.used = send, recv, 0

    def start(self, source, target, axis, bit):
        copy = pltpu.make_async_remote_copy(
            src_ref=source,
            dst_ref=target,
            send_sem=self.send.at[self.used],
            recv_sem=self.recv.at[self.used],
            device_id={axis: other_of(lax.axis_index(axis), bit)},
            device_id_type=MESH,
        )
        self.used += 1
        copy.start()
        return copy


def greet(neighbours):
    barrier = pltpu.get_barrier_semaphore()
    for axis, bit in neighbours:
        pl.semaphore_signal(
            barrier, inc=1, device_id={axis: other_of(lax.axis_index(axis), bit)}, device_id_type=MESH
        )
    pl.semaphore_wait(barrier, len(neighbours))


def set_out(pairs, sems, first):
    copies = [pltpu.make_async_copy(a, b, sems.at[first + k]) for k, (a, b) in enumerate(pairs)]
    for copy in copies:
        copy.start()
    return copies


def forward_kernel(
    heads, seg_lengths, source, packed, weight, out_weight, table, ff_in, ff_out,
    qkv_out, first_cols_out, flat_a_out, flat_b_out, logsum, values, probes, key_states, key_end, rows,
    mixed_0, mixed_1, mixed_2, mixed_3, in_bias, far_in, far_out, far_weight,
    qkv, first_rows, first_cols, flats, near, far, far_flat, small, far_row, bias_row, weight_mine, memory, sums, value_states, carried, value_ends, value_ins,
    projs, proj_ins, cols, keys, discrete, mixed, mixed_in, send, recv, local_sems,
):
    own_rows, model = source.shape
    width = heads * HEAD_DIM
    units = qkv.shape[1]
    half = units // 2
    root = 1.0 / math.sqrt(HEAD_DIM)
    z = lax.axis_index("head")
    flip, run = (z % 2) * half, z // 2
    place = lax.axis_index("dp") % 8
    y, x, c = place // 4, (place // 2) % 2, place % 2
    slice_rows = model // 8
    at = lambda b: (b + flip) % units
    starts, lengths, orders = segments_of(seg_lengths, run, units)
    greet((("head", 1), ("head", 2), ("head", 3), ("dp", 1), ("dp", 2), ("dp", 4)))
    hops = Hops(send, recv)
    started = []

    def go(*args):
        started.append(hops.start(*args))
        return started[-1]

    part_rows, part_cols = far.shape[3:]
    mine = weight.at[
        pl.ds(pl.multiple_of((2 * y + x) * part_rows, 16), part_rows),
        pl.ds(pl.multiple_of(c * part_cols, 128), part_cols),
    ]
    small[...] = packed[0:16]
    bias_row[...] = jnp.broadcast_to(packed[22:23], bias_row.shape)
    narrow = width // 8
    chosen = jnp.zeros((narrow, model), F32)
    for j in range(8):
        chosen += jnp.where(place == j, out_weight[j * narrow : (j + 1) * narrow].astype(F32), 0.0)
    spare = jnp.zeros((weight_mine.shape[0] - narrow, model), F32)
    weight_mine[...] = jnp.concatenate([chosen, spare], axis=0).astype(BF16)
    slice_copy = go(mine, far.at[y, x, c], "head", 2)
    small_copy = go(small, far_row, "head", 2)
    row_copies = []
    for k in range(half):
        part = slice(k * UNIT, (k + 1) * UNIT)
        value = source[part].astype(F32)
        centred = value - jnp.mean(value, axis=-1, keepdims=True)
        factor = lax.rsqrt(jnp.mean(centred * centred, axis=-1, keepdims=True) + EPSILON)
        first_rows[part] = (centred * factor * packed[16:17] + packed[17:18]).astype(BF16)
        row_copies.append(go(first_rows.at[part], near.at[part], "head", 1))
    in_mine = ff_in.at[pl.ds(pl.multiple_of(place * slice_rows, 16), slice_rows)]
    out_mine = ff_out.at[pl.ds(pl.multiple_of(place * slice_rows, 16), slice_rows)]
    gathers = ((far_in, 2, 4), (far_weight, 2, 4), (far_out, 4, 2))
    stage = {}

    def send_chunk(r):
        stage[r] = [
            go(in_mine, far_in.at[r - 1, y, x, c], "head", r),
            go(weight_mine, far_weight.at[r - 1, y, x, c], "head", r),
            go(out_mine, far_out.at[r - 1, y, x, c], "head", r),
        ]

    def advance(r, step):
        for copy in stage[r]:
            copy.wait_recv()
        stage[r] = []
        for array, first, second in gathers:
            block = array.at[r - 1]
            if step == 1:
                part, bit = block.at[y, x, c], first
            elif step == 2:
                part, bit = (block.at[y, :, c] if first == 2 else block.at[:, x, c]), second
            else:
                part, bit = block.at[:, :, c], 1
            stage[r].append(go(part, part, "dp", bit))

    send_chunk(1)
    send_chunk(2)
    send_chunk(3)
    in_bias[0] = bias_row[...]
    bias_copies = [go(bias_row, in_bias.at[r], "head", r) for r in (1, 2, 3)]

    slice_copy.wait_recv()
    x_copy = go(far.at[y, x, c], far.at[y, x, c], "dp", 2)

    def widen(k, read):
        for i in range(3):
            flats[k, i * LANES : i * LANES + width] = read(slice(i * width, (i + 1) * width))
            flats[k, i * LANES + width : (i + 1) * LANES] = jnp.zeros((LANES - width, model), BF16)

    def project(k, unit, shift):
        span = slice(unit * UNIT, (unit + 1) * UNIT)
        qkv[k, unit] = (dot(first_rows[span], flats[k], ((1,), (1,))) + shift).astype(BF16)

    widen(0, lambda span: weight[span])
    for unit in range(half):
        project(0, unit, small[0:1])
    x_copy.wait_recv()
    y_copy = go(far.at[y, :, c], far.at[y, :, c], "dp", 4)
    first_cols[:, :own_rows] = first_rows[:own_rows].astype(F32).T.astype(BF16)
    y_copy.wait_recv()
    core_copy = go(far.at[:, :, c], far.at[:, :, c], "dp", 1)
    small_copy.wait_recv()
    for k, copy in enumerate(row_copies):
        copy.wait_recv()
        part = slice(k * UNIT, (k + 1) * UNIT)
        first_rows[own_rows + k * UNIT : own_rows + (k + 1) * UNIT] = near[part]
        project(0, half + k, small[0:1])

    advance(1, 1)
    first_cols[:, own_rows:] = near[...].astype(F32).T.astype(BF16)
    core_copy.wait_recv()
    for i in range(8):
        row, col = (i // 2) * part_rows, (i % 2) * part_cols
        far_flat[row : row + part_rows, col : col + part_cols] = far[i // 4, (i // 2) % 2, i % 2]
    widen(1, lambda span: far_flat[span])
    for unit in range(units):
        project(1, unit, far_row[0:1])
    saved = set_out(
        [(qkv, qkv_out), (first_cols, first_cols_out), (flats.at[0], flat_a_out), (flats.at[1], flat_b_out)],
        local_sems, 0,
    )

    def probe_of(k):
        return jnp.where(k == 0, small[1:9, :BASIS], far_row[1:9, :BASIS])

    mask = head_rows(heads, LANES)

    def first_state(k, carry):
        memory[k] = jnp.zeros(memory.shape[1:], F32)
        row = probe_of(k)
        rows[k, 0:8] = row
        wide = 2 * (BASIS + LIVE)
        for i in range(1, 4):
            row = three_pass(row, table[:, :BASIS], table[:, wide : wide + BASIS])
            rows[k, 8 * i : 8 * i + 8] = row
        return carry

    lax.fori_loop(0, 2, first_state, 0)

    def state(b, k, carry):
        start, length = starts[b], lengths[b]
        now = memory[k]
        value_states[k, b] = now[:, LANES:]
        key_states[k, b] = now[:, :LANES].astype(BF16)
        if b > 0:
            probes[k, b] = jnp.where(mask, dot(rows[k, 0:8], now[:, :LANES], precision=HIGHEST), 0.0)
        else:
            probes[k, b] = jnp.zeros((8, LANES), F32)
        token = lax.broadcasted_iota(jnp.int32, (LIVE, UNIT), 1) + (b - start) * UNIT
        centre = (lax.broadcasted_iota(jnp.int32, (LIVE, UNIT), 0) + LIVE).astype(F32) / (BASIS - 1)
        gap = place_of(token, length) - centre
        psi = jnp.exp(gap * gap * (-0.5 / (WIDTH * WIDTH)))
        psi_high = psi.astype(BF16)
        psi_low = (psi - psi_high.astype(F32)).astype(BF16)
        pairs = qkv[k, at(b), :, LANES : 3 * LANES]
        exact = dot(psi_high, pairs[:, :LANES]) + dot(psi_low, pairs[:, :LANES])
        fresh = jnp.concatenate([exact, dot(psi_high, pairs[:, LANES:])], axis=1)
        gathered = fresh if b == 0 else jnp.where(start == b, 0.0, sums[k]) + fresh
        sums[k] = gathered
        stacked = jnp.concatenate([now, gathered * term_scale(length)], axis=0)
        later = jnp.concatenate(
            [
                dot(table[...], split3(stacked[:, :LANES])),
                dot(table[:, : BASIS + LIVE], stacked[:, LANES:].astype(BF16)),
            ],
            axis=1,
        )
        memory[k] = jnp.where(start + length == b + 1, later, now)
        return carry

    def end_state(k, carry):
        key = memory[k, :, :LANES]
        key_end[k] = key
        value_ends[k] = memory[k, :, LANES : LANES + width].T.astype(BF16)
        seen = dot(rows[k], key, precision=HIGHEST)
        for i in range(4):
            projs[k, 8 * i : 8 * i + 8] = jnp.where(mask, seen[8 * i : 8 * i + 8], 0.0)
        return carry

    def attend(b, k, carry):
        cols[k, :, b * UNIT : (b + 1) * UNIT] = qkv[k, at(b), :, 2 * LANES : 3 * LANES].astype(F32).T.astype(BF16)
        keys[k, b * UNIT : (b + 1) * UNIT] = qkv[k, at(b), :, LANES : 2 * LANES]
        query = qkv[k, at(b), :, 0:LANES].astype(F32) * root
        lane_head = lax.broadcasted_iota(jnp.int32, (UNIT, LANES), 1) // HEAD_DIM
        causal = lax.broadcasted_iota(jnp.int32, (UNIT, UNIT), 0) <= lax.broadcasted_iota(
            jnp.int32, (UNIT, UNIT), 1
        )
        away = [jnp.where(starts[b] <= j, 0.0, 1e30) for j in range(b)] + [0.0]
        owns = jnp.concatenate([jnp.where(lane_head == h, query, 0.0).astype(BF16) for h in range(heads)], axis=0)
        seen = (b + 1) * UNIT
        products = dot(keys[k, :seen], owns, ((1,), (1,)))
        for h in range(heads):
            scores = [products[j * UNIT : (j + 1) * UNIT, h * UNIT : (h + 1) * UNIT] for j in range(b + 1)]
            scores[b] = jnp.where(causal, scores[b], -1e30)
            highest = functools.reduce(
                jnp.maximum, [jnp.max(s, axis=0, keepdims=True) - away[j] for j, s in enumerate(scores)]
            )
            weights = [jnp.exp(s - (highest + away[j])) for j, s in enumerate(scores)]
            total = sum(jnp.sum(w, axis=0, keepdims=True) for w in weights)
            span = slice(h * HEAD_DIM, (h + 1) * HEAD_DIM)
            part = dot(cols[k, span, :seen], jnp.concatenate([w.astype(BF16) for w in weights], axis=0))
            discrete[k, b, span] = part * (1.0 / total)
            logsum[k, b, h : h + 1] = highest + jnp.log(total)
        return carry

    def seen_value(k, carry):
        incoming = jnp.where(run > 0, value_ins[k].astype(F32), 0.0).T
        carried[:, :width] = incoming
        carried[:, width:] = jnp.zeros((BASIS, LANES - width), F32)
        for b in range(units):
            if b > 0:
                carried[...] = jnp.where(starts[b] == b, advance_values(table, carried[...]), carried[...])
            values[k, b] = (value_states[k, b] + carried[...]).astype(BF16)
            gained = jnp.zeros((8, LANES), F32)
            for i in range(4):
                gained += jnp.where((orders[b] == i) & (run > 0), proj_ins[k, 8 * i : 8 * i + 8], 0.0)
            probes[k, b] = (probes[k, b] + gained) * root
        return carry

    def read(rel, k, carry):
        b = at(rel)
        query = qkv[k, rel, :, 0:LANES]
        logits = logits_of(probes[k, b], query)
        location, variance = read_parts(logits, heads)
        fall = -0.5 / variance
        peak = WIDTH * lax.rsqrt(variance)
        centres = lax.broadcasted_iota(jnp.int32, (BASIS, UNIT), 0).astype(F32) / (BASIS - 1)
        value_cols = values[k, b].astype(F32).T.astype(BF16)
        parts = []
        for h in range(heads):
            gap = centres - location[h : h + 1]
            density = jnp.exp(gap * gap * fall[h : h + 1]).astype(BF16)
            span = slice(h * HEAD_DIM, (h + 1) * HEAD_DIM)
            parts.append(discrete[k, b, span] + dot(value_cols[span], density) * peak[h : h + 1])
        mixed[k, rel] = jnp.concatenate(parts, axis=0).T.astype(BF16)
        return carry

    advance(1, 2)
    state_copies = []
    for k in range(2):
        for b in range(units):
            state(b, k, 0)
        end_state(k, 0)
        state_copies.append([
            go(value_ends.at[k], value_ins.at[1 - k], "head", 2), go(projs.at[k], proj_ins.at[1 - k], "head", 2)
        ])
        if k == 0:
            advance(2, 1)
            advance(3, 1)
        if k == 1:
            advance(1, 3)
    for b in range(units):
        lax.fori_loop(0, 2, functools.partial(attend, b), 0)
        if b == 0:
            advance(2, 2)
        if b == 2:
            advance(3, 2)
        if b == 3:
            advance(2, 3)
    mixed_copies = [None, None]
    for k in (1, 0):
        for copy in state_copies[1 - k]:
            copy.wait_recv()
        seen_value(k, 0)
        read(2, k, 0)
        read(3, k, 0)
        mixed_copies[k] = go(mixed.at[k, half:], mixed_in.at[k], "head", 1)
        if k == 1:
            advance(3, 3)
    lax.fori_loop(0, 2, functools.partial(read, 0), 0)
    lax.fori_loop(0, 2, functools.partial(read, 1), 0)
    mixed_0[...] = mixed[0, :half].reshape(own_rows, width)
    mixed_2[...] = mixed[1, :half].reshape(own_rows, width)
    for copy in mixed_copies:
        copy.wait_recv()
    mixed_1[...] = mixed_in[0].reshape(own_rows, width)
    mixed_3[...] = mixed_in[1].reshape(own_rows, width)
    for copy in bias_copies + stage[1] + stage[2] + stage[3]:
        copy.wait_recv()
    for copy in started:
        copy.wait_send()
    for copy in saved:
        copy.wait()


def forward(seg_lengths, source, packed, weight, out_weight, ff_in, ff_out, heads):
    own_rows, model = source.shape
    units = 2 * own_rows // UNIT
    width = heads * HEAD_DIM
    hidden_part = ff_in.shape[1]
    rows = model // 8
    spaced = -(-width // 8 // 16) * 16
    table = jnp.asarray(basis_tables()[0])
    vmem, anywhere = pl.BlockSpec(memory_space=pltpu.VMEM), pl.BlockSpec(memory_space=pl.ANY)
    shape = jax.ShapeDtypeStruct
    hops = 2 + units // 2 + 3 + 3 * 3 * 4 + 3 + 4 + 2
    return pl.pallas_call(
        functools.partial(forward_kernel, heads),
        in_specs=[pl.BlockSpec(memory_space=pltpu.SMEM)] + [vmem] * 5 + [anywhere] * 2,
        out_specs=[anywhere] * 4 + [vmem] * 11 + [anywhere] * 3,
        out_shape=[
            shape((2, units, UNIT, 3 * LANES), BF16),
            shape((model, 2 * own_rows), BF16),
            shape((3 * LANES, model), BF16),
            shape((3 * LANES, model), BF16),
            shape((2, units, 8, UNIT), F32),
            shape((2, units, BASIS, LANES), BF16),
            shape((2, units, 8, LANES), F32),
            shape((2, units, BASIS, LANES), BF16),
            shape((2, BASIS, LANES), F32),
            shape((2, 32, BASIS), F32),
        ] + [shape((own_rows, width), BF16)] * 4 + [
            shape((4, 8, hidden_part), F32),
            shape((3, 2, 2, 2, rows, hidden_part), BF16),
            shape((3, 2, 2, 2, rows, model), BF16),
            shape((3, 2, 2, 2, spaced, model), BF16),
        ],
        scratch_shapes=[
            pltpu.VMEM((2, units, UNIT, 3 * LANES), BF16),
            pltpu.VMEM((2 * own_rows, model), BF16),
            pltpu.VMEM((model, 2 * own_rows), BF16),
            pltpu.VMEM((2, 3 * LANES, model), BF16),
            pltpu.VMEM((own_rows, model), BF16),
            pltpu.VMEM((2, 2, 2, 3 * width // 4, model // 2), BF16),
            pltpu.VMEM((3 * width, model), BF16),
            pltpu.VMEM((16, 3 * LANES), F32),
            pltpu.VMEM((16, 3 * LANES), F32),
            pltpu.VMEM((8, hidden_part), F32),
            pltpu.VMEM((spaced, model), BF16),
            pltpu.VMEM((2, BASIS, 2 * LANES), F32),
            pltpu.VMEM((2, LIVE, 2 * LANES), F32),
            pltpu.VMEM((2, units, BASIS, LANES), F32),
            pltpu.VMEM((BASIS, LANES), F32),
            pltpu.VMEM((2, width, BASIS), BF16),
            pltpu.VMEM((2, width, BASIS), BF16),
            pltpu.VMEM((2, 32, LANES), F32),
            pltpu.VMEM((2, 32, LANES), F32),
            pltpu.VMEM((2, LANES, units * UNIT), BF16),
            pltpu.VMEM((2, units * UNIT, LANES), BF16),
            pltpu.VMEM((2, units, width, UNIT), F32),
            pltpu.VMEM((2, units, UNIT, width), BF16),
            pltpu.VMEM((2, units // 2, UNIT, width), BF16),
            pltpu.SemaphoreType.DMA((hops,)),
            pltpu.SemaphoreType.DMA((hops,)),
            pltpu.SemaphoreType.DMA((4,)),
        ],
        compiler_params=pltpu.CompilerParams(
            collective_id=1, has_side_effects=True, vmem_limit_bytes=60 << 20
        ),
        name="forward",
    )(seg_lengths, source, packed, weight, out_weight, table, ff_in, ff_out)


def whole(shape):
    return pl.BlockSpec(shape, lambda i: (0,) * len(shape))


def finish_kernel(given_in, given_out, given_weight, given_qkv, grad_in, grad_out, grad_weight, grad_qkv):
    step = pl.program_id(0)
    grad_in[...] = given_in[...].astype(F32)
    grad_out[...] = given_out[...].astype(F32)
    width = grad_qkv.shape[1]
    turned = given_qkv[...].astype(F32).T
    for i in range(3):

        @pl.when(step == i)
        def _():
            grad_qkv[0] = turned[i * width : (i + 1) * width]

    @pl.when(step == 0)
    def _():
        narrow = grad_weight.shape[0] // given_weight.shape[0]
        for j in range(given_weight.shape[0]):
            grad_weight[j * narrow : (j + 1) * narrow] = given_weight[j].astype(F32)[:narrow]


def finish(given_in, given_out, given_weight, given_qkv, width):
    model, columns = given_in.shape
    hidden_part = given_out.shape[0]
    return pl.pallas_call(
        finish_kernel,
        grid=(3,),
        in_specs=[
            pl.BlockSpec((model // 3, columns), lambda i: (i, 0)),
            pl.BlockSpec((hidden_part // 3, model), lambda i: (i, 0)),
            pl.BlockSpec(given_weight.shape, lambda i: (0, 0, 0)),
            pl.BlockSpec(given_qkv.shape, lambda i: (0, 0)),
        ],
        out_specs=[
            pl.BlockSpec((model // 3, columns), lambda i: (i, 0)),
            pl.BlockSpec((hidden_part // 3, model), lambda i: (i, 0)),
            pl.BlockSpec((width, model), lambda i: (0, 0)),
            pl.BlockSpec((1, width, model), lambda i: (i, 0, 0)),
        ],
        out_shape=[
            jax.ShapeDtypeStruct((model, columns), F32), jax.ShapeDtypeStruct((hidden_part, model), F32),
            jax.ShapeDtypeStruct((width, model), F32), jax.ShapeDtypeStruct((3, width, model), F32),
        ],
        compiler_params=pltpu.CompilerParams(vmem_limit_bytes=62 << 20),
        name="finish",
    )(given_in, given_out, given_weight, given_qkv)


def middle_kernel(
    source, cotangent, mixed_0, mixed_1, mixed_2, mixed_3, own_weight, far_weight, vectors, in_bias, own_in, own_out,
    far_in, far_out, outputs, grad_residual, grad_mixed_0, grad_mixed_1, grad_mixed_2, grad_mixed_3, grad_in, grad_out,
    grad_out_weight, sums, grad_in_bias,
    residual, inverse, second, second_cols, total, grad_second, in_now, out_now, out_weight,
):
    r = pl.program_id(0)
    slices, rows = own_in.shape[0], own_in.shape[1]
    model = source.shape[1]
    hidden_part = own_in.shape[2]
    out_bias, gain, shift, last_bias = (vectors[k : k + 1] for k in range(18, 22))

    @pl.when(r == 0)
    def _():
        value = source[...].astype(F32) + out_bias
        out_weight[0] = own_weight[...]
        narrow = own_weight.shape[0] // slices
        for k in range(far_weight.shape[0]):
            parts = [far_weight[k, j].astype(F32)[:narrow] for j in range(slices)]
            out_weight[k + 1] = jnp.concatenate(parts, axis=0).astype(BF16)
        for k, mixed in enumerate((mixed_0, mixed_1, mixed_2, mixed_3)):
            value += dot(mixed[...], out_weight[k])
        residual[...] = value
        centred = value - jnp.mean(value, axis=-1, keepdims=True)
        factor = lax.rsqrt(jnp.mean(centred * centred, axis=-1, keepdims=True) + EPSILON)
        inverse[...] = factor
        normal = centred * factor
        grad_residual[...] = normal
        rounded = (normal * gain + shift).astype(BF16)
        second[...] = rounded
        second_cols[...] = rounded.astype(F32).T.astype(BF16)
        total[...] = jnp.zeros_like(total)
        grad_second[...] = jnp.zeros_like(grad_second)
        grad_in_bias[...] = jnp.zeros_like(grad_in_bias)
        for j in range(slices):
            in_now[j * rows : (j + 1) * rows] = own_in[j]
            out_now[j * rows : (j + 1) * rows] = own_out[j]

    @pl.when(r > 0)
    def _():
        for j in range(slices):
            in_now[j * rows : (j + 1) * rows] = far_in[0, j]
            out_now[j * rows : (j + 1) * rows] = far_out[0, j]

    half = hidden_part
    for t in range(1):
        span = slice(t * half, (t + 1) * half)
        hidden = dot(second[...], in_now[:, span]) + in_bias[r, 0:1, span]
        cube = hidden * hidden
        root = math.sqrt(2.0 / math.pi)
        bent = jnp.tanh(hidden * (root + (root * 0.044715) * cube))
        lifted = 0.5 + 0.5 * bent
        activation = (hidden * lifted).astype(BF16)
        slope = lifted + hidden * ((0.5 - 0.5 * bent * bent) * (root + (3.0 * root * 0.044715) * cube))
        total[...] += dot(activation, out_now[span])
        given = dot(cotangent[...], out_now[span], ((1,), (1,)))
        grad_hidden = (given * slope).astype(BF16)
        grad_second[...] += dot(grad_hidden, in_now[:, span], ((1,), (1,)))
        grad_in_bias[pl.ds(r, 1), span] = jnp.sum(grad_hidden.astype(F32), axis=0, keepdims=True)
        part = dot(activation, cotangent[...], ((0,), (0,))).astype(BF16)
        per = half // rows
        for k in range(per):
            grad_out[0, t * per + k] = part[k * rows : (k + 1) * rows]
        part = dot(second_cols[...], grad_hidden).astype(BF16)
        for j in range(slices):
            grad_in[0, j, :, span] = part[j * rows : (j + 1) * rows]

    @pl.when(r == pl.num_programs(0) - 1)
    def _():
        given = cotangent[...].astype(F32)
        outputs[...] = (residual[...] + total[...] + last_bias).astype(BF16)
        normal = grad_residual[...]
        grad = grad_second[...]
        scaled = grad * gain
        value = given + inverse[...] * (
            scaled
            - jnp.mean(scaled, axis=-1, keepdims=True)
            - normal * jnp.mean(scaled * normal, axis=-1, keepdims=True)
        )
        sums[0:1] = jnp.sum(value, axis=0, keepdims=True)
        sums[1:2] = jnp.sum(grad * normal, axis=0, keepdims=True)
        sums[2:3] = jnp.sum(grad, axis=0, keepdims=True)
        sums[3:4] = jnp.sum(given, axis=0, keepdims=True)
        sums[4:8] = jnp.zeros((4, model), F32)
        grad_residual[...] = value
        rounded = value.astype(BF16)
        grads = (grad_mixed_0, grad_mixed_1, grad_mixed_2, grad_mixed_3)
        for k, mixed in enumerate((mixed_0, mixed_1, mixed_2, mixed_3)):
            grads[k][...] = dot(rounded, out_weight[k], ((1,), (1,))).astype(BF16)
            product = dot(mixed[...], rounded, ((0,), (0,)))
            narrow = product.shape[0] // slices
            spare = jnp.zeros((grad_out_weight.shape[2] - narrow, model), F32)
            for j in range(slices):
                part = jnp.concatenate([product[j * narrow : (j + 1) * narrow], spare], axis=0)
                grad_out_weight[k, j] = part.astype(BF16)


def middle(source, cotangent, mixed, out_weight, far_weight, vectors, in_bias, own_in, own_out, far_in, far_out):
    own_rows, model = source.shape
    shards = far_in.shape[0] + 1
    slices, rows, hidden_part = own_in.shape
    narrow = mixed[0].shape
    far = pl.BlockSpec((1,) + own_in.shape, lambda r: (jnp.maximum(r - 1, 0), 0, 0, 0))
    part = pl.BlockSpec((1,) + own_in.shape, lambda r: (r, 0, 0, 0))
    macs = own_rows * model * (6 * shards * hidden_part + 3 * model)
    return pl.pallas_call(
        middle_kernel,
        grid_spec=pltpu.PrefetchScalarGridSpec(
            num_scalar_prefetch=0,
            grid=(shards,),
            in_specs=[whole(source.shape)] * 2 + [whole(narrow)] * 4 + [
                whole(out_weight.shape), whole(far_weight.shape), whole(vectors.shape), whole(in_bias.shape), whole(own_in.shape),
                whole(own_out.shape), far, far,
            ],
            out_specs=[whole(source.shape)] * 2 + [whole(narrow)] * 4 + [
                part, part, whole((shards,) + far_weight.shape[1:]), whole((8, model)), whole((shards, hidden_part))
            ],
            scratch_shapes=[
                pltpu.VMEM((own_rows, model), F32),
                pltpu.VMEM((own_rows, 1), F32),
                pltpu.VMEM((own_rows, model), BF16),
                pltpu.VMEM((model, own_rows), BF16),
                pltpu.VMEM((own_rows, model), F32),
                pltpu.VMEM((own_rows, model), F32),
                pltpu.VMEM((model, hidden_part), BF16),
                pltpu.VMEM((hidden_part, model), BF16),
                pltpu.VMEM((shards,) + narrow[1:] + (model,), BF16),
            ],
        ),
        out_shape=[
            jax.ShapeDtypeStruct(source.shape, BF16),
            jax.ShapeDtypeStruct(source.shape, F32),
        ] + [jax.ShapeDtypeStruct(narrow, BF16)] * 4 + [
            jax.ShapeDtypeStruct((shards, slices, rows, hidden_part), BF16),
            jax.ShapeDtypeStruct((shards, slices, rows, hidden_part), BF16),
            jax.ShapeDtypeStruct((shards,) + far_weight.shape[1:], BF16),
            jax.ShapeDtypeStruct((8, model), F32),
            jax.ShapeDtypeStruct((shards, hidden_part), F32),
        ],
        compiler_params=pltpu.CompilerParams(vmem_limit_bytes=60 << 20),
        cost_estimate=pl.CostEstimate(
            flops=2 * macs, bytes_accessed=30 << 20, transcendentals=own_rows * shards * hidden_part
        ),
        name="middle",
    )(source, cotangent, *mixed, out_weight, far_weight, vectors, in_bias, own_in, own_out, far_in, far_out)


def added(a, b):
    return (a.astype(F32) + b.astype(F32)).astype(BF16)


def backward_kernel(
    heads, seg_lengths, qkv, gm_0, gm_1, gm_2, gm_3, logsum, values, probes, key_states, key_end, rows, table,
    grad_in, grad_out, grad_weight, out, probe_grad, slice_in, slice_out, slice_weight,
    given, query_grad, memory_grad, row_grad, value_carried, value_back, value_in, row_back, row_in, carried, spread, key_grad, value_grad, cols, keys, vals,
    keep_in, keep_out, keep_weight, core_in, core_out, core_weight, one_in, one_out, one_weight,
    two_in, two_out, two_weight, z_in, z_out, z_weight, send, recv, local_sems,
):
    units = qkv.shape[1]
    half = units // 2
    width = heads * HEAD_DIM
    root = 1.0 / math.sqrt(HEAD_DIM)
    z = lax.axis_index("head")
    flip, run = (z % 2) * half, z // 2
    place = lax.axis_index("dp") % 8
    y, x, c = place // 4, (place // 2) % 2, place % 2
    at = lambda b: (b + flip) % units
    starts, lengths, orders = segments_of(seg_lengths, run, units)
    greet((("head", 1), ("head", 2), ("head", 3), ("dp", 1), ("dp", 2), ("dp", 4)))
    hops = Hops(send, recv)
    started = []

    def go(*args):
        started.append(hops.start(*args))
        return started[-1]

    given_copies = [go(gm_1, given.at[0, half:], "head", 1), go(gm_3, given.at[1, half:], "head", 1)]
    sums = (
        (grad_in, keep_in, core_in, one_in, two_in, z_in, True),
        (grad_weight, keep_weight, core_weight, one_weight, two_weight, z_weight, True),
        (grad_out, keep_out, core_out, one_out, two_out, z_out, False),
    )
    stage, local_copies = {}, {}
    for i, r in enumerate((2, 1, 3, 0)):
        stage[r], local_copies[r] = [], []
        for n, (term, keep, core, _, _, _, _) in enumerate(sums):
            stage[r].append(go(term.at[r, :, :, 1 - c], core.at[r], "dp", 1))
            copy = pltpu.make_async_copy(term.at[r, :, :, c], keep.at[r], local_sems.at[3 * i + n])
            copy.start()
            local_copies[r].append(copy)

    def first_hop(r):
        for n, (_, keep, core, one, _, _, along_x) in enumerate(sums):
            local_copies[r][n].wait()
            stage[r][n].wait_recv()
            keep[r] = added(keep[r], core[r])
            part = keep.at[r, :, 1 - x] if along_x else keep.at[r, 1 - y]
            stage[r][n] = go(part, one.at[r], "dp", 2 if along_x else 4)

    def second_hop(r):
        for n, (_, keep, _, one, two, _, along_x) in enumerate(sums):
            stage[r][n].wait_recv()
            kept = keep[r, :, x] if along_x else keep[r, y]
            one[r] = added(kept, one[r])
            part = one.at[r, 1 - y] if along_x else one.at[r, 1 - x]
            stage[r][n] = go(part, two.at[r], "dp", 4 if along_x else 2)

    def third_hop(r):
        for n, (_, _, _, one, two, far, along_x) in enumerate(sums):
            stage[r][n].wait_recv()
            kept = one[r, y] if along_x else one[r, x]
            two[r] = added(kept, two[r])
            if r:
                stage[r][n] = go(two.at[r], far.at[r - 1], "head", r)

    for k, own in enumerate((gm_0, gm_2)):
        given[k, :half] = own[...]
    mask = head_rows(heads, LANES)
    lane_head = lax.broadcasted_iota(jnp.int32, (UNIT, LANES), 1) // HEAD_DIM

    def given_of(k, b):
        return jnp.concatenate([given[k, at(b)], jnp.zeros((UNIT, LANES - width), BF16)], axis=1).astype(F32)

    def read_back(rel, k, carry):
        b = at(rel)
        query = qkv[k, rel, :, 0:LANES]
        full = given_of(k, b)
        probe = probes[k, b]
        logits = logits_of(probe, query)
        location, variance = read_parts(logits, heads)
        inverse = 1.0 / variance
        fall = -0.5 * inverse
        peak = WIDTH * lax.rsqrt(variance)
        centres = lax.broadcasted_iota(jnp.int32, (BASIS, UNIT), 0).astype(F32) / (BASIS - 1)
        along, across = [], []
        total = jnp.zeros((BASIS, LANES), F32)
        for h in range(heads):
            own_given = jnp.where(lane_head == h, full, 0.0).astype(BF16)
            gap = centres - location[h : h + 1]
            square = gap * gap
            density = jnp.exp(square * fall[h : h + 1]) * peak[h : h + 1]
            grad_density = dot(values[k, b], own_given, ((1,), (1,)))
            total += dot(density.astype(BF16), own_given)
            weighed = density * grad_density
            moment = weighed * gap
            zeroth = jnp.sum(weighed, axis=0, keepdims=True)
            first = jnp.sum(moment, axis=0, keepdims=True)
            second = jnp.sum(moment * gap, axis=0, keepdims=True)
            along.append(first * inverse[h : h + 1])
            across.append(0.5 * inverse[h : h + 1] * (second * inverse[h : h + 1] - zeroth))
        sigmoid = 1.0 / (1.0 + jnp.exp(-logits))
        grad_location = jnp.concatenate(along, axis=0) * location * (1.0 - location)
        grad_variance = jnp.concatenate(across, axis=0) * SPREAD * sigmoid[heads : 2 * heads]
        grad_logits = jnp.concatenate(
            [grad_location, grad_variance, jnp.zeros((8 - 2 * heads, UNIT), F32)], axis=0
        )
        padded = jnp.concatenate([grad_logits, jnp.zeros((120, UNIT), F32)], axis=0)
        probe_cols = jnp.concatenate([probe, jnp.zeros((120, LANES), F32)], axis=0).T
        query_grad[k, b] = dot(probe_cols.astype(BF16), padded.astype(BF16))[:width]
        fresh = jnp.where(mask, dot(grad_logits.astype(BF16), query), 0.0) * root
        memory_grad[k, b] = total
        row_grad[k, b] = fresh
        return carry

    def gather_back(k, carry):
        probe = jnp.zeros((8, BASIS), F32)
        for i in range(4):
            row_back[k, 8 * i : 8 * i + 8] = jnp.zeros((8, LANES), F32)
        for b in range(units - 1, -1, -1):
            fresh, total = row_grad[k, b], memory_grad[k, b]
            if b > 0:
                probe += dot(fresh.astype(BF16), key_states[k, b], ((1,), (1,)))
            for i in range(4):
                row_back[k, 8 * i : 8 * i + 8] += jnp.where(orders[b] == i, fresh, 0.0)
            if b < units - 1:
                ends = starts[b] + lengths[b] == b + 1
                total = jnp.where(ends, 0.0, memory_grad[k, b + 1]) + total
                memory_grad[k, b] = total
                row_grad[k, b] = jnp.where(ends, 0.0, row_grad[k, b + 1]) + fresh
            before = jnp.zeros((BASIS, LANES), F32) if b == units - 1 else value_carried[k]
            if b > 0:
                value_carried[k] = jnp.where(starts[b] == b, advance_values(table, before + total), before)
            else:
                value_back[k] = (before + total)[:, :width].T.astype(BF16)
        probe_grad[k] = probe
        return carry

    def attend_back(b, k, carry):
        query = qkv[k, at(b), :, 0:LANES].astype(F32) * root
        full = given_of(k, b)
        causal = lax.broadcasted_iota(jnp.int32, (UNIT, UNIT), 0) <= lax.broadcasted_iota(
            jnp.int32, (UNIT, UNIT), 1
        )
        away = [jnp.where(starts[b] <= j, 0.0, 1e30) for j in range(b)] + [0.0]
        owns = [jnp.where(lane_head == h, query, 0.0).astype(BF16) for h in range(heads)]
        own_givens = [jnp.where(lane_head == h, full, 0.0).astype(BF16) for h in range(heads)]
        own_all = jnp.concatenate(owns, axis=0)
        given_all = jnp.concatenate(own_givens, axis=0)
        seen = (b + 1) * UNIT
        scores = dot(keys[k, :seen], own_all, ((1,), (1,)))
        grad_probs = dot(vals[k, :seen], given_all, ((1,), (1,)))
        grads, probs = [], []
        for h in range(heads):
            prob_h, product_h = [], []
            inner = jnp.zeros((1, UNIT), F32)
            for j in range(b + 1):
                tile = (slice(j * UNIT, (j + 1) * UNIT), slice(h * UNIT, (h + 1) * UNIT))
                score = scores[tile]
                if j == b:
                    score = jnp.where(causal, score, -1e30)
                prob = jnp.exp(score - (logsum[k, b, h : h + 1] + away[j]))
                product = prob * grad_probs[tile]
                inner += jnp.sum(product, axis=0, keepdims=True)
                prob_h.append(prob)
                product_h.append(product)
            span = slice(h * HEAD_DIM, (h + 1) * HEAD_DIM)
            grad_h = [(product_h[j] - prob_h[j] * inner).astype(BF16) for j in range(b + 1)]
            result = dot(cols[k, span, :seen], jnp.concatenate(grad_h, axis=0))
            query_grad[k, b, span] = query_grad[k, b, span] + result * root
            grads.append(grad_h)
            probs.append([prob.astype(BF16) for prob in prob_h])
        fresh_keys = dot(jnp.concatenate([jnp.concatenate(g, axis=0) for g in grads], axis=1), own_all)
        fresh_vals = dot(jnp.concatenate([jnp.concatenate(p, axis=0) for p in probs], axis=1), given_all)
        for j in range(b + 1):
            part = slice(j * UNIT, (j + 1) * UNIT)
            if b == units - 1:
                key_grad[k, j], value_grad[k, j] = fresh_keys[part], fresh_vals[part]
            else:
                key_grad[k, j] += fresh_keys[part]
                value_grad[k, j] += fresh_vals[part]
        return carry

    def carry_back(k, total, units_before):
        moved = dot(table[...], total.astype(BF16))
        return moved[:BASIS], (moved[BASIS:] * term_scale(units_before)).astype(BF16)

    def end_back(k, carry):
        row = jnp.where(run == 0, row_in[k], 0.0)
        value = jnp.where(run == 0, value_in[k].astype(F32), 0.0).T
        grad_keys = dot(rows[k].astype(BF16), row.astype(BF16), ((0,), (0,)))
        total = jnp.concatenate([grad_keys, value, jnp.zeros((BASIS, LANES - width), F32)], axis=1)
        carried[k], spread[k] = carry_back(k, total, lengths[units - 1])
        seen = dot(row, key_end[k], ((1,), (1,)), HIGHEST)
        gained = seen[24:32]
        for i in (2, 1, 0):
            high = gained.astype(BF16)
            low = (gained - high.astype(F32)).astype(BF16)
            gained = dot(high, table[:BASIS]) + dot(low, table[:BASIS])
            gained = gained + seen[8 * i : 8 * i + 8]
        probe_grad[k] += gained
        return carry

    def finish(b, k, carry):
        start, length = starts[b], lengths[b]
        token = lax.broadcasted_iota(jnp.int32, (UNIT, LIVE), 0) + (b - start) * UNIT
        centre = (lax.broadcasted_iota(jnp.int32, (UNIT, LIVE), 1) + LIVE).astype(F32) / (BASIS - 1)
        gap = place_of(token, length) - centre
        psi = jnp.exp(gap * gap * (-0.5 / (WIDTH * WIDTH))).astype(BF16)
        pair_grad = dot(psi, spread[k])
        query_rows = query_grad[k, b].T.astype(BF16)
        out[k, at(b), :, :LANES] = jnp.concatenate([query_rows, jnp.zeros((UNIT, LANES - width), BF16)], axis=1)
        out[k, at(b), :, LANES : 2 * LANES] = (key_grad[k, b] + pair_grad[:, :LANES]).astype(BF16)
        out[k, at(b), :, 2 * LANES :] = (value_grad[k, b] + pair_grad[:, LANES:]).astype(BF16)
        if b > 0:
            grad_keys = dot(rows[k, 0:8].astype(BF16), row_grad[k, b].astype(BF16), ((0,), (0,)))
            total = carried[k] + jnp.concatenate([grad_keys, memory_grad[k, b]], axis=1)
            moved, spread_now = carry_back(k, total, lengths[b - 1])
            carried[k] = jnp.where(start == b, moved, carried[k])
            spread[k] = jnp.where(start == b, spread_now.astype(F32), spread[k].astype(F32)).astype(BF16)
        return carry

    def both(step, *args):
        lax.fori_loop(0, 2, functools.partial(step, *args), 0)

    def turn(k, carry):
        for b in range(units):
            part = slice(b * UNIT, (b + 1) * UNIT)
            keys[k, part] = qkv[k, at(b), :, LANES : 2 * LANES]
            vals[k, part] = qkv[k, at(b), :, 2 * LANES : 3 * LANES]
            cols[k, :, part] = qkv[k, at(b), :, LANES : 2 * LANES].astype(F32).T.astype(BF16)
        return carry

    lax.fori_loop(0, 2, turn, 0)
    both(read_back, 0)
    first_hop(2)
    both(read_back, 1)
    first_hop(1)
    for copy in given_copies:
        copy.wait_recv()
    both(read_back, 2)
    first_hop(3)
    first_hop(0)
    both(read_back, 3)
    second_hop(2)
    back_copies = []
    for k in range(2):
        gather_back(k, 0)
        back_copies += [
            go(value_back.at[k], value_in.at[1 - k], "head", 2), go(row_back.at[k], row_in.at[1 - k], "head", 2)
        ]
    second_hop(1)
    both(attend_back, 3)
    second_hop(3)
    second_hop(0)
    third_hop(2)
    both(attend_back, 2)
    third_hop(1)
    third_hop(3)
    both(attend_back, 1)
    third_hop(0)
    both(attend_back, 0)
    for copy in back_copies:
        copy.wait_recv()
    lax.fori_loop(0, 2, end_back, 0)
    for b in range(units - 1, -1, -1):
        both(finish, b)
    for n, (_, _, _, _, two, far, _) in enumerate(sums):
        total = two[0].astype(F32)
        for r in (1, 2, 3):
            stage[r][n].wait_recv()
            total += far[r - 1].astype(F32)
        (slice_in, slice_weight, slice_out)[n][...] = total.astype(BF16)
    for copy in started:
        copy.wait_send()


def backward(seg_lengths, qkv, grad_mixed, logsum, values, probes, key_states, key_end, rows, grad_in, grad_out, grad_weight, heads):
    units = qkv.shape[1]
    width = heads * HEAD_DIM
    table = jnp.asarray(basis_tables()[1])
    vmem, anywhere = pl.BlockSpec(memory_space=pltpu.VMEM), pl.BlockSpec(memory_space=pl.ANY)
    shape = jax.ShapeDtypeStruct
    slices = [grad_in.shape[4:], grad_out.shape[4:], grad_weight.shape[4:]]
    hops = 2 + 3 * 4 * 3 + 3 * 3 + 4
    return pl.pallas_call(
        functools.partial(backward_kernel, heads),
        in_specs=[pl.BlockSpec(memory_space=pltpu.SMEM)] + [vmem] * 12 + [anywhere] * 3,
        out_specs=[vmem] * 5,
        out_shape=[shape(qkv.shape, BF16), shape((2, 8, BASIS), F32)] + [shape(part, BF16) for part in slices],
        scratch_shapes=[
            pltpu.VMEM((2, units, UNIT, width), BF16),
            pltpu.VMEM((2, units, width, UNIT), F32),
            pltpu.VMEM((2, units, BASIS, LANES), F32),
            pltpu.VMEM((2, units, 8, LANES), F32),
            pltpu.VMEM((2, BASIS, LANES), F32),
            pltpu.VMEM((2, width, BASIS), BF16),
            pltpu.VMEM((2, width, BASIS), BF16),
            pltpu.VMEM((2, 32, LANES), F32),
            pltpu.VMEM((2, 32, LANES), F32),
            pltpu.VMEM((2, BASIS, 2 * LANES), F32),
            pltpu.VMEM((2, LIVE, 2 * LANES), BF16),
            pltpu.VMEM((2, units, UNIT, LANES), F32),
            pltpu.VMEM((2, units, UNIT, LANES), F32),
            pltpu.VMEM((2, LANES, units * UNIT), BF16),
            pltpu.VMEM((2, units * UNIT, LANES), BF16),
            pltpu.VMEM((2, units * UNIT, LANES), BF16),
        ]
        + [pltpu.VMEM((4, 2, 2) + part, BF16) for part in slices]
        + [pltpu.VMEM((4, 2, 2) + part, BF16) for part in slices]
        + [pltpu.VMEM((4, 2) + part, BF16) for part in slices]
        + [pltpu.VMEM((4,) + part, BF16) for part in slices]
        + [pltpu.VMEM((3,) + part, BF16) for part in slices]
        + [
            pltpu.SemaphoreType.DMA((hops,)),
            pltpu.SemaphoreType.DMA((hops,)),
            pltpu.SemaphoreType.DMA((12,)),
        ],
        compiler_params=pltpu.CompilerParams(
            collective_id=2, has_side_effects=True, vmem_limit_bytes=62 << 20
        ),
        name="backward",
    )(
        seg_lengths, qkv, *grad_mixed, logsum, values, probes, key_states, key_end, rows, table, grad_in, grad_out, grad_weight
    )


def tail_kernel(
    heads, outer, grads, first_cols, flat_a, flat_b, grad_residual, source, packed, slice_in, slice_out, slice_weight,
    sums, in_bias_part, probe_grad, input_grad, whole_in, whole_out, whole_weight, whole_qkv, shared_out, owned_out,
    row_grad, near, kept, part_a, part_b, core_a, core_b, one_a, one_b, two_a, two_b, far_b, total, outer_in,
    gather_in, gather_out, gather_weight, gather_qkv,
    shared, shared_in, block, block_in, bias_block, bias_in, joined, joined_in, send, recv,
):
    own_rows, model = source.shape
    units = grads.shape[1]
    half = units // 2
    width = heads * HEAD_DIM
    z = lax.axis_index("head")
    place = lax.axis_index("dp") % 8
    y, x, c = place // 4, (place // 2) % 2, place % 2
    rows = model // 8
    greet(
        (("head", 1), ("head", 2), ("head", 3), ("dp", 1), ("dp", 2), ("dp", 4)) + tuple(("dp", bit) for bit in outer)
    )
    hops = Hops(send, recv)
    started = []

    def go(*args):
        started.append(hops.start(*args))
        return started[-1]

    def row_of(rel):
        return dot(grads[0, rel], flat_a[...]) + dot(grads[1, rel], flat_b[...])

    row_copies = []
    for k in range(half):
        row_grad[k] = row_of(half + k).astype(BF16)
        row_copies.append(go(row_grad.at[k], near.at[k], "head", 1))

    gathers = ((slice_in, gather_in, True), (slice_weight, gather_weight, True), (slice_out, gather_out, False))
    for own, gather, _ in gathers:
        gather[y, x, c] = own[...]

    def spread_first(gather, along_x):
        part = gather.at[y, x, c]
        return go(part, part, "dp", 2 if along_x else 4)

    def spread_second(gather, along_x):
        part = gather.at[y, :, c] if along_x else gather.at[:, x, c]
        return go(part, part, "dp", 4 if along_x else 2)

    def spread_third(gather):
        part = gather.at[:, :, c]
        return go(part, part, "dp", 1)

    core_copies = []
    for k, part, core in ((1, part_b, core_b), (0, part_a, core_a)):
        product = dot(first_cols[...], grads[k].reshape(2 * own_rows, 3 * LANES))
        product = jnp.concatenate([product[:, i * LANES : i * LANES + width] for i in range(3)], axis=1).astype(BF16)
        for j in range(8):
            part[j // 4, (j // 2) % 2, j % 2] = product[j * rows : (j + 1) * rows]
        core_copies.append(go(part.at[:, :, 1 - c], core, "dp", 1))
    spreads = [spread_first(gather, along_x) for _, gather, along_x in gathers]
    for k in range(half):
        kept[k] = row_of(k)

    core_copies[0].wait_recv()
    core_b[...] = added(part_b[:, :, c], core_b[...])
    one_copy_b = go(core_b.at[1 - y], one_b, "dp", 4)
    core_copies[1].wait_recv()
    core_a[...] = added(part_a[:, :, c], core_a[...])
    one_copy_a = go(core_a.at[:, 1 - x], one_a, "dp", 2)

    bias_a = jnp.sum(grads[0].reshape(2 * own_rows, 3 * LANES).astype(F32), axis=0, keepdims=True)
    bias_b = jnp.sum(grads[1].reshape(2 * own_rows, 3 * LANES).astype(F32), axis=0, keepdims=True)
    edge = jnp.zeros((8, model - BASIS), F32)
    fill = jnp.zeros((6, model), F32)
    for k, bias in ((0, bias_a), (1, bias_b)):
        block[k, 0:8] = jnp.concatenate([probe_grad[k], edge], axis=1)
        block[k, 8:16] = jnp.concatenate([bias, in_bias_part[2 * k : 2 * k + 1], fill], axis=0)
        bias_block[k] = jnp.concatenate([in_bias_part[2 * k + 1 : 2 * k + 2], jnp.zeros((7, model), F32)], axis=0)
    block_copy = go(block.at[1], block_in, "head", 2)
    bias_copies = [go(bias_block.at[0], bias_in.at[0], "head", 1), go(bias_block.at[1], bias_in.at[1], "head", 3)]

    value = source[...].astype(F32)
    centred = value - jnp.mean(value, axis=-1, keepdims=True)
    factor = lax.rsqrt(jnp.mean(centred * centred, axis=-1, keepdims=True) + EPSILON)
    normal = centred * factor

    one_copy_b.wait_recv()
    one_b[...] = added(core_b[y], one_b[...])
    two_copy_b = go(one_b.at[1 - x], two_b, "dp", 2)
    one_copy_a.wait_recv()
    one_a[...] = added(core_a[:, x], one_a[...])
    two_copy_a = go(one_a.at[1 - y], two_a, "dp", 4)
    for copy in row_copies:
        copy.wait_recv()
    two_copy_b.wait_recv()
    two_b[...] = added(one_b[x], two_b[...])
    far_copy = go(two_b, far_b, "head", 2)

    grad = kept[...].reshape(own_rows, model) + near[...].reshape(own_rows, model).astype(F32)
    scaled = grad * packed[16:17]
    change = factor * (
        scaled
        - jnp.mean(scaled, axis=-1, keepdims=True)
        - normal * jnp.mean(scaled * normal, axis=-1, keepdims=True)
    )
    input_grad[...] = (grad_residual[...] + change).astype(BF16)
    shared[...] = jnp.concatenate(
        [jnp.sum(grad * normal, axis=0, keepdims=True), jnp.sum(grad, axis=0, keepdims=True), sums[0:6]], axis=0
    )
    shared_copies = [go(shared, shared_in.at[r - 1], "head", r) for r in (1, 2, 3)]
    spreads = [copy.wait_recv() or spread_second(gather, along_x) for copy, (_, gather, along_x) in zip(spreads, gathers)]

    two_copy_a.wait_recv()
    own_sum = added(one_a[y], two_a[...]).astype(F32)
    far_copy.wait_recv()
    total[0] = (own_sum + far_b[...].astype(F32)).astype(BF16)
    for n, bit in enumerate(outer):
        copy = go(total.at[n], outer_in.at[n], "dp", bit)
        copy.wait_recv()
        total[n + 1] = added(total[n], outer_in[n])
    gather_qkv[y, x, c] = total[len(outer)]
    cut = rows // 2
    upper, lower = pl.ds(0, cut), pl.ds(cut, cut)
    qkv_parts = [gather_qkv.at[y, x, c, upper], gather_qkv.at[y, x, c, lower]]
    qkv_copies = [go(qkv_parts[0], qkv_parts[0], "dp", 2), go(qkv_parts[1], qkv_parts[1], "dp", 4)]

    block_copy.wait_recv()
    for copy in bias_copies + shared_copies:
        copy.wait_recv()
    owned = block[0] + block_in[...]
    bias_rows = bias_in[0] + bias_in[1]
    owned_rows = jnp.concatenate([owned[8:9], owned[9:10] + bias_rows[0:1], owned[10:16]], axis=0)
    joined[0] = jnp.concatenate(
        [shared[...] + shared_in[0] + shared_in[1] + shared_in[2], owned[0:8], owned_rows], axis=0
    )
    spreads = [copy.wait_recv() or spread_third(gather) for copy, (_, gather, _) in zip(spreads, gathers)]
    for n, bit in enumerate((2, 4, 1) + outer):
        copy = go(joined.at[n], joined_in.at[n], "dp", bit)
        if n == 1:
            for copy_one in qkv_copies:
                copy_one.wait_recv()
            qkv_parts = [gather_qkv.at[y, :, c, upper], gather_qkv.at[:, x, c, lower]]
            qkv_copies = [go(qkv_parts[0], qkv_parts[0], "dp", 4), go(qkv_parts[1], qkv_parts[1], "dp", 2)]
        copy.wait_recv()
        joined[n + 1] = joined[n] + joined_in[n]
    last = joined[3 + len(outer)]
    shared_out[...] = last[0:8]
    owned_out[...] = last[8:24]
    for copy, (_, gather, _), out in zip(spreads, gathers, (whole_in, whole_weight, whole_out)):
        copy.wait_recv()
        out[...] = gather[...]
    for copy in qkv_copies:
        copy.wait_recv()
    spread_third(gather_qkv).wait_recv()
    whole_qkv[...] = gather_qkv[...]
    for copy in started:
        copy.wait_send()


def tail(grads, first_cols, flat_a, flat_b, grad_residual, source, packed, slices, sums, in_bias_part, probe_grad, outer, heads):
    own_rows, model = source.shape
    units = grads.shape[1]
    rows = model // 8
    vmem = pl.BlockSpec(memory_space=pltpu.VMEM)
    shape = jax.ShapeDtypeStruct
    slice_in, slice_out, slice_weight = slices
    plane = lambda part: (2, 2, 2) + part
    part = (rows, 3 * heads * HEAD_DIM)
    hops = units // 2 + 9 + 2 + 2 + 2 + 1 + 5 + 1 + 2 + 3 + 3 + 2 * len(outer)
    return pl.pallas_call(
        functools.partial(tail_kernel, heads, outer),
        in_specs=[vmem] * 13,
        out_specs=[vmem] * 7,
        out_shape=[
            shape(source.shape, BF16), shape(plane(slice_in.shape), BF16), shape(plane(slice_out.shape), BF16),
            shape(plane(slice_weight.shape), BF16), shape(plane(part), BF16), shape((8, model), F32),
            shape((16, model), F32),
        ],
        scratch_shapes=[
            pltpu.VMEM((units // 2, UNIT, model), BF16),
            pltpu.VMEM((units // 2, UNIT, model), BF16),
            pltpu.VMEM((units // 2, UNIT, model), F32),
            pltpu.VMEM(plane(part), BF16),
            pltpu.VMEM(plane(part), BF16),
            pltpu.VMEM((2, 2) + part, BF16),
            pltpu.VMEM((2, 2) + part, BF16),
            pltpu.VMEM((2,) + part, BF16),
            pltpu.VMEM((2,) + part, BF16),
            pltpu.VMEM(part, BF16),
            pltpu.VMEM(part, BF16),
            pltpu.VMEM(part, BF16),
            pltpu.VMEM((1 + len(outer),) + part, BF16),
            pltpu.VMEM((max(1, len(outer)),) + part, BF16),
            pltpu.VMEM(plane(slice_in.shape), BF16),
            pltpu.VMEM(plane(slice_out.shape), BF16),
            pltpu.VMEM(plane(slice_weight.shape), BF16),
            pltpu.VMEM(plane(part), BF16),
            pltpu.VMEM((8, model), F32),
            pltpu.VMEM((3, 8, model), F32),
            pltpu.VMEM((2, 16, model), F32),
            pltpu.VMEM((16, model), F32),
            pltpu.VMEM((2, 8, model), F32),
            pltpu.VMEM((2, 8, model), F32),
            pltpu.VMEM((4 + len(outer), 24, model), F32),
            pltpu.VMEM((3 + len(outer), 24, model), F32),
            pltpu.SemaphoreType.DMA((hops,)),
            pltpu.SemaphoreType.DMA((hops,)),
        ],
        compiler_params=pltpu.CompilerParams(
            collective_id=3, has_side_effects=True, vmem_limit_bytes=60 << 20
        ),
        name="tail",
    )(
        grads, first_cols, flat_a, flat_b, grad_residual, source, packed, slice_in, slice_out, slice_weight, sums,
        in_bias_part, probe_grad,
    )


def exchange(value, axis, bit):
    size = lax.axis_size(axis)
    return lax.ppermute(value, axis, [(j, j ^ bit) for j in range(size)])


def local(
    inputs, seg_lengths, ln1_gain, ln1_bias, qkv_weight, qkv_bias, out_weight, out_bias, mem_mu, mem_sig,
    ln2_gain, ln2_bias, ff_in, ff_in_bias, ff_out, ff_out_bias, cotangent,
):
    own_rows, model = inputs.shape
    shards = lax.axis_size("head")
    members = lax.axis_size("dp")
    width = qkv_weight.shape[2]
    heads = width // HEAD_DIM
    hidden_part = ff_in.shape[1]
    units = 2 * own_rows // UNIT
    slices = 8
    outer = tuple(1 << k for k in range(3, 16) if 1 << k < members)
    rows = model // slices

    bias_row = jnp.pad(qkv_bias, ((0, 0), (0, LANES - width))).reshape(1, 3 * LANES)
    edge = 3 * LANES - BASIS
    packed = jnp.pad(bias_row, ((0, 23), (0, 0))).astype(F32)
    packed += jnp.pad(mem_mu, ((1, 23 - heads), (0, edge))).astype(F32)
    packed += jnp.pad(mem_sig, ((1 + heads, 23 - 2 * heads), (0, edge))).astype(F32)
    given = (ln1_gain, ln1_bias, out_bias, ln2_gain, ln2_bias, ff_out_bias, ff_in_bias)
    line = sum(jnp.pad(vector.astype(F32), (k * model, (6 - k) * model)) for k, vector in enumerate(given))
    packed += jnp.pad(line.reshape(7, model), ((16, 1), (0, 0)))

    turned_weight = jnp.transpose(qkv_weight, (1, 2, 0)).reshape(3 * width, model)
    (
        qkv, first_cols, flat_a, flat_b, logsum, values, probes, key_states, key_end, state_rows,
        *mixed, in_bias, far_in, far_out, far_weight,
    ) = forward(seg_lengths, inputs, packed, turned_weight, out_weight, ff_in, ff_out, heads)
    flat = lambda array: array.reshape((shards - 1, slices) + array.shape[4:])
    outputs, grad_residual, *rest = middle(
        inputs, cotangent, mixed, out_weight, flat(far_weight), packed, in_bias,
        ff_in.reshape(slices, rows, hidden_part), ff_out.reshape(slices, rows, model), flat(far_in), flat(far_out),
    )
    grad_mixed, (ff_in_part, ff_out_part, out_weight_part, sums, in_bias_part) = rest[:4], rest[4:]
    paired = [part.reshape(units // 2, UNIT, width) for part in grad_mixed]
    plane = lambda array: array.reshape((shards, 2, 2, 2) + array.shape[2:])
    grads, probe_grad, *parts = backward(
        seg_lengths, qkv, paired, logsum, values, probes, key_states, key_end, state_rows, plane(ff_in_part),
        plane(ff_out_part), plane(out_weight_part), heads,
    )
    for bit in outer:
        parts = [added(part, exchange(part, "dp", bit)) for part in parts]
    input_grad, whole_in, whole_out, whole_weight, whole_qkv, shared, owned = tail(
        grads, first_cols, flat_a, flat_b, grad_residual, inputs, packed, parts, sums, in_bias_part, probe_grad,
        outer, heads,
    )
    ff_in_sum, ff_out_sum, out_weight_sum, qkv_weight_sum = finish(
        whole_in.reshape(model, hidden_part), whole_out.reshape(hidden_part, model),
        whole_weight.reshape((slices,) + whole_weight.shape[3:]), whole_qkv.reshape(model, 3 * width), width,
    )
    return (
        outputs, input_grad, shared[0], shared[1], jnp.transpose(qkv_weight_sum, (2, 0, 1)),
        owned[8].reshape(3, LANES)[:, :width], out_weight_sum, shared[2], owned[:heads, :BASIS],
        owned[heads : 2 * heads, :BASIS], shared[3], shared[4], ff_in_sum, owned[9, :hidden_part], ff_out_sum, shared[5],
    )


def solution(mesh):
    rows, whole = P(("dp", "head"), None), P()
    return jax.shard_map(
        local,
        mesh=mesh,
        in_specs=(
            rows, P("dp", None), whole, whole, P(None, None, "head"), P(None, "head"), P("head", None), whole,
            P("head", None), P("head", None), whole, whole, P(None, "head"), P("head"), P("head", None), whole, rows,
        ),
        out_specs=(
            rows, rows, whole, whole, P(None, None, "head"), P(None, "head"), P("head", None), whole,
            P("head", None), P("head", None), whole, whole, P(None, "head"), P("head"), P("head", None), whole,
        ),
        check_vma=False,
    )
```

```python
import functools
import math

import jax
import jax.numpy as jnp
import ml_dtypes
import numpy as np
from jax import lax
from jax.experimental import pallas as pl
from jax.experimental.pallas import tpu as pltpu
from jax.sharding import PartitionSpec as P

HEAD_DIM = 64
BASIS = 512
UNIT = 256
LANES = 256
TAU = 0.75
RIDGE = 0.5
EPSILON = 1e-05
MESH = pl.DeviceIdType.MESH
SPREAD = 1.0 / 64.0
WIDTH = 1.0 / BASIS
LIVE = BASIS // 2
HIGHEST = lax.Precision.HIGHEST
F32 = jnp.float32
BF16 = jnp.bfloat16


def split_table(table):
    high = table.astype(np.float32).astype(ml_dtypes.bfloat16)
    low = (table.astype(np.float32) - high.astype(np.float32)).astype(ml_dtypes.bfloat16)
    return high, low


@functools.lru_cache(maxsize=None)
def basis_tables():
    centres = np.arange(BASIS) / (BASIS - 1)
    apart = centres[:, None] - centres[None, :]
    gram = np.exp(-apart * apart / (4.0 * WIDTH * WIDTH)) + RIDGE * np.eye(BASIS)
    solve = np.linalg.inv(gram)
    samples = (np.arange(BASIS) + 0.5) / BASIS
    near_gap = TAU * samples[:, None] - centres[None, :]
    far_gap = samples[:, None] - centres[None, :]
    near = np.exp(-near_gap * near_gap / (2.0 * WIDTH * WIDTH))
    far = np.exp(-far_gap * far_gap / (2.0 * WIDTH * WIDTH))
    contract = (near.T @ far) * (TAU / (BASIS * WIDTH * math.sqrt(math.pi)))
    joined = np.concatenate([solve @ contract, solve[:, LIVE:]], axis=1)
    high, low = split_table(joined)
    forward = np.concatenate([high, high, low], axis=1)
    backward = np.ascontiguousarray(high.T)
    return forward, backward


def term_scale(units):
    return (1.0 - TAU) / (WIDTH * math.sqrt(math.pi) * UNIT) / units.astype(F32)


def split3(value):
    high = value.astype(BF16)
    low = (value - high.astype(F32)).astype(BF16)
    return jnp.concatenate([high, low, high], axis=0)


def dot(a, b, contract=((1,), (0,)), precision=None):
    return lax.dot_general(a, b, (contract, ((), ())), precision=precision, preferred_element_type=F32)


def head_rows(heads, width):
    row = lax.broadcasted_iota(jnp.int32, (8, width), 0)
    lane = lax.broadcasted_iota(jnp.int32, (8, width), 1) // HEAD_DIM
    return ((row == lane) | (row == lane + heads)) & (lane < heads)


def read_parts(logits, heads):
    location = 1.0 / (1.0 + jnp.exp(-logits))
    variance = (jnp.maximum(logits, 0.0) + jnp.log1p(jnp.exp(-jnp.abs(logits)))) * SPREAD + WIDTH * WIDTH
    return location[:heads], variance[heads : 2 * heads]


def place_of(index, length):
    return TAU + (1.0 - TAU) * (index.astype(F32) + 0.5) / (length.astype(F32) * UNIT)


def split_rows(value):
    high = value.astype(BF16)
    rest = value - high.astype(F32)
    mid = rest.astype(BF16)
    return high, mid, (rest - mid.astype(F32)).astype(BF16)


def three_pass(left, right_high, right_low, contract=((1,), (0,))):
    high = left.astype(BF16)
    low = (left - high.astype(F32)).astype(BF16)
    return dot(high, right_high, contract) + dot(low, right_high, contract) + dot(high, right_low, contract)


def advance_values(table, value):
    return dot(table[:BASIS, :BASIS], value.astype(BF16))


def logits_of(probes, query):
    parts = dot(jnp.concatenate(split_rows(probes), axis=0), query, ((1,), (1,)))
    return parts[0:8] + parts[8:16] + parts[16:24]


def segments_of(lengths, run, units):
    sizes = [lengths[0, run * units + s] // UNIT for s in range(units)]
    ends, total = [], 0
    for size in sizes:
        total = total + size
        ends.append(total)
    starts, spans, orders = [], [], []
    for b in range(units):
        start, span, order = 0, 0, 0
        for size, end in zip(sizes, ends):
            inside = (end > b) & (end - size <= b)
            start = start + jnp.where(inside, end - size, 0)
            span = span + jnp.where(inside, size, 0)
            order = order + jnp.where((end <= b) & (size > 0), 1, 0)
        starts.append(start)
        spans.append(span)
        orders.append(order)
    return starts, spans, orders


def other_of(index, distance):
    bit = 1
    while bit <= distance:
        if distance & bit:
            index = index + bit - 2 * bit * ((index // bit) % 2)
        bit *= 2
    return index


class Hops:
    def __init__(self, send, recv):
        self.send, self.recv, self.used = send, recv, 0

    def start(self, source, target, axis, bit):
        copy = pltpu.make_async_remote_copy(
            src_ref=source,
            dst_ref=target,
            send_sem=self.send.at[self.used],
            recv_sem=self.recv.at[self.used],
            device_id={axis: other_of(lax.axis_index(axis), bit)},
            device_id_type=MESH,
        )
        self.used += 1
        copy.start()
        return copy


def greet(neighbours):
    barrier = pltpu.get_barrier_semaphore()
    for axis, bit in neighbours:
        pl.semaphore_signal(
            barrier, inc=1, device_id={axis: other_of(lax.axis_index(axis), bit)}, device_id_type=MESH
        )
    pl.semaphore_wait(barrier, len(neighbours))


def set_out(pairs, sems, first):
    copies = [pltpu.make_async_copy(a, b, sems.at[first + k]) for k, (a, b) in enumerate(pairs)]
    for copy in copies:
        copy.start()
    return copies


def forward_kernel(
    heads, seg_lengths, source, packed, weight, out_weight, table, ff_in, ff_out,
    qkv_out, first_cols_out, flat_a_out, flat_b_out, values_out, key_states_out, key_end_out, logsum, probes, rows,
    mixed_0, mixed_1, mixed_2, mixed_3, in_bias, far_in, far_out, far_weight,
    qkv, first_rows, first_cols, flats, near, far, far_flat, small, far_row, bias_row, weight_mine, memory, sums, value_states, carried, value_ends, value_ins,
    projs, proj_ins, cols, keys, discrete, mixed, mixed_in, values, key_states, key_end, send, recv, local_sems,
):
    own_rows, model = source.shape
    width = heads * HEAD_DIM
    units = qkv.shape[1]
    half = units // 2
    root = 1.0 / math.sqrt(HEAD_DIM)
    z = lax.axis_index("head")
    flip, run = (z % 2) * half, z // 2
    place = lax.axis_index("dp") % 8
    y, x, c = place // 4, (place // 2) % 2, place % 2
    slice_rows = model // 8
    at = lambda b: (b + flip) % units
    starts, lengths, orders = segments_of(seg_lengths, run, units)
    greet((("head", 1), ("head", 2), ("head", 3), ("dp", 1), ("dp", 2), ("dp", 4)))
    hops = Hops(send, recv)
    started = []

    def go(*args):
        started.append(hops.start(*args))
        return started[-1]

    part_rows, part_cols = far.shape[3:]
    mine = weight.at[
        pl.ds(pl.multiple_of((2 * y + x) * part_rows, 16), part_rows),
        pl.ds(pl.multiple_of(c * part_cols, 128), part_cols),
    ]
    small[...] = packed[0:16]
    bias_row[...] = jnp.broadcast_to(packed[22:23], bias_row.shape)
    narrow = width // 8
    chosen = jnp.zeros((narrow, model), F32)
    for j in range(8):
        chosen += jnp.where(place == j, out_weight[j * narrow : (j + 1) * narrow].astype(F32), 0.0)
    spare = jnp.zeros((weight_mine.shape[0] - narrow, model), F32)
    weight_mine[...] = jnp.concatenate([chosen, spare], axis=0).astype(BF16)
    slice_copy = go(mine, far.at[y, x, c], "head", 2)
    small_copy = go(small, far_row, "head", 2)
    row_copies = []
    for k in range(half):
        part = slice(k * UNIT, (k + 1) * UNIT)
        value = source[part].astype(F32)
        centred = value - jnp.mean(value, axis=-1, keepdims=True)
        factor = lax.rsqrt(jnp.mean(centred * centred, axis=-1, keepdims=True) + EPSILON)
        first_rows[part] = (centred * factor * packed[16:17] + packed[17:18]).astype(BF16)
        row_copies.append(go(first_rows.at[part], near.at[part], "head", 1))
    in_mine = ff_in.at[pl.ds(pl.multiple_of(place * slice_rows, 16), slice_rows)]
    out_mine = ff_out.at[pl.ds(pl.multiple_of(place * slice_rows, 16), slice_rows)]
    gathers = ((far_in, 2, 4), (far_weight, 2, 4), (far_out, 4, 2))
    stage = {}

    def send_chunk(r):
        stage[r] = [
            go(in_mine, far_in.at[r - 1, y, x, c], "head", r),
            go(weight_mine, far_weight.at[r - 1, y, x, c], "head", r),
            go(out_mine, far_out.at[r - 1, y, x, c], "head", r),
        ]

    def advance(r, step):
        for copy in stage[r]:
            copy.wait_recv()
        stage[r] = []
        for array, first, second in gathers:
            block = array.at[r - 1]
            if step == 1:
                part, bit = block.at[y, x, c], first
            elif step == 2:
                part, bit = (block.at[y, :, c] if first == 2 else block.at[:, x, c]), second
            else:
                part, bit = block.at[:, :, c], 1
            stage[r].append(go(part, part, "dp", bit))

    send_chunk(1)
    send_chunk(2)
    send_chunk(3)
    in_bias[0] = bias_row[...]
    bias_copies = [go(bias_row, in_bias.at[r], "head", r) for r in (1, 2, 3)]

    slice_copy.wait_recv()
    x_copy = go(far.at[y, x, c], far.at[y, x, c], "dp", 2)

    def widen(k, read):
        for i in range(3):
            flats[k, i * LANES : i * LANES + width] = read(slice(i * width, (i + 1) * width))
            flats[k, i * LANES + width : (i + 1) * LANES] = jnp.zeros((LANES - width, model), BF16)

    def project(k, unit, shift):
        span = slice(unit * UNIT, (unit + 1) * UNIT)
        qkv[k, unit] = (dot(first_rows[span], flats[k], ((1,), (1,))) + shift).astype(BF16)

    widen(0, lambda span: weight[span])
    for unit in range(half):
        project(0, unit, small[0:1])
    x_copy.wait_recv()
    y_copy = go(far.at[y, :, c], far.at[y, :, c], "dp", 4)
    first_cols[:, :own_rows] = first_rows[:own_rows].astype(F32).T.astype(BF16)
    y_copy.wait_recv()
    core_copy = go(far.at[:, :, c], far.at[:, :, c], "dp", 1)
    small_copy.wait_recv()
    for k, copy in enumerate(row_copies):
        copy.wait_recv()
        part = slice(k * UNIT, (k + 1) * UNIT)
        first_rows[own_rows + k * UNIT : own_rows + (k + 1) * UNIT] = near[part]
        project(0, half + k, small[0:1])

    advance(1, 1)
    first_cols[:, own_rows:] = near[...].astype(F32).T.astype(BF16)
    core_copy.wait_recv()
    for i in range(8):
        row, col = (i // 2) * part_rows, (i % 2) * part_cols
        far_flat[row : row + part_rows, col : col + part_cols] = far[i // 4, (i // 2) % 2, i % 2]
    widen(1, lambda span: far_flat[span])
    for unit in range(units):
        project(1, unit, far_row[0:1])
    saved = set_out(
        [(qkv, qkv_out), (first_cols, first_cols_out), (flats.at[0], flat_a_out), (flats.at[1], flat_b_out)],
        local_sems, 0,
    )

    def probe_of(k):
        return jnp.where(k == 0, small[1:9, :BASIS], far_row[1:9, :BASIS])

    mask = head_rows(heads, LANES)

    def first_state(k, carry):
        memory[k] = jnp.zeros(memory.shape[1:], F32)
        row = probe_of(k)
        rows[k, 0:8] = row
        wide = 2 * (BASIS + LIVE)
        for i in range(1, 4):
            row = three_pass(row, table[:, :BASIS], table[:, wide : wide + BASIS])
            rows[k, 8 * i : 8 * i + 8] = row
        return carry

    lax.fori_loop(0, 2, first_state, 0)

    def state(b, k, carry):
        start, length = starts[b], lengths[b]
        now = memory[k]
        value_states[k, b] = now[:, LANES:]
        key_states[k, b] = now[:, :LANES].astype(BF16)
        if b > 0:
            probes[k, b] = jnp.where(mask, dot(rows[k, 0:8], now[:, :LANES], precision=HIGHEST), 0.0)
        else:
            probes[k, b] = jnp.zeros((8, LANES), F32)
        token = lax.broadcasted_iota(jnp.int32, (LIVE, UNIT), 1) + (b - start) * UNIT
        centre = (lax.broadcasted_iota(jnp.int32, (LIVE, UNIT), 0) + LIVE).astype(F32) / (BASIS - 1)
        gap = place_of(token, length) - centre
        psi = jnp.exp(gap * gap * (-0.5 / (WIDTH * WIDTH)))
        psi_high = psi.astype(BF16)
        psi_low = (psi - psi_high.astype(F32)).astype(BF16)
        pairs = qkv[k, at(b), :, LANES : 3 * LANES]
        exact = dot(psi_high, pairs[:, :LANES]) + dot(psi_low, pairs[:, :LANES])
        fresh = jnp.concatenate([exact, dot(psi_high, pairs[:, LANES:])], axis=1)
        gathered = fresh if b == 0 else jnp.where(start == b, 0.0, sums[k]) + fresh
        sums[k] = gathered
        stacked = jnp.concatenate([now, gathered * term_scale(length)], axis=0)
        later = jnp.concatenate(
            [
                dot(table[...], split3(stacked[:, :LANES])),
                dot(table[:, : BASIS + LIVE], stacked[:, LANES:].astype(BF16)),
            ],
            axis=1,
        )
        memory[k] = jnp.where(start + length == b + 1, later, now)
        return carry

    def end_state(k, carry):
        key = memory[k, :, :LANES]
        key_end[k] = key
        value_ends[k] = memory[k, :, LANES : LANES + width].T.astype(BF16)
        seen = dot(rows[k], key, precision=HIGHEST)
        for i in range(4):
            projs[k, 8 * i : 8 * i + 8] = jnp.where(mask, seen[8 * i : 8 * i + 8], 0.0)
        return carry

    def attend(b, k, carry):
        cols[k, :, b * UNIT : (b + 1) * UNIT] = qkv[k, at(b), :, 2 * LANES : 3 * LANES].astype(F32).T.astype(BF16)
        keys[k, b * UNIT : (b + 1) * UNIT] = qkv[k, at(b), :, LANES : 2 * LANES]
        query = qkv[k, at(b), :, 0:LANES].astype(F32) * root
        lane_head = lax.broadcasted_iota(jnp.int32, (UNIT, LANES), 1) // HEAD_DIM
        causal = lax.broadcasted_iota(jnp.int32, (UNIT, UNIT), 0) <= lax.broadcasted_iota(
            jnp.int32, (UNIT, UNIT), 1
        )
        away = [jnp.where(starts[b] <= j, 0.0, 1e30) for j in range(b)] + [0.0]
        owns = jnp.concatenate([jnp.where(lane_head == h, query, 0.0).astype(BF16) for h in range(heads)], axis=0)
        seen = (b + 1) * UNIT
        products = dot(keys[k, :seen], owns, ((1,), (1,)))
        for h in range(heads):
            scores = [products[j * UNIT : (j + 1) * UNIT, h * UNIT : (h + 1) * UNIT] for j in range(b + 1)]
            scores[b] = jnp.where(causal, scores[b], -1e30)
            highest = functools.reduce(
                jnp.maximum, [jnp.max(s, axis=0, keepdims=True) - away[j] for j, s in enumerate(scores)]
            )
            weights = [jnp.exp(s - (highest + away[j])) for j, s in enumerate(scores)]
            total = sum(jnp.sum(w, axis=0, keepdims=True) for w in weights)
            span = slice(h * HEAD_DIM, (h + 1) * HEAD_DIM)
            part = dot(cols[k, span, :seen], jnp.concatenate([w.astype(BF16) for w in weights], axis=0))
            discrete[k, b, span] = part * (1.0 / total)
            logsum[k, b, h : h + 1] = highest + jnp.log(total)
        return carry

    def seen_value(k, carry):
        incoming = jnp.where(run > 0, value_ins[k].astype(F32), 0.0).T
        carried[:, :width] = incoming
        carried[:, width:] = jnp.zeros((BASIS, LANES - width), F32)
        for b in range(units):
            if b > 0:
                carried[...] = jnp.where(starts[b] == b, advance_values(table, carried[...]), carried[...])
            values[k, b] = (value_states[k, b] + carried[...]).astype(BF16)
            gained = jnp.zeros((8, LANES), F32)
            for i in range(4):
                gained += jnp.where((orders[b] == i) & (run > 0), proj_ins[k, 8 * i : 8 * i + 8], 0.0)
            probes[k, b] = (probes[k, b] + gained) * root
        return carry

    def read(rel, k, carry):
        b = at(rel)
        query = qkv[k, rel, :, 0:LANES]
        logits = logits_of(probes[k, b], query)
        location, variance = read_parts(logits, heads)
        fall = -0.5 / variance
        peak = WIDTH * lax.rsqrt(variance)
        centres = lax.broadcasted_iota(jnp.int32, (BASIS, UNIT), 0).astype(F32) / (BASIS - 1)
        value_cols = values[k, b].astype(F32).T.astype(BF16)
        parts = []
        for h in range(heads):
            gap = centres - location[h : h + 1]
            density = jnp.exp(gap * gap * fall[h : h + 1]).astype(BF16)
            span = slice(h * HEAD_DIM, (h + 1) * HEAD_DIM)
            parts.append(discrete[k, b, span] + dot(value_cols[span], density) * peak[h : h + 1])
        mixed[k, rel] = jnp.concatenate(parts, axis=0).T.astype(BF16)
        return carry

    advance(1, 2)
    state_copies = []
    for k in range(2):
        for b in range(units):
            state(b, k, 0)
        end_state(k, 0)
        state_copies.append([
            go(value_ends.at[k], value_ins.at[1 - k], "head", 2), go(projs.at[k], proj_ins.at[1 - k], "head", 2)
        ])
        if k == 0:
            advance(2, 1)
            advance(3, 1)
        if k == 1:
            advance(1, 3)
    for b in range(units):
        lax.fori_loop(0, 2, functools.partial(attend, b), 0)
        if b == 0:
            advance(2, 2)
        if b == 2:
            advance(3, 2)
        if b == 3:
            advance(2, 3)
    saved += set_out([(key_states, key_states_out), (key_end, key_end_out)], local_sems, 4)
    mixed_copies = [None, None]
    for k in (1, 0):
        for copy in state_copies[1 - k]:
            copy.wait_recv()
        seen_value(k, 0)
        read(2, k, 0)
        read(3, k, 0)
        mixed_copies[k] = go(mixed.at[k, half:], mixed_in.at[k], "head", 1)
        if k == 1:
            advance(3, 3)
    saved += set_out([(values, values_out)], local_sems, 6)
    lax.fori_loop(0, 2, functools.partial(read, 0), 0)
    lax.fori_loop(0, 2, functools.partial(read, 1), 0)
    mixed_0[...] = mixed[0, :half].reshape(own_rows, width)
    mixed_2[...] = mixed[1, :half].reshape(own_rows, width)
    for copy in mixed_copies:
        copy.wait_recv()
    mixed_1[...] = mixed_in[0].reshape(own_rows, width)
    mixed_3[...] = mixed_in[1].reshape(own_rows, width)
    for copy in bias_copies + stage[1] + stage[2] + stage[3]:
        copy.wait_recv()
    for copy in started:
        copy.wait_send()
    for copy in saved:
        copy.wait()


def forward(seg_lengths, source, packed, weight, out_weight, ff_in, ff_out, heads):
    own_rows, model = source.shape
    units = 2 * own_rows // UNIT
    width = heads * HEAD_DIM
    hidden_part = ff_in.shape[1]
    rows = model // 8
    spaced = -(-width // 8 // 16) * 16
    table = jnp.asarray(basis_tables()[0])
    vmem, anywhere = pl.BlockSpec(memory_space=pltpu.VMEM), pl.BlockSpec(memory_space=pl.ANY)
    shape = jax.ShapeDtypeStruct
    hops = 2 + units // 2 + 3 + 3 * 3 * 4 + 3 + 4 + 2
    return pl.pallas_call(
        functools.partial(forward_kernel, heads),
        in_specs=[pl.BlockSpec(memory_space=pltpu.SMEM)] + [vmem] * 5 + [anywhere] * 2,
        out_specs=[anywhere] * 7 + [vmem] * 8 + [anywhere] * 3,
        out_shape=[
            shape((2, units, UNIT, 3 * LANES), BF16),
            shape((model, 2 * own_rows), BF16),
            shape((3 * LANES, model), BF16),
            shape((3 * LANES, model), BF16),
            shape((2, units, BASIS, LANES), BF16),
            shape((2, units, BASIS, LANES), BF16),
            shape((2, BASIS, LANES), F32),
            shape((2, units, 8, UNIT), F32),
            shape((2, units, 8, LANES), F32),
            shape((2, 32, BASIS), F32),
        ] + [shape((own_rows, width), BF16)] * 4 + [
            shape((4, 8, hidden_part), F32),
            shape((3, 2, 2, 2, rows, hidden_part), BF16),
            shape((3, 2, 2, 2, rows, model), BF16),
            shape((3, 2, 2, 2, spaced, model), BF16),
        ],
        scratch_shapes=[
            pltpu.VMEM((2, units, UNIT, 3 * LANES), BF16),
            pltpu.VMEM((2 * own_rows, model), BF16),
            pltpu.VMEM((model, 2 * own_rows), BF16),
            pltpu.VMEM((2, 3 * LANES, model), BF16),
            pltpu.VMEM((own_rows, model), BF16),
            pltpu.VMEM((2, 2, 2, 3 * width // 4, model // 2), BF16),
            pltpu.VMEM((3 * width, model), BF16),
            pltpu.VMEM((16, 3 * LANES), F32),
            pltpu.VMEM((16, 3 * LANES), F32),
            pltpu.VMEM((8, hidden_part), F32),
            pltpu.VMEM((spaced, model), BF16),
            pltpu.VMEM((2, BASIS, 2 * LANES), F32),
            pltpu.VMEM((2, LIVE, 2 * LANES), F32),
            pltpu.VMEM((2, units, BASIS, LANES), F32),
            pltpu.VMEM((BASIS, LANES), F32),
            pltpu.VMEM((2, width, BASIS), BF16),
            pltpu.VMEM((2, width, BASIS), BF16),
            pltpu.VMEM((2, 32, LANES), F32),
            pltpu.VMEM((2, 32, LANES), F32),
            pltpu.VMEM((2, LANES, units * UNIT), BF16),
            pltpu.VMEM((2, units * UNIT, LANES), BF16),
            pltpu.VMEM((2, units, width, UNIT), F32),
            pltpu.VMEM((2, units, UNIT, width), BF16),
            pltpu.VMEM((2, units // 2, UNIT, width), BF16),
            pltpu.VMEM((2, units, BASIS, LANES), BF16),
            pltpu.VMEM((2, units, BASIS, LANES), BF16),
            pltpu.VMEM((2, BASIS, LANES), F32),
            pltpu.SemaphoreType.DMA((hops,)),
            pltpu.SemaphoreType.DMA((hops,)),
            pltpu.SemaphoreType.DMA((7,)),
        ],
        compiler_params=pltpu.CompilerParams(
            collective_id=1, has_side_effects=True, vmem_limit_bytes=60 << 20
        ),
        name="forward",
    )(seg_lengths, source, packed, weight, out_weight, table, ff_in, ff_out)


def whole(shape):
    return pl.BlockSpec(shape, lambda i: (0,) * len(shape))


def finish_kernel(given_in, given_out, given_weight, given_qkv, grad_in, grad_out, grad_weight, grad_qkv):
    step = pl.program_id(0)
    grad_in[...] = given_in[...].astype(F32)
    grad_out[...] = given_out[...].astype(F32)
    width = grad_qkv.shape[1]
    for i in range(3):

        @pl.when(step == i)
        def _():
            grad_qkv[0] = given_qkv[:, i * width : (i + 1) * width].astype(F32).T

    @pl.when(step == 0)
    def _():
        narrow = grad_weight.shape[0] // given_weight.shape[0]
        for j in range(given_weight.shape[0]):
            grad_weight[j * narrow : (j + 1) * narrow] = given_weight[j].astype(F32)[:narrow]


def finish(given_in, given_out, given_weight, given_qkv, width):
    model, columns = given_in.shape
    hidden_part = given_out.shape[0]
    return pl.pallas_call(
        finish_kernel,
        grid=(3,),
        in_specs=[
            pl.BlockSpec((model // 3, columns), lambda i: (i, 0)),
            pl.BlockSpec((hidden_part // 3, model), lambda i: (i, 0)),
            pl.BlockSpec(given_weight.shape, lambda i: (0, 0, 0)),
            pl.BlockSpec(given_qkv.shape, lambda i: (0, 0)),
        ],
        out_specs=[
            pl.BlockSpec((model // 3, columns), lambda i: (i, 0)),
            pl.BlockSpec((hidden_part // 3, model), lambda i: (i, 0)),
            pl.BlockSpec((width, model), lambda i: (0, 0)),
            pl.BlockSpec((1, width, model), lambda i: (i, 0, 0)),
        ],
        out_shape=[
            jax.ShapeDtypeStruct((model, columns), F32), jax.ShapeDtypeStruct((hidden_part, model), F32),
            jax.ShapeDtypeStruct((width, model), F32), jax.ShapeDtypeStruct((3, width, model), F32),
        ],
        compiler_params=pltpu.CompilerParams(vmem_limit_bytes=62 << 20),
        name="finish",
    )(given_in, given_out, given_weight, given_qkv)


def middle_kernel(
    source, cotangent, mixed_0, mixed_1, mixed_2, mixed_3, own_weight, far_weight, vectors, in_bias, own_in, own_out,
    far_in, far_out, outputs, grad_residual, grad_mixed_0, grad_mixed_1, grad_mixed_2, grad_mixed_3, grad_in, grad_out,
    grad_out_weight, sums, grad_in_bias,
    residual, inverse, second, second_cols, total, grad_second, in_now, out_now, out_weight,
):
    r = pl.program_id(0)
    slices, rows = own_in.shape[0], own_in.shape[1]
    model = source.shape[1]
    hidden_part = own_in.shape[2]
    out_bias, gain, shift, last_bias = (vectors[k : k + 1] for k in range(18, 22))

    @pl.when(r == 0)
    def _():
        value = source[...].astype(F32) + out_bias
        out_weight[0] = own_weight[...]
        narrow = own_weight.shape[0] // slices
        for k in range(far_weight.shape[0]):
            parts = [far_weight[k, j].astype(F32)[:narrow] for j in range(slices)]
            out_weight[k + 1] = jnp.concatenate(parts, axis=0).astype(BF16)
        for k, mixed in enumerate((mixed_0, mixed_1, mixed_2, mixed_3)):
            value += dot(mixed[...], out_weight[k])
        residual[...] = value
        centred = value - jnp.mean(value, axis=-1, keepdims=True)
        factor = lax.rsqrt(jnp.mean(centred * centred, axis=-1, keepdims=True) + EPSILON)
        inverse[...] = factor
        normal = centred * factor
        grad_residual[...] = normal
        rounded = (normal * gain + shift).astype(BF16)
        second[...] = rounded
        second_cols[...] = rounded.astype(F32).T.astype(BF16)
        total[...] = jnp.zeros_like(total)
        grad_second[...] = jnp.zeros_like(grad_second)
        grad_in_bias[...] = jnp.zeros_like(grad_in_bias)
        for j in range(slices):
            in_now[j * rows : (j + 1) * rows] = own_in[j]
            out_now[j * rows : (j + 1) * rows] = own_out[j]

    @pl.when(r > 0)
    def _():
        for j in range(slices):
            in_now[j * rows : (j + 1) * rows] = far_in[0, j]
            out_now[j * rows : (j + 1) * rows] = far_out[0, j]

    half = hidden_part
    for t in range(1):
        span = slice(t * half, (t + 1) * half)
        hidden = dot(second[...], in_now[:, span]) + in_bias[r, 0:1, span]
        cube = hidden * hidden
        root = math.sqrt(2.0 / math.pi)
        bent = jnp.tanh(hidden * (root + (root * 0.044715) * cube))
        lifted = 0.5 + 0.5 * bent
        activation = (hidden * lifted).astype(BF16)
        slope = lifted + hidden * ((0.5 - 0.5 * bent * bent) * (root + (3.0 * root * 0.044715) * cube))
        total[...] += dot(activation, out_now[span])
        given = dot(cotangent[...], out_now[span], ((1,), (1,)))
        grad_hidden = (given * slope).astype(BF16)
        grad_second[...] += dot(grad_hidden, in_now[:, span], ((1,), (1,)))
        grad_in_bias[pl.ds(r, 1), span] = jnp.sum(grad_hidden.astype(F32), axis=0, keepdims=True)
        part = dot(activation, cotangent[...], ((0,), (0,))).astype(BF16)
        per = half // rows
        for k in range(per):
            grad_out[0, t * per + k] = part[k * rows : (k + 1) * rows]
        part = dot(second_cols[...], grad_hidden).astype(BF16)
        for j in range(slices):
            grad_in[0, j, :, span] = part[j * rows : (j + 1) * rows]

    @pl.when(r == pl.num_programs(0) - 1)
    def _():
        given = cotangent[...].astype(F32)
        outputs[...] = (residual[...] + total[...] + last_bias).astype(BF16)
        normal = grad_residual[...]
        grad = grad_second[...]
        scaled = grad * gain
        value = given + inverse[...] * (
            scaled
            - jnp.mean(scaled, axis=-1, keepdims=True)
            - normal * jnp.mean(scaled * normal, axis=-1, keepdims=True)
        )
        sums[0:1] = jnp.sum(value, axis=0, keepdims=True)
        sums[1:2] = jnp.sum(grad * normal, axis=0, keepdims=True)
        sums[2:3] = jnp.sum(grad, axis=0, keepdims=True)
        sums[3:4] = jnp.sum(given, axis=0, keepdims=True)
        sums[4:8] = jnp.zeros((4, model), F32)
        grad_residual[...] = value
        rounded = value.astype(BF16)
        grads = (grad_mixed_0, grad_mixed_1, grad_mixed_2, grad_mixed_3)
        for k, mixed in enumerate((mixed_0, mixed_1, mixed_2, mixed_3)):
            grads[k][...] = dot(rounded, out_weight[k], ((1,), (1,))).astype(BF16)
            product = dot(mixed[...], rounded, ((0,), (0,)))
            narrow = product.shape[0] // slices
            spare = jnp.zeros((grad_out_weight.shape[2] - narrow, model), F32)
            for j in range(slices):
                part = jnp.concatenate([product[j * narrow : (j + 1) * narrow], spare], axis=0)
                grad_out_weight[k, j] = part.astype(BF16)


def middle(source, cotangent, mixed, out_weight, far_weight, vectors, in_bias, own_in, own_out, far_in, far_out):
    own_rows, model = source.shape
    shards = far_in.shape[0] + 1
    slices, rows, hidden_part = own_in.shape
    narrow = mixed[0].shape
    far = pl.BlockSpec((1,) + own_in.shape, lambda r: (jnp.maximum(r - 1, 0), 0, 0, 0))
    part = pl.BlockSpec((1,) + own_in.shape, lambda r: (r, 0, 0, 0))
    macs = own_rows * model * (6 * shards * hidden_part + 3 * model)
    return pl.pallas_call(
        middle_kernel,
        grid_spec=pltpu.PrefetchScalarGridSpec(
            num_scalar_prefetch=0,
            grid=(shards,),
            in_specs=[whole(source.shape)] * 2 + [whole(narrow)] * 4 + [
                whole(out_weight.shape), whole(far_weight.shape), whole(vectors.shape), whole(in_bias.shape), whole(own_in.shape),
                whole(own_out.shape), far, far,
            ],
            out_specs=[whole(source.shape)] * 2 + [whole(narrow)] * 4 + [
                part, part, whole((shards,) + far_weight.shape[1:]), whole((8, model)), whole((shards, hidden_part))
            ],
            scratch_shapes=[
                pltpu.VMEM((own_rows, model), F32),
                pltpu.VMEM((own_rows, 1), F32),
                pltpu.VMEM((own_rows, model), BF16),
                pltpu.VMEM((model, own_rows), BF16),
                pltpu.VMEM((own_rows, model), F32),
                pltpu.VMEM((own_rows, model), F32),
                pltpu.VMEM((model, hidden_part), BF16),
                pltpu.VMEM((hidden_part, model), BF16),
                pltpu.VMEM((shards,) + narrow[1:] + (model,), BF16),
            ],
        ),
        out_shape=[
            jax.ShapeDtypeStruct(source.shape, BF16),
            jax.ShapeDtypeStruct(source.shape, F32),
        ] + [jax.ShapeDtypeStruct(narrow, BF16)] * 4 + [
            jax.ShapeDtypeStruct((shards, slices, rows, hidden_part), BF16),
            jax.ShapeDtypeStruct((shards, slices, rows, hidden_part), BF16),
            jax.ShapeDtypeStruct((shards,) + far_weight.shape[1:], BF16),
            jax.ShapeDtypeStruct((8, model), F32),
            jax.ShapeDtypeStruct((shards, hidden_part), F32),
        ],
        compiler_params=pltpu.CompilerParams(vmem_limit_bytes=60 << 20),
        cost_estimate=pl.CostEstimate(
            flops=2 * macs, bytes_accessed=30 << 20, transcendentals=own_rows * shards * hidden_part
        ),
        name="middle",
    )(source, cotangent, *mixed, out_weight, far_weight, vectors, in_bias, own_in, own_out, far_in, far_out)


def added(a, b):
    return (a.astype(F32) + b.astype(F32)).astype(BF16)


def backward_kernel(
    heads, seg_lengths, qkv, gm_0, gm_1, gm_2, gm_3, logsum, values, probes, key_states_in, key_end_in, rows_in, table_in,
    grad_in, grad_out, grad_weight, out, probe_grad, slice_in, slice_out, slice_weight,
    given, query_grad, memory_grad, row_grad, value_carried, value_back, value_in, row_back, row_in, carried, spread, key_grad, value_grad, cols, keys, vals,
    key_states, key_end, rows, table,
    keep_in, keep_out, keep_weight, core_in, core_out, core_weight, one_in, one_out, one_weight,
    two_in, two_out, two_weight, z_in, z_out, z_weight, send, recv, local_sems,
):
    units = qkv.shape[1]
    half = units // 2
    width = heads * HEAD_DIM
    root = 1.0 / math.sqrt(HEAD_DIM)
    z = lax.axis_index("head")
    flip, run = (z % 2) * half, z // 2
    place = lax.axis_index("dp") % 8
    y, x, c = place // 4, (place // 2) % 2, place % 2
    at = lambda b: (b + flip) % units
    starts, lengths, orders = segments_of(seg_lengths, run, units)
    greet((("head", 1), ("head", 2), ("head", 3), ("dp", 1), ("dp", 2), ("dp", 4)))
    hops = Hops(send, recv)
    started = []

    def go(*args):
        started.append(hops.start(*args))
        return started[-1]

    tables = set_out(
        [(key_states_in, key_states), (key_end_in, key_end), (rows_in, rows), (table_in, table)], local_sems, 12
    )
    given_copies = [go(gm_1, given.at[0, half:], "head", 1), go(gm_3, given.at[1, half:], "head", 1)]
    sums = (
        (grad_in, keep_in, core_in, one_in, two_in, z_in, True),
        (grad_weight, keep_weight, core_weight, one_weight, two_weight, z_weight, True),
        (grad_out, keep_out, core_out, one_out, two_out, z_out, False),
    )
    stage, local_copies = {}, {}
    for i, r in enumerate((2, 1, 3, 0)):
        stage[r], local_copies[r] = [], []
        for n, (term, keep, core, _, _, _, _) in enumerate(sums):
            stage[r].append(go(term.at[r, :, :, 1 - c], core.at[r], "dp", 1))
            copy = pltpu.make_async_copy(term.at[r, :, :, c], keep.at[r], local_sems.at[3 * i + n])
            copy.start()
            local_copies[r].append(copy)

    def first_hop(r):
        for n, (_, keep, core, one, _, _, along_x) in enumerate(sums):
            local_copies[r][n].wait()
            stage[r][n].wait_recv()
            keep[r] = added(keep[r], core[r])
            part = keep.at[r, :, 1 - x] if along_x else keep.at[r, 1 - y]
            stage[r][n] = go(part, one.at[r], "dp", 2 if along_x else 4)

    def second_hop(r):
        for n, (_, keep, _, one, two, _, along_x) in enumerate(sums):
            stage[r][n].wait_recv()
            kept = keep[r, :, x] if along_x else keep[r, y]
            one[r] = added(kept, one[r])
            part = one.at[r, 1 - y] if along_x else one.at[r, 1 - x]
            stage[r][n] = go(part, two.at[r], "dp", 4 if along_x else 2)

    def third_hop(r):
        for n, (_, _, _, one, two, far, along_x) in enumerate(sums):
            stage[r][n].wait_recv()
            kept = one[r, y] if along_x else one[r, x]
            two[r] = added(kept, two[r])
            if r:
                stage[r][n] = go(two.at[r], far.at[r - 1], "head", r)

    for k, own in enumerate((gm_0, gm_2)):
        given[k, :half] = own[...]
    mask = head_rows(heads, LANES)
    lane_head = lax.broadcasted_iota(jnp.int32, (UNIT, LANES), 1) // HEAD_DIM

    def given_of(k, b):
        return jnp.concatenate([given[k, at(b)], jnp.zeros((UNIT, LANES - width), BF16)], axis=1).astype(F32)

    def read_back(rel, k, carry):
        b = at(rel)
        query = qkv[k, rel, :, 0:LANES]
        full = given_of(k, b)
        probe = probes[k, b]
        logits = logits_of(probe, query)
        location, variance = read_parts(logits, heads)
        inverse = 1.0 / variance
        fall = -0.5 * inverse
        peak = WIDTH * lax.rsqrt(variance)
        centres = lax.broadcasted_iota(jnp.int32, (BASIS, UNIT), 0).astype(F32) / (BASIS - 1)
        along, across = [], []
        total = jnp.zeros((BASIS, LANES), F32)
        for h in range(heads):
            own_given = jnp.where(lane_head == h, full, 0.0).astype(BF16)
            gap = centres - location[h : h + 1]
            square = gap * gap
            density = jnp.exp(square * fall[h : h + 1]) * peak[h : h + 1]
            grad_density = dot(values[k, b], own_given, ((1,), (1,)))
            total += dot(density.astype(BF16), own_given)
            weighed = density * grad_density
            moment = weighed * gap
            zeroth = jnp.sum(weighed, axis=0, keepdims=True)
            first = jnp.sum(moment, axis=0, keepdims=True)
            second = jnp.sum(moment * gap, axis=0, keepdims=True)
            along.append(first * inverse[h : h + 1])
            across.append(0.5 * inverse[h : h + 1] * (second * inverse[h : h + 1] - zeroth))
        sigmoid = 1.0 / (1.0 + jnp.exp(-logits))
        grad_location = jnp.concatenate(along, axis=0) * location * (1.0 - location)
        grad_variance = jnp.concatenate(across, axis=0) * SPREAD * sigmoid[heads : 2 * heads]
        grad_logits = jnp.concatenate(
            [grad_location, grad_variance, jnp.zeros((8 - 2 * heads, UNIT), F32)], axis=0
        )
        padded = jnp.concatenate([grad_logits, jnp.zeros((120, UNIT), F32)], axis=0)
        probe_cols = jnp.concatenate([probe, jnp.zeros((120, LANES), F32)], axis=0).T
        query_grad[k, b] = dot(probe_cols.astype(BF16), padded.astype(BF16))[:width]
        fresh = jnp.where(mask, dot(grad_logits.astype(BF16), query), 0.0) * root
        memory_grad[k, b] = total
        row_grad[k, b] = fresh
        return carry

    def gather_back(k, carry):
        probe = jnp.zeros((8, BASIS), F32)
        for i in range(4):
            row_back[k, 8 * i : 8 * i + 8] = jnp.zeros((8, LANES), F32)
        for b in range(units - 1, -1, -1):
            fresh, total = row_grad[k, b], memory_grad[k, b]
            if b > 0:
                probe += dot(fresh.astype(BF16), key_states[k, b], ((1,), (1,)))
            for i in range(4):
                row_back[k, 8 * i : 8 * i + 8] += jnp.where(orders[b] == i, fresh, 0.0)
            if b < units - 1:
                ends = starts[b] + lengths[b] == b + 1
                total = jnp.where(ends, 0.0, memory_grad[k, b + 1]) + total
                memory_grad[k, b] = total
                row_grad[k, b] = jnp.where(ends, 0.0, row_grad[k, b + 1]) + fresh
            before = jnp.zeros((BASIS, LANES), F32) if b == units - 1 else value_carried[k]
            if b > 0:
                value_carried[k] = jnp.where(starts[b] == b, advance_values(table, before + total), before)
            else:
                value_back[k] = (before + total)[:, :width].T.astype(BF16)
        probe_grad[k] = probe
        return carry

    def attend_back(b, k, carry):
        query = qkv[k, at(b), :, 0:LANES].astype(F32) * root
        full = given_of(k, b)
        causal = lax.broadcasted_iota(jnp.int32, (UNIT, UNIT), 0) <= lax.broadcasted_iota(
            jnp.int32, (UNIT, UNIT), 1
        )
        away = [jnp.where(starts[b] <= j, 0.0, 1e30) for j in range(b)] + [0.0]
        owns = [jnp.where(lane_head == h, query, 0.0).astype(BF16) for h in range(heads)]
        own_givens = [jnp.where(lane_head == h, full, 0.0).astype(BF16) for h in range(heads)]
        own_all = jnp.concatenate(owns, axis=0)
        given_all = jnp.concatenate(own_givens, axis=0)
        seen = (b + 1) * UNIT
        scores = dot(keys[k, :seen], own_all, ((1,), (1,)))
        grad_probs = dot(vals[k, :seen], given_all, ((1,), (1,)))
        grads, probs = [], []
        for h in range(heads):
            prob_h, product_h = [], []
            inner = jnp.zeros((1, UNIT), F32)
            for j in range(b + 1):
                tile = (slice(j * UNIT, (j + 1) * UNIT), slice(h * UNIT, (h + 1) * UNIT))
                score = scores[tile]
                if j == b:
                    score = jnp.where(causal, score, -1e30)
                prob = jnp.exp(score - (logsum[k, b, h : h + 1] + away[j]))
                product = prob * grad_probs[tile]
                inner += jnp.sum(product, axis=0, keepdims=True)
                prob_h.append(prob)
                product_h.append(product)
            span = slice(h * HEAD_DIM, (h + 1) * HEAD_DIM)
            grad_h = [(product_h[j] - prob_h[j] * inner).astype(BF16) for j in range(b + 1)]
            result = dot(cols[k, span, :seen], jnp.concatenate(grad_h, axis=0))
            query_grad[k, b, span] = query_grad[k, b, span] + result * root
            grads.append(grad_h)
            probs.append([prob.astype(BF16) for prob in prob_h])
        fresh_keys = dot(jnp.concatenate([jnp.concatenate(g, axis=0) for g in grads], axis=1), own_all)
        fresh_vals = dot(jnp.concatenate([jnp.concatenate(p, axis=0) for p in probs], axis=1), given_all)
        for j in range(b + 1):
            part = slice(j * UNIT, (j + 1) * UNIT)
            if b == units - 1:
                key_grad[k, j], value_grad[k, j] = fresh_keys[part], fresh_vals[part]
            else:
                key_grad[k, j] += fresh_keys[part]
                value_grad[k, j] += fresh_vals[part]
        return carry

    def carry_back(k, total, units_before):
        moved = dot(table[...], total.astype(BF16))
        return moved[:BASIS], (moved[BASIS:] * term_scale(units_before)).astype(BF16)

    def end_back(k, carry):
        row = jnp.where(run == 0, row_in[k], 0.0)
        value = jnp.where(run == 0, value_in[k].astype(F32), 0.0).T
        grad_keys = dot(rows[k].astype(BF16), row.astype(BF16), ((0,), (0,)))
        total = jnp.concatenate([grad_keys, value, jnp.zeros((BASIS, LANES - width), F32)], axis=1)
        carried[k], spread[k] = carry_back(k, total, lengths[units - 1])
        seen = dot(row, key_end[k], ((1,), (1,)), HIGHEST)
        gained = seen[24:32]
        for i in (2, 1, 0):
            high = gained.astype(BF16)
            low = (gained - high.astype(F32)).astype(BF16)
            gained = dot(high, table[:BASIS]) + dot(low, table[:BASIS])
            gained = gained + seen[8 * i : 8 * i + 8]
        probe_grad[k] += gained
        return carry

    def finish(b, k, carry):
        start, length = starts[b], lengths[b]
        token = lax.broadcasted_iota(jnp.int32, (UNIT, LIVE), 0) + (b - start) * UNIT
        centre = (lax.broadcasted_iota(jnp.int32, (UNIT, LIVE), 1) + LIVE).astype(F32) / (BASIS - 1)
        gap = place_of(token, length) - centre
        psi = jnp.exp(gap * gap * (-0.5 / (WIDTH * WIDTH))).astype(BF16)
        pair_grad = dot(psi, spread[k])
        query_rows = query_grad[k, b].T.astype(BF16)
        out[k, at(b), :, :LANES] = jnp.concatenate([query_rows, jnp.zeros((UNIT, LANES - width), BF16)], axis=1)
        out[k, at(b), :, LANES : 2 * LANES] = (key_grad[k, b] + pair_grad[:, :LANES]).astype(BF16)
        out[k, at(b), :, 2 * LANES :] = (value_grad[k, b] + pair_grad[:, LANES:]).astype(BF16)
        if b > 0:
            grad_keys = dot(rows[k, 0:8].astype(BF16), row_grad[k, b].astype(BF16), ((0,), (0,)))
            total = carried[k] + jnp.concatenate([grad_keys, memory_grad[k, b]], axis=1)
            moved, spread_now = carry_back(k, total, lengths[b - 1])
            carried[k] = jnp.where(start == b, moved, carried[k])
            spread[k] = jnp.where(start == b, spread_now.astype(F32), spread[k].astype(F32)).astype(BF16)
        return carry

    def both(step, *args):
        lax.fori_loop(0, 2, functools.partial(step, *args), 0)

    def turn(k, carry):
        for b in range(units):
            part = slice(b * UNIT, (b + 1) * UNIT)
            keys[k, part] = qkv[k, at(b), :, LANES : 2 * LANES]
            vals[k, part] = qkv[k, at(b), :, 2 * LANES : 3 * LANES]
            cols[k, :, part] = qkv[k, at(b), :, LANES : 2 * LANES].astype(F32).T.astype(BF16)
        return carry

    lax.fori_loop(0, 2, turn, 0)
    both(read_back, 0)
    first_hop(2)
    both(read_back, 1)
    first_hop(1)
    for copy in given_copies:
        copy.wait_recv()
    both(read_back, 2)
    first_hop(3)
    first_hop(0)
    both(read_back, 3)
    second_hop(2)
    for copy in tables:
        copy.wait()
    back_copies = []
    for k in range(2):
        gather_back(k, 0)
        back_copies += [
            go(value_back.at[k], value_in.at[1 - k], "head", 2), go(row_back.at[k], row_in.at[1 - k], "head", 2)
        ]
    second_hop(1)
    both(attend_back, 3)
    second_hop(3)
    second_hop(0)
    third_hop(2)
    both(attend_back, 2)
    third_hop(1)
    third_hop(3)
    both(attend_back, 1)
    third_hop(0)
    both(attend_back, 0)
    for copy in back_copies:
        copy.wait_recv()
    lax.fori_loop(0, 2, end_back, 0)
    for b in range(units - 1, -1, -1):
        both(finish, b)
    for n, (_, _, _, _, two, far, _) in enumerate(sums):
        total = two[0].astype(F32)
        for r in (1, 2, 3):
            stage[r][n].wait_recv()
            total += far[r - 1].astype(F32)
        (slice_in, slice_weight, slice_out)[n][...] = total.astype(BF16)
    for copy in started:
        copy.wait_send()


def backward(seg_lengths, qkv, grad_mixed, logsum, values, probes, key_states, key_end, rows, grad_in, grad_out, grad_weight, heads):
    units = qkv.shape[1]
    width = heads * HEAD_DIM
    table = jnp.asarray(basis_tables()[1])
    vmem, anywhere = pl.BlockSpec(memory_space=pltpu.VMEM), pl.BlockSpec(memory_space=pl.ANY)
    shape = jax.ShapeDtypeStruct
    slices = [grad_in.shape[4:], grad_out.shape[4:], grad_weight.shape[4:]]
    hops = 2 + 3 * 4 * 3 + 3 * 3 + 4
    return pl.pallas_call(
        functools.partial(backward_kernel, heads),
        in_specs=[pl.BlockSpec(memory_space=pltpu.SMEM)] + [vmem] * 8 + [anywhere] * 7,
        out_specs=[vmem] * 5,
        out_shape=[shape(qkv.shape, BF16), shape((2, 8, BASIS), F32)] + [shape(part, BF16) for part in slices],
        scratch_shapes=[
            pltpu.VMEM((2, units, UNIT, width), BF16),
            pltpu.VMEM((2, units, width, UNIT), F32),
            pltpu.VMEM((2, units, BASIS, LANES), F32),
            pltpu.VMEM((2, units, 8, LANES), F32),
            pltpu.VMEM((2, BASIS, LANES), F32),
            pltpu.VMEM((2, width, BASIS), BF16),
            pltpu.VMEM((2, width, BASIS), BF16),
            pltpu.VMEM((2, 32, LANES), F32),
            pltpu.VMEM((2, 32, LANES), F32),
            pltpu.VMEM((2, BASIS, 2 * LANES), F32),
            pltpu.VMEM((2, LIVE, 2 * LANES), BF16),
            pltpu.VMEM((2, units, UNIT, LANES), F32),
            pltpu.VMEM((2, units, UNIT, LANES), F32),
            pltpu.VMEM((2, LANES, units * UNIT), BF16),
            pltpu.VMEM((2, units * UNIT, LANES), BF16),
            pltpu.VMEM((2, units * UNIT, LANES), BF16),
            pltpu.VMEM(key_states.shape, BF16),
            pltpu.VMEM(key_end.shape, F32),
            pltpu.VMEM(rows.shape, F32),
            pltpu.VMEM(table.shape, BF16),
        ]
        + [pltpu.VMEM((4, 2, 2) + part, BF16) for part in slices]
        + [pltpu.VMEM((4, 2, 2) + part, BF16) for part in slices]
        + [pltpu.VMEM((4, 2) + part, BF16) for part in slices]
        + [pltpu.VMEM((4,) + part, BF16) for part in slices]
        + [pltpu.VMEM((3,) + part, BF16) for part in slices]
        + [
            pltpu.SemaphoreType.DMA((hops,)),
            pltpu.SemaphoreType.DMA((hops,)),
            pltpu.SemaphoreType.DMA((16,)),
        ],
        compiler_params=pltpu.CompilerParams(
            collective_id=2, has_side_effects=True, vmem_limit_bytes=62 << 20
        ),
        name="backward",
    )(
        seg_lengths, qkv, *grad_mixed, logsum, values, probes, key_states, key_end, rows, table, grad_in, grad_out, grad_weight
    )


def tail_kernel(
    heads, outer, grads, flat_a, flat_b, packed, slice_in, slice_out, slice_weight, sums, in_bias_part, probe_grad,
    first_cols_in, grad_residual_in, source_in, input_grad, whole_in, whole_out, whole_weight, whole_qkv, shared_out, owned_out,
    row_grad, near, kept, part_a, part_b, core_a, core_b, one_a, one_b, two_a, two_b, far_b, total, outer_in,
    gather_in, gather_out, gather_weight, gather_qkv,
    shared, shared_in, block, block_in, bias_block, bias_in, joined, joined_in, first_cols, grad_residual, source,
    send, recv, local_sems,
):
    own_rows, model = source.shape
    loads = set_out(
        [(first_cols_in, first_cols), (grad_residual_in, grad_residual), (source_in, source)], local_sems, 0
    )
    units = grads.shape[1]
    half = units // 2
    width = heads * HEAD_DIM
    z = lax.axis_index("head")
    place = lax.axis_index("dp") % 8
    y, x, c = place // 4, (place // 2) % 2, place % 2
    rows = model // 8
    greet(
        (("head", 1), ("head", 2), ("head", 3), ("dp", 1), ("dp", 2), ("dp", 4)) + tuple(("dp", bit) for bit in outer)
    )
    hops = Hops(send, recv)
    started = []

    def go(*args):
        started.append(hops.start(*args))
        return started[-1]

    def row_of(rel):
        return dot(grads[0, rel], flat_a[...]) + dot(grads[1, rel], flat_b[...])

    row_copies = []
    for k in range(half):
        row_grad[k] = row_of(half + k).astype(BF16)
        row_copies.append(go(row_grad.at[k], near.at[k], "head", 1))

    gathers = ((slice_in, gather_in, True), (slice_weight, gather_weight, True), (slice_out, gather_out, False))
    for own, gather, _ in gathers:
        gather[y, x, c] = own[...]

    def spread_first(gather, along_x):
        part = gather.at[y, x, c]
        return go(part, part, "dp", 2 if along_x else 4)

    def spread_second(gather, along_x):
        part = gather.at[y, :, c] if along_x else gather.at[:, x, c]
        return go(part, part, "dp", 4 if along_x else 2)

    def spread_third(gather):
        part = gather.at[:, :, c]
        return go(part, part, "dp", 1)

    loads[0].wait()
    core_copies = []
    for k, part, core in ((1, part_b, core_b), (0, part_a, core_a)):
        product = dot(first_cols[...], grads[k].reshape(2 * own_rows, 3 * LANES))
        product = jnp.concatenate([product[:, i * LANES : i * LANES + width] for i in range(3)], axis=1).astype(BF16)
        for j in range(8):
            part[j // 4, (j // 2) % 2, j % 2] = product[j * rows : (j + 1) * rows]
        core_copies.append(go(part.at[:, :, 1 - c], core, "dp", 1))
    spreads = [spread_first(gather, along_x) for _, gather, along_x in gathers]
    for k in range(half):
        kept[k] = row_of(k)

    core_copies[0].wait_recv()
    core_b[...] = added(part_b[:, :, c], core_b[...])
    one_copy_b = go(core_b.at[1 - y], one_b, "dp", 4)
    core_copies[1].wait_recv()
    core_a[...] = added(part_a[:, :, c], core_a[...])
    one_copy_a = go(core_a.at[:, 1 - x], one_a, "dp", 2)

    bias_a = jnp.sum(grads[0].reshape(2 * own_rows, 3 * LANES).astype(F32), axis=0, keepdims=True)
    bias_b = jnp.sum(grads[1].reshape(2 * own_rows, 3 * LANES).astype(F32), axis=0, keepdims=True)
    edge = jnp.zeros((8, model - BASIS), F32)
    fill = jnp.zeros((6, model), F32)
    for k, bias in ((0, bias_a), (1, bias_b)):
        block[k, 0:8] = jnp.concatenate([probe_grad[k], edge], axis=1)
        block[k, 8:16] = jnp.concatenate([bias, in_bias_part[2 * k : 2 * k + 1], fill], axis=0)
        bias_block[k] = jnp.concatenate([in_bias_part[2 * k + 1 : 2 * k + 2], jnp.zeros((7, model), F32)], axis=0)
    block_copy = go(block.at[1], block_in, "head", 2)
    bias_copies = [go(bias_block.at[0], bias_in.at[0], "head", 1), go(bias_block.at[1], bias_in.at[1], "head", 3)]

    loads[1].wait()
    loads[2].wait()
    value = source[...].astype(F32)
    centred = value - jnp.mean(value, axis=-1, keepdims=True)
    factor = lax.rsqrt(jnp.mean(centred * centred, axis=-1, keepdims=True) + EPSILON)
    normal = centred * factor

    one_copy_b.wait_recv()
    one_b[...] = added(core_b[y], one_b[...])
    two_copy_b = go(one_b.at[1 - x], two_b, "dp", 2)
    one_copy_a.wait_recv()
    one_a[...] = added(core_a[:, x], one_a[...])
    two_copy_a = go(one_a.at[1 - y], two_a, "dp", 4)
    for copy in row_copies:
        copy.wait_recv()
    two_copy_b.wait_recv()
    two_b[...] = added(one_b[x], two_b[...])
    far_copy = go(two_b, far_b, "head", 2)

    grad = kept[...].reshape(own_rows, model) + near[...].reshape(own_rows, model).astype(F32)
    scaled = grad * packed[16:17]
    change = factor * (
        scaled
        - jnp.mean(scaled, axis=-1, keepdims=True)
        - normal * jnp.mean(scaled * normal, axis=-1, keepdims=True)
    )
    input_grad[...] = (grad_residual[...] + change).astype(BF16)
    shared[...] = jnp.concatenate(
        [jnp.sum(grad * normal, axis=0, keepdims=True), jnp.sum(grad, axis=0, keepdims=True), sums[0:6]], axis=0
    )
    shared_copies = [go(shared, shared_in.at[r - 1], "head", r) for r in (1, 2, 3)]
    spreads = [copy.wait_recv() or spread_second(gather, along_x) for copy, (_, gather, along_x) in zip(spreads, gathers)]

    two_copy_a.wait_recv()
    own_sum = added(one_a[y], two_a[...]).astype(F32)
    far_copy.wait_recv()
    total[0] = (own_sum + far_b[...].astype(F32)).astype(BF16)
    for n, bit in enumerate(outer):
        copy = go(total.at[n], outer_in.at[n], "dp", bit)
        copy.wait_recv()
        total[n + 1] = added(total[n], outer_in[n])
    gather_qkv[y, x, c] = total[len(outer)]
    cut = rows // 2
    upper, lower = pl.ds(0, cut), pl.ds(cut, cut)
    qkv_parts = [gather_qkv.at[y, x, c, upper], gather_qkv.at[y, x, c, lower]]
    qkv_copies = [go(qkv_parts[0], qkv_parts[0], "dp", 2), go(qkv_parts[1], qkv_parts[1], "dp", 4)]

    block_copy.wait_recv()
    for copy in bias_copies + shared_copies:
        copy.wait_recv()
    owned = block[0] + block_in[...]
    bias_rows = bias_in[0] + bias_in[1]
    owned_rows = jnp.concatenate([owned[8:9], owned[9:10] + bias_rows[0:1], owned[10:16]], axis=0)
    joined[0] = jnp.concatenate(
        [shared[...] + shared_in[0] + shared_in[1] + shared_in[2], owned[0:8], owned_rows], axis=0
    )
    spreads = [copy.wait_recv() or spread_third(gather) for copy, (_, gather, _) in zip(spreads, gathers)]
    for n, bit in enumerate((2, 4, 1) + outer):
        copy = go(joined.at[n], joined_in.at[n], "dp", bit)
        if n == 1:
            for copy_one in qkv_copies:
                copy_one.wait_recv()
            qkv_parts = [gather_qkv.at[y, :, c, upper], gather_qkv.at[:, x, c, lower]]
            qkv_copies = [go(qkv_parts[0], qkv_parts[0], "dp", 4), go(qkv_parts[1], qkv_parts[1], "dp", 2)]
        copy.wait_recv()
        joined[n + 1] = joined[n] + joined_in[n]
    last = joined[3 + len(outer)]
    shared_out[...] = last[0:8]
    owned_out[...] = last[8:24]
    for copy, (_, gather, _), out in zip(spreads, gathers, (whole_in, whole_weight, whole_out)):
        copy.wait_recv()
        out[...] = gather[...]
    for copy in qkv_copies:
        copy.wait_recv()
    spread_third(gather_qkv).wait_recv()
    whole_qkv[...] = gather_qkv[...]
    for copy in started:
        copy.wait_send()


def tail(grads, first_cols, flat_a, flat_b, grad_residual, source, packed, slices, sums, in_bias_part, probe_grad, outer, heads):
    own_rows, model = source.shape
    units = grads.shape[1]
    rows = model // 8
    vmem = pl.BlockSpec(memory_space=pltpu.VMEM)
    shape = jax.ShapeDtypeStruct
    slice_in, slice_out, slice_weight = slices
    plane = lambda part: (2, 2, 2) + part
    part = (rows, 3 * heads * HEAD_DIM)
    hops = units // 2 + 9 + 2 + 2 + 2 + 1 + 5 + 1 + 2 + 3 + 3 + 2 * len(outer)
    return pl.pallas_call(
        functools.partial(tail_kernel, heads, outer),
        in_specs=[vmem] * 10 + [pl.BlockSpec(memory_space=pl.ANY)] * 3,
        out_specs=[vmem] * 7,
        out_shape=[
            shape(source.shape, BF16), shape(plane(slice_in.shape), BF16), shape(plane(slice_out.shape), BF16),
            shape(plane(slice_weight.shape), BF16), shape(plane(part), BF16), shape((8, model), F32),
            shape((16, model), F32),
        ],
        scratch_shapes=[
            pltpu.VMEM((units // 2, UNIT, model), BF16),
            pltpu.VMEM((units // 2, UNIT, model), BF16),
            pltpu.VMEM((units // 2, UNIT, model), F32),
            pltpu.VMEM(plane(part), BF16),
            pltpu.VMEM(plane(part), BF16),
            pltpu.VMEM((2, 2) + part, BF16),
            pltpu.VMEM((2, 2) + part, BF16),
            pltpu.VMEM((2,) + part, BF16),
            pltpu.VMEM((2,) + part, BF16),
            pltpu.VMEM(part, BF16),
            pltpu.VMEM(part, BF16),
            pltpu.VMEM(part, BF16),
            pltpu.VMEM((1 + len(outer),) + part, BF16),
            pltpu.VMEM((max(1, len(outer)),) + part, BF16),
            pltpu.VMEM(plane(slice_in.shape), BF16),
            pltpu.VMEM(plane(slice_out.shape), BF16),
            pltpu.VMEM(plane(slice_weight.shape), BF16),
            pltpu.VMEM(plane(part), BF16),
            pltpu.VMEM((8, model), F32),
            pltpu.VMEM((3, 8, model), F32),
            pltpu.VMEM((2, 16, model), F32),
            pltpu.VMEM((16, model), F32),
            pltpu.VMEM((2, 8, model), F32),
            pltpu.VMEM((2, 8, model), F32),
            pltpu.VMEM((4 + len(outer), 24, model), F32),
            pltpu.VMEM((3 + len(outer), 24, model), F32),
            pltpu.VMEM(first_cols.shape, BF16),
            pltpu.VMEM(grad_residual.shape, F32),
            pltpu.VMEM(source.shape, BF16),
            pltpu.SemaphoreType.DMA((hops,)),
            pltpu.SemaphoreType.DMA((hops,)),
            pltpu.SemaphoreType.DMA((3,)),
        ],
        compiler_params=pltpu.CompilerParams(
            collective_id=3, has_side_effects=True, vmem_limit_bytes=60 << 20
        ),
        name="tail",
    )(
        grads, flat_a, flat_b, packed, slice_in, slice_out, slice_weight, sums, in_bias_part, probe_grad, first_cols,
        grad_residual, source,
    )


def exchange(value, axis, bit):
    size = lax.axis_size(axis)
    return lax.ppermute(value, axis, [(j, j ^ bit) for j in range(size)])


def local(
    inputs, seg_lengths, ln1_gain, ln1_bias, qkv_weight, qkv_bias, out_weight, out_bias, mem_mu, mem_sig,
    ln2_gain, ln2_bias, ff_in, ff_in_bias, ff_out, ff_out_bias, cotangent,
):
    own_rows, model = inputs.shape
    shards = lax.axis_size("head")
    members = lax.axis_size("dp")
    width = qkv_weight.shape[2]
    heads = width // HEAD_DIM
    hidden_part = ff_in.shape[1]
    units = 2 * own_rows // UNIT
    slices = 8
    outer = tuple(1 << k for k in range(3, 16) if 1 << k < members)
    rows = model // slices

    bias_row = jnp.pad(qkv_bias, ((0, 0), (0, LANES - width))).reshape(1, 3 * LANES)
    edge = 3 * LANES - BASIS
    packed = jnp.pad(bias_row, ((0, 23), (0, 0))).astype(F32)
    packed += jnp.pad(mem_mu, ((1, 23 - heads), (0, edge))).astype(F32)
    packed += jnp.pad(mem_sig, ((1 + heads, 23 - 2 * heads), (0, edge))).astype(F32)
    given = (ln1_gain, ln1_bias, out_bias, ln2_gain, ln2_bias, ff_out_bias, ff_in_bias)
    line = sum(jnp.pad(vector.astype(F32), (k * model, (6 - k) * model)) for k, vector in enumerate(given))
    packed += jnp.pad(line.reshape(7, model), ((16, 1), (0, 0)))

    turned_weight = jnp.transpose(qkv_weight, (1, 2, 0)).reshape(3 * width, model)
    (
        qkv, first_cols, flat_a, flat_b, values, key_states, key_end, logsum, probes, state_rows,
        *mixed, in_bias, far_in, far_out, far_weight,
    ) = forward(seg_lengths, inputs, packed, turned_weight, out_weight, ff_in, ff_out, heads)
    flat = lambda array: array.reshape((shards - 1, slices) + array.shape[4:])
    outputs, grad_residual, *rest = middle(
        inputs, cotangent, mixed, out_weight, flat(far_weight), packed, in_bias,
        ff_in.reshape(slices, rows, hidden_part), ff_out.reshape(slices, rows, model), flat(far_in), flat(far_out),
    )
    grad_mixed, (ff_in_part, ff_out_part, out_weight_part, sums, in_bias_part) = rest[:4], rest[4:]
    paired = [part.reshape(units // 2, UNIT, width) for part in grad_mixed]
    plane = lambda array: array.reshape((shards, 2, 2, 2) + array.shape[2:])
    grads, probe_grad, *parts = backward(
        seg_lengths, qkv, paired, logsum, values, probes, key_states, key_end, state_rows, plane(ff_in_part),
        plane(ff_out_part), plane(out_weight_part), heads,
    )
    for bit in outer:
        parts = [added(part, exchange(part, "dp", bit)) for part in parts]
    input_grad, whole_in, whole_out, whole_weight, whole_qkv, shared, owned = tail(
        grads, first_cols, flat_a, flat_b, grad_residual, inputs, packed, parts, sums, in_bias_part, probe_grad,
        outer, heads,
    )
    ff_in_sum, ff_out_sum, out_weight_sum, qkv_weight_sum = finish(
        whole_in.reshape(model, hidden_part), whole_out.reshape(hidden_part, model),
        whole_weight.reshape((slices,) + whole_weight.shape[3:]), whole_qkv.reshape(model, 3 * width), width,
    )
    return (
        outputs, input_grad, shared[0], shared[1], jnp.transpose(qkv_weight_sum, (2, 0, 1)),
        owned[8].reshape(3, LANES)[:, :width], out_weight_sum, shared[2], owned[:heads, :BASIS],
        owned[heads : 2 * heads, :BASIS], shared[3], shared[4], ff_in_sum, owned[9, :hidden_part], ff_out_sum, shared[5],
    )


def solution(mesh):
    rows, whole = P(("dp", "head"), None), P()
    return jax.shard_map(
        local,
        mesh=mesh,
        in_specs=(
            rows, P("dp", None), whole, whole, P(None, None, "head"), P(None, "head"), P("head", None), whole,
            P("head", None), P("head", None), whole, whole, P(None, "head"), P("head"), P("head", None), whole, rows,
        ),
        out_specs=(
            rows, rows, whole, whole, P(None, None, "head"), P(None, "head"), P("head", None), whole,
            P("head", None), P("head", None), whole, whole, P(None, "head"), P("head"), P("head", None), whole,
        ),
        check_vma=False,
    )
```

```python
import functools
import math

import jax
import jax.numpy as jnp
import ml_dtypes
import numpy as np
from jax import lax
from jax.experimental import pallas as pl
from jax.experimental.pallas import tpu as pltpu
from jax.sharding import PartitionSpec as P

HEAD_DIM = 64
BASIS = 512
UNIT = 256
LANES = 256
TAU = 0.75
RIDGE = 0.5
EPSILON = 1e-05
MESH = pl.DeviceIdType.MESH
SPREAD = 1.0 / 64.0
WIDTH = 1.0 / BASIS
LIVE = BASIS // 2
HIGHEST = lax.Precision.HIGHEST
F32 = jnp.float32
BF16 = jnp.bfloat16


def split_table(table):
    high = table.astype(np.float32).astype(ml_dtypes.bfloat16)
    low = (table.astype(np.float32) - high.astype(np.float32)).astype(ml_dtypes.bfloat16)
    return high, low


@functools.lru_cache(maxsize=None)
def basis_tables():
    centres = np.arange(BASIS) / (BASIS - 1)
    apart = centres[:, None] - centres[None, :]
    gram = np.exp(-apart * apart / (4.0 * WIDTH * WIDTH)) + RIDGE * np.eye(BASIS)
    solve = np.linalg.inv(gram)
    samples = (np.arange(BASIS) + 0.5) / BASIS
    near_gap = TAU * samples[:, None] - centres[None, :]
    far_gap = samples[:, None] - centres[None, :]
    near = np.exp(-near_gap * near_gap / (2.0 * WIDTH * WIDTH))
    far = np.exp(-far_gap * far_gap / (2.0 * WIDTH * WIDTH))
    contract = (near.T @ far) * (TAU / (BASIS * WIDTH * math.sqrt(math.pi)))
    joined = np.concatenate([solve @ contract, solve[:, LIVE:]], axis=1)
    high, low = split_table(joined)
    forward = np.concatenate([high, high, low], axis=1)
    backward = np.ascontiguousarray(high.T)
    return forward, backward


def term_scale(units):
    return (1.0 - TAU) / (WIDTH * math.sqrt(math.pi) * UNIT) / units.astype(F32)


def split3(value):
    high = value.astype(BF16)
    low = (value - high.astype(F32)).astype(BF16)
    return jnp.concatenate([high, low, high], axis=0)


def dot(a, b, contract=((1,), (0,)), precision=None):
    return lax.dot_general(a, b, (contract, ((), ())), precision=precision, preferred_element_type=F32)


def head_rows(heads, width):
    row = lax.broadcasted_iota(jnp.int32, (8, width), 0)
    lane = lax.broadcasted_iota(jnp.int32, (8, width), 1) // HEAD_DIM
    return ((row == lane) | (row == lane + heads)) & (lane < heads)


def read_parts(logits, heads):
    location = 1.0 / (1.0 + jnp.exp(-logits))
    variance = (jnp.maximum(logits, 0.0) + jnp.log1p(jnp.exp(-jnp.abs(logits)))) * SPREAD + WIDTH * WIDTH
    return location[:heads], variance[heads : 2 * heads]


def place_of(index, length):
    return TAU + (1.0 - TAU) * (index.astype(F32) + 0.5) / (length.astype(F32) * UNIT)


def split_rows(value):
    high = value.astype(BF16)
    rest = value - high.astype(F32)
    mid = rest.astype(BF16)
    return high, mid, (rest - mid.astype(F32)).astype(BF16)


def three_pass(left, right_high, right_low, contract=((1,), (0,))):
    high = left.astype(BF16)
    low = (left - high.astype(F32)).astype(BF16)
    return dot(high, right_high, contract) + dot(low, right_high, contract) + dot(high, right_low, contract)


def advance_values(table, value):
    return dot(table[:BASIS, :BASIS], value.astype(BF16))


def logits_of(probes, query):
    parts = dot(jnp.concatenate(split_rows(probes), axis=0), query, ((1,), (1,)))
    return parts[0:8] + parts[8:16] + parts[16:24]


def segments_of(lengths, run, units):
    sizes = [lengths[0, run * units + s] // UNIT for s in range(units)]
    ends, total = [], 0
    for size in sizes:
        total = total + size
        ends.append(total)
    starts, spans, orders = [], [], []
    for b in range(units):
        start, span, order = 0, 0, 0
        for size, end in zip(sizes, ends):
            inside = (end > b) & (end - size <= b)
            start = start + jnp.where(inside, end - size, 0)
            span = span + jnp.where(inside, size, 0)
            order = order + jnp.where((end <= b) & (size > 0), 1, 0)
        starts.append(start)
        spans.append(span)
        orders.append(order)
    return starts, spans, orders


def other_of(index, distance):
    bit = 1
    while bit <= distance:
        if distance & bit:
            index = index + bit - 2 * bit * ((index // bit) % 2)
        bit *= 2
    return index


class Hops:
    def __init__(self, send, recv):
        self.send, self.recv, self.used = send, recv, 0

    def start(self, source, target, axis, bit):
        copy = self.make(source, target, axis, bit)
        copy.start()
        return copy

    def make(self, source, target, axis, bit):
        copy = pltpu.make_async_remote_copy(
            src_ref=source,
            dst_ref=target,
            send_sem=self.send.at[self.used],
            recv_sem=self.recv.at[self.used],
            device_id={axis: other_of(lax.axis_index(axis), bit)},
            device_id_type=MESH,
        )
        self.used += 1
        return copy


def greet(neighbours):
    barrier = pltpu.get_barrier_semaphore()
    for axis, bit in neighbours:
        pl.semaphore_signal(
            barrier, inc=1, device_id={axis: other_of(lax.axis_index(axis), bit)}, device_id_type=MESH
        )
    pl.semaphore_wait(barrier, len(neighbours))


def set_out(pairs, sems, first):
    copies = [pltpu.make_async_copy(a, b, sems.at[first + k]) for k, (a, b) in enumerate(pairs)]
    for copy in copies:
        copy.start()
    return copies


def forward_kernel(
    heads, seg_lengths, source, packed, weight, out_weight, table, ff_in, ff_out,
    qkv_out, first_cols_out, flat_a_out, flat_b_out, values_out, key_states_out, key_end_out, logsum, probes, rows,
    mixed_0, mixed_1, mixed_2, mixed_3, in_bias, far_in, far_out, far_weight,
    qkv, first_rows, first_cols, flats, near, far, far_flat, small, far_row, bias_row, weight_mine, memory, sums, value_states, carried, value_ends, value_ins,
    projs, proj_ins, cols, keys, discrete, mixed, mixed_in, values, key_states, key_end, send, recv, local_sems,
):
    own_rows, model = source.shape
    width = heads * HEAD_DIM
    units = qkv.shape[1]
    half = units // 2
    root = 1.0 / math.sqrt(HEAD_DIM)
    z = lax.axis_index("head")
    flip, run = (z % 2) * half, z // 2
    place = lax.axis_index("dp") % 8
    y, x, c = place // 4, (place // 2) % 2, place % 2
    slice_rows = model // 8
    at = lambda b: (b + flip) % units
    starts, lengths, orders = segments_of(seg_lengths, run, units)
    greet((("head", 1), ("head", 2), ("head", 3), ("dp", 1), ("dp", 2), ("dp", 4)))
    hops = Hops(send, recv)
    started = []

    def go(*args):
        started.append(hops.start(*args))
        return started[-1]

    part_rows, part_cols = far.shape[3:]
    mine = weight.at[
        pl.ds(pl.multiple_of((2 * y + x) * part_rows, 16), part_rows),
        pl.ds(pl.multiple_of(c * part_cols, 128), part_cols),
    ]
    small[...] = packed[0:16]
    bias_row[...] = jnp.broadcast_to(packed[22:23], bias_row.shape)
    narrow = width // 8
    chosen = jnp.zeros((narrow, model), F32)
    for j in range(8):
        chosen += jnp.where(place == j, out_weight[j * narrow : (j + 1) * narrow].astype(F32), 0.0)
    spare = jnp.zeros((weight_mine.shape[0] - narrow, model), F32)
    weight_mine[...] = jnp.concatenate([chosen, spare], axis=0).astype(BF16)
    slice_copy = go(mine, far.at[y, x, c], "head", 2)
    small_copy = go(small, far_row, "head", 2)
    row_copies = []
    for k in range(half):
        part = slice(k * UNIT, (k + 1) * UNIT)
        value = source[part].astype(F32)
        centred = value - jnp.mean(value, axis=-1, keepdims=True)
        factor = lax.rsqrt(jnp.mean(centred * centred, axis=-1, keepdims=True) + EPSILON)
        first_rows[part] = (centred * factor * packed[16:17] + packed[17:18]).astype(BF16)
        row_copies.append(go(first_rows.at[part], near.at[part], "head", 1))
    in_mine = ff_in.at[pl.ds(pl.multiple_of(place * slice_rows, 16), slice_rows)]
    out_mine = ff_out.at[pl.ds(pl.multiple_of(place * slice_rows, 16), slice_rows)]
    gathers = ((far_in, 2, 4), (far_weight, 2, 4), (far_out, 4, 2))
    stage = {}

    for r in (1, 2, 3):
        stage[r] = [
            hops.make(in_mine, far_in.at[r - 1, y, x, c], "head", r),
            hops.make(weight_mine, far_weight.at[r - 1, y, x, c], "head", r),
            hops.make(out_mine, far_out.at[r - 1, y, x, c], "head", r),
        ]
        started.extend(stage[r])
    at_end = (z == 0) | (z == 3)

    def send_chunk(r):
        for copy in stage[r]:
            copy.start()

    def send_early(first):
        pl.when(at_end)(functools.partial(send_chunk, 2 if first else 3))
        pl.when(jnp.logical_not(at_end))(functools.partial(send_chunk, 3 if first else 2))


    def advance(r, step):
        for copy in stage[r]:
            copy.wait_recv()
        stage[r] = []
        for array, first, second in gathers:
            block = array.at[r - 1]
            if step == 1:
                part, bit = block.at[y, x, c], first
            elif step == 2:
                part, bit = (block.at[y, :, c] if first == 2 else block.at[:, x, c]), second
            else:
                part, bit = block.at[:, :, c], 1
            stage[r].append(go(part, part, "dp", bit))

    send_chunk(1)
    send_early(True)
    in_bias[0] = bias_row[...]
    bias_copies = [go(bias_row, in_bias.at[r], "head", r) for r in (1, 2, 3)]

    slice_copy.wait_recv()
    x_copy = go(far.at[y, x, c], far.at[y, x, c], "dp", 2)

    def widen(k, read):
        for i in range(3):
            flats[k, i * LANES : i * LANES + width] = read(slice(i * width, (i + 1) * width))
            flats[k, i * LANES + width : (i + 1) * LANES] = jnp.zeros((LANES - width, model), BF16)

    def project(k, unit, shift):
        span = slice(unit * UNIT, (unit + 1) * UNIT)
        qkv[k, unit] = (dot(first_rows[span], flats[k], ((1,), (1,))) + shift).astype(BF16)

    widen(0, lambda span: weight[span])
    for unit in range(half):
        project(0, unit, small[0:1])
    x_copy.wait_recv()
    y_copy = go(far.at[y, :, c], far.at[y, :, c], "dp", 4)
    first_cols[:, :own_rows] = first_rows[:own_rows].astype(F32).T.astype(BF16)
    y_copy.wait_recv()
    core_copy = go(far.at[:, :, c], far.at[:, :, c], "dp", 1)
    small_copy.wait_recv()
    for k, copy in enumerate(row_copies):
        copy.wait_recv()
        part = slice(k * UNIT, (k + 1) * UNIT)
        first_rows[own_rows + k * UNIT : own_rows + (k + 1) * UNIT] = near[part]
        project(0, half + k, small[0:1])
    send_early(False)

    advance(1, 1)
    first_cols[:, own_rows:] = near[...].astype(F32).T.astype(BF16)
    core_copy.wait_recv()
    for i in range(8):
        row, col = (i // 2) * part_rows, (i % 2) * part_cols
        far_flat[row : row + part_rows, col : col + part_cols] = far[i // 4, (i // 2) % 2, i % 2]
    widen(1, lambda span: far_flat[span])
    for unit in range(units):
        project(1, unit, far_row[0:1])
    saved = set_out(
        [(qkv, qkv_out), (first_cols, first_cols_out), (flats.at[0], flat_a_out), (flats.at[1], flat_b_out)],
        local_sems, 0,
    )

    def probe_of(k):
        return jnp.where(k == 0, small[1:9, :BASIS], far_row[1:9, :BASIS])

    mask = head_rows(heads, LANES)

    def first_state(k, carry):
        memory[k] = jnp.zeros(memory.shape[1:], F32)
        row = probe_of(k)
        rows[k, 0:8] = row
        wide = 2 * (BASIS + LIVE)
        for i in range(1, 4):
            row = three_pass(row, table[:, :BASIS], table[:, wide : wide + BASIS])
            rows[k, 8 * i : 8 * i + 8] = row
        return carry

    lax.fori_loop(0, 2, first_state, 0)

    def state(b, k, carry):
        start, length = starts[b], lengths[b]
        now = memory[k]
        value_states[k, b] = now[:, LANES:]
        key_states[k, b] = now[:, :LANES].astype(BF16)
        if b > 0:
            probes[k, b] = jnp.where(mask, dot(rows[k, 0:8], now[:, :LANES], precision=HIGHEST), 0.0)
        else:
            probes[k, b] = jnp.zeros((8, LANES), F32)
        token = lax.broadcasted_iota(jnp.int32, (LIVE, UNIT), 1) + (b - start) * UNIT
        centre = (lax.broadcasted_iota(jnp.int32, (LIVE, UNIT), 0) + LIVE).astype(F32) / (BASIS - 1)
        gap = place_of(token, length) - centre
        psi = jnp.exp(gap * gap * (-0.5 / (WIDTH * WIDTH)))
        psi_high = psi.astype(BF16)
        psi_low = (psi - psi_high.astype(F32)).astype(BF16)
        pairs = qkv[k, at(b), :, LANES : 3 * LANES]
        exact = dot(psi_high, pairs[:, :LANES]) + dot(psi_low, pairs[:, :LANES])
        fresh = jnp.concatenate([exact, dot(psi_high, pairs[:, LANES:])], axis=1)
        gathered = fresh if b == 0 else jnp.where(start == b, 0.0, sums[k]) + fresh
        sums[k] = gathered
        stacked = jnp.concatenate([now, gathered * term_scale(length)], axis=0)
        later = jnp.concatenate(
            [
                dot(table[...], split3(stacked[:, :LANES])),
                dot(table[:, : BASIS + LIVE], stacked[:, LANES:].astype(BF16)),
            ],
            axis=1,
        )
        memory[k] = jnp.where(start + length == b + 1, later, now)
        return carry

    def end_state(k, carry):
        key = memory[k, :, :LANES]
        key_end[k] = key
        value_ends[k] = memory[k, :, LANES : LANES + width].T.astype(BF16)
        seen = dot(rows[k], key, precision=HIGHEST)
        for i in range(4):
            projs[k, 8 * i : 8 * i + 8] = jnp.where(mask, seen[8 * i : 8 * i + 8], 0.0)
        return carry

    def attend(b, k, carry):
        cols[k, :, b * UNIT : (b + 1) * UNIT] = qkv[k, at(b), :, 2 * LANES : 3 * LANES].astype(F32).T.astype(BF16)
        keys[k, b * UNIT : (b + 1) * UNIT] = qkv[k, at(b), :, LANES : 2 * LANES]
        query = qkv[k, at(b), :, 0:LANES].astype(F32) * root
        lane_head = lax.broadcasted_iota(jnp.int32, (UNIT, LANES), 1) // HEAD_DIM
        causal = lax.broadcasted_iota(jnp.int32, (UNIT, UNIT), 0) <= lax.broadcasted_iota(
            jnp.int32, (UNIT, UNIT), 1
        )
        away = [jnp.where(starts[b] <= j, 0.0, 1e30) for j in range(b)] + [0.0]
        owns = jnp.concatenate([jnp.where(lane_head == h, query, 0.0).astype(BF16) for h in range(heads)], axis=0)
        seen = (b + 1) * UNIT
        products = dot(keys[k, :seen], owns, ((1,), (1,)))
        for h in range(heads):
            scores = [products[j * UNIT : (j + 1) * UNIT, h * UNIT : (h + 1) * UNIT] for j in range(b + 1)]
            scores[b] = jnp.where(causal, scores[b], -1e30)
            highest = functools.reduce(
                jnp.maximum, [jnp.max(s, axis=0, keepdims=True) - away[j] for j, s in enumerate(scores)]
            )
            weights = [jnp.exp(s - (highest + away[j])) for j, s in enumerate(scores)]
            total = sum(jnp.sum(w, axis=0, keepdims=True) for w in weights)
            span = slice(h * HEAD_DIM, (h + 1) * HEAD_DIM)
            part = dot(cols[k, span, :seen], jnp.concatenate([w.astype(BF16) for w in weights], axis=0))
            discrete[k, b, span] = part * (1.0 / total)
            logsum[k, b, h : h + 1] = highest + jnp.log(total)
        return carry

    def seen_value(k, carry):
        incoming = jnp.where(run > 0, value_ins[k].astype(F32), 0.0).T
        carried[:, :width] = incoming
        carried[:, width:] = jnp.zeros((BASIS, LANES - width), F32)
        for b in range(units):
            if b > 0:
                carried[...] = jnp.where(starts[b] == b, advance_values(table, carried[...]), carried[...])
            values[k, b] = (value_states[k, b] + carried[...]).astype(BF16)
            gained = jnp.zeros((8, LANES), F32)
            for i in range(4):
                gained += jnp.where((orders[b] == i) & (run > 0), proj_ins[k, 8 * i : 8 * i + 8], 0.0)
            probes[k, b] = (probes[k, b] + gained) * root
        return carry

    def read(rel, k, carry):
        b = at(rel)
        query = qkv[k, rel, :, 0:LANES]
        logits = logits_of(probes[k, b], query)
        location, variance = read_parts(logits, heads)
        fall = -0.5 / variance
        peak = WIDTH * lax.rsqrt(variance)
        centres = lax.broadcasted_iota(jnp.int32, (BASIS, UNIT), 0).astype(F32) / (BASIS - 1)
        value_cols = values[k, b].astype(F32).T.astype(BF16)
        parts = []
        for h in range(heads):
            gap = centres - location[h : h + 1]
            density = jnp.exp(gap * gap * fall[h : h + 1]).astype(BF16)
            span = slice(h * HEAD_DIM, (h + 1) * HEAD_DIM)
            parts.append(discrete[k, b, span] + dot(value_cols[span], density) * peak[h : h + 1])
        mixed[k, rel] = jnp.concatenate(parts, axis=0).T.astype(BF16)
        return carry

    advance(1, 2)
    state_copies = []
    for k in range(2):
        for b in range(units):
            state(b, k, 0)
        end_state(k, 0)
        state_copies.append([
            go(value_ends.at[k], value_ins.at[1 - k], "head", 2), go(projs.at[k], proj_ins.at[1 - k], "head", 2)
        ])
        if k == 0:
            advance(2, 1)
            advance(3, 1)
        if k == 1:
            advance(1, 3)
    for b in range(units):
        lax.fori_loop(0, 2, functools.partial(attend, b), 0)
        if b == 0:
            advance(2, 2)
        if b == 2:
            advance(3, 2)
        if b == 3:
            advance(2, 3)
    saved += set_out([(key_states, key_states_out), (key_end, key_end_out)], local_sems, 4)
    mixed_copies = [None, None]
    for k in (1, 0):
        for copy in state_copies[1 - k]:
            copy.wait_recv()
        seen_value(k, 0)
        read(2, k, 0)
        read(3, k, 0)
        mixed_copies[k] = go(mixed.at[k, half:], mixed_in.at[k], "head", 1)
        if k == 1:
            advance(3, 3)
    saved += set_out([(values, values_out)], local_sems, 6)
    lax.fori_loop(0, 2, functools.partial(read, 0), 0)
    lax.fori_loop(0, 2, functools.partial(read, 1), 0)
    mixed_0[...] = mixed[0, :half].reshape(own_rows, width)
    mixed_2[...] = mixed[1, :half].reshape(own_rows, width)
    for copy in mixed_copies:
        copy.wait_recv()
    mixed_1[...] = mixed_in[0].reshape(own_rows, width)
    mixed_3[...] = mixed_in[1].reshape(own_rows, width)
    for copy in bias_copies + stage[1] + stage[2] + stage[3]:
        copy.wait_recv()
    for copy in started:
        copy.wait_send()
    for copy in saved:
        copy.wait()


def forward(seg_lengths, source, packed, weight, out_weight, ff_in, ff_out, heads):
    own_rows, model = source.shape
    units = 2 * own_rows // UNIT
    width = heads * HEAD_DIM
    hidden_part = ff_in.shape[1]
    rows = model // 8
    spaced = -(-width // 8 // 16) * 16
    table = jnp.asarray(basis_tables()[0])
    vmem, anywhere = pl.BlockSpec(memory_space=pltpu.VMEM), pl.BlockSpec(memory_space=pl.ANY)
    shape = jax.ShapeDtypeStruct
    hops = 2 + units // 2 + 3 + 3 * 3 * 4 + 3 + 4 + 2
    return pl.pallas_call(
        functools.partial(forward_kernel, heads),
        in_specs=[pl.BlockSpec(memory_space=pltpu.SMEM)] + [vmem] * 5 + [anywhere] * 2,
        out_specs=[anywhere] * 7 + [vmem] * 8 + [anywhere] * 3,
        out_shape=[
            shape((2, units, UNIT, 3 * LANES), BF16),
            shape((model, 2 * own_rows), BF16),
            shape((3 * LANES, model), BF16),
            shape((3 * LANES, model), BF16),
            shape((2, units, BASIS, LANES), BF16),
            shape((2, units, BASIS, LANES), BF16),
            shape((2, BASIS, LANES), F32),
            shape((2, units, 8, UNIT), F32),
            shape((2, units, 8, LANES), F32),
            shape((2, 32, BASIS), F32),
        ] + [shape((own_rows, width), BF16)] * 4 + [
            shape((4, 8, hidden_part), F32),
            shape((3, 2, 2, 2, rows, hidden_part), BF16),
            shape((3, 2, 2, 2, rows, model), BF16),
            shape((3, 2, 2, 2, spaced, model), BF16),
        ],
        scratch_shapes=[
            pltpu.VMEM((2, units, UNIT, 3 * LANES), BF16),
            pltpu.VMEM((2 * own_rows, model), BF16),
            pltpu.VMEM((model, 2 * own_rows), BF16),
            pltpu.VMEM((2, 3 * LANES, model), BF16),
            pltpu.VMEM((own_rows, model), BF16),
            pltpu.VMEM((2, 2, 2, 3 * width // 4, model // 2), BF16),
            pltpu.VMEM((3 * width, model), BF16),
            pltpu.VMEM((16, 3 * LANES), F32),
            pltpu.VMEM((16, 3 * LANES), F32),
            pltpu.VMEM((8, hidden_part), F32),
            pltpu.VMEM((spaced, model), BF16),
            pltpu.VMEM((2, BASIS, 2 * LANES), F32),
            pltpu.VMEM((2, LIVE, 2 * LANES), F32),
            pltpu.VMEM((2, units, BASIS, LANES), F32),
            pltpu.VMEM((BASIS, LANES), F32),
            pltpu.VMEM((2, width, BASIS), BF16),
            pltpu.VMEM((2, width, BASIS), BF16),
            pltpu.VMEM((2, 32, LANES), F32),
            pltpu.VMEM((2, 32, LANES), F32),
            pltpu.VMEM((2, LANES, units * UNIT), BF16),
            pltpu.VMEM((2, units * UNIT, LANES), BF16),
            pltpu.VMEM((2, units, width, UNIT), F32),
            pltpu.VMEM((2, units, UNIT, width), BF16),
            pltpu.VMEM((2, units // 2, UNIT, width), BF16),
            pltpu.VMEM((2, units, BASIS, LANES), BF16),
            pltpu.VMEM((2, units, BASIS, LANES), BF16),
            pltpu.VMEM((2, BASIS, LANES), F32),
            pltpu.SemaphoreType.DMA((hops,)),
            pltpu.SemaphoreType.DMA((hops,)),
            pltpu.SemaphoreType.DMA((7,)),
        ],
        compiler_params=pltpu.CompilerParams(
            collective_id=1, has_side_effects=True, vmem_limit_bytes=60 << 20
        ),
        name="forward",
    )(seg_lengths, source, packed, weight, out_weight, table, ff_in, ff_out)


def whole(shape):
    return pl.BlockSpec(shape, lambda i: (0,) * len(shape))


def finish_kernel(given_in, given_out, given_weight, given_qkv, grad_in, grad_out, grad_weight, grad_qkv):
    step = pl.program_id(0)
    grad_in[...] = given_in[...].astype(F32)
    grad_out[...] = given_out[...].astype(F32)
    width = grad_qkv.shape[1]
    for i in range(3):

        @pl.when(step == i)
        def _():
            grad_qkv[0] = given_qkv[:, i * width : (i + 1) * width].astype(F32).T

    @pl.when(step == 0)
    def _():
        narrow = grad_weight.shape[0] // given_weight.shape[0]
        for j in range(given_weight.shape[0]):
            grad_weight[j * narrow : (j + 1) * narrow] = given_weight[j].astype(F32)[:narrow]


def finish(given_in, given_out, given_weight, given_qkv, width):
    model, columns = given_in.shape
    hidden_part = given_out.shape[0]
    return pl.pallas_call(
        finish_kernel,
        grid=(3,),
        in_specs=[
            pl.BlockSpec((model // 3, columns), lambda i: (i, 0)),
            pl.BlockSpec((hidden_part // 3, model), lambda i: (i, 0)),
            pl.BlockSpec(given_weight.shape, lambda i: (0, 0, 0)),
            pl.BlockSpec(given_qkv.shape, lambda i: (0, 0)),
        ],
        out_specs=[
            pl.BlockSpec((model // 3, columns), lambda i: (i, 0)),
            pl.BlockSpec((hidden_part // 3, model), lambda i: (i, 0)),
            pl.BlockSpec((width, model), lambda i: (0, 0)),
            pl.BlockSpec((1, width, model), lambda i: (i, 0, 0)),
        ],
        out_shape=[
            jax.ShapeDtypeStruct((model, columns), F32), jax.ShapeDtypeStruct((hidden_part, model), F32),
            jax.ShapeDtypeStruct((width, model), F32), jax.ShapeDtypeStruct((3, width, model), F32),
        ],
        compiler_params=pltpu.CompilerParams(vmem_limit_bytes=62 << 20),
        name="finish",
    )(given_in, given_out, given_weight, given_qkv)


def middle_kernel(
    source, cotangent, mixed_0, mixed_1, mixed_2, mixed_3, own_weight, far_weight, vectors, in_bias, own_in, own_out,
    far_in, far_out, outputs, grad_residual, grad_mixed_0, grad_mixed_1, grad_mixed_2, grad_mixed_3, grad_in, grad_out,
    grad_out_weight, sums, grad_in_bias,
    residual, inverse, second, second_cols, total, grad_second, in_now, out_now, out_weight,
):
    r = pl.program_id(0)
    slices, rows = own_in.shape[0], own_in.shape[1]
    model = source.shape[1]
    hidden_part = own_in.shape[2]
    out_bias, gain, shift, last_bias = (vectors[k : k + 1] for k in range(18, 22))

    @pl.when(r == 0)
    def _():
        value = source[...].astype(F32) + out_bias
        out_weight[0] = own_weight[...]
        narrow = own_weight.shape[0] // slices
        for k in range(far_weight.shape[0]):
            parts = [far_weight[k, j].astype(F32)[:narrow] for j in range(slices)]
            out_weight[k + 1] = jnp.concatenate(parts, axis=0).astype(BF16)
        for k, mixed in enumerate((mixed_0, mixed_1, mixed_2, mixed_3)):
            value += dot(mixed[...], out_weight[k])
        residual[...] = value
        centred = value - jnp.mean(value, axis=-1, keepdims=True)
        factor = lax.rsqrt(jnp.mean(centred * centred, axis=-1, keepdims=True) + EPSILON)
        inverse[...] = factor
        normal = centred * factor
        grad_residual[...] = normal
        rounded = (normal * gain + shift).astype(BF16)
        second[...] = rounded
        second_cols[...] = rounded.astype(F32).T.astype(BF16)
        total[...] = jnp.zeros_like(total)
        grad_second[...] = jnp.zeros_like(grad_second)
        grad_in_bias[...] = jnp.zeros_like(grad_in_bias)
        for j in range(slices):
            in_now[j * rows : (j + 1) * rows] = own_in[j]
            out_now[j * rows : (j + 1) * rows] = own_out[j]

    @pl.when(r > 0)
    def _():
        for j in range(slices):
            in_now[j * rows : (j + 1) * rows] = far_in[0, j]
            out_now[j * rows : (j + 1) * rows] = far_out[0, j]

    half = hidden_part
    for t in range(1):
        span = slice(t * half, (t + 1) * half)
        hidden = dot(second[...], in_now[:, span]) + in_bias[r, 0:1, span]
        cube = hidden * hidden
        root = math.sqrt(2.0 / math.pi)
        bent = jnp.tanh(hidden * (root + (root * 0.044715) * cube))
        lifted = 0.5 + 0.5 * bent
        activation = (hidden * lifted).astype(BF16)
        slope = lifted + hidden * ((0.5 - 0.5 * bent * bent) * (root + (3.0 * root * 0.044715) * cube))
        total[...] += dot(activation, out_now[span])
        given = dot(cotangent[...], out_now[span], ((1,), (1,)))
        grad_hidden = (given * slope).astype(BF16)
        grad_second[...] += dot(grad_hidden, in_now[:, span], ((1,), (1,)))
        grad_in_bias[pl.ds(r, 1), span] = jnp.sum(grad_hidden.astype(F32), axis=0, keepdims=True)
        part = dot(activation, cotangent[...], ((0,), (0,))).astype(BF16)
        per = half // rows
        for k in range(per):
            grad_out[0, t * per + k] = part[k * rows : (k + 1) * rows]
        part = dot(second_cols[...], grad_hidden).astype(BF16)
        for j in range(slices):
            grad_in[0, j, :, span] = part[j * rows : (j + 1) * rows]

    @pl.when(r == pl.num_programs(0) - 1)
    def _():
        given = cotangent[...].astype(F32)
        outputs[...] = (residual[...] + total[...] + last_bias).astype(BF16)
        normal = grad_residual[...]
        grad = grad_second[...]
        scaled = grad * gain
        value = given + inverse[...] * (
            scaled
            - jnp.mean(scaled, axis=-1, keepdims=True)
            - normal * jnp.mean(scaled * normal, axis=-1, keepdims=True)
        )
        sums[0:1] = jnp.sum(value, axis=0, keepdims=True)
        sums[1:2] = jnp.sum(grad * normal, axis=0, keepdims=True)
        sums[2:3] = jnp.sum(grad, axis=0, keepdims=True)
        sums[3:4] = jnp.sum(given, axis=0, keepdims=True)
        sums[4:8] = jnp.zeros((4, model), F32)
        grad_residual[...] = value
        rounded = value.astype(BF16)
        grads = (grad_mixed_0, grad_mixed_1, grad_mixed_2, grad_mixed_3)
        for k, mixed in enumerate((mixed_0, mixed_1, mixed_2, mixed_3)):
            grads[k][...] = dot(rounded, out_weight[k], ((1,), (1,))).astype(BF16)
            product = dot(mixed[...], rounded, ((0,), (0,)))
            narrow = product.shape[0] // slices
            spare = jnp.zeros((grad_out_weight.shape[2] - narrow, model), F32)
            for j in range(slices):
                part = jnp.concatenate([product[j * narrow : (j + 1) * narrow], spare], axis=0)
                grad_out_weight[k, j] = part.astype(BF16)


def middle(source, cotangent, mixed, out_weight, far_weight, vectors, in_bias, own_in, own_out, far_in, far_out):
    own_rows, model = source.shape
    shards = far_in.shape[0] + 1
    slices, rows, hidden_part = own_in.shape
    narrow = mixed[0].shape
    far = pl.BlockSpec((1,) + own_in.shape, lambda r: (jnp.maximum(r - 1, 0), 0, 0, 0))
    part = pl.BlockSpec((1,) + own_in.shape, lambda r: (r, 0, 0, 0))
    macs = own_rows * model * (6 * shards * hidden_part + 3 * model)
    return pl.pallas_call(
        middle_kernel,
        grid_spec=pltpu.PrefetchScalarGridSpec(
            num_scalar_prefetch=0,
            grid=(shards,),
            in_specs=[whole(source.shape)] * 2 + [whole(narrow)] * 4 + [
                whole(out_weight.shape), whole(far_weight.shape), whole(vectors.shape), whole(in_bias.shape), whole(own_in.shape),
                whole(own_out.shape), far, far,
            ],
            out_specs=[whole(source.shape)] * 2 + [whole(narrow)] * 4 + [
                part, part, whole((shards,) + far_weight.shape[1:]), whole((8, model)), whole((shards, hidden_part))
            ],
            scratch_shapes=[
                pltpu.VMEM((own_rows, model), F32),
                pltpu.VMEM((own_rows, 1), F32),
                pltpu.VMEM((own_rows, model), BF16),
                pltpu.VMEM((model, own_rows), BF16),
                pltpu.VMEM((own_rows, model), F32),
                pltpu.VMEM((own_rows, model), F32),
                pltpu.VMEM((model, hidden_part), BF16),
                pltpu.VMEM((hidden_part, model), BF16),
                pltpu.VMEM((shards,) + narrow[1:] + (model,), BF16),
            ],
        ),
        out_shape=[
            jax.ShapeDtypeStruct(source.shape, BF16),
            jax.ShapeDtypeStruct(source.shape, F32),
        ] + [jax.ShapeDtypeStruct(narrow, BF16)] * 4 + [
            jax.ShapeDtypeStruct((shards, slices, rows, hidden_part), BF16),
            jax.ShapeDtypeStruct((shards, slices, rows, hidden_part), BF16),
            jax.ShapeDtypeStruct((shards,) + far_weight.shape[1:], BF16),
            jax.ShapeDtypeStruct((8, model), F32),
            jax.ShapeDtypeStruct((shards, hidden_part), F32),
        ],
        compiler_params=pltpu.CompilerParams(vmem_limit_bytes=60 << 20),
        cost_estimate=pl.CostEstimate(
            flops=2 * macs, bytes_accessed=30 << 20, transcendentals=own_rows * shards * hidden_part
        ),
        name="middle",
    )(source, cotangent, *mixed, out_weight, far_weight, vectors, in_bias, own_in, own_out, far_in, far_out)


def added(a, b):
    return (a.astype(F32) + b.astype(F32)).astype(BF16)


def backward_kernel(
    heads, seg_lengths, qkv, gm_0, gm_1, gm_2, gm_3, logsum, values, probes, key_states_in, key_end_in, rows_in, table_in,
    grad_in, grad_out, grad_weight, out, probe_grad, slice_in, slice_out, slice_weight,
    given, query_grad, memory_grad, row_grad, value_carried, value_back, value_in, row_back, row_in, carried, spread, key_grad, value_grad, cols, keys, vals,
    key_states, key_end, rows, table,
    keep_in, keep_out, keep_weight, core_in, core_out, core_weight, one_in, one_out, one_weight,
    two_in, two_out, two_weight, z_in, z_out, z_weight, send, recv, local_sems,
):
    units = qkv.shape[1]
    half = units // 2
    width = heads * HEAD_DIM
    root = 1.0 / math.sqrt(HEAD_DIM)
    z = lax.axis_index("head")
    flip, run = (z % 2) * half, z // 2
    place = lax.axis_index("dp") % 8
    y, x, c = place // 4, (place // 2) % 2, place % 2
    at = lambda b: (b + flip) % units
    starts, lengths, orders = segments_of(seg_lengths, run, units)
    greet((("head", 1), ("head", 2), ("head", 3), ("dp", 1), ("dp", 2), ("dp", 4)))
    hops = Hops(send, recv)
    started = []

    def go(*args):
        started.append(hops.start(*args))
        return started[-1]

    tables = set_out(
        [(key_states_in, key_states), (key_end_in, key_end), (rows_in, rows), (table_in, table)], local_sems, 12
    )
    given_copies = [go(gm_1, given.at[0, half:], "head", 1), go(gm_3, given.at[1, half:], "head", 1)]
    sums = (
        (grad_in, keep_in, core_in, one_in, two_in, z_in, True),
        (grad_weight, keep_weight, core_weight, one_weight, two_weight, z_weight, True),
        (grad_out, keep_out, core_out, one_out, two_out, z_out, False),
    )
    stage, local_copies = {}, {}
    for i, r in enumerate((2, 1, 3, 0)):
        stage[r], local_copies[r] = [], []
        for n, (term, keep, core, _, _, _, _) in enumerate(sums):
            stage[r].append(go(term.at[r, :, :, 1 - c], core.at[r], "dp", 1))
            copy = pltpu.make_async_copy(term.at[r, :, :, c], keep.at[r], local_sems.at[3 * i + n])
            copy.start()
            local_copies[r].append(copy)

    def first_hop(r):
        for n, (_, keep, core, one, _, _, along_x) in enumerate(sums):
            local_copies[r][n].wait()
            stage[r][n].wait_recv()
            keep[r] = added(keep[r], core[r])
            part = keep.at[r, :, 1 - x] if along_x else keep.at[r, 1 - y]
            stage[r][n] = go(part, one.at[r], "dp", 2 if along_x else 4)

    def second_hop(r):
        for n, (_, keep, _, one, two, _, along_x) in enumerate(sums):
            stage[r][n].wait_recv()
            kept = keep[r, :, x] if along_x else keep[r, y]
            one[r] = added(kept, one[r])
            part = one.at[r, 1 - y] if along_x else one.at[r, 1 - x]
            stage[r][n] = go(part, two.at[r], "dp", 4 if along_x else 2)

    def third_hop(r):
        for n, (_, _, _, one, two, far, along_x) in enumerate(sums):
            stage[r][n].wait_recv()
            kept = one[r, y] if along_x else one[r, x]
            two[r] = added(kept, two[r])
            if r:
                stage[r][n] = go(two.at[r], far.at[r - 1], "head", r)

    for k, own in enumerate((gm_0, gm_2)):
        given[k, :half] = own[...]
    mask = head_rows(heads, LANES)
    lane_head = lax.broadcasted_iota(jnp.int32, (UNIT, LANES), 1) // HEAD_DIM

    def given_of(k, b):
        return jnp.concatenate([given[k, at(b)], jnp.zeros((UNIT, LANES - width), BF16)], axis=1).astype(F32)

    def read_back(rel, k, carry):
        b = at(rel)
        query = qkv[k, rel, :, 0:LANES]
        full = given_of(k, b)
        probe = probes[k, b]
        logits = logits_of(probe, query)
        location, variance = read_parts(logits, heads)
        inverse = 1.0 / variance
        fall = -0.5 * inverse
        peak = WIDTH * lax.rsqrt(variance)
        centres = lax.broadcasted_iota(jnp.int32, (BASIS, UNIT), 0).astype(F32) / (BASIS - 1)
        along, across = [], []
        total = jnp.zeros((BASIS, LANES), F32)
        for h in range(heads):
            own_given = jnp.where(lane_head == h, full, 0.0).astype(BF16)
            gap = centres - location[h : h + 1]
            square = gap * gap
            density = jnp.exp(square * fall[h : h + 1]) * peak[h : h + 1]
            grad_density = dot(values[k, b], own_given, ((1,), (1,)))
            total += dot(density.astype(BF16), own_given)
            weighed = density * grad_density
            moment = weighed * gap
            zeroth = jnp.sum(weighed, axis=0, keepdims=True)
            first = jnp.sum(moment, axis=0, keepdims=True)
            second = jnp.sum(moment * gap, axis=0, keepdims=True)
            along.append(first * inverse[h : h + 1])
            across.append(0.5 * inverse[h : h + 1] * (second * inverse[h : h + 1] - zeroth))
        sigmoid = 1.0 / (1.0 + jnp.exp(-logits))
        grad_location = jnp.concatenate(along, axis=0) * location * (1.0 - location)
        grad_variance = jnp.concatenate(across, axis=0) * SPREAD * sigmoid[heads : 2 * heads]
        grad_logits = jnp.concatenate(
            [grad_location, grad_variance, jnp.zeros((8 - 2 * heads, UNIT), F32)], axis=0
        )
        padded = jnp.concatenate([grad_logits, jnp.zeros((120, UNIT), F32)], axis=0)
        probe_cols = jnp.concatenate([probe, jnp.zeros((120, LANES), F32)], axis=0).T
        query_grad[k, b] = dot(probe_cols.astype(BF16), padded.astype(BF16))[:width]
        fresh = jnp.where(mask, dot(grad_logits.astype(BF16), query), 0.0) * root
        memory_grad[k, b] = total
        row_grad[k, b] = fresh
        return carry

    def gather_back(k, carry):
        probe = jnp.zeros((8, BASIS), F32)
        for i in range(4):
            row_back[k, 8 * i : 8 * i + 8] = jnp.zeros((8, LANES), F32)
        for b in range(units - 1, -1, -1):
            fresh, total = row_grad[k, b], memory_grad[k, b]
            if b > 0:
                probe += dot(fresh.astype(BF16), key_states[k, b], ((1,), (1,)))
            for i in range(4):
                row_back[k, 8 * i : 8 * i + 8] += jnp.where(orders[b] == i, fresh, 0.0)
            if b < units - 1:
                ends = starts[b] + lengths[b] == b + 1
                total = jnp.where(ends, 0.0, memory_grad[k, b + 1]) + total
                memory_grad[k, b] = total
                row_grad[k, b] = jnp.where(ends, 0.0, row_grad[k, b + 1]) + fresh
            before = jnp.zeros((BASIS, LANES), F32) if b == units - 1 else value_carried[k]
            if b > 0:
                value_carried[k] = jnp.where(starts[b] == b, advance_values(table, before + total), before)
            else:
                value_back[k] = (before + total)[:, :width].T.astype(BF16)
        probe_grad[k] = probe
        return carry

    def attend_back(b, k, carry):
        query = qkv[k, at(b), :, 0:LANES].astype(F32) * root
        full = given_of(k, b)
        causal = lax.broadcasted_iota(jnp.int32, (UNIT, UNIT), 0) <= lax.broadcasted_iota(
            jnp.int32, (UNIT, UNIT), 1
        )
        away = [jnp.where(starts[b] <= j, 0.0, 1e30) for j in range(b)] + [0.0]
        owns = [jnp.where(lane_head == h, query, 0.0).astype(BF16) for h in range(heads)]
        own_givens = [jnp.where(lane_head == h, full, 0.0).astype(BF16) for h in range(heads)]
        own_all = jnp.concatenate(owns, axis=0)
        given_all = jnp.concatenate(own_givens, axis=0)
        seen = (b + 1) * UNIT
        scores = dot(keys[k, :seen], own_all, ((1,), (1,)))
        grad_probs = dot(vals[k, :seen], given_all, ((1,), (1,)))
        grads, probs = [], []
        for h in range(heads):
            prob_h, product_h = [], []
            inner = jnp.zeros((1, UNIT), F32)
            for j in range(b + 1):
                tile = (slice(j * UNIT, (j + 1) * UNIT), slice(h * UNIT, (h + 1) * UNIT))
                score = scores[tile]
                if j == b:
                    score = jnp.where(causal, score, -1e30)
                prob = jnp.exp(score - (logsum[k, b, h : h + 1] + away[j]))
                product = prob * grad_probs[tile]
                inner += jnp.sum(product, axis=0, keepdims=True)
                prob_h.append(prob)
                product_h.append(product)
            span = slice(h * HEAD_DIM, (h + 1) * HEAD_DIM)
            grad_h = [(product_h[j] - prob_h[j] * inner).astype(BF16) for j in range(b + 1)]
            result = dot(cols[k, span, :seen], jnp.concatenate(grad_h, axis=0))
            query_grad[k, b, span] = query_grad[k, b, span] + result * root
            grads.append(grad_h)
            probs.append([prob.astype(BF16) for prob in prob_h])
        fresh_keys = dot(jnp.concatenate([jnp.concatenate(g, axis=0) for g in grads], axis=1), own_all)
        fresh_vals = dot(jnp.concatenate([jnp.concatenate(p, axis=0) for p in probs], axis=1), given_all)
        for j in range(b + 1):
            part = slice(j * UNIT, (j + 1) * UNIT)
            if b == units - 1:
                key_grad[k, j], value_grad[k, j] = fresh_keys[part], fresh_vals[part]
            else:
                key_grad[k, j] += fresh_keys[part]
                value_grad[k, j] += fresh_vals[part]
        return carry

    def carry_back(k, total, units_before):
        moved = dot(table[...], total.astype(BF16))
        return moved[:BASIS], (moved[BASIS:] * term_scale(units_before)).astype(BF16)

    def end_back(k, carry):
        row = jnp.where(run == 0, row_in[k], 0.0)
        value = jnp.where(run == 0, value_in[k].astype(F32), 0.0).T
        grad_keys = dot(rows[k].astype(BF16), row.astype(BF16), ((0,), (0,)))
        total = jnp.concatenate([grad_keys, value, jnp.zeros((BASIS, LANES - width), F32)], axis=1)
        carried[k], spread[k] = carry_back(k, total, lengths[units - 1])
        seen = dot(row, key_end[k], ((1,), (1,)), HIGHEST)
        gained = seen[24:32]
        for i in (2, 1, 0):
            high = gained.astype(BF16)
            low = (gained - high.astype(F32)).astype(BF16)
            gained = dot(high, table[:BASIS]) + dot(low, table[:BASIS])
            gained = gained + seen[8 * i : 8 * i + 8]
        probe_grad[k] += gained
        return carry

    def finish(b, k, carry):
        start, length = starts[b], lengths[b]
        token = lax.broadcasted_iota(jnp.int32, (UNIT, LIVE), 0) + (b - start) * UNIT
        centre = (lax.broadcasted_iota(jnp.int32, (UNIT, LIVE), 1) + LIVE).astype(F32) / (BASIS - 1)
        gap = place_of(token, length) - centre
        psi = jnp.exp(gap * gap * (-0.5 / (WIDTH * WIDTH))).astype(BF16)
        pair_grad = dot(psi, spread[k])
        query_rows = query_grad[k, b].T.astype(BF16)
        out[k, at(b), :, :LANES] = jnp.concatenate([query_rows, jnp.zeros((UNIT, LANES - width), BF16)], axis=1)
        out[k, at(b), :, LANES : 2 * LANES] = (key_grad[k, b] + pair_grad[:, :LANES]).astype(BF16)
        out[k, at(b), :, 2 * LANES :] = (value_grad[k, b] + pair_grad[:, LANES:]).astype(BF16)
        if b > 0:
            grad_keys = dot(rows[k, 0:8].astype(BF16), row_grad[k, b].astype(BF16), ((0,), (0,)))
            total = carried[k] + jnp.concatenate([grad_keys, memory_grad[k, b]], axis=1)
            moved, spread_now = carry_back(k, total, lengths[b - 1])
            carried[k] = jnp.where(start == b, moved, carried[k])
            spread[k] = jnp.where(start == b, spread_now.astype(F32), spread[k].astype(F32)).astype(BF16)
        return carry

    def both(step, *args):
        lax.fori_loop(0, 2, functools.partial(step, *args), 0)

    def turn(k, carry):
        for b in range(units):
            part = slice(b * UNIT, (b + 1) * UNIT)
            keys[k, part] = qkv[k, at(b), :, LANES : 2 * LANES]
            vals[k, part] = qkv[k, at(b), :, 2 * LANES : 3 * LANES]
            cols[k, :, part] = qkv[k, at(b), :, LANES : 2 * LANES].astype(F32).T.astype(BF16)
        return carry

    lax.fori_loop(0, 2, turn, 0)
    both(read_back, 0)
    first_hop(2)
    both(read_back, 1)
    first_hop(1)
    for copy in given_copies:
        copy.wait_recv()
    both(read_back, 2)
    first_hop(3)
    first_hop(0)
    both(read_back, 3)
    for copy in tables:
        copy.wait()
    back_copies = []
    for k in range(2):
        gather_back(k, 0)
        back_copies += [
            go(value_back.at[k], value_in.at[1 - k], "head", 2), go(row_back.at[k], row_in.at[1 - k], "head", 2)
        ]
    second_hop(2)
    both(attend_back, 3)
    second_hop(1)
    second_hop(3)
    third_hop(2)
    both(attend_back, 2)
    second_hop(0)
    third_hop(1)
    third_hop(3)
    both(attend_back, 1)
    third_hop(0)
    both(attend_back, 0)
    for copy in back_copies:
        copy.wait_recv()
    lax.fori_loop(0, 2, end_back, 0)
    for b in range(units - 1, -1, -1):
        both(finish, b)
    for n, (_, _, _, _, two, far, _) in enumerate(sums):
        total = two[0].astype(F32)
        for r in (1, 2, 3):
            stage[r][n].wait_recv()
            total += far[r - 1].astype(F32)
        (slice_in, slice_weight, slice_out)[n][...] = total.astype(BF16)
    for copy in started:
        copy.wait_send()


def backward(seg_lengths, qkv, grad_mixed, logsum, values, probes, key_states, key_end, rows, grad_in, grad_out, grad_weight, heads):
    units = qkv.shape[1]
    width = heads * HEAD_DIM
    table = jnp.asarray(basis_tables()[1])
    vmem, anywhere = pl.BlockSpec(memory_space=pltpu.VMEM), pl.BlockSpec(memory_space=pl.ANY)
    shape = jax.ShapeDtypeStruct
    slices = [grad_in.shape[4:], grad_out.shape[4:], grad_weight.shape[4:]]
    hops = 2 + 3 * 4 * 3 + 3 * 3 + 4
    return pl.pallas_call(
        functools.partial(backward_kernel, heads),
        in_specs=[pl.BlockSpec(memory_space=pltpu.SMEM)] + [vmem] * 8 + [anywhere] * 7,
        out_specs=[vmem] * 5,
        out_shape=[shape(qkv.shape, BF16), shape((2, 8, BASIS), F32)] + [shape(part, BF16) for part in slices],
        scratch_shapes=[
            pltpu.VMEM((2, units, UNIT, width), BF16),
            pltpu.VMEM((2, units, width, UNIT), F32),
            pltpu.VMEM((2, units, BASIS, LANES), F32),
            pltpu.VMEM((2, units, 8, LANES), F32),
            pltpu.VMEM((2, BASIS, LANES), F32),
            pltpu.VMEM((2, width, BASIS), BF16),
            pltpu.VMEM((2, width, BASIS), BF16),
            pltpu.VMEM((2, 32, LANES), F32),
            pltpu.VMEM((2, 32, LANES), F32),
            pltpu.VMEM((2, BASIS, 2 * LANES), F32),
            pltpu.VMEM((2, LIVE, 2 * LANES), BF16),
            pltpu.VMEM((2, units, UNIT, LANES), F32),
            pltpu.VMEM((2, units, UNIT, LANES), F32),
            pltpu.VMEM((2, LANES, units * UNIT), BF16),
            pltpu.VMEM((2, units * UNIT, LANES), BF16),
            pltpu.VMEM((2, units * UNIT, LANES), BF16),
            pltpu.VMEM(key_states.shape, BF16),
            pltpu.VMEM(key_end.shape, F32),
            pltpu.VMEM(rows.shape, F32),
            pltpu.VMEM(table.shape, BF16),
        ]
        + [pltpu.VMEM((4, 2, 2) + part, BF16) for part in slices]
        + [pltpu.VMEM((4, 2, 2) + part, BF16) for part in slices]
        + [pltpu.VMEM((4, 2) + part, BF16) for part in slices]
        + [pltpu.VMEM((4,) + part, BF16) for part in slices]
        + [pltpu.VMEM((3,) + part, BF16) for part in slices]
        + [
            pltpu.SemaphoreType.DMA((hops,)),
            pltpu.SemaphoreType.DMA((hops,)),
            pltpu.SemaphoreType.DMA((16,)),
        ],
        compiler_params=pltpu.CompilerParams(
            collective_id=2, has_side_effects=True, vmem_limit_bytes=62 << 20
        ),
        name="backward",
    )(
        seg_lengths, qkv, *grad_mixed, logsum, values, probes, key_states, key_end, rows, table, grad_in, grad_out, grad_weight
    )


def tail_kernel(
    heads, outer, grads, flat_a, flat_b, packed, slice_in, slice_out, slice_weight, sums, in_bias_part, probe_grad,
    first_cols_in, grad_residual_in, source_in, input_grad, whole_in, whole_out, whole_weight, whole_qkv, shared_out, owned_out,
    row_grad, near, kept, part_a, part_b, core_a, core_b, one_a, one_b, two_a, two_b, far_b, total, outer_in,
    gather_in, gather_out, gather_weight, gather_qkv,
    shared, shared_in, block, block_in, bias_block, bias_in, joined, joined_in, first_cols, grad_residual, source,
    send, recv, local_sems,
):
    own_rows, model = source.shape
    loads = set_out(
        [(first_cols_in, first_cols), (grad_residual_in, grad_residual), (source_in, source)], local_sems, 0
    )
    units = grads.shape[1]
    half = units // 2
    width = heads * HEAD_DIM
    z = lax.axis_index("head")
    place = lax.axis_index("dp") % 8
    y, x, c = place // 4, (place // 2) % 2, place % 2
    rows = model // 8
    greet(
        (("head", 1), ("head", 2), ("head", 3), ("dp", 1), ("dp", 2), ("dp", 4)) + tuple(("dp", bit) for bit in outer)
    )
    hops = Hops(send, recv)
    started = []

    def go(*args):
        started.append(hops.start(*args))
        return started[-1]

    def row_of(rel):
        return dot(grads[0, rel], flat_a[...]) + dot(grads[1, rel], flat_b[...])

    row_copies = []
    for k in range(half):
        row_grad[k] = row_of(half + k).astype(BF16)
        row_copies.append(go(row_grad.at[k], near.at[k], "head", 1))

    gathers = ((slice_in, gather_in, True), (slice_weight, gather_weight, True), (slice_out, gather_out, False))
    for own, gather, _ in gathers:
        gather[y, x, c] = own[...]

    def spread_first(gather, along_x):
        part = gather.at[y, x, c]
        return go(part, part, "dp", 2 if along_x else 4)

    def spread_second(gather, along_x):
        part = gather.at[y, :, c] if along_x else gather.at[:, x, c]
        return go(part, part, "dp", 4 if along_x else 2)

    def spread_third(gather):
        part = gather.at[:, :, c]
        return go(part, part, "dp", 1)

    loads[0].wait()
    core_copies = []
    for k, part, core in ((1, part_b, core_b), (0, part_a, core_a)):
        product = dot(first_cols[...], grads[k].reshape(2 * own_rows, 3 * LANES))
        product = jnp.concatenate([product[:, i * LANES : i * LANES + width] for i in range(3)], axis=1).astype(BF16)
        for j in range(8):
            part[j // 4, (j // 2) % 2, j % 2] = product[j * rows : (j + 1) * rows]
        core_copies.append(go(part.at[:, :, 1 - c], core, "dp", 1))
    spreads = [spread_first(gather, along_x) for _, gather, along_x in gathers]
    for k in range(half):
        kept[k] = row_of(k)

    core_copies[0].wait_recv()
    core_b[...] = added(part_b[:, :, c], core_b[...])
    one_copy_b = go(core_b.at[1 - y], one_b, "dp", 4)
    core_copies[1].wait_recv()
    core_a[...] = added(part_a[:, :, c], core_a[...])
    one_copy_a = go(core_a.at[:, 1 - x], one_a, "dp", 2)

    bias_a = jnp.sum(grads[0].reshape(2 * own_rows, 3 * LANES).astype(F32), axis=0, keepdims=True)
    bias_b = jnp.sum(grads[1].reshape(2 * own_rows, 3 * LANES).astype(F32), axis=0, keepdims=True)
    edge = jnp.zeros((8, model - BASIS), F32)
    fill = jnp.zeros((6, model), F32)
    for k, bias in ((0, bias_a), (1, bias_b)):
        block[k, 0:8] = jnp.concatenate([probe_grad[k], edge], axis=1)
        block[k, 8:16] = jnp.concatenate([bias, in_bias_part[2 * k : 2 * k + 1], fill], axis=0)
        bias_block[k] = jnp.concatenate([in_bias_part[2 * k + 1 : 2 * k + 2], jnp.zeros((7, model), F32)], axis=0)
    block_copy = go(block.at[1], block_in, "head", 2)
    bias_copies = [go(bias_block.at[0], bias_in.at[0], "head", 1), go(bias_block.at[1], bias_in.at[1], "head", 3)]

    loads[1].wait()
    loads[2].wait()
    value = source[...].astype(F32)
    centred = value - jnp.mean(value, axis=-1, keepdims=True)
    factor = lax.rsqrt(jnp.mean(centred * centred, axis=-1, keepdims=True) + EPSILON)
    normal = centred * factor

    one_copy_b.wait_recv()
    one_b[...] = added(core_b[y], one_b[...])
    two_copy_b = go(one_b.at[1 - x], two_b, "dp", 2)
    one_copy_a.wait_recv()
    one_a[...] = added(core_a[:, x], one_a[...])
    two_copy_a = go(one_a.at[1 - y], two_a, "dp", 4)
    for copy in row_copies:
        copy.wait_recv()
    two_copy_b.wait_recv()
    two_b[...] = added(one_b[x], two_b[...])
    far_copy = go(two_b, far_b, "head", 2)

    grad = kept[...].reshape(own_rows, model) + near[...].reshape(own_rows, model).astype(F32)
    scaled = grad * packed[16:17]
    change = factor * (
        scaled
        - jnp.mean(scaled, axis=-1, keepdims=True)
        - normal * jnp.mean(scaled * normal, axis=-1, keepdims=True)
    )
    input_grad[...] = (grad_residual[...] + change).astype(BF16)
    shared[...] = jnp.concatenate(
        [jnp.sum(grad * normal, axis=0, keepdims=True), jnp.sum(grad, axis=0, keepdims=True), sums[0:6]], axis=0
    )
    shared_copies = [go(shared, shared_in.at[r - 1], "head", r) for r in (1, 2, 3)]
    spreads = [copy.wait_recv() or spread_second(gather, along_x) for copy, (_, gather, along_x) in zip(spreads, gathers)]

    two_copy_a.wait_recv()
    own_sum = added(one_a[y], two_a[...]).astype(F32)
    far_copy.wait_recv()
    total[0] = (own_sum + far_b[...].astype(F32)).astype(BF16)
    for n, bit in enumerate(outer):
        copy = go(total.at[n], outer_in.at[n], "dp", bit)
        copy.wait_recv()
        total[n + 1] = added(total[n], outer_in[n])
    gather_qkv[y, x, c] = total[len(outer)]
    cut = rows // 2
    upper, lower = pl.ds(0, cut), pl.ds(cut, cut)
    qkv_parts = [gather_qkv.at[y, x, c, upper], gather_qkv.at[y, x, c, lower]]
    qkv_copies = [go(qkv_parts[0], qkv_parts[0], "dp", 2), go(qkv_parts[1], qkv_parts[1], "dp", 4)]

    block_copy.wait_recv()
    for copy in bias_copies + shared_copies:
        copy.wait_recv()
    owned = block[0] + block_in[...]
    bias_rows = bias_in[0] + bias_in[1]
    owned_rows = jnp.concatenate([owned[8:9], owned[9:10] + bias_rows[0:1], owned[10:16]], axis=0)
    joined[0] = jnp.concatenate(
        [shared[...] + shared_in[0] + shared_in[1] + shared_in[2], owned[0:8], owned_rows], axis=0
    )
    spreads = [copy.wait_recv() or spread_third(gather) for copy, (_, gather, _) in zip(spreads, gathers)]
    for n, bit in enumerate((2, 4, 1) + outer):
        copy = go(joined.at[n], joined_in.at[n], "dp", bit)
        if n == 1:
            for copy_one in qkv_copies:
                copy_one.wait_recv()
            qkv_parts = [gather_qkv.at[y, :, c, upper], gather_qkv.at[:, x, c, lower]]
            qkv_copies = [go(qkv_parts[0], qkv_parts[0], "dp", 4), go(qkv_parts[1], qkv_parts[1], "dp", 2)]
        copy.wait_recv()
        joined[n + 1] = joined[n] + joined_in[n]
    last = joined[3 + len(outer)]
    shared_out[...] = last[0:8]
    owned_out[...] = last[8:24]
    for copy, (_, gather, _), out in zip(spreads, gathers, (whole_in, whole_weight, whole_out)):
        copy.wait_recv()
        out[...] = gather[...]
    for copy in qkv_copies:
        copy.wait_recv()
    spread_third(gather_qkv).wait_recv()
    whole_qkv[...] = gather_qkv[...]
    for copy in started:
        copy.wait_send()


def tail(grads, first_cols, flat_a, flat_b, grad_residual, source, packed, slices, sums, in_bias_part, probe_grad, outer, heads):
    own_rows, model = source.shape
    units = grads.shape[1]
    rows = model // 8
    vmem = pl.BlockSpec(memory_space=pltpu.VMEM)
    shape = jax.ShapeDtypeStruct
    slice_in, slice_out, slice_weight = slices
    plane = lambda part: (2, 2, 2) + part
    part = (rows, 3 * heads * HEAD_DIM)
    hops = units // 2 + 9 + 2 + 2 + 2 + 1 + 5 + 1 + 2 + 3 + 3 + 2 * len(outer)
    return pl.pallas_call(
        functools.partial(tail_kernel, heads, outer),
        in_specs=[vmem] * 10 + [pl.BlockSpec(memory_space=pl.ANY)] * 3,
        out_specs=[vmem] * 7,
        out_shape=[
            shape(source.shape, BF16), shape(plane(slice_in.shape), BF16), shape(plane(slice_out.shape), BF16),
            shape(plane(slice_weight.shape), BF16), shape(plane(part), BF16), shape((8, model), F32),
            shape((16, model), F32),
        ],
        scratch_shapes=[
            pltpu.VMEM((units // 2, UNIT, model), BF16),
            pltpu.VMEM((units // 2, UNIT, model), BF16),
            pltpu.VMEM((units // 2, UNIT, model), F32),
            pltpu.VMEM(plane(part), BF16),
            pltpu.VMEM(plane(part), BF16),
            pltpu.VMEM((2, 2) + part, BF16),
            pltpu.VMEM((2, 2) + part, BF16),
            pltpu.VMEM((2,) + part, BF16),
            pltpu.VMEM((2,) + part, BF16),
            pltpu.VMEM(part, BF16),
            pltpu.VMEM(part, BF16),
            pltpu.VMEM(part, BF16),
            pltpu.VMEM((1 + len(outer),) + part, BF16),
            pltpu.VMEM((max(1, len(outer)),) + part, BF16),
            pltpu.VMEM(plane(slice_in.shape), BF16),
            pltpu.VMEM(plane(slice_out.shape), BF16),
            pltpu.VMEM(plane(slice_weight.shape), BF16),
            pltpu.VMEM(plane(part), BF16),
            pltpu.VMEM((8, model), F32),
            pltpu.VMEM((3, 8, model), F32),
            pltpu.VMEM((2, 16, model), F32),
            pltpu.VMEM((16, model), F32),
            pltpu.VMEM((2, 8, model), F32),
            pltpu.VMEM((2, 8, model), F32),
            pltpu.VMEM((4 + len(outer), 24, model), F32),
            pltpu.VMEM((3 + len(outer), 24, model), F32),
            pltpu.VMEM(first_cols.shape, BF16),
            pltpu.VMEM(grad_residual.shape, F32),
            pltpu.VMEM(source.shape, BF16),
            pltpu.SemaphoreType.DMA((hops,)),
            pltpu.SemaphoreType.DMA((hops,)),
            pltpu.SemaphoreType.DMA((3,)),
        ],
        compiler_params=pltpu.CompilerParams(
            collective_id=3, has_side_effects=True, vmem_limit_bytes=60 << 20
        ),
        name="tail",
    )(
        grads, flat_a, flat_b, packed, slice_in, slice_out, slice_weight, sums, in_bias_part, probe_grad, first_cols,
        grad_residual, source,
    )


def exchange(value, axis, bit):
    size = lax.axis_size(axis)
    return lax.ppermute(value, axis, [(j, j ^ bit) for j in range(size)])


def local(
    inputs, seg_lengths, ln1_gain, ln1_bias, qkv_weight, qkv_bias, out_weight, out_bias, mem_mu, mem_sig,
    ln2_gain, ln2_bias, ff_in, ff_in_bias, ff_out, ff_out_bias, cotangent,
):
    own_rows, model = inputs.shape
    shards = lax.axis_size("head")
    members = lax.axis_size("dp")
    width = qkv_weight.shape[2]
    heads = width // HEAD_DIM
    hidden_part = ff_in.shape[1]
    units = 2 * own_rows // UNIT
    slices = 8
    outer = tuple(1 << k for k in range(3, 16) if 1 << k < members)
    rows = model // slices

    bias_row = jnp.pad(qkv_bias, ((0, 0), (0, LANES - width))).reshape(1, 3 * LANES)
    edge = 3 * LANES - BASIS
    packed = jnp.pad(bias_row, ((0, 23), (0, 0))).astype(F32)
    packed += jnp.pad(mem_mu, ((1, 23 - heads), (0, edge))).astype(F32)
    packed += jnp.pad(mem_sig, ((1 + heads, 23 - 2 * heads), (0, edge))).astype(F32)
    given = (ln1_gain, ln1_bias, out_bias, ln2_gain, ln2_bias, ff_out_bias, ff_in_bias)
    line = sum(jnp.pad(vector.astype(F32), (k * model, (6 - k) * model)) for k, vector in enumerate(given))
    packed += jnp.pad(line.reshape(7, model), ((16, 1), (0, 0)))

    turned_weight = jnp.transpose(qkv_weight, (1, 2, 0)).reshape(3 * width, model)
    (
        qkv, first_cols, flat_a, flat_b, values, key_states, key_end, logsum, probes, state_rows,
        *mixed, in_bias, far_in, far_out, far_weight,
    ) = forward(seg_lengths, inputs, packed, turned_weight, out_weight, ff_in, ff_out, heads)
    flat = lambda array: array.reshape((shards - 1, slices) + array.shape[4:])
    outputs, grad_residual, *rest = middle(
        inputs, cotangent, mixed, out_weight, flat(far_weight), packed, in_bias,
        ff_in.reshape(slices, rows, hidden_part), ff_out.reshape(slices, rows, model), flat(far_in), flat(far_out),
    )
    grad_mixed, (ff_in_part, ff_out_part, out_weight_part, sums, in_bias_part) = rest[:4], rest[4:]
    paired = [part.reshape(units // 2, UNIT, width) for part in grad_mixed]
    plane = lambda array: array.reshape((shards, 2, 2, 2) + array.shape[2:])
    grads, probe_grad, *parts = backward(
        seg_lengths, qkv, paired, logsum, values, probes, key_states, key_end, state_rows, plane(ff_in_part),
        plane(ff_out_part), plane(out_weight_part), heads,
    )
    for bit in outer:
        parts = [added(part, exchange(part, "dp", bit)) for part in parts]
    input_grad, whole_in, whole_out, whole_weight, whole_qkv, shared, owned = tail(
        grads, first_cols, flat_a, flat_b, grad_residual, inputs, packed, parts, sums, in_bias_part, probe_grad,
        outer, heads,
    )
    ff_in_sum, ff_out_sum, out_weight_sum, qkv_weight_sum = finish(
        whole_in.reshape(model, hidden_part), whole_out.reshape(hidden_part, model),
        whole_weight.reshape((slices,) + whole_weight.shape[3:]), whole_qkv.reshape(model, 3 * width), width,
    )
    return (
        outputs, input_grad, shared[0], shared[1], jnp.transpose(qkv_weight_sum, (2, 0, 1)),
        owned[8].reshape(3, LANES)[:, :width], out_weight_sum, shared[2], owned[:heads, :BASIS],
        owned[heads : 2 * heads, :BASIS], shared[3], shared[4], ff_in_sum, owned[9, :hidden_part], ff_out_sum, shared[5],
    )


def solution(mesh):
    rows, whole = P(("dp", "head"), None), P()
    return jax.shard_map(
        local,
        mesh=mesh,
        in_specs=(
            rows, P("dp", None), whole, whole, P(None, None, "head"), P(None, "head"), P("head", None), whole,
            P("head", None), P("head", None), whole, whole, P(None, "head"), P("head"), P("head", None), whole, rows,
        ),
        out_specs=(
            rows, rows, whole, whole, P(None, None, "head"), P(None, "head"), P("head", None), whole,
            P("head", None), P("head", None), whole, whole, P(None, "head"), P("head"), P("head", None), whole,
        ),
        check_vma=False,
    )
```

```python
import functools
import math

import jax
import jax.numpy as jnp
import ml_dtypes
import numpy as np
from jax import lax
from jax.experimental import pallas as pl
from jax.experimental.pallas import tpu as pltpu
from jax.sharding import PartitionSpec as P

HEAD_DIM = 64
BASIS = 512
UNIT = 256
LANES = 256
TAU = 0.75
RIDGE = 0.5
EPSILON = 1e-05
MESH = pl.DeviceIdType.MESH
SPREAD = 1.0 / 64.0
WIDTH = 1.0 / BASIS
LIVE = BASIS // 2
HIGHEST = lax.Precision.HIGHEST
F32 = jnp.float32
BF16 = jnp.bfloat16


def split_table(table):
    high = table.astype(np.float32).astype(ml_dtypes.bfloat16)
    low = (table.astype(np.float32) - high.astype(np.float32)).astype(ml_dtypes.bfloat16)
    return high, low


@functools.lru_cache(maxsize=None)
def basis_tables():
    centres = np.arange(BASIS) / (BASIS - 1)
    apart = centres[:, None] - centres[None, :]
    gram = np.exp(-apart * apart / (4.0 * WIDTH * WIDTH)) + RIDGE * np.eye(BASIS)
    solve = np.linalg.inv(gram)
    samples = (np.arange(BASIS) + 0.5) / BASIS
    near_gap = TAU * samples[:, None] - centres[None, :]
    far_gap = samples[:, None] - centres[None, :]
    near = np.exp(-near_gap * near_gap / (2.0 * WIDTH * WIDTH))
    far = np.exp(-far_gap * far_gap / (2.0 * WIDTH * WIDTH))
    contract = (near.T @ far) * (TAU / (BASIS * WIDTH * math.sqrt(math.pi)))
    joined = np.concatenate([solve @ contract, solve[:, LIVE:]], axis=1)
    high, low = split_table(joined)
    forward = np.concatenate([high, high, low], axis=1)
    backward = np.ascontiguousarray(high.T)
    return forward, backward


def term_scale(units):
    return (1.0 - TAU) / (WIDTH * math.sqrt(math.pi) * UNIT) / units.astype(F32)


def split3(value):
    high = value.astype(BF16)
    low = (value - high.astype(F32)).astype(BF16)
    return jnp.concatenate([high, low, high], axis=0)


def dot(a, b, contract=((1,), (0,)), precision=None):
    return lax.dot_general(a, b, (contract, ((), ())), precision=precision, preferred_element_type=F32)


def head_rows(heads, width):
    row = lax.broadcasted_iota(jnp.int32, (8, width), 0)
    lane = lax.broadcasted_iota(jnp.int32, (8, width), 1) // HEAD_DIM
    return ((row == lane) | (row == lane + heads)) & (lane < heads)


def read_parts(logits, heads):
    location = 1.0 / (1.0 + jnp.exp(-logits))
    variance = (jnp.maximum(logits, 0.0) + jnp.log1p(jnp.exp(-jnp.abs(logits)))) * SPREAD + WIDTH * WIDTH
    return location[:heads], variance[heads : 2 * heads]


def place_of(index, length):
    return TAU + (1.0 - TAU) * (index.astype(F32) + 0.5) / (length.astype(F32) * UNIT)


def split_rows(value):
    high = value.astype(BF16)
    rest = value - high.astype(F32)
    mid = rest.astype(BF16)
    return high, mid, (rest - mid.astype(F32)).astype(BF16)


def three_pass(left, right_high, right_low, contract=((1,), (0,))):
    high = left.astype(BF16)
    low = (left - high.astype(F32)).astype(BF16)
    return dot(high, right_high, contract) + dot(low, right_high, contract) + dot(high, right_low, contract)


def advance_values(table, value):
    return dot(table[:BASIS, :BASIS], value.astype(BF16))


def logits_of(probes, query):
    parts = dot(jnp.concatenate(split_rows(probes), axis=0), query, ((1,), (1,)))
    return parts[0:8] + parts[8:16] + parts[16:24]


def segments_of(lengths, run, units):
    sizes = [lengths[0, run * units + s] // UNIT for s in range(units)]
    ends, total = [], 0
    for size in sizes:
        total = total + size
        ends.append(total)
    starts, spans, orders = [], [], []
    for b in range(units):
        start, span, order = 0, 0, 0
        for size, end in zip(sizes, ends):
            inside = (end > b) & (end - size <= b)
            start = start + jnp.where(inside, end - size, 0)
            span = span + jnp.where(inside, size, 0)
            order = order + jnp.where((end <= b) & (size > 0), 1, 0)
        starts.append(start)
        spans.append(span)
        orders.append(order)
    return starts, spans, orders


def other_of(index, distance):
    bit = 1
    while bit <= distance:
        if distance & bit:
            index = index + bit - 2 * bit * ((index // bit) % 2)
        bit *= 2
    return index


class Hops:
    def __init__(self, send, recv):
        self.send, self.recv, self.used = send, recv, 0

    def start(self, source, target, axis, bit):
        copy = self.make(source, target, axis, bit)
        copy.start()
        return copy

    def make(self, source, target, axis, bit):
        copy = pltpu.make_async_remote_copy(
            src_ref=source,
            dst_ref=target,
            send_sem=self.send.at[self.used],
            recv_sem=self.recv.at[self.used],
            device_id={axis: other_of(lax.axis_index(axis), bit)},
            device_id_type=MESH,
        )
        self.used += 1
        return copy


def greet(neighbours):
    barrier = pltpu.get_barrier_semaphore()
    for axis, bit in neighbours:
        pl.semaphore_signal(
            barrier, inc=1, device_id={axis: other_of(lax.axis_index(axis), bit)}, device_id_type=MESH
        )
    pl.semaphore_wait(barrier, len(neighbours))


def set_out(pairs, sems, first):
    copies = [pltpu.make_async_copy(a, b, sems.at[first + k]) for k, (a, b) in enumerate(pairs)]
    for copy in copies:
        copy.start()
    return copies


def forward_kernel(
    heads, seg_lengths, source, packed, weight, out_weight, table, ff_in, ff_out,
    qkv_out, first_cols_out, flat_a_out, flat_b_out, values_out, key_states_out, key_end_out, logsum, probes, rows,
    mixed_0, mixed_1, mixed_2, mixed_3, in_bias, far_in, far_out, far_weight,
    qkv, first_rows, first_cols, flats, near, far, far_flat, small, far_row, bias_row, weight_mine, memory, sums, value_states, carried, value_ends, value_ins,
    projs, proj_ins, cols, keys, discrete, mixed, mixed_in, values, key_states, key_end, send, recv, local_sems,
):
    own_rows, model = source.shape
    width = heads * HEAD_DIM
    units = qkv.shape[1]
    half = units // 2
    root = 1.0 / math.sqrt(HEAD_DIM)
    z = lax.axis_index("head")
    flip, run = (z % 2) * half, z // 2
    place = lax.axis_index("dp") % 8
    y, x, c = place // 4, (place // 2) % 2, place % 2
    slice_rows = model // 8
    at = lambda b: (b + flip) % units
    starts, lengths, orders = segments_of(seg_lengths, run, units)
    greet((("head", 1), ("head", 2), ("head", 3), ("dp", 1), ("dp", 2), ("dp", 4)))
    hops = Hops(send, recv)
    started = []

    def go(*args):
        started.append(hops.start(*args))
        return started[-1]

    part_rows, part_cols = far.shape[3:]
    mine = weight.at[
        pl.ds(pl.multiple_of((2 * y + x) * part_rows, 16), part_rows),
        pl.ds(pl.multiple_of(c * part_cols, 128), part_cols),
    ]
    small[...] = packed[0:16]
    bias_row[...] = jnp.broadcast_to(packed[22:23], bias_row.shape)
    narrow = width // 8
    chosen = jnp.zeros((narrow, model), F32)
    for j in range(8):
        chosen += jnp.where(place == j, out_weight[j * narrow : (j + 1) * narrow].astype(F32), 0.0)
    spare = jnp.zeros((weight_mine.shape[0] - narrow, model), F32)
    weight_mine[...] = jnp.concatenate([chosen, spare], axis=0).astype(BF16)
    slice_copy = go(mine, far.at[y, x, c], "head", 2)
    small_copy = go(small, far_row, "head", 2)
    row_copies = []
    for k in range(half):
        part = slice(k * UNIT, (k + 1) * UNIT)
        value = source[part].astype(F32)
        centred = value - jnp.mean(value, axis=-1, keepdims=True)
        factor = lax.rsqrt(jnp.mean(centred * centred, axis=-1, keepdims=True) + EPSILON)
        first_rows[part] = (centred * factor * packed[16:17] + packed[17:18]).astype(BF16)
        row_copies.append(go(first_rows.at[part], near.at[part], "head", 1))
    in_mine = ff_in.at[pl.ds(pl.multiple_of(place * slice_rows, 16), slice_rows)]
    out_mine = ff_out.at[pl.ds(pl.multiple_of(place * slice_rows, 16), slice_rows)]
    gathers = ((far_in, 2, 4), (far_weight, 2, 4), (far_out, 4, 2))
    stage = {}

    for r in (1, 2, 3):
        stage[r] = [
            hops.make(in_mine, far_in.at[r - 1, y, x, c], "head", r),
            hops.make(weight_mine, far_weight.at[r - 1, y, x, c], "head", r),
            hops.make(out_mine, far_out.at[r - 1, y, x, c], "head", r),
        ]
        started.extend(stage[r])
    at_end = (z == 0) | (z == 3)

    def send_chunk(r):
        for copy in stage[r]:
            copy.start()

    def send_early(first):
        pl.when(at_end)(functools.partial(send_chunk, 2 if first else 3))
        pl.when(jnp.logical_not(at_end))(functools.partial(send_chunk, 3 if first else 2))


    def advance(r, step):
        for copy in stage[r]:
            copy.wait_recv()
        stage[r] = []
        for array, first, second in gathers:
            block = array.at[r - 1]
            if step == 1:
                part, bit = block.at[y, x, c], first
            elif step == 2:
                part, bit = (block.at[y, :, c] if first == 2 else block.at[:, x, c]), second
            else:
                part, bit = block.at[:, :, c], 1
            stage[r].append(go(part, part, "dp", bit))

    send_chunk(1)
    send_early(True)
    in_bias[0] = bias_row[...]
    bias_copies = [go(bias_row, in_bias.at[r], "head", r) for r in (1, 2, 3)]

    slice_copy.wait_recv()
    x_copy = go(far.at[y, x, c], far.at[y, x, c], "dp", 2)

    def widen(k, read):
        for i in range(3):
            flats[k, i * LANES : i * LANES + width] = read(slice(i * width, (i + 1) * width))
            flats[k, i * LANES + width : (i + 1) * LANES] = jnp.zeros((LANES - width, model), BF16)

    def project(k, unit, shift):
        span = slice(unit * UNIT, (unit + 1) * UNIT)
        qkv[k, unit] = (dot(first_rows[span], flats[k], ((1,), (1,))) + shift).astype(BF16)

    widen(0, lambda span: weight[span])
    for unit in range(half):
        project(0, unit, small[0:1])
    x_copy.wait_recv()
    y_copy = go(far.at[y, :, c], far.at[y, :, c], "dp", 4)
    first_cols[:, :own_rows] = first_rows[:own_rows].astype(F32).T.astype(BF16)
    y_copy.wait_recv()
    core_copy = go(far.at[:, :, c], far.at[:, :, c], "dp", 1)
    small_copy.wait_recv()
    for k, copy in enumerate(row_copies):
        copy.wait_recv()
        part = slice(k * UNIT, (k + 1) * UNIT)
        first_rows[own_rows + k * UNIT : own_rows + (k + 1) * UNIT] = near[part]
        project(0, half + k, small[0:1])
    send_early(False)

    advance(1, 1)
    first_cols[:, own_rows:] = near[...].astype(F32).T.astype(BF16)
    core_copy.wait_recv()
    for i in range(8):
        row, col = (i // 2) * part_rows, (i % 2) * part_cols
        far_flat[row : row + part_rows, col : col + part_cols] = far[i // 4, (i // 2) % 2, i % 2]
    widen(1, lambda span: far_flat[span])
    for unit in range(units):
        project(1, unit, far_row[0:1])
    saved = set_out(
        [(qkv, qkv_out), (first_cols, first_cols_out), (flats.at[0], flat_a_out), (flats.at[1], flat_b_out)],
        local_sems, 0,
    )

    def probe_of(k):
        return jnp.where(k == 0, small[1:9, :BASIS], far_row[1:9, :BASIS])

    mask = head_rows(heads, LANES)

    def first_state(k, carry):
        memory[k] = jnp.zeros(memory.shape[1:], F32)
        row = probe_of(k)
        rows[k, 0:8] = row
        wide = 2 * (BASIS + LIVE)
        for i in range(1, 4):
            row = three_pass(row, table[:, :BASIS], table[:, wide : wide + BASIS])
            rows[k, 8 * i : 8 * i + 8] = row
        return carry

    lax.fori_loop(0, 2, first_state, 0)

    def state(b, k, carry):
        start, length = starts[b], lengths[b]
        now = memory[k]
        value_states[k, b] = now[:, LANES:]
        key_states[k, b] = now[:, :LANES].astype(BF16)
        if b > 0:
            probes[k, b] = jnp.where(mask, dot(rows[k, 0:8], now[:, :LANES], precision=HIGHEST), 0.0)
        else:
            probes[k, b] = jnp.zeros((8, LANES), F32)
        token = lax.broadcasted_iota(jnp.int32, (LIVE, UNIT), 1) + (b - start) * UNIT
        centre = (lax.broadcasted_iota(jnp.int32, (LIVE, UNIT), 0) + LIVE).astype(F32) / (BASIS - 1)
        gap = place_of(token, length) - centre
        psi = jnp.exp(gap * gap * (-0.5 / (WIDTH * WIDTH)))
        psi_high = psi.astype(BF16)
        psi_low = (psi - psi_high.astype(F32)).astype(BF16)
        pairs = qkv[k, at(b), :, LANES : 3 * LANES]
        exact = dot(psi_high, pairs[:, :LANES]) + dot(psi_low, pairs[:, :LANES])
        fresh = jnp.concatenate([exact, dot(psi_high, pairs[:, LANES:])], axis=1)
        gathered = fresh if b == 0 else jnp.where(start == b, 0.0, sums[k]) + fresh
        sums[k] = gathered
        stacked = jnp.concatenate([now, gathered * term_scale(length)], axis=0)
        later = jnp.concatenate(
            [
                dot(table[...], split3(stacked[:, :LANES])),
                dot(table[:, : BASIS + LIVE], stacked[:, LANES:].astype(BF16)),
            ],
            axis=1,
        )
        memory[k] = jnp.where(start + length == b + 1, later, now)
        return carry

    def end_state(k, carry):
        key = memory[k, :, :LANES]
        key_end[k] = key
        value_ends[k] = memory[k, :, LANES : LANES + width].T.astype(BF16)
        seen = dot(rows[k], key, precision=HIGHEST)
        for i in range(4):
            projs[k, 8 * i : 8 * i + 8] = jnp.where(mask, seen[8 * i : 8 * i + 8], 0.0)
        return carry

    def attend(b, k, carry):
        cols[k, :, b * UNIT : (b + 1) * UNIT] = qkv[k, at(b), :, 2 * LANES : 3 * LANES].astype(F32).T.astype(BF16)
        keys[k, b * UNIT : (b + 1) * UNIT] = qkv[k, at(b), :, LANES : 2 * LANES]
        query = qkv[k, at(b), :, 0:LANES].astype(F32) * root
        lane_head = lax.broadcasted_iota(jnp.int32, (UNIT, LANES), 1) // HEAD_DIM
        causal = lax.broadcasted_iota(jnp.int32, (UNIT, UNIT), 0) <= lax.broadcasted_iota(
            jnp.int32, (UNIT, UNIT), 1
        )
        away = [jnp.where(starts[b] <= j, 0.0, 1e30) for j in range(b)] + [0.0]
        owns = jnp.concatenate([jnp.where(lane_head == h, query, 0.0).astype(BF16) for h in range(heads)], axis=0)
        seen = (b + 1) * UNIT
        products = dot(keys[k, :seen], owns, ((1,), (1,)))
        for h in range(heads):
            scores = [products[j * UNIT : (j + 1) * UNIT, h * UNIT : (h + 1) * UNIT] for j in range(b + 1)]
            scores[b] = jnp.where(causal, scores[b], -1e30)
            highest = functools.reduce(
                jnp.maximum, [jnp.max(s, axis=0, keepdims=True) - away[j] for j, s in enumerate(scores)]
            )
            weights = [jnp.exp(s - (highest + away[j])) for j, s in enumerate(scores)]
            total = sum(jnp.sum(w, axis=0, keepdims=True) for w in weights)
            span = slice(h * HEAD_DIM, (h + 1) * HEAD_DIM)
            part = dot(cols[k, span, :seen], jnp.concatenate([w.astype(BF16) for w in weights], axis=0))
            discrete[k, b, span] = part * (1.0 / total)
            logsum[k, b, h : h + 1] = highest + jnp.log(total)
        return carry

    def seen_value(k, carry):
        incoming = jnp.where(run > 0, value_ins[k].astype(F32), 0.0).T
        carried[:, :width] = incoming
        carried[:, width:] = jnp.zeros((BASIS, LANES - width), F32)
        for b in range(units):
            if b > 0:
                carried[...] = jnp.where(starts[b] == b, advance_values(table, carried[...]), carried[...])
            values[k, b] = (value_states[k, b] + carried[...]).astype(BF16)
            gained = jnp.zeros((8, LANES), F32)
            for i in range(4):
                gained += jnp.where((orders[b] == i) & (run > 0), proj_ins[k, 8 * i : 8 * i + 8], 0.0)
            probes[k, b] = (probes[k, b] + gained) * root
        return carry

    def read(rel, k, carry):
        b = at(rel)
        query = qkv[k, rel, :, 0:LANES]
        logits = logits_of(probes[k, b], query)
        location, variance = read_parts(logits, heads)
        fall = -0.5 / variance
        peak = WIDTH * lax.rsqrt(variance)
        centres = lax.broadcasted_iota(jnp.int32, (BASIS, UNIT), 0).astype(F32) / (BASIS - 1)
        value_cols = values[k, b].astype(F32).T.astype(BF16)
        parts = []
        for h in range(heads):
            gap = centres - location[h : h + 1]
            density = jnp.exp(gap * gap * fall[h : h + 1]).astype(BF16)
            span = slice(h * HEAD_DIM, (h + 1) * HEAD_DIM)
            parts.append(discrete[k, b, span] + dot(value_cols[span], density) * peak[h : h + 1])
        mixed[k, rel] = jnp.concatenate(parts, axis=0).T.astype(BF16)
        return carry

    advance(1, 2)
    state_copies = []
    for k in range(2):
        for b in range(units):
            state(b, k, 0)
        end_state(k, 0)
        state_copies.append([
            go(value_ends.at[k], value_ins.at[1 - k], "head", 2), go(projs.at[k], proj_ins.at[1 - k], "head", 2)
        ])
        if k == 0:
            advance(2, 1)
            advance(3, 1)
        if k == 1:
            advance(1, 3)
    for b in range(units):
        lax.fori_loop(0, 2, functools.partial(attend, b), 0)
        if b == 0:
            advance(2, 2)
        if b == 2:
            advance(3, 2)
        if b == 3:
            advance(2, 3)
    saved += set_out([(key_states, key_states_out), (key_end, key_end_out)], local_sems, 4)
    mixed_copies = [None, None]
    for k in (1, 0):
        for copy in state_copies[1 - k]:
            copy.wait_recv()
        seen_value(k, 0)
        read(2, k, 0)
        read(3, k, 0)
        mixed_copies[k] = go(mixed.at[k, half:], mixed_in.at[k], "head", 1)
        if k == 1:
            advance(3, 3)
    saved += set_out([(values, values_out)], local_sems, 6)
    lax.fori_loop(0, 2, functools.partial(read, 0), 0)
    lax.fori_loop(0, 2, functools.partial(read, 1), 0)
    mixed_0[...] = mixed[0, :half].reshape(own_rows, width)
    mixed_2[...] = mixed[1, :half].reshape(own_rows, width)
    for copy in mixed_copies:
        copy.wait_recv()
    mixed_1[...] = mixed_in[0].reshape(own_rows, width)
    mixed_3[...] = mixed_in[1].reshape(own_rows, width)
    for copy in bias_copies + stage[1] + stage[2] + stage[3]:
        copy.wait_recv()
    for copy in started:
        copy.wait_send()
    for copy in saved:
        copy.wait()


def forward(seg_lengths, source, packed, weight, out_weight, ff_in, ff_out, heads):
    own_rows, model = source.shape
    units = 2 * own_rows // UNIT
    width = heads * HEAD_DIM
    hidden_part = ff_in.shape[1]
    rows = model // 8
    spaced = -(-width // 8 // 16) * 16
    table = jnp.asarray(basis_tables()[0])
    vmem, anywhere = pl.BlockSpec(memory_space=pltpu.VMEM), pl.BlockSpec(memory_space=pl.ANY)
    shape = jax.ShapeDtypeStruct
    hops = 2 + units // 2 + 3 + 3 * 3 * 4 + 3 + 4 + 2
    return pl.pallas_call(
        functools.partial(forward_kernel, heads),
        in_specs=[pl.BlockSpec(memory_space=pltpu.SMEM)] + [vmem] * 5 + [anywhere] * 2,
        out_specs=[anywhere] * 7 + [vmem] * 8 + [anywhere] * 3,
        out_shape=[
            shape((2, units, UNIT, 3 * LANES), BF16),
            shape((model, 2 * own_rows), BF16),
            shape((3 * LANES, model), BF16),
            shape((3 * LANES, model), BF16),
            shape((2, units, BASIS, LANES), BF16),
            shape((2, units, BASIS, LANES), BF16),
            shape((2, BASIS, LANES), F32),
            shape((2, units, 8, UNIT), F32),
            shape((2, units, 8, LANES), F32),
            shape((2, 32, BASIS), F32),
        ] + [shape((own_rows, width), BF16)] * 4 + [
            shape((4, 8, hidden_part), F32),
            shape((3, 2, 2, 2, rows, hidden_part), BF16),
            shape((3, 2, 2, 2, rows, model), BF16),
            shape((3, 2, 2, 2, spaced, model), BF16),
        ],
        scratch_shapes=[
            pltpu.VMEM((2, units, UNIT, 3 * LANES), BF16),
            pltpu.VMEM((2 * own_rows, model), BF16),
            pltpu.VMEM((model, 2 * own_rows), BF16),
            pltpu.VMEM((2, 3 * LANES, model), BF16),
            pltpu.VMEM((own_rows, model), BF16),
            pltpu.VMEM((2, 2, 2, 3 * width // 4, model // 2), BF16),
            pltpu.VMEM((3 * width, model), BF16),
            pltpu.VMEM((16, 3 * LANES), F32),
            pltpu.VMEM((16, 3 * LANES), F32),
            pltpu.VMEM((8, hidden_part), F32),
            pltpu.VMEM((spaced, model), BF16),
            pltpu.VMEM((2, BASIS, 2 * LANES), F32),
            pltpu.VMEM((2, LIVE, 2 * LANES), F32),
            pltpu.VMEM((2, units, BASIS, LANES), F32),
            pltpu.VMEM((BASIS, LANES), F32),
            pltpu.VMEM((2, width, BASIS), BF16),
            pltpu.VMEM((2, width, BASIS), BF16),
            pltpu.VMEM((2, 32, LANES), F32),
            pltpu.VMEM((2, 32, LANES), F32),
            pltpu.VMEM((2, LANES, units * UNIT), BF16),
            pltpu.VMEM((2, units * UNIT, LANES), BF16),
            pltpu.VMEM((2, units, width, UNIT), F32),
            pltpu.VMEM((2, units, UNIT, width), BF16),
            pltpu.VMEM((2, units // 2, UNIT, width), BF16),
            pltpu.VMEM((2, units, BASIS, LANES), BF16),
            pltpu.VMEM((2, units, BASIS, LANES), BF16),
            pltpu.VMEM((2, BASIS, LANES), F32),
            pltpu.SemaphoreType.DMA((hops,)),
            pltpu.SemaphoreType.DMA((hops,)),
            pltpu.SemaphoreType.DMA((7,)),
        ],
        compiler_params=pltpu.CompilerParams(
            collective_id=1, has_side_effects=True, vmem_limit_bytes=60 << 20
        ),
        name="forward",
    )(seg_lengths, source, packed, weight, out_weight, table, ff_in, ff_out)


def whole(shape):
    return pl.BlockSpec(shape, lambda i: (0,) * len(shape))


def finish_kernel(given_in, given_out, given_weight, given_qkv, grad_in, grad_out, grad_weight, grad_qkv):
    step = pl.program_id(0)
    grad_in[...] = given_in[...].astype(F32)
    grad_out[...] = given_out[...].astype(F32)
    width = grad_qkv.shape[1]
    for i in range(3):

        @pl.when(step == i)
        def _():
            grad_qkv[0] = given_qkv[:, i * width : (i + 1) * width].astype(F32).T

    @pl.when(step == 0)
    def _():
        narrow = grad_weight.shape[0] // given_weight.shape[0]
        for j in range(given_weight.shape[0]):
            grad_weight[j * narrow : (j + 1) * narrow] = given_weight[j].astype(F32)[:narrow]


def finish(given_in, given_out, given_weight, given_qkv, width):
    model, columns = given_in.shape
    hidden_part = given_out.shape[0]
    return pl.pallas_call(
        finish_kernel,
        grid=(3,),
        in_specs=[
            pl.BlockSpec((model // 3, columns), lambda i: (i, 0)),
            pl.BlockSpec((hidden_part // 3, model), lambda i: (i, 0)),
            pl.BlockSpec(given_weight.shape, lambda i: (0, 0, 0)),
            pl.BlockSpec(given_qkv.shape, lambda i: (0, 0)),
        ],
        out_specs=[
            pl.BlockSpec((model // 3, columns), lambda i: (i, 0)),
            pl.BlockSpec((hidden_part // 3, model), lambda i: (i, 0)),
            pl.BlockSpec((width, model), lambda i: (0, 0)),
            pl.BlockSpec((1, width, model), lambda i: (i, 0, 0)),
        ],
        out_shape=[
            jax.ShapeDtypeStruct((model, columns), F32), jax.ShapeDtypeStruct((hidden_part, model), F32),
            jax.ShapeDtypeStruct((width, model), F32), jax.ShapeDtypeStruct((3, width, model), F32),
        ],
        compiler_params=pltpu.CompilerParams(vmem_limit_bytes=62 << 20),
        name="finish",
    )(given_in, given_out, given_weight, given_qkv)


def middle_kernel(
    source, cotangent, mixed_0, mixed_1, mixed_2, mixed_3, own_weight, far_weight, vectors, in_bias, own_in, own_out,
    far_in, far_out, outputs, grad_residual, grad_mixed_0, grad_mixed_1, grad_mixed_2, grad_mixed_3, grad_in, grad_out,
    grad_out_weight, sums, grad_in_bias,
    residual, inverse, second, second_cols, total, grad_second, in_now, out_now, out_weight,
):
    r = pl.program_id(0)
    slices, rows = own_in.shape[0], own_in.shape[1]
    model = source.shape[1]
    hidden_part = own_in.shape[2]
    out_bias, gain, shift, last_bias = (vectors[k : k + 1] for k in range(18, 22))

    @pl.when(r == 0)
    def _():
        value = source[...].astype(F32) + out_bias
        out_weight[0] = own_weight[...]
        narrow = own_weight.shape[0] // slices
        for k in range(far_weight.shape[0]):
            parts = [far_weight[k, j].astype(F32)[:narrow] for j in range(slices)]
            out_weight[k + 1] = jnp.concatenate(parts, axis=0).astype(BF16)
        for k, mixed in enumerate((mixed_0, mixed_1, mixed_2, mixed_3)):
            value += dot(mixed[...], out_weight[k])
        residual[...] = value
        centred = value - jnp.mean(value, axis=-1, keepdims=True)
        factor = lax.rsqrt(jnp.mean(centred * centred, axis=-1, keepdims=True) + EPSILON)
        inverse[...] = factor
        normal = centred * factor
        grad_residual[...] = normal
        rounded = (normal * gain + shift).astype(BF16)
        second[...] = rounded
        second_cols[...] = rounded.astype(F32).T.astype(BF16)
        total[...] = jnp.zeros_like(total)
        grad_second[...] = jnp.zeros_like(grad_second)
        grad_in_bias[...] = jnp.zeros_like(grad_in_bias)
        for j in range(slices):
            in_now[j * rows : (j + 1) * rows] = own_in[j]
            out_now[j * rows : (j + 1) * rows] = own_out[j]

    @pl.when(r > 0)
    def _():
        for j in range(slices):
            in_now[j * rows : (j + 1) * rows] = far_in[0, j]
            out_now[j * rows : (j + 1) * rows] = far_out[0, j]

    half = hidden_part
    for t in range(1):
        span = slice(t * half, (t + 1) * half)
        hidden = dot(second[...], in_now[:, span]) + in_bias[r, 0:1, span]
        cube = hidden * hidden
        root = math.sqrt(2.0 / math.pi)
        bent = jnp.tanh(hidden * (root + (root * 0.044715) * cube))
        lifted = 0.5 + 0.5 * bent
        activation = (hidden * lifted).astype(BF16)
        slope = lifted + hidden * ((0.5 - 0.5 * bent * bent) * (root + (3.0 * root * 0.044715) * cube))
        total[...] += dot(activation, out_now[span])
        given = dot(cotangent[...], out_now[span], ((1,), (1,)))
        grad_hidden = (given * slope).astype(BF16)
        grad_second[...] += dot(grad_hidden, in_now[:, span], ((1,), (1,)))
        grad_in_bias[pl.ds(r, 1), span] = jnp.sum(grad_hidden.astype(F32), axis=0, keepdims=True)
        part = dot(activation, cotangent[...], ((0,), (0,))).astype(BF16)
        per = half // rows
        for k in range(per):
            grad_out[0, t * per + k] = part[k * rows : (k + 1) * rows]
        part = dot(second_cols[...], grad_hidden).astype(BF16)
        for j in range(slices):
            grad_in[0, j, :, span] = part[j * rows : (j + 1) * rows]

    @pl.when(r == pl.num_programs(0) - 1)
    def _():
        given = cotangent[...].astype(F32)
        outputs[...] = (residual[...] + total[...] + last_bias).astype(BF16)
        normal = grad_residual[...]
        grad = grad_second[...]
        scaled = grad * gain
        value = given + inverse[...] * (
            scaled
            - jnp.mean(scaled, axis=-1, keepdims=True)
            - normal * jnp.mean(scaled * normal, axis=-1, keepdims=True)
        )
        sums[0:1] = jnp.sum(value, axis=0, keepdims=True)
        sums[1:2] = jnp.sum(grad * normal, axis=0, keepdims=True)
        sums[2:3] = jnp.sum(grad, axis=0, keepdims=True)
        sums[3:4] = jnp.sum(given, axis=0, keepdims=True)
        sums[4:8] = jnp.zeros((4, model), F32)
        grad_residual[...] = value
        rounded = value.astype(BF16)
        grads = (grad_mixed_0, grad_mixed_1, grad_mixed_2, grad_mixed_3)
        for k, mixed in enumerate((mixed_0, mixed_1, mixed_2, mixed_3)):
            grads[k][...] = dot(rounded, out_weight[k], ((1,), (1,))).astype(BF16)
            product = dot(mixed[...], rounded, ((0,), (0,)))
            narrow = product.shape[0] // slices
            spare = jnp.zeros((grad_out_weight.shape[2] - narrow, model), F32)
            for j in range(slices):
                part = jnp.concatenate([product[j * narrow : (j + 1) * narrow], spare], axis=0)
                grad_out_weight[k, j] = part.astype(BF16)


def middle(source, cotangent, mixed, out_weight, far_weight, vectors, in_bias, own_in, own_out, far_in, far_out):
    own_rows, model = source.shape
    shards = far_in.shape[0] + 1
    slices, rows, hidden_part = own_in.shape
    narrow = mixed[0].shape
    far = pl.BlockSpec((1,) + own_in.shape, lambda r: (jnp.maximum(r - 1, 0), 0, 0, 0))
    part = pl.BlockSpec((1,) + own_in.shape, lambda r: (r, 0, 0, 0))
    macs = own_rows * model * (6 * shards * hidden_part + 3 * model)
    return pl.pallas_call(
        middle_kernel,
        grid_spec=pltpu.PrefetchScalarGridSpec(
            num_scalar_prefetch=0,
            grid=(shards,),
            in_specs=[whole(source.shape)] * 2 + [whole(narrow)] * 4 + [
                whole(out_weight.shape), whole(far_weight.shape), whole(vectors.shape), whole(in_bias.shape), whole(own_in.shape),
                whole(own_out.shape), far, far,
            ],
            out_specs=[whole(source.shape)] * 2 + [whole(narrow)] * 4 + [
                part, part, whole((shards,) + far_weight.shape[1:]), whole((8, model)), whole((shards, hidden_part))
            ],
            scratch_shapes=[
                pltpu.VMEM((own_rows, model), F32),
                pltpu.VMEM((own_rows, 1), F32),
                pltpu.VMEM((own_rows, model), BF16),
                pltpu.VMEM((model, own_rows), BF16),
                pltpu.VMEM((own_rows, model), F32),
                pltpu.VMEM((own_rows, model), F32),
                pltpu.VMEM((model, hidden_part), BF16),
                pltpu.VMEM((hidden_part, model), BF16),
                pltpu.VMEM((shards,) + narrow[1:] + (model,), BF16),
            ],
        ),
        out_shape=[
            jax.ShapeDtypeStruct(source.shape, BF16),
            jax.ShapeDtypeStruct(source.shape, F32),
        ] + [jax.ShapeDtypeStruct(narrow, BF16)] * 4 + [
            jax.ShapeDtypeStruct((shards, slices, rows, hidden_part), BF16),
            jax.ShapeDtypeStruct((shards, slices, rows, hidden_part), BF16),
            jax.ShapeDtypeStruct((shards,) + far_weight.shape[1:], BF16),
            jax.ShapeDtypeStruct((8, model), F32),
            jax.ShapeDtypeStruct((shards, hidden_part), F32),
        ],
        compiler_params=pltpu.CompilerParams(vmem_limit_bytes=60 << 20),
        cost_estimate=pl.CostEstimate(
            flops=2 * macs, bytes_accessed=30 << 20, transcendentals=own_rows * shards * hidden_part
        ),
        name="middle",
    )(source, cotangent, *mixed, out_weight, far_weight, vectors, in_bias, own_in, own_out, far_in, far_out)


def added(a, b):
    return (a.astype(F32) + b.astype(F32)).astype(BF16)


def backward_kernel(
    heads, seg_lengths, qkv, gm_0, gm_1, gm_2, gm_3, logsum, values, probes, key_states_in, key_end_in, rows_in, table_in,
    grad_in, grad_out, grad_weight, out, probe_grad, slice_in, slice_out, slice_weight,
    given, query_grad, memory_grad, row_grad, value_carried, value_back, value_in, row_back, row_in, carried, spread, key_grad, value_grad, cols, keys, vals,
    key_states, key_end, rows, table,
    keep_in, keep_out, keep_weight, core_in, core_out, core_weight, one_in, one_out, one_weight,
    two_in, two_out, two_weight, z_in, z_out, z_weight, send, recv, local_sems,
):
    units = qkv.shape[1]
    half = units // 2
    width = heads * HEAD_DIM
    root = 1.0 / math.sqrt(HEAD_DIM)
    z = lax.axis_index("head")
    flip, run = (z % 2) * half, z // 2
    place = lax.axis_index("dp") % 8
    y, x, c = place // 4, (place // 2) % 2, place % 2
    at = lambda b: (b + flip) % units
    starts, lengths, orders = segments_of(seg_lengths, run, units)
    greet((("head", 1), ("head", 2), ("head", 3), ("dp", 1), ("dp", 2), ("dp", 4)))
    hops = Hops(send, recv)
    started = []

    def go(*args):
        started.append(hops.start(*args))
        return started[-1]

    tables = set_out(
        [(key_states_in, key_states), (key_end_in, key_end), (rows_in, rows), (table_in, table)], local_sems, 12
    )
    given_copies = [go(gm_1, given.at[0, half:], "head", 1), go(gm_3, given.at[1, half:], "head", 1)]
    sums = (
        (grad_in, keep_in, core_in, one_in, two_in, z_in, True),
        (grad_weight, keep_weight, core_weight, one_weight, two_weight, z_weight, True),
        (grad_out, keep_out, core_out, one_out, two_out, z_out, False),
    )
    stage, local_copies = {}, {}
    for i, r in enumerate((2, 1, 3, 0)):
        stage[r], local_copies[r] = [], []
        for n, (term, keep, core, _, _, _, _) in enumerate(sums):
            stage[r].append(go(term.at[r, :, :, 1 - c], core.at[r], "dp", 1))
            copy = pltpu.make_async_copy(term.at[r, :, :, c], keep.at[r], local_sems.at[3 * i + n])
            copy.start()
            local_copies[r].append(copy)

    def first_hop(r):
        for n, (_, keep, core, one, _, _, along_x) in enumerate(sums):
            local_copies[r][n].wait()
            stage[r][n].wait_recv()
            keep[r] = added(keep[r], core[r])
            part = keep.at[r, :, 1 - x] if along_x else keep.at[r, 1 - y]
            stage[r][n] = go(part, one.at[r], "dp", 2 if along_x else 4)

    def second_hop(r):
        for n, (_, keep, _, one, two, _, along_x) in enumerate(sums):
            stage[r][n].wait_recv()
            kept = keep[r, :, x] if along_x else keep[r, y]
            one[r] = added(kept, one[r])
            part = one.at[r, 1 - y] if along_x else one.at[r, 1 - x]
            stage[r][n] = go(part, two.at[r], "dp", 4 if along_x else 2)

    def third_hop(r):
        for n, (_, _, _, one, two, far, along_x) in enumerate(sums):
            stage[r][n].wait_recv()
            kept = one[r, y] if along_x else one[r, x]
            two[r] = added(kept, two[r])
            if r:
                stage[r][n] = go(two.at[r], far.at[r - 1], "head", r)

    for k, own in enumerate((gm_0, gm_2)):
        given[k, :half] = own[...]
    mask = head_rows(heads, LANES)
    lane_head = lax.broadcasted_iota(jnp.int32, (UNIT, LANES), 1) // HEAD_DIM

    def given_of(k, b):
        return jnp.concatenate([given[k, at(b)], jnp.zeros((UNIT, LANES - width), BF16)], axis=1).astype(F32)

    def read_back(rel, k, carry):
        b = at(rel)
        query = qkv[k, rel, :, 0:LANES]
        full = given_of(k, b)
        probe = probes[k, b]
        logits = logits_of(probe, query)
        location, variance = read_parts(logits, heads)
        inverse = 1.0 / variance
        fall = -0.5 * inverse
        peak = WIDTH * lax.rsqrt(variance)
        centres = lax.broadcasted_iota(jnp.int32, (BASIS, UNIT), 0).astype(F32) / (BASIS - 1)
        along, across = [], []
        total = jnp.zeros((BASIS, LANES), F32)
        for h in range(heads):
            own_given = jnp.where(lane_head == h, full, 0.0).astype(BF16)
            gap = centres - location[h : h + 1]
            square = gap * gap
            density = jnp.exp(square * fall[h : h + 1]) * peak[h : h + 1]
            grad_density = dot(values[k, b], own_given, ((1,), (1,)))
            total += dot(density.astype(BF16), own_given)
            weighed = density * grad_density
            moment = weighed * gap
            zeroth = jnp.sum(weighed, axis=0, keepdims=True)
            first = jnp.sum(moment, axis=0, keepdims=True)
            second = jnp.sum(moment * gap, axis=0, keepdims=True)
            along.append(first * inverse[h : h + 1])
            across.append(0.5 * inverse[h : h + 1] * (second * inverse[h : h + 1] - zeroth))
        sigmoid = 1.0 / (1.0 + jnp.exp(-logits))
        grad_location = jnp.concatenate(along, axis=0) * location * (1.0 - location)
        grad_variance = jnp.concatenate(across, axis=0) * SPREAD * sigmoid[heads : 2 * heads]
        grad_logits = jnp.concatenate(
            [grad_location, grad_variance, jnp.zeros((8 - 2 * heads, UNIT), F32)], axis=0
        )
        padded = jnp.concatenate([grad_logits, jnp.zeros((120, UNIT), F32)], axis=0)
        probe_cols = jnp.concatenate([probe, jnp.zeros((120, LANES), F32)], axis=0).T
        query_grad[k, b] = dot(probe_cols.astype(BF16), padded.astype(BF16))[:width]
        fresh = jnp.where(mask, dot(grad_logits.astype(BF16), query), 0.0) * root
        memory_grad[k, b] = total
        row_grad[k, b] = fresh
        return carry

    def gather_back(k, carry):
        probe = jnp.zeros((8, BASIS), F32)
        for i in range(4):
            row_back[k, 8 * i : 8 * i + 8] = jnp.zeros((8, LANES), F32)
        for b in range(units - 1, -1, -1):
            fresh, total = row_grad[k, b], memory_grad[k, b]
            if b > 0:
                probe += dot(fresh.astype(BF16), key_states[k, b], ((1,), (1,)))
            for i in range(4):
                row_back[k, 8 * i : 8 * i + 8] += jnp.where(orders[b] == i, fresh, 0.0)
            if b < units - 1:
                ends = starts[b] + lengths[b] == b + 1
                total = jnp.where(ends, 0.0, memory_grad[k, b + 1]) + total
                memory_grad[k, b] = total
                row_grad[k, b] = jnp.where(ends, 0.0, row_grad[k, b + 1]) + fresh
            before = jnp.zeros((BASIS, LANES), F32) if b == units - 1 else value_carried[k]
            if b > 0:
                value_carried[k] = jnp.where(starts[b] == b, advance_values(table, before + total), before)
            else:
                value_back[k] = (before + total)[:, :width].T.astype(BF16)
        probe_grad[k] = probe
        return carry

    def attend_back(b, k, carry):
        query = qkv[k, at(b), :, 0:LANES].astype(F32) * root
        full = given_of(k, b)
        causal = lax.broadcasted_iota(jnp.int32, (UNIT, UNIT), 0) <= lax.broadcasted_iota(
            jnp.int32, (UNIT, UNIT), 1
        )
        away = [jnp.where(starts[b] <= j, 0.0, 1e30) for j in range(b)] + [0.0]
        owns = [jnp.where(lane_head == h, query, 0.0).astype(BF16) for h in range(heads)]
        own_givens = [jnp.where(lane_head == h, full, 0.0).astype(BF16) for h in range(heads)]
        own_all = jnp.concatenate(owns, axis=0)
        given_all = jnp.concatenate(own_givens, axis=0)
        seen = (b + 1) * UNIT
        scores = dot(keys[k, :seen], own_all, ((1,), (1,)))
        grad_probs = dot(vals[k, :seen], given_all, ((1,), (1,)))
        grads, probs = [], []
        for h in range(heads):
            prob_h, product_h = [], []
            inner = jnp.zeros((1, UNIT), F32)
            for j in range(b + 1):
                tile = (slice(j * UNIT, (j + 1) * UNIT), slice(h * UNIT, (h + 1) * UNIT))
                score = scores[tile]
                if j == b:
                    score = jnp.where(causal, score, -1e30)
                prob = jnp.exp(score - (logsum[k, b, h : h + 1] + away[j]))
                product = prob * grad_probs[tile]
                inner += jnp.sum(product, axis=0, keepdims=True)
                prob_h.append(prob)
                product_h.append(product)
            span = slice(h * HEAD_DIM, (h + 1) * HEAD_DIM)
            grad_h = [(product_h[j] - prob_h[j] * inner).astype(BF16) for j in range(b + 1)]
            result = dot(cols[k, span, :seen], jnp.concatenate(grad_h, axis=0))
            query_grad[k, b, span] = query_grad[k, b, span] + result * root
            grads.append(grad_h)
            probs.append([prob.astype(BF16) for prob in prob_h])
        fresh_keys = dot(jnp.concatenate([jnp.concatenate(g, axis=0) for g in grads], axis=1), own_all)
        fresh_vals = dot(jnp.concatenate([jnp.concatenate(p, axis=0) for p in probs], axis=1), given_all)
        for j in range(b + 1):
            part = slice(j * UNIT, (j + 1) * UNIT)
            if b == units - 1:
                key_grad[k, j], value_grad[k, j] = fresh_keys[part], fresh_vals[part]
            else:
                key_grad[k, j] += fresh_keys[part]
                value_grad[k, j] += fresh_vals[part]
        return carry

    def carry_back(k, total, units_before):
        moved = dot(table[...], total.astype(BF16))
        return moved[:BASIS], (moved[BASIS:] * term_scale(units_before)).astype(BF16)

    def end_back(k, carry):
        row = jnp.where(run == 0, row_in[k], 0.0)
        value = jnp.where(run == 0, value_in[k].astype(F32), 0.0).T
        grad_keys = dot(rows[k].astype(BF16), row.astype(BF16), ((0,), (0,)))
        total = jnp.concatenate([grad_keys, value, jnp.zeros((BASIS, LANES - width), F32)], axis=1)
        carried[k], spread[k] = carry_back(k, total, lengths[units - 1])
        seen = dot(row, key_end[k], ((1,), (1,)), HIGHEST)
        gained = seen[24:32]
        for i in (2, 1, 0):
            high = gained.astype(BF16)
            low = (gained - high.astype(F32)).astype(BF16)
            gained = dot(high, table[:BASIS]) + dot(low, table[:BASIS])
            gained = gained + seen[8 * i : 8 * i + 8]
        probe_grad[k] += gained
        return carry

    def finish(b, k, carry):
        start, length = starts[b], lengths[b]
        token = lax.broadcasted_iota(jnp.int32, (UNIT, LIVE), 0) + (b - start) * UNIT
        centre = (lax.broadcasted_iota(jnp.int32, (UNIT, LIVE), 1) + LIVE).astype(F32) / (BASIS - 1)
        gap = place_of(token, length) - centre
        psi = jnp.exp(gap * gap * (-0.5 / (WIDTH * WIDTH))).astype(BF16)
        pair_grad = dot(psi, spread[k])
        query_rows = query_grad[k, b].T.astype(BF16)
        out[k, at(b), :, :LANES] = jnp.concatenate([query_rows, jnp.zeros((UNIT, LANES - width), BF16)], axis=1)
        out[k, at(b), :, LANES : 2 * LANES] = (key_grad[k, b] + pair_grad[:, :LANES]).astype(BF16)
        out[k, at(b), :, 2 * LANES :] = (value_grad[k, b] + pair_grad[:, LANES:]).astype(BF16)
        if b > 0:
            grad_keys = dot(rows[k, 0:8].astype(BF16), row_grad[k, b].astype(BF16), ((0,), (0,)))
            total = carried[k] + jnp.concatenate([grad_keys, memory_grad[k, b]], axis=1)
            moved, spread_now = carry_back(k, total, lengths[b - 1])
            carried[k] = jnp.where(start == b, moved, carried[k])
            spread[k] = jnp.where(start == b, spread_now.astype(F32), spread[k].astype(F32)).astype(BF16)
        return carry

    def both(step, *args):
        lax.fori_loop(0, 2, functools.partial(step, *args), 0)

    def turn(k, carry):
        for b in range(units):
            part = slice(b * UNIT, (b + 1) * UNIT)
            keys[k, part] = qkv[k, at(b), :, LANES : 2 * LANES]
            vals[k, part] = qkv[k, at(b), :, 2 * LANES : 3 * LANES]
            cols[k, :, part] = qkv[k, at(b), :, LANES : 2 * LANES].astype(F32).T.astype(BF16)
        return carry

    lax.fori_loop(0, 2, turn, 0)
    both(read_back, 0)
    first_hop(2)
    both(read_back, 1)
    first_hop(1)
    for copy in given_copies:
        copy.wait_recv()
    both(read_back, 2)
    first_hop(3)
    first_hop(0)
    both(read_back, 3)
    for copy in tables:
        copy.wait()
    back_copies = []
    for k in range(2):
        gather_back(k, 0)
        back_copies += [
            go(value_back.at[k], value_in.at[1 - k], "head", 2), go(row_back.at[k], row_in.at[1 - k], "head", 2)
        ]
    second_hop(2)
    both(attend_back, 3)
    second_hop(1)
    second_hop(3)
    third_hop(2)
    both(attend_back, 2)
    second_hop(0)
    third_hop(1)
    third_hop(3)
    both(attend_back, 1)
    third_hop(0)
    both(attend_back, 0)
    for copy in back_copies:
        copy.wait_recv()
    lax.fori_loop(0, 2, end_back, 0)
    for b in range(units - 1, -1, -1):
        both(finish, b)
    for n, (_, _, _, _, two, far, _) in enumerate(sums):
        total = two[0].astype(F32)
        for r in (1, 2, 3):
            stage[r][n].wait_recv()
            total += far[r - 1].astype(F32)
        (slice_in, slice_weight, slice_out)[n][...] = total.astype(BF16)
    for copy in started:
        copy.wait_send()


def backward(seg_lengths, qkv, grad_mixed, logsum, values, probes, key_states, key_end, rows, grad_in, grad_out, grad_weight, heads):
    units = qkv.shape[1]
    width = heads * HEAD_DIM
    table = jnp.asarray(basis_tables()[1])
    vmem, anywhere = pl.BlockSpec(memory_space=pltpu.VMEM), pl.BlockSpec(memory_space=pl.ANY)
    shape = jax.ShapeDtypeStruct
    slices = [grad_in.shape[4:], grad_out.shape[4:], grad_weight.shape[4:]]
    hops = 2 + 3 * 4 * 3 + 3 * 3 + 4
    return pl.pallas_call(
        functools.partial(backward_kernel, heads),
        in_specs=[pl.BlockSpec(memory_space=pltpu.SMEM)] + [vmem] * 8 + [anywhere] * 7,
        out_specs=[vmem] * 5,
        out_shape=[shape(qkv.shape, BF16), shape((2, 8, BASIS), F32)] + [shape(part, BF16) for part in slices],
        scratch_shapes=[
            pltpu.VMEM((2, units, UNIT, width), BF16),
            pltpu.VMEM((2, units, width, UNIT), F32),
            pltpu.VMEM((2, units, BASIS, LANES), F32),
            pltpu.VMEM((2, units, 8, LANES), F32),
            pltpu.VMEM((2, BASIS, LANES), F32),
            pltpu.VMEM((2, width, BASIS), BF16),
            pltpu.VMEM((2, width, BASIS), BF16),
            pltpu.VMEM((2, 32, LANES), F32),
            pltpu.VMEM((2, 32, LANES), F32),
            pltpu.VMEM((2, BASIS, 2 * LANES), F32),
            pltpu.VMEM((2, LIVE, 2 * LANES), BF16),
            pltpu.VMEM((2, units, UNIT, LANES), F32),
            pltpu.VMEM((2, units, UNIT, LANES), F32),
            pltpu.VMEM((2, LANES, units * UNIT), BF16),
            pltpu.VMEM((2, units * UNIT, LANES), BF16),
            pltpu.VMEM((2, units * UNIT, LANES), BF16),
            pltpu.VMEM(key_states.shape, BF16),
            pltpu.VMEM(key_end.shape, F32),
            pltpu.VMEM(rows.shape, F32),
            pltpu.VMEM(table.shape, BF16),
        ]
        + [pltpu.VMEM((4, 2, 2) + part, BF16) for part in slices]
        + [pltpu.VMEM((4, 2, 2) + part, BF16) for part in slices]
        + [pltpu.VMEM((4, 2) + part, BF16) for part in slices]
        + [pltpu.VMEM((4,) + part, BF16) for part in slices]
        + [pltpu.VMEM((3,) + part, BF16) for part in slices]
        + [
            pltpu.SemaphoreType.DMA((hops,)),
            pltpu.SemaphoreType.DMA((hops,)),
            pltpu.SemaphoreType.DMA((16,)),
        ],
        compiler_params=pltpu.CompilerParams(
            collective_id=2, has_side_effects=True, vmem_limit_bytes=62 << 20
        ),
        name="backward",
    )(
        seg_lengths, qkv, *grad_mixed, logsum, values, probes, key_states, key_end, rows, table, grad_in, grad_out, grad_weight
    )


def tail_kernel(
    heads, outer, grads, flat_a, flat_b, packed, slice_in, slice_out, slice_weight, sums, in_bias_part, probe_grad,
    first_cols_in, grad_residual_in, source_in, input_grad, whole_in, whole_out, whole_weight, whole_qkv, shared_out, owned_out,
    row_grad, near, kept, part_a, part_b, core_a, core_b, one_a, one_b, two_a, two_b, far_b, total, outer_in,
    gather_in, gather_out, gather_weight, gather_qkv,
    shared, shared_in, block, block_in, bias_block, bias_in, joined, joined_in, first_cols, grad_residual, source,
    send, recv, local_sems,
):
    own_rows, model = source.shape
    loads = set_out(
        [(first_cols_in, first_cols), (grad_residual_in, grad_residual), (source_in, source)], local_sems, 0
    )
    units = grads.shape[1]
    half = units // 2
    width = heads * HEAD_DIM
    z = lax.axis_index("head")
    place = lax.axis_index("dp") % 8
    y, x, c = place // 4, (place // 2) % 2, place % 2
    rows = model // 8
    greet(
        (("head", 1), ("head", 2), ("head", 3), ("dp", 1), ("dp", 2), ("dp", 4)) + tuple(("dp", bit) for bit in outer)
    )
    hops = Hops(send, recv)
    started = []

    def go(*args):
        started.append(hops.start(*args))
        return started[-1]

    def row_of(rel):
        return dot(grads[0, rel], flat_a[...]) + dot(grads[1, rel], flat_b[...])

    row_copies = []
    for k in range(half):
        row_grad[k] = row_of(half + k).astype(BF16)
        row_copies.append(go(row_grad.at[k], near.at[k], "head", 1))

    gathers = ((slice_in, gather_in, True), (slice_weight, gather_weight, True), (slice_out, gather_out, False))
    for own, gather, _ in gathers:
        gather[y, x, c] = own[...]

    def spread_first(gather, along_x):
        part = gather.at[y, x, c]
        return go(part, part, "dp", 2 if along_x else 4)

    def spread_second(gather, along_x):
        part = gather.at[y, :, c] if along_x else gather.at[:, x, c]
        return go(part, part, "dp", 4 if along_x else 2)

    def spread_third(gather):
        part = gather.at[:, :, c]
        return go(part, part, "dp", 1)

    spreads = [spread_first(gather, along_x) for _, gather, along_x in gathers]

    loads[0].wait()
    core_copies = []
    for k, part, core in ((1, part_b, core_b), (0, part_a, core_a)):
        product = dot(first_cols[...], grads[k].reshape(2 * own_rows, 3 * LANES))
        product = jnp.concatenate([product[:, i * LANES : i * LANES + width] for i in range(3)], axis=1).astype(BF16)
        for j in range(8):
            part[j // 4, (j // 2) % 2, j % 2] = product[j * rows : (j + 1) * rows]
        core_copies.append(go(part.at[:, :, 1 - c], core, "dp", 1))
    for k in range(half):
        kept[k] = row_of(k)

    core_copies[0].wait_recv()
    core_b[...] = added(part_b[:, :, c], core_b[...])
    one_copy_b = go(core_b.at[1 - y], one_b, "dp", 4)
    core_copies[1].wait_recv()
    core_a[...] = added(part_a[:, :, c], core_a[...])
    one_copy_a = go(core_a.at[:, 1 - x], one_a, "dp", 2)

    bias_a = jnp.sum(grads[0].reshape(2 * own_rows, 3 * LANES).astype(F32), axis=0, keepdims=True)
    bias_b = jnp.sum(grads[1].reshape(2 * own_rows, 3 * LANES).astype(F32), axis=0, keepdims=True)
    edge = jnp.zeros((8, model - BASIS), F32)
    fill = jnp.zeros((6, model), F32)
    for k, bias in ((0, bias_a), (1, bias_b)):
        block[k, 0:8] = jnp.concatenate([probe_grad[k], edge], axis=1)
        block[k, 8:16] = jnp.concatenate([bias, in_bias_part[2 * k : 2 * k + 1], fill], axis=0)
        bias_block[k] = jnp.concatenate([in_bias_part[2 * k + 1 : 2 * k + 2], jnp.zeros((7, model), F32)], axis=0)
    block_copy = go(block.at[1], block_in, "head", 2)
    bias_copies = [go(bias_block.at[0], bias_in.at[0], "head", 1), go(bias_block.at[1], bias_in.at[1], "head", 3)]

    loads[1].wait()
    loads[2].wait()
    value = source[...].astype(F32)
    centred = value - jnp.mean(value, axis=-1, keepdims=True)
    factor = lax.rsqrt(jnp.mean(centred * centred, axis=-1, keepdims=True) + EPSILON)
    normal = centred * factor

    one_copy_b.wait_recv()
    one_b[...] = added(core_b[y], one_b[...])
    two_copy_b = go(one_b.at[1 - x], two_b, "dp", 2)
    one_copy_a.wait_recv()
    one_a[...] = added(core_a[:, x], one_a[...])
    two_copy_a = go(one_a.at[1 - y], two_a, "dp", 4)
    spreads = [copy.wait_recv() or spread_second(gather, along_x) for copy, (_, gather, along_x) in zip(spreads, gathers)]
    for copy in row_copies:
        copy.wait_recv()
    two_copy_b.wait_recv()
    two_b[...] = added(one_b[x], two_b[...])
    far_copy = go(two_b, far_b, "head", 2)

    grad = kept[...].reshape(own_rows, model) + near[...].reshape(own_rows, model).astype(F32)
    scaled = grad * packed[16:17]
    change = factor * (
        scaled
        - jnp.mean(scaled, axis=-1, keepdims=True)
        - normal * jnp.mean(scaled * normal, axis=-1, keepdims=True)
    )
    input_grad[...] = (grad_residual[...] + change).astype(BF16)
    shared[...] = jnp.concatenate(
        [jnp.sum(grad * normal, axis=0, keepdims=True), jnp.sum(grad, axis=0, keepdims=True), sums[0:6]], axis=0
    )
    shared_copies = [go(shared, shared_in.at[r - 1], "head", r) for r in (1, 2, 3)]

    two_copy_a.wait_recv()
    own_sum = added(one_a[y], two_a[...]).astype(F32)
    far_copy.wait_recv()
    total[0] = (own_sum + far_b[...].astype(F32)).astype(BF16)
    for n, bit in enumerate(outer):
        copy = go(total.at[n], outer_in.at[n], "dp", bit)
        copy.wait_recv()
        total[n + 1] = added(total[n], outer_in[n])
    gather_qkv[y, x, c] = total[len(outer)]
    cut = rows // 2
    upper, lower = pl.ds(0, cut), pl.ds(cut, cut)
    qkv_parts = [gather_qkv.at[y, x, c, upper], gather_qkv.at[y, x, c, lower]]
    qkv_copies = [go(qkv_parts[0], qkv_parts[0], "dp", 2), go(qkv_parts[1], qkv_parts[1], "dp", 4)]

    block_copy.wait_recv()
    for copy in bias_copies + shared_copies:
        copy.wait_recv()
    owned = block[0] + block_in[...]
    bias_rows = bias_in[0] + bias_in[1]
    owned_rows = jnp.concatenate([owned[8:9], owned[9:10] + bias_rows[0:1], owned[10:16]], axis=0)
    joined[0] = jnp.concatenate(
        [shared[...] + shared_in[0] + shared_in[1] + shared_in[2], owned[0:8], owned_rows], axis=0
    )
    spreads = [copy.wait_recv() or spread_third(gather) for copy, (_, gather, _) in zip(spreads, gathers)]
    for n, bit in enumerate((2, 4, 1) + outer):
        copy = go(joined.at[n], joined_in.at[n], "dp", bit)
        if n == 1:
            for copy_one in qkv_copies:
                copy_one.wait_recv()
            qkv_parts = [gather_qkv.at[y, :, c, upper], gather_qkv.at[:, x, c, lower]]
            qkv_copies = [go(qkv_parts[0], qkv_parts[0], "dp", 4), go(qkv_parts[1], qkv_parts[1], "dp", 2)]
        copy.wait_recv()
        joined[n + 1] = joined[n] + joined_in[n]
    last = joined[3 + len(outer)]
    shared_out[...] = last[0:8]
    owned_out[...] = last[8:24]
    for copy, (_, gather, _), out in zip(spreads, gathers, (whole_in, whole_weight, whole_out)):
        copy.wait_recv()
        out[...] = gather[...]
    for copy in qkv_copies:
        copy.wait_recv()
    spread_third(gather_qkv).wait_recv()
    whole_qkv[...] = gather_qkv[...]
    for copy in started:
        copy.wait_send()


def tail(grads, first_cols, flat_a, flat_b, grad_residual, source, packed, slices, sums, in_bias_part, probe_grad, outer, heads):
    own_rows, model = source.shape
    units = grads.shape[1]
    rows = model // 8
    vmem = pl.BlockSpec(memory_space=pltpu.VMEM)
    shape = jax.ShapeDtypeStruct
    slice_in, slice_out, slice_weight = slices
    plane = lambda part: (2, 2, 2) + part
    part = (rows, 3 * heads * HEAD_DIM)
    hops = units // 2 + 9 + 2 + 2 + 2 + 1 + 5 + 1 + 2 + 3 + 3 + 2 * len(outer)
    return pl.pallas_call(
        functools.partial(tail_kernel, heads, outer),
        in_specs=[vmem] * 10 + [pl.BlockSpec(memory_space=pl.ANY)] * 3,
        out_specs=[vmem] * 7,
        out_shape=[
            shape(source.shape, BF16), shape(plane(slice_in.shape), BF16), shape(plane(slice_out.shape), BF16),
            shape(plane(slice_weight.shape), BF16), shape(plane(part), BF16), shape((8, model), F32),
            shape((16, model), F32),
        ],
        scratch_shapes=[
            pltpu.VMEM((units // 2, UNIT, model), BF16),
            pltpu.VMEM((units // 2, UNIT, model), BF16),
            pltpu.VMEM((units // 2, UNIT, model), F32),
            pltpu.VMEM(plane(part), BF16),
            pltpu.VMEM(plane(part), BF16),
            pltpu.VMEM((2, 2) + part, BF16),
            pltpu.VMEM((2, 2) + part, BF16),
            pltpu.VMEM((2,) + part, BF16),
            pltpu.VMEM((2,) + part, BF16),
            pltpu.VMEM(part, BF16),
            pltpu.VMEM(part, BF16),
            pltpu.VMEM(part, BF16),
            pltpu.VMEM((1 + len(outer),) + part, BF16),
            pltpu.VMEM((max(1, len(outer)),) + part, BF16),
            pltpu.VMEM(plane(slice_in.shape), BF16),
            pltpu.VMEM(plane(slice_out.shape), BF16),
            pltpu.VMEM(plane(slice_weight.shape), BF16),
            pltpu.VMEM(plane(part), BF16),
            pltpu.VMEM((8, model), F32),
            pltpu.VMEM((3, 8, model), F32),
            pltpu.VMEM((2, 16, model), F32),
            pltpu.VMEM((16, model), F32),
            pltpu.VMEM((2, 8, model), F32),
            pltpu.VMEM((2, 8, model), F32),
            pltpu.VMEM((4 + len(outer), 24, model), F32),
            pltpu.VMEM((3 + len(outer), 24, model), F32),
            pltpu.VMEM(first_cols.shape, BF16),
            pltpu.VMEM(grad_residual.shape, F32),
            pltpu.VMEM(source.shape, BF16),
            pltpu.SemaphoreType.DMA((hops,)),
            pltpu.SemaphoreType.DMA((hops,)),
            pltpu.SemaphoreType.DMA((3,)),
        ],
        compiler_params=pltpu.CompilerParams(
            collective_id=3, has_side_effects=True, vmem_limit_bytes=60 << 20
        ),
        name="tail",
    )(
        grads, flat_a, flat_b, packed, slice_in, slice_out, slice_weight, sums, in_bias_part, probe_grad, first_cols,
        grad_residual, source,
    )


def exchange(value, axis, bit):
    size = lax.axis_size(axis)
    return lax.ppermute(value, axis, [(j, j ^ bit) for j in range(size)])


def local(
    inputs, seg_lengths, ln1_gain, ln1_bias, qkv_weight, qkv_bias, out_weight, out_bias, mem_mu, mem_sig,
    ln2_gain, ln2_bias, ff_in, ff_in_bias, ff_out, ff_out_bias, cotangent,
):
    own_rows, model = inputs.shape
    shards = lax.axis_size("head")
    members = lax.axis_size("dp")
    width = qkv_weight.shape[2]
    heads = width // HEAD_DIM
    hidden_part = ff_in.shape[1]
    units = 2 * own_rows // UNIT
    slices = 8
    outer = tuple(1 << k for k in range(3, 16) if 1 << k < members)
    rows = model // slices

    bias_row = jnp.pad(qkv_bias, ((0, 0), (0, LANES - width))).reshape(1, 3 * LANES)
    edge = 3 * LANES - BASIS
    packed = jnp.pad(bias_row, ((0, 23), (0, 0))).astype(F32)
    packed += jnp.pad(mem_mu, ((1, 23 - heads), (0, edge))).astype(F32)
    packed += jnp.pad(mem_sig, ((1 + heads, 23 - 2 * heads), (0, edge))).astype(F32)
    given = (ln1_gain, ln1_bias, out_bias, ln2_gain, ln2_bias, ff_out_bias, ff_in_bias)
    line = sum(jnp.pad(vector.astype(F32), (k * model, (6 - k) * model)) for k, vector in enumerate(given))
    packed += jnp.pad(line.reshape(7, model), ((16, 1), (0, 0)))

    turned_weight = jnp.transpose(qkv_weight, (1, 2, 0)).reshape(3 * width, model)
    (
        qkv, first_cols, flat_a, flat_b, values, key_states, key_end, logsum, probes, state_rows,
        *mixed, in_bias, far_in, far_out, far_weight,
    ) = forward(seg_lengths, inputs, packed, turned_weight, out_weight, ff_in, ff_out, heads)
    flat = lambda array: array.reshape((shards - 1, slices) + array.shape[4:])
    outputs, grad_residual, *rest = middle(
        inputs, cotangent, mixed, out_weight, flat(far_weight), packed, in_bias,
        ff_in.reshape(slices, rows, hidden_part), ff_out.reshape(slices, rows, model), flat(far_in), flat(far_out),
    )
    grad_mixed, (ff_in_part, ff_out_part, out_weight_part, sums, in_bias_part) = rest[:4], rest[4:]
    paired = [part.reshape(units // 2, UNIT, width) for part in grad_mixed]
    plane = lambda array: array.reshape((shards, 2, 2, 2) + array.shape[2:])
    grads, probe_grad, *parts = backward(
        seg_lengths, qkv, paired, logsum, values, probes, key_states, key_end, state_rows, plane(ff_in_part),
        plane(ff_out_part), plane(out_weight_part), heads,
    )
    for bit in outer:
        parts = [added(part, exchange(part, "dp", bit)) for part in parts]
    input_grad, whole_in, whole_out, whole_weight, whole_qkv, shared, owned = tail(
        grads, first_cols, flat_a, flat_b, grad_residual, inputs, packed, parts, sums, in_bias_part, probe_grad,
        outer, heads,
    )
    ff_in_sum, ff_out_sum, out_weight_sum, qkv_weight_sum = finish(
        whole_in.reshape(model, hidden_part), whole_out.reshape(hidden_part, model),
        whole_weight.reshape((slices,) + whole_weight.shape[3:]), whole_qkv.reshape(model, 3 * width), width,
    )
    return (
        outputs, input_grad, shared[0], shared[1], jnp.transpose(qkv_weight_sum, (2, 0, 1)),
        owned[8].reshape(3, LANES)[:, :width], out_weight_sum, shared[2], owned[:heads, :BASIS],
        owned[heads : 2 * heads, :BASIS], shared[3], shared[4], ff_in_sum, owned[9, :hidden_part], ff_out_sum, shared[5],
    )


def solution(mesh):
    rows, whole = P(("dp", "head"), None), P()
    return jax.shard_map(
        local,
        mesh=mesh,
        in_specs=(
            rows, P("dp", None), whole, whole, P(None, None, "head"), P(None, "head"), P("head", None), whole,
            P("head", None), P("head", None), whole, whole, P(None, "head"), P("head"), P("head", None), whole, rows,
        ),
        out_specs=(
            rows, rows, whole, whole, P(None, None, "head"), P(None, "head"), P("head", None), whole,
            P("head", None), P("head", None), whole, whole, P(None, "head"), P("head"), P("head", None), whole,
        ),
        check_vma=False,
    )
```

```python
import functools
import math

import jax
import jax.numpy as jnp
import ml_dtypes
import numpy as np
from jax import lax
from jax.experimental import pallas as pl
from jax.experimental.pallas import tpu as pltpu
from jax.sharding import PartitionSpec as P

HEAD_DIM = 64
BASIS = 512
UNIT = 256
LANES = 256
TAU = 0.75
RIDGE = 0.5
EPSILON = 1e-05
MESH = pl.DeviceIdType.MESH
SPREAD = 1.0 / 64.0
WIDTH = 1.0 / BASIS
LIVE = BASIS // 2
HIGHEST = lax.Precision.HIGHEST
F32 = jnp.float32
BF16 = jnp.bfloat16


def split_table(table):
    high = table.astype(np.float32).astype(ml_dtypes.bfloat16)
    low = (table.astype(np.float32) - high.astype(np.float32)).astype(ml_dtypes.bfloat16)
    return high, low


@functools.lru_cache(maxsize=None)
def basis_tables():
    centres = np.arange(BASIS) / (BASIS - 1)
    apart = centres[:, None] - centres[None, :]
    gram = np.exp(-apart * apart / (4.0 * WIDTH * WIDTH)) + RIDGE * np.eye(BASIS)
    solve = np.linalg.inv(gram)
    samples = (np.arange(BASIS) + 0.5) / BASIS
    near_gap = TAU * samples[:, None] - centres[None, :]
    far_gap = samples[:, None] - centres[None, :]
    near = np.exp(-near_gap * near_gap / (2.0 * WIDTH * WIDTH))
    far = np.exp(-far_gap * far_gap / (2.0 * WIDTH * WIDTH))
    contract = (near.T @ far) * (TAU / (BASIS * WIDTH * math.sqrt(math.pi)))
    joined = np.concatenate([solve @ contract, solve[:, LIVE:]], axis=1)
    high, low = split_table(joined)
    forward = np.concatenate([high, high, low], axis=1)
    backward = np.ascontiguousarray(high.T)
    return forward, backward


def term_scale(units):
    return (1.0 - TAU) / (WIDTH * math.sqrt(math.pi) * UNIT) / units.astype(F32)


def split3(value):
    high = value.astype(BF16)
    low = (value - high.astype(F32)).astype(BF16)
    return jnp.concatenate([high, low, high], axis=0)


def dot(a, b, contract=((1,), (0,)), precision=None):
    return lax.dot_general(a, b, (contract, ((), ())), precision=precision, preferred_element_type=F32)


def head_rows(heads, width):
    row = lax.broadcasted_iota(jnp.int32, (8, width), 0)
    lane = lax.broadcasted_iota(jnp.int32, (8, width), 1) // HEAD_DIM
    return ((row == lane) | (row == lane + heads)) & (lane < heads)


def read_parts(logits, heads):
    location = 1.0 / (1.0 + jnp.exp(-logits))
    variance = (jnp.maximum(logits, 0.0) + jnp.log1p(jnp.exp(-jnp.abs(logits)))) * SPREAD + WIDTH * WIDTH
    return location[:heads], variance[heads : 2 * heads]


def place_of(index, length):
    return TAU + (1.0 - TAU) * (index.astype(F32) + 0.5) / (length.astype(F32) * UNIT)


def split_rows(value):
    high = value.astype(BF16)
    rest = value - high.astype(F32)
    mid = rest.astype(BF16)
    return high, mid, (rest - mid.astype(F32)).astype(BF16)


def three_pass(left, right_high, right_low, contract=((1,), (0,))):
    high = left.astype(BF16)
    low = (left - high.astype(F32)).astype(BF16)
    return dot(high, right_high, contract) + dot(low, right_high, contract) + dot(high, right_low, contract)


def advance_values(table, value):
    return dot(table[:BASIS, :BASIS], value.astype(BF16))


def logits_of(probes, query):
    parts = dot(jnp.concatenate(split_rows(probes), axis=0), query, ((1,), (1,)))
    return parts[0:8] + parts[8:16] + parts[16:24]


def segments_of(lengths, run, units):
    sizes = [lengths[0, run * units + s] // UNIT for s in range(units)]
    ends, total = [], 0
    for size in sizes:
        total = total + size
        ends.append(total)
    starts, spans, orders = [], [], []
    for b in range(units):
        start, span, order = 0, 0, 0
        for size, end in zip(sizes, ends):
            inside = (end > b) & (end - size <= b)
            start = start + jnp.where(inside, end - size, 0)
            span = span + jnp.where(inside, size, 0)
            order = order + jnp.where((end <= b) & (size > 0), 1, 0)
        starts.append(start)
        spans.append(span)
        orders.append(order)
    return starts, spans, orders


def other_of(index, distance):
    bit = 1
    while bit <= distance:
        if distance & bit:
            index = index + bit - 2 * bit * ((index // bit) % 2)
        bit *= 2
    return index


class Hops:
    def __init__(self, send, recv):
        self.send, self.recv, self.used = send, recv, 0

    def start(self, source, target, axis, bit):
        copy = self.make(source, target, axis, bit)
        copy.start()
        return copy

    def make(self, source, target, axis, bit):
        copy = pltpu.make_async_remote_copy(
            src_ref=source,
            dst_ref=target,
            send_sem=self.send.at[self.used],
            recv_sem=self.recv.at[self.used],
            device_id={axis: other_of(lax.axis_index(axis), bit)},
            device_id_type=MESH,
        )
        self.used += 1
        return copy


def greet(neighbours):
    barrier = pltpu.get_barrier_semaphore()
    for axis, bit in neighbours:
        pl.semaphore_signal(
            barrier, inc=1, device_id={axis: other_of(lax.axis_index(axis), bit)}, device_id_type=MESH
        )
    pl.semaphore_wait(barrier, len(neighbours))


def set_out(pairs, sems, first):
    copies = [pltpu.make_async_copy(a, b, sems.at[first + k]) for k, (a, b) in enumerate(pairs)]
    for copy in copies:
        copy.start()
    return copies


def forward_kernel(
    heads, seg_lengths, source, packed, weight, out_weight, table, ff_in, ff_out,
    qkv_out, first_cols_out, flat_a_out, flat_b_out, values_out, key_states_out, key_end_out, logsum, probes, rows,
    mixed_0, mixed_1, mixed_2, mixed_3, in_bias, far_in, far_out, far_weight,
    qkv, first_rows, first_cols, flats, near, far, far_flat, small, far_row, bias_row, weight_mine, memory, sums, value_states, carried, value_ends, value_ins,
    projs, proj_ins, cols, keys, discrete, mixed, mixed_in, values, key_states, key_end, send, recv, local_sems,
):
    own_rows, model = source.shape
    width = heads * HEAD_DIM
    units = qkv.shape[1]
    half = units // 2
    root = 1.0 / math.sqrt(HEAD_DIM)
    z = lax.axis_index("head")
    flip, run = (z % 2) * half, z // 2
    place = lax.axis_index("dp") % 8
    y, x, c = place // 4, (place // 2) % 2, place % 2
    slice_rows = model // 8
    at = lambda b: (b + flip) % units
    starts, lengths, orders = segments_of(seg_lengths, run, units)
    greet((("head", 1), ("head", 2), ("head", 3), ("dp", 1), ("dp", 2), ("dp", 4)))
    hops = Hops(send, recv)
    started = []

    def go(*args):
        started.append(hops.start(*args))
        return started[-1]

    part_rows, part_cols = far.shape[3:]
    mine = weight.at[
        pl.ds(pl.multiple_of((2 * y + x) * part_rows, 16), part_rows),
        pl.ds(pl.multiple_of(c * part_cols, 128), part_cols),
    ]
    small[...] = packed[0:16]
    bias_row[...] = jnp.broadcast_to(packed[22:23], bias_row.shape)
    narrow = width // 8
    chosen = jnp.zeros((narrow, model), F32)
    for j in range(8):
        chosen += jnp.where(place == j, out_weight[j * narrow : (j + 1) * narrow].astype(F32), 0.0)
    spare = jnp.zeros((weight_mine.shape[0] - narrow, model), F32)
    weight_mine[...] = jnp.concatenate([chosen, spare], axis=0).astype(BF16)
    slice_copy = go(mine, far.at[y, x, c], "head", 2)
    small_copy = go(small, far_row, "head", 2)
    row_copies = []
    for k in range(half):
        part = slice(k * UNIT, (k + 1) * UNIT)
        value = source[part].astype(F32)
        centred = value - jnp.mean(value, axis=-1, keepdims=True)
        factor = lax.rsqrt(jnp.mean(centred * centred, axis=-1, keepdims=True) + EPSILON)
        first_rows[part] = (centred * factor * packed[16:17] + packed[17:18]).astype(BF16)
        row_copies.append(go(first_rows.at[part], near.at[part], "head", 1))
    in_mine = ff_in.at[pl.ds(pl.multiple_of(place * slice_rows, 16), slice_rows)]
    out_mine = ff_out.at[pl.ds(pl.multiple_of(place * slice_rows, 16), slice_rows)]
    gathers = ((far_in, 2, 4), (far_weight, 2, 4), (far_out, 4, 2))
    stage = {}

    for r in (1, 2, 3):
        stage[r] = [
            hops.make(in_mine, far_in.at[r - 1, y, x, c], "head", r),
            hops.make(weight_mine, far_weight.at[r - 1, y, x, c], "head", r),
            hops.make(out_mine, far_out.at[r - 1, y, x, c], "head", r),
        ]
        started.extend(stage[r])
    at_end = (z == 0) | (z == 3)

    def send_chunk(r):
        for copy in stage[r]:
            copy.start()

    def send_early(first):
        pl.when(at_end)(functools.partial(send_chunk, 2 if first else 3))
        pl.when(jnp.logical_not(at_end))(functools.partial(send_chunk, 3 if first else 2))


    def advance(r, step):
        for copy in stage[r]:
            copy.wait_recv()
        stage[r] = []
        for array, first, second in gathers:
            block = array.at[r - 1]
            if step == 1:
                part, bit = block.at[y, x, c], first
            elif step == 2:
                part, bit = (block.at[y, :, c] if first == 2 else block.at[:, x, c]), second
            else:
                part, bit = block.at[:, :, c], 1
            stage[r].append(go(part, part, "dp", bit))

    send_chunk(1)
    send_early(True)
    in_bias[0] = bias_row[...]
    bias_copies = [go(bias_row, in_bias.at[r], "head", r) for r in (1, 2, 3)]

    slice_copy.wait_recv()
    x_copy = go(far.at[y, x, c], far.at[y, x, c], "dp", 2)

    def widen(k, read):
        for i in range(3):
            flats[k, i * LANES : i * LANES + width] = read(slice(i * width, (i + 1) * width))
            flats[k, i * LANES + width : (i + 1) * LANES] = jnp.zeros((LANES - width, model), BF16)

    def project(k, unit, shift):
        span = slice(unit * UNIT, (unit + 1) * UNIT)
        qkv[k, unit] = (dot(first_rows[span], flats[k], ((1,), (1,))) + shift).astype(BF16)

    widen(0, lambda span: weight[span])
    for unit in range(half):
        project(0, unit, small[0:1])
    x_copy.wait_recv()
    y_copy = go(far.at[y, :, c], far.at[y, :, c], "dp", 4)
    first_cols[:, :own_rows] = first_rows[:own_rows].astype(F32).T.astype(BF16)
    y_copy.wait_recv()
    core_copy = go(far.at[:, :, c], far.at[:, :, c], "dp", 1)
    small_copy.wait_recv()
    for k, copy in enumerate(row_copies):
        copy.wait_recv()
        part = slice(k * UNIT, (k + 1) * UNIT)
        first_rows[own_rows + k * UNIT : own_rows + (k + 1) * UNIT] = near[part]
        project(0, half + k, small[0:1])
    send_early(False)

    advance(1, 1)
    first_cols[:, own_rows:] = near[...].astype(F32).T.astype(BF16)
    core_copy.wait_recv()
    for i in range(8):
        row, col = (i // 2) * part_rows, (i % 2) * part_cols
        far_flat[row : row + part_rows, col : col + part_cols] = far[i // 4, (i // 2) % 2, i % 2]
    widen(1, lambda span: far_flat[span])
    for unit in range(units):
        project(1, unit, far_row[0:1])
    saved = set_out(
        [(qkv, qkv_out), (first_cols, first_cols_out), (flats.at[0], flat_a_out), (flats.at[1], flat_b_out)],
        local_sems, 0,
    )

    def probe_of(k):
        return jnp.where(k == 0, small[1:9, :BASIS], far_row[1:9, :BASIS])

    mask = head_rows(heads, LANES)

    def first_state(k, carry):
        memory[k] = jnp.zeros(memory.shape[1:], F32)
        row = probe_of(k)
        rows[k, 0:8] = row
        wide = 2 * (BASIS + LIVE)
        for i in range(1, 4):
            row = three_pass(row, table[:, :BASIS], table[:, wide : wide + BASIS])
            rows[k, 8 * i : 8 * i + 8] = row
        return carry

    lax.fori_loop(0, 2, first_state, 0)

    def state(b, k, carry):
        start, length = starts[b], lengths[b]
        now = memory[k]
        value_states[k, b] = now[:, LANES:]
        key_states[k, b] = now[:, :LANES].astype(BF16)
        if b > 0:
            probes[k, b] = jnp.where(mask, dot(rows[k, 0:8], now[:, :LANES], precision=HIGHEST), 0.0)
        else:
            probes[k, b] = jnp.zeros((8, LANES), F32)
        token = lax.broadcasted_iota(jnp.int32, (LIVE, UNIT), 1) + (b - start) * UNIT
        centre = (lax.broadcasted_iota(jnp.int32, (LIVE, UNIT), 0) + LIVE).astype(F32) / (BASIS - 1)
        gap = place_of(token, length) - centre
        psi = jnp.exp(gap * gap * (-0.5 / (WIDTH * WIDTH)))
        psi_high = psi.astype(BF16)
        psi_low = (psi - psi_high.astype(F32)).astype(BF16)
        pairs = qkv[k, at(b), :, LANES : 3 * LANES]
        exact = dot(psi_high, pairs[:, :LANES]) + dot(psi_low, pairs[:, :LANES])
        fresh = jnp.concatenate([exact, dot(psi_high, pairs[:, LANES:])], axis=1)
        gathered = fresh if b == 0 else jnp.where(start == b, 0.0, sums[k]) + fresh
        sums[k] = gathered
        stacked = jnp.concatenate([now, gathered * term_scale(length)], axis=0)
        later = jnp.concatenate(
            [
                dot(table[...], split3(stacked[:, :LANES])),
                dot(table[:, : BASIS + LIVE], stacked[:, LANES:].astype(BF16)),
            ],
            axis=1,
        )
        memory[k] = jnp.where(start + length == b + 1, later, now)
        return carry

    def end_state(k, carry):
        key = memory[k, :, :LANES]
        key_end[k] = key
        value_ends[k] = memory[k, :, LANES : LANES + width].T.astype(BF16)
        seen = dot(rows[k], key, precision=HIGHEST)
        for i in range(4):
            projs[k, 8 * i : 8 * i + 8] = jnp.where(mask, seen[8 * i : 8 * i + 8], 0.0)
        return carry

    def attend(b, k, carry):
        cols[k, :, b * UNIT : (b + 1) * UNIT] = qkv[k, at(b), :, 2 * LANES : 3 * LANES].astype(F32).T.astype(BF16)
        keys[k, b * UNIT : (b + 1) * UNIT] = qkv[k, at(b), :, LANES : 2 * LANES]
        query = qkv[k, at(b), :, 0:LANES].astype(F32) * root
        lane_head = lax.broadcasted_iota(jnp.int32, (UNIT, LANES), 1) // HEAD_DIM
        causal = lax.broadcasted_iota(jnp.int32, (UNIT, UNIT), 0) <= lax.broadcasted_iota(
            jnp.int32, (UNIT, UNIT), 1
        )
        away = [jnp.where(starts[b] <= j, 0.0, 1e30) for j in range(b)] + [0.0]
        owns = jnp.concatenate([jnp.where(lane_head == h, query, 0.0).astype(BF16) for h in range(heads)], axis=0)
        seen = (b + 1) * UNIT
        products = dot(keys[k, :seen], owns, ((1,), (1,)))
        for h in range(heads):
            scores = [products[j * UNIT : (j + 1) * UNIT, h * UNIT : (h + 1) * UNIT] for j in range(b + 1)]
            scores[b] = jnp.where(causal, scores[b], -1e30)
            highest = functools.reduce(
                jnp.maximum, [jnp.max(s, axis=0, keepdims=True) - away[j] for j, s in enumerate(scores)]
            )
            weights = [jnp.exp(s - (highest + away[j])) for j, s in enumerate(scores)]
            total = sum(jnp.sum(w, axis=0, keepdims=True) for w in weights)
            span = slice(h * HEAD_DIM, (h + 1) * HEAD_DIM)
            part = dot(cols[k, span, :seen], jnp.concatenate([w.astype(BF16) for w in weights], axis=0))
            discrete[k, b, span] = part * (1.0 / total)
            logsum[k, b, h : h + 1] = highest + jnp.log(total)
        return carry

    def seen_value(k, carry):
        incoming = jnp.where(run > 0, value_ins[k].astype(F32), 0.0).T
        carried[:, :width] = incoming
        carried[:, width:] = jnp.zeros((BASIS, LANES - width), F32)
        for b in range(units):
            if b > 0:
                carried[...] = jnp.where(starts[b] == b, advance_values(table, carried[...]), carried[...])
            values[k, b] = (value_states[k, b] + carried[...]).astype(BF16)
            gained = jnp.zeros((8, LANES), F32)
            for i in range(4):
                gained += jnp.where((orders[b] == i) & (run > 0), proj_ins[k, 8 * i : 8 * i + 8], 0.0)
            probes[k, b] = (probes[k, b] + gained) * root
        return carry

    def read(rel, k, carry):
        b = at(rel)
        query = qkv[k, rel, :, 0:LANES]
        logits = logits_of(probes[k, b], query)
        location, variance = read_parts(logits, heads)
        fall = -0.5 / variance
        peak = WIDTH * lax.rsqrt(variance)
        centres = lax.broadcasted_iota(jnp.int32, (BASIS, UNIT), 0).astype(F32) / (BASIS - 1)
        value_cols = values[k, b].astype(F32).T.astype(BF16)
        parts = []
        for h in range(heads):
            gap = centres - location[h : h + 1]
            density = jnp.exp(gap * gap * fall[h : h + 1]).astype(BF16)
            span = slice(h * HEAD_DIM, (h + 1) * HEAD_DIM)
            parts.append(discrete[k, b, span] + dot(value_cols[span], density) * peak[h : h + 1])
        mixed[k, rel] = jnp.concatenate(parts, axis=0).T.astype(BF16)
        return carry

    advance(1, 2)
    state_copies = []
    for k in range(2):
        for b in range(units):
            state(b, k, 0)
        end_state(k, 0)
        state_copies.append([
            go(value_ends.at[k], value_ins.at[1 - k], "head", 2), go(projs.at[k], proj_ins.at[1 - k], "head", 2)
        ])
        if k == 0:
            advance(2, 1)
            advance(3, 1)
        if k == 1:
            advance(1, 3)
    for b in range(units):
        lax.fori_loop(0, 2, functools.partial(attend, b), 0)
        if b == 0:
            advance(2, 2)
        if b == 2:
            advance(3, 2)
        if b == 3:
            advance(2, 3)
    saved += set_out([(key_states, key_states_out), (key_end, key_end_out)], local_sems, 4)
    mixed_copies = [None, None]
    for k in (1, 0):
        for copy in state_copies[1 - k]:
            copy.wait_recv()
        seen_value(k, 0)
        read(2, k, 0)
        read(3, k, 0)
        mixed_copies[k] = go(mixed.at[k, half:], mixed_in.at[k], "head", 1)
        if k == 1:
            advance(3, 3)
    saved += set_out([(values, values_out)], local_sems, 6)
    lax.fori_loop(0, 2, functools.partial(read, 0), 0)
    lax.fori_loop(0, 2, functools.partial(read, 1), 0)
    mixed_0[...] = mixed[0, :half].reshape(own_rows, width)
    mixed_2[...] = mixed[1, :half].reshape(own_rows, width)
    for copy in mixed_copies:
        copy.wait_recv()
    mixed_1[...] = mixed_in[0].reshape(own_rows, width)
    mixed_3[...] = mixed_in[1].reshape(own_rows, width)
    for copy in bias_copies + stage[1] + stage[2] + stage[3]:
        copy.wait_recv()
    for copy in started:
        copy.wait_send()
    for copy in saved:
        copy.wait()


def forward(seg_lengths, source, packed, weight, out_weight, ff_in, ff_out, heads):
    own_rows, model = source.shape
    units = 2 * own_rows // UNIT
    width = heads * HEAD_DIM
    hidden_part = ff_in.shape[1]
    rows = model // 8
    spaced = -(-width // 8 // 16) * 16
    table = jnp.asarray(basis_tables()[0])
    vmem, anywhere = pl.BlockSpec(memory_space=pltpu.VMEM), pl.BlockSpec(memory_space=pl.ANY)
    shape = jax.ShapeDtypeStruct
    hops = 2 + units // 2 + 3 + 3 * 3 * 4 + 3 + 4 + 2
    return pl.pallas_call(
        functools.partial(forward_kernel, heads),
        in_specs=[pl.BlockSpec(memory_space=pltpu.SMEM)] + [vmem] * 5 + [anywhere] * 2,
        out_specs=[anywhere] * 7 + [vmem] * 8 + [anywhere] * 3,
        out_shape=[
            shape((2, units, UNIT, 3 * LANES), BF16),
            shape((model, 2 * own_rows), BF16),
            shape((3 * LANES, model), BF16),
            shape((3 * LANES, model), BF16),
            shape((2, units, BASIS, LANES), BF16),
            shape((2, units, BASIS, LANES), BF16),
            shape((2, BASIS, LANES), F32),
            shape((2, units, 8, UNIT), F32),
            shape((2, units, 8, LANES), F32),
            shape((2, 32, BASIS), F32),
        ] + [shape((own_rows, width), BF16)] * 4 + [
            shape((4, 8, hidden_part), F32),
            shape((3, 2, 2, 2, rows, hidden_part), BF16),
            shape((3, 2, 2, 2, rows, model), BF16),
            shape((3, 2, 2, 2, spaced, model), BF16),
        ],
        scratch_shapes=[
            pltpu.VMEM((2, units, UNIT, 3 * LANES), BF16),
            pltpu.VMEM((2 * own_rows, model), BF16),
            pltpu.VMEM((model, 2 * own_rows), BF16),
            pltpu.VMEM((2, 3 * LANES, model), BF16),
            pltpu.VMEM((own_rows, model), BF16),
            pltpu.VMEM((2, 2, 2, 3 * width // 4, model // 2), BF16),
            pltpu.VMEM((3 * width, model), BF16),
            pltpu.VMEM((16, 3 * LANES), F32),
            pltpu.VMEM((16, 3 * LANES), F32),
            pltpu.VMEM((8, hidden_part), F32),
            pltpu.VMEM((spaced, model), BF16),
            pltpu.VMEM((2, BASIS, 2 * LANES), F32),
            pltpu.VMEM((2, LIVE, 2 * LANES), F32),
            pltpu.VMEM((2, units, BASIS, LANES), F32),
            pltpu.VMEM((BASIS, LANES), F32),
            pltpu.VMEM((2, width, BASIS), BF16),
            pltpu.VMEM((2, width, BASIS), BF16),
            pltpu.VMEM((2, 32, LANES), F32),
            pltpu.VMEM((2, 32, LANES), F32),
            pltpu.VMEM((2, LANES, units * UNIT), BF16),
            pltpu.VMEM((2, units * UNIT, LANES), BF16),
            pltpu.VMEM((2, units, width, UNIT), F32),
            pltpu.VMEM((2, units, UNIT, width), BF16),
            pltpu.VMEM((2, units // 2, UNIT, width), BF16),
            pltpu.VMEM((2, units, BASIS, LANES), BF16),
            pltpu.VMEM((2, units, BASIS, LANES), BF16),
            pltpu.VMEM((2, BASIS, LANES), F32),
            pltpu.SemaphoreType.DMA((hops,)),
            pltpu.SemaphoreType.DMA((hops,)),
            pltpu.SemaphoreType.DMA((7,)),
        ],
        compiler_params=pltpu.CompilerParams(
            collective_id=1, has_side_effects=True, vmem_limit_bytes=60 << 20
        ),
        name="forward",
    )(seg_lengths, source, packed, weight, out_weight, table, ff_in, ff_out)


def whole(shape):
    return pl.BlockSpec(shape, lambda i: (0,) * len(shape))


def finish_kernel(given_in, given_out, given_weight, given_qkv, grad_in, grad_out, grad_weight, grad_qkv):
    step = pl.program_id(0)
    grad_in[...] = given_in[...].astype(F32)
    grad_out[...] = given_out[...].astype(F32)
    width = grad_qkv.shape[1]
    for i in range(3):

        @pl.when(step == i)
        def _():
            grad_qkv[0] = given_qkv[:, i * width : (i + 1) * width].astype(F32).T

    @pl.when(step == 0)
    def _():
        narrow = grad_weight.shape[0] // given_weight.shape[0]
        for j in range(given_weight.shape[0]):
            grad_weight[j * narrow : (j + 1) * narrow] = given_weight[j].astype(F32)[:narrow]


def finish(given_in, given_out, given_weight, given_qkv, width):
    model, columns = given_in.shape
    hidden_part = given_out.shape[0]
    return pl.pallas_call(
        finish_kernel,
        grid=(3,),
        in_specs=[
            pl.BlockSpec((model // 3, columns), lambda i: (i, 0)),
            pl.BlockSpec((hidden_part // 3, model), lambda i: (i, 0)),
            pl.BlockSpec(given_weight.shape, lambda i: (0, 0, 0)),
            pl.BlockSpec(given_qkv.shape, lambda i: (0, 0)),
        ],
        out_specs=[
            pl.BlockSpec((model // 3, columns), lambda i: (i, 0)),
            pl.BlockSpec((hidden_part // 3, model), lambda i: (i, 0)),
            pl.BlockSpec((width, model), lambda i: (0, 0)),
            pl.BlockSpec((1, width, model), lambda i: (i, 0, 0)),
        ],
        out_shape=[
            jax.ShapeDtypeStruct((model, columns), F32), jax.ShapeDtypeStruct((hidden_part, model), F32),
            jax.ShapeDtypeStruct((width, model), F32), jax.ShapeDtypeStruct((3, width, model), F32),
        ],
        compiler_params=pltpu.CompilerParams(vmem_limit_bytes=62 << 20),
        name="finish",
    )(given_in, given_out, given_weight, given_qkv)


def middle_kernel(
    source, cotangent, mixed_0, mixed_1, mixed_2, mixed_3, own_weight, far_weight, vectors, in_bias, own_in, own_out,
    far_in, far_out, outputs, grad_residual, grad_mixed_0, grad_mixed_1, grad_mixed_2, grad_mixed_3, grad_in, grad_out,
    grad_out_weight, sums, grad_in_bias,
    residual, inverse, second, second_cols, total, grad_second, in_now, out_now, out_weight,
):
    r = pl.program_id(0)
    slices, rows = own_in.shape[0], own_in.shape[1]
    model = source.shape[1]
    hidden_part = own_in.shape[2]
    out_bias, gain, shift, last_bias = (vectors[k : k + 1] for k in range(18, 22))

    @pl.when(r == 0)
    def _():
        value = source[...].astype(F32) + out_bias
        out_weight[0] = own_weight[...]
        narrow = own_weight.shape[0] // slices
        for k in range(far_weight.shape[0]):
            parts = [far_weight[k, j].astype(F32)[:narrow] for j in range(slices)]
            out_weight[k + 1] = jnp.concatenate(parts, axis=0).astype(BF16)
        for k, mixed in enumerate((mixed_0, mixed_1, mixed_2, mixed_3)):
            value += dot(mixed[...], out_weight[k])
        residual[...] = value
        centred = value - jnp.mean(value, axis=-1, keepdims=True)
        factor = lax.rsqrt(jnp.mean(centred * centred, axis=-1, keepdims=True) + EPSILON)
        inverse[...] = factor
        normal = centred * factor
        grad_residual[...] = normal
        rounded = (normal * gain + shift).astype(BF16)
        second[...] = rounded
        second_cols[...] = rounded.astype(F32).T.astype(BF16)
        total[...] = jnp.zeros_like(total)
        grad_second[...] = jnp.zeros_like(grad_second)
        grad_in_bias[...] = jnp.zeros_like(grad_in_bias)
        for j in range(slices):
            in_now[j * rows : (j + 1) * rows] = own_in[j]
            out_now[j * rows : (j + 1) * rows] = own_out[j]

    @pl.when(r > 0)
    def _():
        for j in range(slices):
            in_now[j * rows : (j + 1) * rows] = far_in[0, j]
            out_now[j * rows : (j + 1) * rows] = far_out[0, j]

    half = hidden_part
    for t in range(1):
        span = slice(t * half, (t + 1) * half)
        hidden = dot(second[...], in_now[:, span]) + in_bias[r, 0:1, span]
        cube = hidden * hidden
        root = math.sqrt(2.0 / math.pi)
        bent = jnp.tanh(hidden * (root + (root * 0.044715) * cube))
        lifted = 0.5 + 0.5 * bent
        activation = (hidden * lifted).astype(BF16)
        slope = lifted + hidden * ((0.5 - 0.5 * bent * bent) * (root + (3.0 * root * 0.044715) * cube))
        total[...] += dot(activation, out_now[span])
        given = dot(cotangent[...], out_now[span], ((1,), (1,)))
        grad_hidden = (given * slope).astype(BF16)
        grad_second[...] += dot(grad_hidden, in_now[:, span], ((1,), (1,)))
        grad_in_bias[pl.ds(r, 1), span] = jnp.sum(grad_hidden.astype(F32), axis=0, keepdims=True)
        part = dot(activation, cotangent[...], ((0,), (0,))).astype(BF16)
        per = half // rows
        for k in range(per):
            grad_out[0, t * per + k] = part[k * rows : (k + 1) * rows]
        part = dot(second_cols[...], grad_hidden).astype(BF16)
        for j in range(slices):
            grad_in[0, j, :, span] = part[j * rows : (j + 1) * rows]

    @pl.when(r == pl.num_programs(0) - 1)
    def _():
        given = cotangent[...].astype(F32)
        outputs[...] = (residual[...] + total[...] + last_bias).astype(BF16)
        normal = grad_residual[...]
        grad = grad_second[...]
        scaled = grad * gain
        value = given + inverse[...] * (
            scaled
            - jnp.mean(scaled, axis=-1, keepdims=True)
            - normal * jnp.mean(scaled * normal, axis=-1, keepdims=True)
        )
        sums[0:1] = jnp.sum(value, axis=0, keepdims=True)
        sums[1:2] = jnp.sum(grad * normal, axis=0, keepdims=True)
        sums[2:3] = jnp.sum(grad, axis=0, keepdims=True)
        sums[3:4] = jnp.sum(given, axis=0, keepdims=True)
        sums[4:8] = jnp.zeros((4, model), F32)
        grad_residual[...] = value
        rounded = value.astype(BF16)
        grads = (grad_mixed_0, grad_mixed_1, grad_mixed_2, grad_mixed_3)
        for k, mixed in enumerate((mixed_0, mixed_1, mixed_2, mixed_3)):
            grads[k][...] = dot(rounded, out_weight[k], ((1,), (1,))).astype(BF16)
            product = dot(mixed[...], rounded, ((0,), (0,)))
            narrow = product.shape[0] // slices
            spare = jnp.zeros((grad_out_weight.shape[2] - narrow, model), F32)
            for j in range(slices):
                part = jnp.concatenate([product[j * narrow : (j + 1) * narrow], spare], axis=0)
                grad_out_weight[k, j] = part.astype(BF16)


def middle(source, cotangent, mixed, out_weight, far_weight, vectors, in_bias, own_in, own_out, far_in, far_out):
    own_rows, model = source.shape
    shards = far_in.shape[0] + 1
    slices, rows, hidden_part = own_in.shape
    narrow = mixed[0].shape
    far = pl.BlockSpec((1,) + own_in.shape, lambda r: (jnp.maximum(r - 1, 0), 0, 0, 0))
    part = pl.BlockSpec((1,) + own_in.shape, lambda r: (r, 0, 0, 0))
    macs = own_rows * model * (6 * shards * hidden_part + 3 * model)
    return pl.pallas_call(
        middle_kernel,
        grid_spec=pltpu.PrefetchScalarGridSpec(
            num_scalar_prefetch=0,
            grid=(shards,),
            in_specs=[whole(source.shape)] * 2 + [whole(narrow)] * 4 + [
                whole(out_weight.shape), whole(far_weight.shape), whole(vectors.shape), whole(in_bias.shape), whole(own_in.shape),
                whole(own_out.shape), far, far,
            ],
            out_specs=[whole(source.shape)] * 2 + [whole(narrow)] * 4 + [
                part, part, whole((shards,) + far_weight.shape[1:]), whole((8, model)), whole((shards, hidden_part))
            ],
            scratch_shapes=[
                pltpu.VMEM((own_rows, model), F32),
                pltpu.VMEM((own_rows, 1), F32),
                pltpu.VMEM((own_rows, model), BF16),
                pltpu.VMEM((model, own_rows), BF16),
                pltpu.VMEM((own_rows, model), F32),
                pltpu.VMEM((own_rows, model), F32),
                pltpu.VMEM((model, hidden_part), BF16),
                pltpu.VMEM((hidden_part, model), BF16),
                pltpu.VMEM((shards,) + narrow[1:] + (model,), BF16),
            ],
        ),
        out_shape=[
            jax.ShapeDtypeStruct(source.shape, BF16),
            jax.ShapeDtypeStruct(source.shape, F32),
        ] + [jax.ShapeDtypeStruct(narrow, BF16)] * 4 + [
            jax.ShapeDtypeStruct((shards, slices, rows, hidden_part), BF16),
            jax.ShapeDtypeStruct((shards, slices, rows, hidden_part), BF16),
            jax.ShapeDtypeStruct((shards,) + far_weight.shape[1:], BF16),
            jax.ShapeDtypeStruct((8, model), F32),
            jax.ShapeDtypeStruct((shards, hidden_part), F32),
        ],
        compiler_params=pltpu.CompilerParams(vmem_limit_bytes=60 << 20),
        cost_estimate=pl.CostEstimate(
            flops=2 * macs, bytes_accessed=30 << 20, transcendentals=own_rows * shards * hidden_part
        ),
        name="middle",
    )(source, cotangent, *mixed, out_weight, far_weight, vectors, in_bias, own_in, own_out, far_in, far_out)


def added(a, b):
    return (a.astype(F32) + b.astype(F32)).astype(BF16)


def backward_kernel(
    heads, seg_lengths, qkv, gm_0, gm_1, gm_2, gm_3, logsum, values, probes, key_states_in, key_end_in, rows_in, table_in,
    grad_in, grad_out, grad_weight, out, probe_grad, slice_in, slice_out, slice_weight,
    given, query_grad, memory_grad, row_grad, value_carried, value_back, value_in, row_back, row_in, carried, spread, key_grad, value_grad, cols, keys, vals,
    key_states, key_end, rows, table,
    keep_in, keep_out, keep_weight, core_in, core_out, core_weight, one_in, one_out, one_weight,
    two_in, two_out, two_weight, z_in, z_out, z_weight, send, recv, local_sems,
):
    units = qkv.shape[1]
    half = units // 2
    width = heads * HEAD_DIM
    root = 1.0 / math.sqrt(HEAD_DIM)
    z = lax.axis_index("head")
    flip, run = (z % 2) * half, z // 2
    place = lax.axis_index("dp") % 8
    y, x, c = place // 4, (place // 2) % 2, place % 2
    at = lambda b: (b + flip) % units
    starts, lengths, orders = segments_of(seg_lengths, run, units)
    greet((("head", 1), ("head", 2), ("head", 3), ("dp", 1), ("dp", 2), ("dp", 4)))
    hops = Hops(send, recv)
    started = []

    def go(*args):
        started.append(hops.start(*args))
        return started[-1]

    tables = set_out(
        [(key_states_in, key_states), (key_end_in, key_end), (rows_in, rows), (table_in, table)], local_sems, 12
    )
    given_copies = [go(gm_1, given.at[0, half:], "head", 1), go(gm_3, given.at[1, half:], "head", 1)]
    sums = (
        (grad_in, keep_in, core_in, one_in, two_in, z_in, True),
        (grad_weight, keep_weight, core_weight, one_weight, two_weight, z_weight, True),
        (grad_out, keep_out, core_out, one_out, two_out, z_out, False),
    )
    stage, local_copies = {}, {}
    for i, r in enumerate((2, 1, 3, 0)):
        stage[r], local_copies[r] = [], []
        for n, (term, keep, core, _, _, _, _) in enumerate(sums):
            stage[r].append(go(term.at[r, :, :, 1 - c], core.at[r], "dp", 1))
            copy = pltpu.make_async_copy(term.at[r, :, :, c], keep.at[r], local_sems.at[3 * i + n])
            copy.start()
            local_copies[r].append(copy)

    def first_hop(r):
        for n, (_, keep, core, one, _, _, along_x) in enumerate(sums):
            local_copies[r][n].wait()
            stage[r][n].wait_recv()
            keep[r] = added(keep[r], core[r])
            part = keep.at[r, :, 1 - x] if along_x else keep.at[r, 1 - y]
            stage[r][n] = go(part, one.at[r], "dp", 2 if along_x else 4)

    def second_hop(r):
        for n, (_, keep, _, one, two, _, along_x) in enumerate(sums):
            stage[r][n].wait_recv()
            kept = keep[r, :, x] if along_x else keep[r, y]
            one[r] = added(kept, one[r])
            part = one.at[r, 1 - y] if along_x else one.at[r, 1 - x]
            stage[r][n] = go(part, two.at[r], "dp", 4 if along_x else 2)

    def third_hop(r):
        for n, (_, _, _, one, two, far, along_x) in enumerate(sums):
            stage[r][n].wait_recv()
            kept = one[r, y] if along_x else one[r, x]
            two[r] = added(kept, two[r])
            if r:
                stage[r][n] = go(two.at[r], far.at[r - 1], "head", r)

    for k, own in enumerate((gm_0, gm_2)):
        given[k, :half] = own[...]
    mask = head_rows(heads, LANES)
    lane_head = lax.broadcasted_iota(jnp.int32, (UNIT, LANES), 1) // HEAD_DIM

    def given_of(k, b):
        return jnp.concatenate([given[k, at(b)], jnp.zeros((UNIT, LANES - width), BF16)], axis=1).astype(F32)

    def read_back(rel, k, carry):
        b = at(rel)
        query = qkv[k, rel, :, 0:LANES]
        full = given_of(k, b)
        probe = probes[k, b]
        logits = logits_of(probe, query)
        location, variance = read_parts(logits, heads)
        inverse = 1.0 / variance
        fall = -0.5 * inverse
        peak = WIDTH * lax.rsqrt(variance)
        centres = lax.broadcasted_iota(jnp.int32, (BASIS, UNIT), 0).astype(F32) / (BASIS - 1)
        along, across = [], []
        total = jnp.zeros((BASIS, LANES), F32)
        for h in range(heads):
            own_given = jnp.where(lane_head == h, full, 0.0).astype(BF16)
            gap = centres - location[h : h + 1]
            square = gap * gap
            density = jnp.exp(square * fall[h : h + 1]) * peak[h : h + 1]
            grad_density = dot(values[k, b], own_given, ((1,), (1,)))
            total += dot(density.astype(BF16), own_given)
            weighed = density * grad_density
            moment = weighed * gap
            zeroth = jnp.sum(weighed, axis=0, keepdims=True)
            first = jnp.sum(moment, axis=0, keepdims=True)
            second = jnp.sum(moment * gap, axis=0, keepdims=True)
            along.append(first * inverse[h : h + 1])
            across.append(0.5 * inverse[h : h + 1] * (second * inverse[h : h + 1] - zeroth))
        sigmoid = 1.0 / (1.0 + jnp.exp(-logits))
        grad_location = jnp.concatenate(along, axis=0) * location * (1.0 - location)
        grad_variance = jnp.concatenate(across, axis=0) * SPREAD * sigmoid[heads : 2 * heads]
        grad_logits = jnp.concatenate(
            [grad_location, grad_variance, jnp.zeros((8 - 2 * heads, UNIT), F32)], axis=0
        )
        padded = jnp.concatenate([grad_logits, jnp.zeros((120, UNIT), F32)], axis=0)
        probe_cols = jnp.concatenate([probe, jnp.zeros((120, LANES), F32)], axis=0).T
        query_grad[k, b] = dot(probe_cols.astype(BF16), padded.astype(BF16))[:width]
        fresh = jnp.where(mask, dot(grad_logits.astype(BF16), query), 0.0) * root
        memory_grad[k, b] = total
        row_grad[k, b] = fresh
        return carry

    def gather_back(k, carry):
        probe = jnp.zeros((8, BASIS), F32)
        for i in range(4):
            row_back[k, 8 * i : 8 * i + 8] = jnp.zeros((8, LANES), F32)
        for b in range(units - 1, -1, -1):
            fresh, total = row_grad[k, b], memory_grad[k, b]
            if b > 0:
                probe += dot(fresh.astype(BF16), key_states[k, b], ((1,), (1,)))
            for i in range(4):
                row_back[k, 8 * i : 8 * i + 8] += jnp.where(orders[b] == i, fresh, 0.0)
            if b < units - 1:
                ends = starts[b] + lengths[b] == b + 1
                total = jnp.where(ends, 0.0, memory_grad[k, b + 1]) + total
                memory_grad[k, b] = total
                row_grad[k, b] = jnp.where(ends, 0.0, row_grad[k, b + 1]) + fresh
            before = jnp.zeros((BASIS, LANES), F32) if b == units - 1 else value_carried[k]
            if b > 0:
                value_carried[k] = jnp.where(starts[b] == b, advance_values(table, before + total), before)
            else:
                value_back[k] = (before + total)[:, :width].T.astype(BF16)
        probe_grad[k] = probe
        return carry

    def attend_back(b, k, carry):
        query = qkv[k, at(b), :, 0:LANES].astype(F32) * root
        full = given_of(k, b)
        causal = lax.broadcasted_iota(jnp.int32, (UNIT, UNIT), 0) <= lax.broadcasted_iota(
            jnp.int32, (UNIT, UNIT), 1
        )
        away = [jnp.where(starts[b] <= j, 0.0, 1e30) for j in range(b)] + [0.0]
        owns = [jnp.where(lane_head == h, query, 0.0).astype(BF16) for h in range(heads)]
        own_givens = [jnp.where(lane_head == h, full, 0.0).astype(BF16) for h in range(heads)]
        own_all = jnp.concatenate(owns, axis=0)
        given_all = jnp.concatenate(own_givens, axis=0)
        seen = (b + 1) * UNIT
        scores = dot(keys[k, :seen], own_all, ((1,), (1,)))
        grad_probs = dot(vals[k, :seen], given_all, ((1,), (1,)))
        grads, probs = [], []
        for h in range(heads):
            prob_h, product_h = [], []
            inner = jnp.zeros((1, UNIT), F32)
            for j in range(b + 1):
                tile = (slice(j * UNIT, (j + 1) * UNIT), slice(h * UNIT, (h + 1) * UNIT))
                score = scores[tile]
                if j == b:
                    score = jnp.where(causal, score, -1e30)
                prob = jnp.exp(score - (logsum[k, b, h : h + 1] + away[j]))
                product = prob * grad_probs[tile]
                inner += jnp.sum(product, axis=0, keepdims=True)
                prob_h.append(prob)
                product_h.append(product)
            span = slice(h * HEAD_DIM, (h + 1) * HEAD_DIM)
            grad_h = [(product_h[j] - prob_h[j] * inner).astype(BF16) for j in range(b + 1)]
            result = dot(cols[k, span, :seen], jnp.concatenate(grad_h, axis=0))
            query_grad[k, b, span] = query_grad[k, b, span] + result * root
            grads.append(grad_h)
            probs.append([prob.astype(BF16) for prob in prob_h])
        fresh_keys = dot(jnp.concatenate([jnp.concatenate(g, axis=0) for g in grads], axis=1), own_all)
        fresh_vals = dot(jnp.concatenate([jnp.concatenate(p, axis=0) for p in probs], axis=1), given_all)
        for j in range(b + 1):
            part = slice(j * UNIT, (j + 1) * UNIT)
            if b == units - 1:
                key_grad[k, j], value_grad[k, j] = fresh_keys[part], fresh_vals[part]
            else:
                key_grad[k, j] += fresh_keys[part]
                value_grad[k, j] += fresh_vals[part]
        return carry

    def carry_back(k, total, units_before):
        moved = dot(table[...], total.astype(BF16))
        return moved[:BASIS], (moved[BASIS:] * term_scale(units_before)).astype(BF16)

    def end_back(k, carry):
        row = jnp.where(run == 0, row_in[k], 0.0)
        value = jnp.where(run == 0, value_in[k].astype(F32), 0.0).T
        grad_keys = dot(rows[k].astype(BF16), row.astype(BF16), ((0,), (0,)))
        total = jnp.concatenate([grad_keys, value, jnp.zeros((BASIS, LANES - width), F32)], axis=1)
        carried[k], spread[k] = carry_back(k, total, lengths[units - 1])
        seen = dot(row, key_end[k], ((1,), (1,)), HIGHEST)
        gained = seen[24:32]
        for i in (2, 1, 0):
            high = gained.astype(BF16)
            low = (gained - high.astype(F32)).astype(BF16)
            gained = dot(high, table[:BASIS]) + dot(low, table[:BASIS])
            gained = gained + seen[8 * i : 8 * i + 8]
        probe_grad[k] += gained
        return carry

    def finish(b, k, carry):
        start, length = starts[b], lengths[b]
        token = lax.broadcasted_iota(jnp.int32, (UNIT, LIVE), 0) + (b - start) * UNIT
        centre = (lax.broadcasted_iota(jnp.int32, (UNIT, LIVE), 1) + LIVE).astype(F32) / (BASIS - 1)
        gap = place_of(token, length) - centre
        psi = jnp.exp(gap * gap * (-0.5 / (WIDTH * WIDTH))).astype(BF16)
        pair_grad = dot(psi, spread[k])
        query_rows = query_grad[k, b].T.astype(BF16)
        out[k, at(b), :, :LANES] = jnp.concatenate([query_rows, jnp.zeros((UNIT, LANES - width), BF16)], axis=1)
        out[k, at(b), :, LANES : 2 * LANES] = (key_grad[k, b] + pair_grad[:, :LANES]).astype(BF16)
        out[k, at(b), :, 2 * LANES :] = (value_grad[k, b] + pair_grad[:, LANES:]).astype(BF16)
        if b > 0:
            grad_keys = dot(rows[k, 0:8].astype(BF16), row_grad[k, b].astype(BF16), ((0,), (0,)))
            total = carried[k] + jnp.concatenate([grad_keys, memory_grad[k, b]], axis=1)
            moved, spread_now = carry_back(k, total, lengths[b - 1])
            carried[k] = jnp.where(start == b, moved, carried[k])
            spread[k] = jnp.where(start == b, spread_now.astype(F32), spread[k].astype(F32)).astype(BF16)
        return carry

    def both(step, *args):
        lax.fori_loop(0, 2, functools.partial(step, *args), 0)

    def turn(k, carry):
        for b in range(units):
            part = slice(b * UNIT, (b + 1) * UNIT)
            keys[k, part] = qkv[k, at(b), :, LANES : 2 * LANES]
            vals[k, part] = qkv[k, at(b), :, 2 * LANES : 3 * LANES]
            cols[k, :, part] = qkv[k, at(b), :, LANES : 2 * LANES].astype(F32).T.astype(BF16)
        return carry

    lax.fori_loop(0, 2, turn, 0)
    both(read_back, 0)
    first_hop(2)
    both(read_back, 1)
    first_hop(1)
    for copy in given_copies:
        copy.wait_recv()
    both(read_back, 2)
    first_hop(3)
    first_hop(0)
    both(read_back, 3)
    for copy in tables:
        copy.wait()
    back_copies = []
    for k in range(2):
        gather_back(k, 0)
        back_copies += [
            go(value_back.at[k], value_in.at[1 - k], "head", 2), go(row_back.at[k], row_in.at[1 - k], "head", 2)
        ]
    second_hop(2)
    both(attend_back, 3)
    second_hop(1)
    second_hop(3)
    third_hop(2)
    both(attend_back, 2)
    second_hop(0)
    third_hop(1)
    third_hop(3)
    both(attend_back, 1)
    third_hop(0)
    both(attend_back, 0)
    for copy in back_copies:
        copy.wait_recv()
    lax.fori_loop(0, 2, end_back, 0)
    for b in range(units - 1, -1, -1):
        both(finish, b)
    for n, (_, _, _, _, two, far, _) in enumerate(sums):
        total = two[0].astype(F32)
        for r in (1, 2, 3):
            stage[r][n].wait_recv()
            total += far[r - 1].astype(F32)
        (slice_in, slice_weight, slice_out)[n][...] = total.astype(BF16)
    for copy in started:
        copy.wait_send()


def backward(seg_lengths, qkv, grad_mixed, logsum, values, probes, key_states, key_end, rows, grad_in, grad_out, grad_weight, heads):
    units = qkv.shape[1]
    width = heads * HEAD_DIM
    table = jnp.asarray(basis_tables()[1])
    vmem, anywhere = pl.BlockSpec(memory_space=pltpu.VMEM), pl.BlockSpec(memory_space=pl.ANY)
    shape = jax.ShapeDtypeStruct
    slices = [grad_in.shape[4:], grad_out.shape[4:], grad_weight.shape[4:]]
    hops = 2 + 3 * 4 * 3 + 3 * 3 + 4
    return pl.pallas_call(
        functools.partial(backward_kernel, heads),
        in_specs=[pl.BlockSpec(memory_space=pltpu.SMEM)] + [vmem] * 8 + [anywhere] * 7,
        out_specs=[vmem] * 5,
        out_shape=[shape(qkv.shape, BF16), shape((2, 8, BASIS), F32)] + [shape(part, BF16) for part in slices],
        scratch_shapes=[
            pltpu.VMEM((2, units, UNIT, width), BF16),
            pltpu.VMEM((2, units, width, UNIT), F32),
            pltpu.VMEM((2, units, BASIS, LANES), F32),
            pltpu.VMEM((2, units, 8, LANES), F32),
            pltpu.VMEM((2, BASIS, LANES), F32),
            pltpu.VMEM((2, width, BASIS), BF16),
            pltpu.VMEM((2, width, BASIS), BF16),
            pltpu.VMEM((2, 32, LANES), F32),
            pltpu.VMEM((2, 32, LANES), F32),
            pltpu.VMEM((2, BASIS, 2 * LANES), F32),
            pltpu.VMEM((2, LIVE, 2 * LANES), BF16),
            pltpu.VMEM((2, units, UNIT, LANES), F32),
            pltpu.VMEM((2, units, UNIT, LANES), F32),
            pltpu.VMEM((2, LANES, units * UNIT), BF16),
            pltpu.VMEM((2, units * UNIT, LANES), BF16),
            pltpu.VMEM((2, units * UNIT, LANES), BF16),
            pltpu.VMEM(key_states.shape, BF16),
            pltpu.VMEM(key_end.shape, F32),
            pltpu.VMEM(rows.shape, F32),
            pltpu.VMEM(table.shape, BF16),
        ]
        + [pltpu.VMEM((4, 2, 2) + part, BF16) for part in slices]
        + [pltpu.VMEM((4, 2, 2) + part, BF16) for part in slices]
        + [pltpu.VMEM((4, 2) + part, BF16) for part in slices]
        + [pltpu.VMEM((4,) + part, BF16) for part in slices]
        + [pltpu.VMEM((3,) + part, BF16) for part in slices]
        + [
            pltpu.SemaphoreType.DMA((hops,)),
            pltpu.SemaphoreType.DMA((hops,)),
            pltpu.SemaphoreType.DMA((16,)),
        ],
        compiler_params=pltpu.CompilerParams(
            collective_id=2, has_side_effects=True, vmem_limit_bytes=62 << 20
        ),
        name="backward",
    )(
        seg_lengths, qkv, *grad_mixed, logsum, values, probes, key_states, key_end, rows, table, grad_in, grad_out, grad_weight
    )


def tail_kernel(
    heads, outer, grads, flat_a, flat_b, packed, slice_in, slice_out, slice_weight, sums, in_bias_part, probe_grad,
    first_cols_in, grad_residual_in, source_in, input_grad, whole_in, whole_out, whole_weight, whole_qkv, shared_out, owned_out,
    row_grad, near, kept, part_a, part_b, core_a, core_b, one_a, one_b, two_a, two_b, far_b, total, outer_in,
    gather_in, gather_out, gather_weight, gather_qkv,
    shared, shared_in, block, block_in, bias_block, bias_in, joined, joined_in, first_cols, grad_residual, source,
    send, recv, local_sems,
):
    own_rows, model = source.shape
    loads = set_out(
        [(first_cols_in, first_cols), (grad_residual_in, grad_residual), (source_in, source)], local_sems, 0
    )
    units = grads.shape[1]
    half = units // 2
    width = heads * HEAD_DIM
    z = lax.axis_index("head")
    place = lax.axis_index("dp") % 8
    y, x, c = place // 4, (place // 2) % 2, place % 2
    rows = model // 8
    greet(
        (("head", 1), ("head", 2), ("head", 3), ("dp", 1), ("dp", 2), ("dp", 4)) + tuple(("dp", bit) for bit in outer)
    )
    hops = Hops(send, recv)
    started = []

    def go(*args):
        started.append(hops.start(*args))
        return started[-1]

    def row_of(rel):
        return dot(grads[0, rel], flat_a[...]) + dot(grads[1, rel], flat_b[...])

    row_copies = []
    for k in range(half):
        row_grad[k] = row_of(half + k).astype(BF16)
        row_copies.append(go(row_grad.at[k], near.at[k], "head", 1))

    gathers = ((slice_in, gather_in, True), (slice_weight, gather_weight, True), (slice_out, gather_out, False))
    for own, gather, _ in gathers:
        gather[y, x, c] = own[...]

    def spread_first(gather, along_x):
        part = gather.at[y, x, c]
        return go(part, part, "dp", 2 if along_x else 4)

    def spread_second(gather, along_x):
        part = gather.at[y, :, c] if along_x else gather.at[:, x, c]
        return go(part, part, "dp", 4 if along_x else 2)

    def spread_third(gather):
        part = gather.at[:, :, c]
        return go(part, part, "dp", 1)

    spreads = [spread_first(gather, along_x) for _, gather, along_x in gathers]

    loads[0].wait()
    core_copies = []
    for k, part, core in ((1, part_b, core_b), (0, part_a, core_a)):
        product = dot(first_cols[...], grads[k].reshape(2 * own_rows, 3 * LANES))
        product = jnp.concatenate([product[:, i * LANES : i * LANES + width] for i in range(3)], axis=1).astype(BF16)
        for j in range(8):
            part[j // 4, (j // 2) % 2, j % 2] = product[j * rows : (j + 1) * rows]
        core_copies.append(go(part.at[:, :, 1 - c], core, "dp", 1))
    for k in range(half):
        kept[k] = row_of(k)

    core_copies[0].wait_recv()
    core_b[...] = added(part_b[:, :, c], core_b[...])
    one_copy_b = go(core_b.at[1 - y], one_b, "dp", 4)
    core_copies[1].wait_recv()
    core_a[...] = added(part_a[:, :, c], core_a[...])
    one_copy_a = go(core_a.at[:, 1 - x], one_a, "dp", 2)

    bias_a = jnp.sum(grads[0].reshape(2 * own_rows, 3 * LANES).astype(F32), axis=0, keepdims=True)
    bias_b = jnp.sum(grads[1].reshape(2 * own_rows, 3 * LANES).astype(F32), axis=0, keepdims=True)
    edge = jnp.zeros((8, model - BASIS), F32)
    fill = jnp.zeros((6, model), F32)
    for k, bias in ((0, bias_a), (1, bias_b)):
        block[k, 0:8] = jnp.concatenate([probe_grad[k], edge], axis=1)
        block[k, 8:16] = jnp.concatenate([bias, in_bias_part[2 * k : 2 * k + 1], fill], axis=0)
        bias_block[k] = jnp.concatenate([in_bias_part[2 * k + 1 : 2 * k + 2], jnp.zeros((7, model), F32)], axis=0)
    block_copy = go(block.at[1], block_in, "head", 2)
    bias_copies = [go(bias_block.at[0], bias_in.at[0], "head", 1), go(bias_block.at[1], bias_in.at[1], "head", 3)]

    loads[1].wait()
    loads[2].wait()
    value = source[...].astype(F32)
    centred = value - jnp.mean(value, axis=-1, keepdims=True)
    factor = lax.rsqrt(jnp.mean(centred * centred, axis=-1, keepdims=True) + EPSILON)
    normal = centred * factor

    one_copy_b.wait_recv()
    one_b[...] = added(core_b[y], one_b[...])
    two_copy_b = go(one_b.at[1 - x], two_b, "dp", 2)
    one_copy_a.wait_recv()
    one_a[...] = added(core_a[:, x], one_a[...])
    two_copy_a = go(one_a.at[1 - y], two_a, "dp", 4)
    spreads = [copy.wait_recv() or spread_second(gather, along_x) for copy, (_, gather, along_x) in zip(spreads, gathers)]
    for copy in row_copies:
        copy.wait_recv()
    two_copy_b.wait_recv()
    two_b[...] = added(one_b[x], two_b[...])
    far_copy = go(two_b, far_b, "head", 2)

    grad = kept[...].reshape(own_rows, model) + near[...].reshape(own_rows, model).astype(F32)
    scaled = grad * packed[16:17]
    change = factor * (
        scaled
        - jnp.mean(scaled, axis=-1, keepdims=True)
        - normal * jnp.mean(scaled * normal, axis=-1, keepdims=True)
    )
    input_grad[...] = (grad_residual[...] + change).astype(BF16)
    shared[...] = jnp.concatenate(
        [jnp.sum(grad * normal, axis=0, keepdims=True), jnp.sum(grad, axis=0, keepdims=True), sums[0:6]], axis=0
    )
    shared_copies = [go(shared, shared_in.at[r - 1], "head", r) for r in (1, 2, 3)]

    two_copy_a.wait_recv()
    own_sum = added(one_a[y], two_a[...]).astype(F32)
    far_copy.wait_recv()
    total[0] = (own_sum + far_b[...].astype(F32)).astype(BF16)
    for n, bit in enumerate(outer):
        copy = go(total.at[n], outer_in.at[n], "dp", bit)
        copy.wait_recv()
        total[n + 1] = added(total[n], outer_in[n])
    gather_qkv[y, x, c] = total[len(outer)]
    cut = rows // 2
    upper, lower = pl.ds(0, cut), pl.ds(cut, cut)
    qkv_parts = [gather_qkv.at[y, x, c, upper], gather_qkv.at[y, x, c, lower]]
    qkv_copies = [go(qkv_parts[0], qkv_parts[0], "dp", 2), go(qkv_parts[1], qkv_parts[1], "dp", 4)]

    block_copy.wait_recv()
    for copy in bias_copies + shared_copies:
        copy.wait_recv()
    owned = block[0] + block_in[...]
    bias_rows = bias_in[0] + bias_in[1]
    owned_rows = jnp.concatenate([owned[8:9], owned[9:10] + bias_rows[0:1], owned[10:16]], axis=0)
    joined[0] = jnp.concatenate(
        [shared[...] + shared_in[0] + shared_in[1] + shared_in[2], owned[0:8], owned_rows], axis=0
    )
    spreads = [copy.wait_recv() or spread_third(gather) for copy, (_, gather, _) in zip(spreads, gathers)]
    for n, bit in enumerate((2, 4, 1) + outer):
        copy = go(joined.at[n], joined_in.at[n], "dp", bit)
        if n == 1:
            for copy_one in qkv_copies:
                copy_one.wait_recv()
            qkv_parts = [gather_qkv.at[y, :, c, upper], gather_qkv.at[:, x, c, lower]]
            qkv_copies = [go(qkv_parts[0], qkv_parts[0], "dp", 4), go(qkv_parts[1], qkv_parts[1], "dp", 2)]
        copy.wait_recv()
        joined[n + 1] = joined[n] + joined_in[n]
    last = joined[3 + len(outer)]
    shared_out[...] = last[0:8]
    owned_out[...] = last[8:24]
    saves = []
    for copy, (_, gather, _), out in zip(spreads, gathers, (whole_in, whole_weight, whole_out)):
        copy.wait_recv()
        saves += set_out([(gather, out)], local_sems, 3 + len(saves))
    for copy in qkv_copies:
        copy.wait_recv()
    spread_third(gather_qkv).wait_recv()
    saves += set_out([(gather_qkv, whole_qkv)], local_sems, 6)
    for copy in saves:
        copy.wait()
    for copy in started:
        copy.wait_send()


def tail(grads, first_cols, flat_a, flat_b, grad_residual, source, packed, slices, sums, in_bias_part, probe_grad, outer, heads):
    own_rows, model = source.shape
    units = grads.shape[1]
    rows = model // 8
    vmem = pl.BlockSpec(memory_space=pltpu.VMEM)
    shape = jax.ShapeDtypeStruct
    slice_in, slice_out, slice_weight = slices
    plane = lambda part: (2, 2, 2) + part
    part = (rows, 3 * heads * HEAD_DIM)
    hops = units // 2 + 9 + 2 + 2 + 2 + 1 + 5 + 1 + 2 + 3 + 3 + 2 * len(outer)
    return pl.pallas_call(
        functools.partial(tail_kernel, heads, outer),
        in_specs=[vmem] * 10 + [pl.BlockSpec(memory_space=pl.ANY)] * 3,
        out_specs=[vmem] + [pl.BlockSpec(memory_space=pl.ANY)] * 4 + [vmem] * 2,
        out_shape=[
            shape(source.shape, BF16), shape(plane(slice_in.shape), BF16), shape(plane(slice_out.shape), BF16),
            shape(plane(slice_weight.shape), BF16), shape(plane(part), BF16), shape((8, model), F32),
            shape((16, model), F32),
        ],
        scratch_shapes=[
            pltpu.VMEM((units // 2, UNIT, model), BF16),
            pltpu.VMEM((units // 2, UNIT, model), BF16),
            pltpu.VMEM((units // 2, UNIT, model), F32),
            pltpu.VMEM(plane(part), BF16),
            pltpu.VMEM(plane(part), BF16),
            pltpu.VMEM((2, 2) + part, BF16),
            pltpu.VMEM((2, 2) + part, BF16),
            pltpu.VMEM((2,) + part, BF16),
            pltpu.VMEM((2,) + part, BF16),
            pltpu.VMEM(part, BF16),
            pltpu.VMEM(part, BF16),
            pltpu.VMEM(part, BF16),
            pltpu.VMEM((1 + len(outer),) + part, BF16),
            pltpu.VMEM((max(1, len(outer)),) + part, BF16),
            pltpu.VMEM(plane(slice_in.shape), BF16),
            pltpu.VMEM(plane(slice_out.shape), BF16),
            pltpu.VMEM(plane(slice_weight.shape), BF16),
            pltpu.VMEM(plane(part), BF16),
            pltpu.VMEM((8, model), F32),
            pltpu.VMEM((3, 8, model), F32),
            pltpu.VMEM((2, 16, model), F32),
            pltpu.VMEM((16, model), F32),
            pltpu.VMEM((2, 8, model), F32),
            pltpu.VMEM((2, 8, model), F32),
            pltpu.VMEM((4 + len(outer), 24, model), F32),
            pltpu.VMEM((3 + len(outer), 24, model), F32),
            pltpu.VMEM(first_cols.shape, BF16),
            pltpu.VMEM(grad_residual.shape, F32),
            pltpu.VMEM(source.shape, BF16),
            pltpu.SemaphoreType.DMA((hops,)),
            pltpu.SemaphoreType.DMA((hops,)),
            pltpu.SemaphoreType.DMA((7,)),
        ],
        compiler_params=pltpu.CompilerParams(
            collective_id=3, has_side_effects=True, vmem_limit_bytes=60 << 20
        ),
        name="tail",
    )(
        grads, flat_a, flat_b, packed, slice_in, slice_out, slice_weight, sums, in_bias_part, probe_grad, first_cols,
        grad_residual, source,
    )


def exchange(value, axis, bit):
    size = lax.axis_size(axis)
    return lax.ppermute(value, axis, [(j, j ^ bit) for j in range(size)])


def local(
    inputs, seg_lengths, ln1_gain, ln1_bias, qkv_weight, qkv_bias, out_weight, out_bias, mem_mu, mem_sig,
    ln2_gain, ln2_bias, ff_in, ff_in_bias, ff_out, ff_out_bias, cotangent,
):
    own_rows, model = inputs.shape
    shards = lax.axis_size("head")
    members = lax.axis_size("dp")
    width = qkv_weight.shape[2]
    heads = width // HEAD_DIM
    hidden_part = ff_in.shape[1]
    units = 2 * own_rows // UNIT
    slices = 8
    outer = tuple(1 << k for k in range(3, 16) if 1 << k < members)
    rows = model // slices

    bias_row = jnp.pad(qkv_bias, ((0, 0), (0, LANES - width))).reshape(1, 3 * LANES)
    edge = 3 * LANES - BASIS
    packed = jnp.pad(bias_row, ((0, 23), (0, 0))).astype(F32)
    packed += jnp.pad(mem_mu, ((1, 23 - heads), (0, edge))).astype(F32)
    packed += jnp.pad(mem_sig, ((1 + heads, 23 - 2 * heads), (0, edge))).astype(F32)
    given = (ln1_gain, ln1_bias, out_bias, ln2_gain, ln2_bias, ff_out_bias, ff_in_bias)
    line = sum(jnp.pad(vector.astype(F32), (k * model, (6 - k) * model)) for k, vector in enumerate(given))
    packed += jnp.pad(line.reshape(7, model), ((16, 1), (0, 0)))

    turned_weight = jnp.transpose(qkv_weight, (1, 2, 0)).reshape(3 * width, model)
    (
        qkv, first_cols, flat_a, flat_b, values, key_states, key_end, logsum, probes, state_rows,
        *mixed, in_bias, far_in, far_out, far_weight,
    ) = forward(seg_lengths, inputs, packed, turned_weight, out_weight, ff_in, ff_out, heads)
    flat = lambda array: array.reshape((shards - 1, slices) + array.shape[4:])
    outputs, grad_residual, *rest = middle(
        inputs, cotangent, mixed, out_weight, flat(far_weight), packed, in_bias,
        ff_in.reshape(slices, rows, hidden_part), ff_out.reshape(slices, rows, model), flat(far_in), flat(far_out),
    )
    grad_mixed, (ff_in_part, ff_out_part, out_weight_part, sums, in_bias_part) = rest[:4], rest[4:]
    paired = [part.reshape(units // 2, UNIT, width) for part in grad_mixed]
    plane = lambda array: array.reshape((shards, 2, 2, 2) + array.shape[2:])
    grads, probe_grad, *parts = backward(
        seg_lengths, qkv, paired, logsum, values, probes, key_states, key_end, state_rows, plane(ff_in_part),
        plane(ff_out_part), plane(out_weight_part), heads,
    )
    for bit in outer:
        parts = [added(part, exchange(part, "dp", bit)) for part in parts]
    input_grad, whole_in, whole_out, whole_weight, whole_qkv, shared, owned = tail(
        grads, first_cols, flat_a, flat_b, grad_residual, inputs, packed, parts, sums, in_bias_part, probe_grad,
        outer, heads,
    )
    ff_in_sum, ff_out_sum, out_weight_sum, qkv_weight_sum = finish(
        whole_in.reshape(model, hidden_part), whole_out.reshape(hidden_part, model),
        whole_weight.reshape((slices,) + whole_weight.shape[3:]), whole_qkv.reshape(model, 3 * width), width,
    )
    return (
        outputs, input_grad, shared[0], shared[1], jnp.transpose(qkv_weight_sum, (2, 0, 1)),
        owned[8].reshape(3, LANES)[:, :width], out_weight_sum, shared[2], owned[:heads, :BASIS],
        owned[heads : 2 * heads, :BASIS], shared[3], shared[4], ff_in_sum, owned[9, :hidden_part], ff_out_sum, shared[5],
    )


def solution(mesh):
    rows, whole = P(("dp", "head"), None), P()
    return jax.shard_map(
        local,
        mesh=mesh,
        in_specs=(
            rows, P("dp", None), whole, whole, P(None, None, "head"), P(None, "head"), P("head", None), whole,
            P("head", None), P("head", None), whole, whole, P(None, "head"), P("head"), P("head", None), whole, rows,
        ),
        out_specs=(
            rows, rows, whole, whole, P(None, None, "head"), P(None, "head"), P("head", None), whole,
            P("head", None), P("head", None), whole, whole, P(None, "head"), P("head"), P("head", None), whole,
        ),
        check_vma=False,
    )
```
